32 devices in a mesh: fsdp: 8 (over z, core), dp: 4 (over y, x).
Axes of the slice: x: 2, y: 2, z: 4, core: 2. Of those that a mesh axis runs over, the one named last changes fastest.
Arguments:
- tokens: bfloat16 [8192, 1536], P(('fsdp', 'dp')), may hold values from -6 to 6
- w_query: bfloat16 [1536, 1536], P('fsdp'), may hold values from -0.15625 to 0.15625
- key_weight: bfloat16 [1536, 512], P('fsdp'), may hold values from -0.15625 to 0.15625
- value_weight: bfloat16 [1536, 512], P('fsdp'), may hold values from -0.15625 to 0.15625
- w_out: bfloat16 [1536, 1536], P('fsdp'), may hold values from -1.25 to 1.25
- gain_attn: bfloat16 [1536], P('fsdp'), may hold values from 0.099609375 to 1.8984375
- gain_ffn: bfloat16 [1536], P('fsdp'), may hold values from 0.099609375 to 1.8984375
- w_router: bfloat16 [1536, 16], P('fsdp'), may hold values from -0.078125 to 0.078125
- w_gate: bfloat16 [16, 1536, 512], P('fsdp'), may hold values from -0.15625 to 0.15625
- w_up: bfloat16 [16, 1536, 512], P('fsdp'), may hold values from -0.15625 to 0.15625
- w_down: bfloat16 [16, 512, 1536], P('fsdp'), may hold values from -0.75 to 0.75
- routes: int32 [8192, 8], P(('fsdp', 'dp')), may hold values from 0 to 15, all different within a row; in each aligned block of 256 rows (0 to 255, 256 to 511, ...) at most 144 rows name the same one
- cotangent: bfloat16 [8192, 1536], P(('fsdp', 'dp')), may hold values from -6 to 6
Outputs:
- output: bfloat16 [8192, 1536], P(('fsdp', 'dp'))
- grad_tokens: bfloat16 [8192, 1536], P(('fsdp', 'dp'))
- grad_w_query: float32 [1536, 1536], P('fsdp')
- grad_w_key: float32 [1536, 512], P('fsdp')
- grad_w_value: float32 [1536, 512], P('fsdp')
- grad_w_out: float32 [1536, 1536], P('fsdp')
- grad_gain_attn: float32 [1536], P('fsdp')
- grad_gain_ffn: float32 [1536], P('fsdp')
- grad_w_router: float32 [1536, 16], P('fsdp')
- grad_w_gate: float32 [16, 1536, 512], P('fsdp')
- grad_w_up: float32 [16, 1536, 512], P('fsdp')
- grad_w_down: float32 [16, 512, 1536], P('fsdp')
The draws below stay inside these ranges and needn't reach their ends.
Inputs may be any that keep to these rules, and one draw needn't show every extreme that they name: `routes`: each row names 8 different experts. In each aligned block of 256 rows (the tokens of one sequence) no expert is named by more than 144 rows, and in some such blocks one expert is named by exactly 144 rows.
All inputs are finite; a program needn't handle non-finite values.
Results may differ from the reference program's by a relative error of at most 0.022.
Values may be sent and summed in bfloat16 or wider, within the bound.
A program may use at most 256 MiB of HBM per device.

```python
import math
import jax
import jax.numpy as jnp
import numpy as np
from jax import lax

MODEL_WIDTH = 1536
QUERY_HEADS = 24
KEY_VALUE_HEADS = 8
HEAD_SIZE = 64
FF = 512
TOP = 8
TOK_DEV = 256
EXPERTS = 16
CAP = 144
TOKENS = 8192


def levels(own_key, dims, pieces, least, largest):
    def one(axis_at, blocks):
        draws = jax.random.uniform(jax.random.fold_in(jax.random.fold_in(own_key, 6), axis_at), (blocks,), jnp.float32, least / len(pieces), largest / len(pieces))
        return jnp.repeat(jnp.exp(draws), dims[axis_at] // blocks).reshape((-1,) + (1,) * (len(dims) - axis_at - 1))

    gain = one(*pieces[0])
    for cut in pieces[1:]:
        gain = gain * one(*cut)
    return gain


def routed_block(own_key, own, number, rows, number_of, top, reach, slope):
    ranking = jax.random.permutation(own_key, number_of)
    heavy_load, common = shares(number_of, rows * top, reach, slope, True), shares(number_of, rows * top, reach, slope, False)
    places = jnp.arange(number_of)

    def named(lengths, rotation):
        used = int((lengths > 0).sum())
        fixed = max(1, used // 4)
        moved = fixed + (places - fixed + rotation * (used - fixed)) % max(1, number_of - fixed)
        return jnp.zeros((number_of,), jnp.int32).at[ranking[jnp.where(places < fixed, places, moved)]].set(jnp.asarray(lengths, jnp.int32))

    lengths = jnp.where(number % 4 == 0, named(heavy_load, number // 4), named(common, number - number // 4 - 1))
    mixed = jax.random.permutation(jax.random.fold_in(own, 3), number_of)
    giver, sink = mixed[0:number_of // 2 * 2:2], mixed[1:number_of // 2 * 2:2]
    room = jnp.minimum(lengths[giver] - 1, reach - lengths[sink]) // 2
    room = jnp.where((giver == ranking[0]) | (sink == ranking[0]) | (lengths[sink] == 0), 0, jnp.maximum(room, 0))
    moved = jax.random.randint(jax.random.fold_in(own, 4), (number_of // 2,), 0, 1 << 20) % (room + 1)
    lengths = lengths.at[giver].add(-moved).at[sink].add(moved)
    members = jnp.searchsorted(jnp.cumsum(lengths), jnp.arange(rows * top), side="right").astype(jnp.int32)
    table = members.reshape(top, rows).T
    table = table[jax.random.permutation(jax.random.fold_in(own, 1), rows)]
    rotation = jax.random.randint(jax.random.fold_in(own, 2), (rows, 1), 0, top)
    return jnp.take_along_axis(table, (jnp.arange(top)[None, :] + rotation) % top, axis=1)


def shares(amount, total, most, skew, full):
    weights = [(1 << 20) // math.isqrt(grade ** skew) + 1 for grade in range(1, amount + 1)]
    largest = most if full else min(most, max(-(-total // amount), total * weights[0] // sum(weights)))
    least = 1 if total - largest >= amount - 1 else 0
    holding, rest = [largest] + [least] * (amount - 1), total - largest - least * (amount - 1)
    while rest > 0:
        candidates = [i for i in range(1, amount) if holding[i] < largest] or [i for i in range(1, amount) if holding[i] < most]
        pool, budget = sum([weights[i] for i in candidates]), rest
        for i in candidates:
            addition = min(most - holding[i], max(1, budget * weights[i] // pool), rest)
            holding[i] = holding[i] + addition
            rest = rest - addition
    return np.array(holding)


def centred(own_key, shape, spread, most, pieces=(), kind=jnp.bfloat16):
    values = jax.random.normal(own_key, shape, jnp.float32) * spread
    if len(pieces) > 0:
        values = levels(own_key, shape, pieces, -0.22, 0.18) * values
    return jnp.clip(values, min=-most, max=most).astype(kind)


def setup_inputs(seed: int = 0) -> dict:
    streams_of = jax.random.split(jax.random.key(seed), 14)
    tokens = centred(streams_of[0], (TOKENS, MODEL_WIDTH), 1.0, 6.0, ((0, 32),))
    w_query = centred(streams_of[1], (MODEL_WIDTH, QUERY_HEADS * HEAD_SIZE), MODEL_WIDTH ** -0.5, 0.15625, ((0, 8),))
    key_weight = centred(streams_of[2], (MODEL_WIDTH, KEY_VALUE_HEADS * HEAD_SIZE), MODEL_WIDTH ** -0.5, 0.15625, ((0, 8),))
    value_weight = centred(streams_of[3], (MODEL_WIDTH, KEY_VALUE_HEADS * HEAD_SIZE), MODEL_WIDTH ** -0.5, 0.15625, ((0, 8),))
    w_out = centred(streams_of[4], (QUERY_HEADS * HEAD_SIZE, MODEL_WIDTH), (max(QUERY_HEADS * HEAD_SIZE // 64, 1)) ** -0.5, 1.25, ((0, 8),))
    gain_attn = jnp.clip(1.0 + 0.18 * jax.random.normal(streams_of[5], (MODEL_WIDTH,), jnp.float32), 0.099609375, 1.8984375).astype(jnp.bfloat16)
    gain_ffn = jnp.clip(1.0 + 0.18 * jax.random.normal(streams_of[6], (MODEL_WIDTH,), jnp.float32), 0.099609375, 1.8984375).astype(jnp.bfloat16)
    w_router = centred(streams_of[7], (MODEL_WIDTH, EXPERTS), (4 * MODEL_WIDTH) ** -0.5, 0.078125, ((0, 8),))
    w_gate = centred(streams_of[8], (EXPERTS, MODEL_WIDTH, FF), MODEL_WIDTH ** -0.5, 0.15625, ((0, 8),))
    w_up = centred(streams_of[9], (EXPERTS, MODEL_WIDTH, FF), MODEL_WIDTH ** -0.5, 0.15625, ((0, 8),))
    w_down = centred(streams_of[10], (EXPERTS, FF, MODEL_WIDTH), (max(FF // 8, 1)) ** -0.5, 0.75, ((0, 8),))
    routes_keys = jax.random.split(jax.random.fold_in(streams_of[11], 1), TOKENS // TOK_DEV)
    routes_turns = jax.random.permutation(jax.random.fold_in(streams_of[11], 3), TOKENS // TOK_DEV)
    routes = jax.vmap(lambda own, number: routed_block(jax.random.fold_in(streams_of[11], 2), own, number, TOK_DEV, EXPERTS, TOP, CAP, 1))(routes_keys, routes_turns).reshape((TOKENS, TOP))
    cotangent = centred(streams_of[12], (TOKENS, MODEL_WIDTH), 1.0, 6.0, ((0, 32),))
    return dict(tokens=tokens, w_query=w_query, key_weight=key_weight, value_weight=value_weight, w_out=w_out, gain_attn=gain_attn, gain_ffn=gain_ffn, w_router=w_router, w_gate=w_gate, w_up=w_up, w_down=w_down, routes=routes, cotangent=cotangent)


EPSILON = 1e-06
ROPE_BASE = 10000.0
MASKED = -1e+30

@jax.custom_vjp
def lower_precision(v):
    return lax.optimization_barrier(v.astype(jnp.bfloat16)).astype(jnp.float32)

@jax.custom_vjp
def lower_backward(v):
    return v

def low_keep(v):
    return (lower_precision(v), None)

def low_pass(kept, grad):
    return (grad,)

def back_keep(v):
    return (v, None)

def back_low(kept, grad):
    return (lower_precision(grad),)
lower_precision.defvjp(low_keep, low_pass)
lower_backward.defvjp(back_keep, back_low)

def rope_tables(sequence_length):
    half_size = HEAD_SIZE // 2
    positions = jnp.arange(sequence_length, dtype=jnp.float32)
    frequency = ROPE_BASE ** (-2.0 * jnp.arange(half_size, dtype=jnp.float32) / HEAD_SIZE)
    angles = positions[:, None] * frequency[None, :]
    return (jnp.cos(angles)[:, None, :], jnp.sin(angles)[:, None, :])

def apply_rotary(values, cosine_table, sine_table):
    half_size = values.shape[-1] // 2
    first_half = values[..., :half_size]
    second_half = values[..., half_size:]
    return jnp.concatenate([first_half * cosine_table - second_half * sine_table, first_half * sine_table + second_half * cosine_table], -1)

def destinations(route_ids):
    onehot = (route_ids[:, :, None] == jnp.arange(EXPERTS, dtype=jnp.int32)[None, None, :]).astype(jnp.int32)
    counts = lax.optimization_barrier(jnp.sum(onehot, 1)).astype(jnp.int32)
    before = (jnp.cumsum(counts, 0) - counts).astype(jnp.int32)
    slot_ids = jnp.take_along_axis(before, route_ids, 1).astype(jnp.int32)
    return (route_ids * CAP + slot_ids).astype(jnp.int32)

def layer(tokens_f, query_w, key_matrix, value_matrix, out_w, gain_one, gain_two, router_w, gate_w, up_w, down_w, route_ids, target_rows):
    highest_precision = lax.Precision.HIGHEST
    sequence_length = tokens_f.shape[0]
    normed_one = tokens_f * lax.rsqrt(lax.optimization_barrier(jnp.mean(tokens_f * tokens_f, -1, keepdims=True)) + EPSILON)
    attention_input = lower_precision(normed_one * gain_one)
    query_projected = lower_backward(jnp.dot(attention_input, query_w, precision=highest_precision)).reshape(sequence_length, QUERY_HEADS, HEAD_SIZE)
    key_projected = lower_backward(jnp.dot(attention_input, key_matrix, precision=highest_precision)).reshape(sequence_length, KEY_VALUE_HEADS, HEAD_SIZE)
    value_per_head = lower_precision(lower_backward(jnp.dot(attention_input, value_matrix, precision=highest_precision))).reshape(sequence_length, KEY_VALUE_HEADS, HEAD_SIZE)
    cosine_table, sine_table = rope_tables(sequence_length)
    query_rotated = lower_precision(apply_rotary(query_projected, cosine_table, sine_table)).reshape(sequence_length, KEY_VALUE_HEADS, QUERY_HEADS // KEY_VALUE_HEADS, HEAD_SIZE)
    key_rot = lower_precision(apply_rotary(key_projected, cosine_table, sine_table))
    block_rows = min(512, sequence_length)
    factor = HEAD_SIZE ** (-0.5)

    def attend(block_index):
        start_row = (block_index * block_rows).astype(jnp.int32)
        query_block = lax.dynamic_slice_in_dim(query_rotated, start_row, block_rows, 0)
        scores = lower_backward(jnp.einsum('qgrd,kgd->grqk', query_block, key_rot, precision=highest_precision) * factor)
        query_pos = start_row + jnp.arange(block_rows, dtype=jnp.int32)
        key_pos = jnp.arange(sequence_length, dtype=jnp.int32)
        scores = jnp.where(key_pos[None, :] <= query_pos[:, None], scores, MASKED)
        attn_probs = jax.nn.softmax(scores, axis=-1)
        return jnp.einsum('grqk,kgd->qgrd', lower_precision(attn_probs), value_per_head, precision=highest_precision)
    mixed = lax.map(jax.checkpoint(attend), jnp.arange(sequence_length // block_rows, dtype=jnp.int32))
    attn_mixed = lower_precision(lower_backward(mixed.reshape(sequence_length, QUERY_HEADS * HEAD_SIZE)))
    hidden = tokens_f + lower_backward(jnp.dot(attn_mixed, out_w, precision=highest_precision))
    normed_two = hidden * lax.rsqrt(lax.optimization_barrier(jnp.mean(hidden * hidden, -1, keepdims=True)) + EPSILON)
    ffn_in = lower_precision(normed_two * gain_two)
    logits = lower_backward(jnp.dot(ffn_in, router_w, precision=highest_precision))
    chosen = jnp.take_along_axis(logits, route_ids, 1)
    gate_probs = jax.nn.softmax(chosen, axis=-1)
    expert_in = jnp.zeros((EXPERTS * CAP, MODEL_WIDTH), jnp.float32).at[target_rows].set(jnp.broadcast_to(ffn_in[:, None, :], (sequence_length, TOP, MODEL_WIDTH)))
    expert_in = lower_backward(expert_in).reshape(EXPERTS, CAP, MODEL_WIDTH)
    gate_val = lower_backward(jnp.einsum('ecd,edf->ecf', expert_in, gate_w, precision=highest_precision))
    up_val = lower_backward(jnp.einsum('ecd,edf->ecf', expert_in, up_w, precision=highest_precision))
    expert_hid = lower_precision(jax.nn.silu(gate_val) * up_val)
    expert_out = lower_precision(lower_backward(jnp.einsum('ecf,efd->ecd', expert_hid, down_w, precision=highest_precision)))
    picked = expert_out.reshape(EXPERTS * CAP, MODEL_WIDTH)[target_rows]
    return hidden + lax.optimization_barrier(jnp.sum(gate_probs[:, :, None] * picked, 1))

def reference(tokens, w_query, key_weight, value_weight, w_out, gain_attn, gain_ffn, w_router, w_gate, w_up, w_down, routes, cotangent):
    weights_f = tuple((item.astype(jnp.float32) for item in (w_query, key_weight, value_weight, w_out, gain_attn, gain_ffn, w_router, w_gate, w_up, w_down)))
    seq_count = TOKENS // TOK_DEV
    blocks = (tokens.reshape(seq_count, TOK_DEV, MODEL_WIDTH), cotangent.reshape(seq_count, TOK_DEV, MODEL_WIDTH), routes.reshape(seq_count, TOK_DEV, TOP))

    def step_block(totals, block_items):
        tokens_blk, cot_blk, route_blk = block_items
        target_rows = destinations(route_blk)

        def forward(tokens_f, *weight_list):
            return layer(tokens_f, *weight_list, route_blk, target_rows)
        result, pullback = jax.vjp(forward, tokens_blk.astype(jnp.float32), *weights_f)
        grads_all = pullback(cot_blk.astype(jnp.float32))
        new_totals = tuple((left + right for left, right in zip(totals, grads_all[1:])))
        return (new_totals, (result.astype(jnp.bfloat16), grads_all[0].astype(jnp.bfloat16)))
    zero_totals = tuple((jnp.zeros_like(item) for item in weights_f))
    totals, (outputs, grad_rows) = lax.scan(step_block, zero_totals, blocks)
    return (outputs.reshape(TOKENS, MODEL_WIDTH), grad_rows.reshape(TOKENS, MODEL_WIDTH), totals[0], totals[1], totals[2], totals[3], totals[4], totals[5], totals[6], totals[7], totals[8], totals[9])
```

```python
import jax
import jax.numpy as jnp
from jax import lax
from jax.sharding import PartitionSpec as P

MODEL_WIDTH = 1536
QUERY_HEADS = 24
KEY_VALUE_HEADS = 8
HEAD_SIZE = 64
TOP = 8
GROUP = QUERY_HEADS // KEY_VALUE_HEADS
QW = QUERY_HEADS * HEAD_SIZE
KW = KEY_VALUE_HEADS * HEAD_SIZE

EPSILON = 1e-06
ROPE_BASE = 10000.0
MASKED = -1e30
F32 = jnp.float32
BF = jnp.bfloat16


def rope_tables(sequence_length):
    half_size = HEAD_SIZE // 2
    positions = jnp.arange(sequence_length, dtype=F32)
    frequency = ROPE_BASE ** (-2.0 * jnp.arange(half_size, dtype=F32) / HEAD_SIZE)
    angles = positions[:, None] * frequency[None, :]
    return (jnp.cos(angles)[:, None, :], jnp.sin(angles)[:, None, :])


def rotate(values, c, s):
    h = values.shape[-1] // 2
    a, b = values[..., :h], values[..., h:]
    return jnp.concatenate([a * c - b * s, a * s + b * c], -1)


def rms_scale(values):
    return lax.rsqrt(jnp.mean(values * values, -1, keepdims=True) + EPSILON)


def norm_back(grad_normed, normed, inv_rms, gain_vec):
    scaled = grad_normed * gain_vec
    grad_input = inv_rms * (scaled - normed * jnp.mean(scaled * normed, -1, keepdims=True))
    return (grad_input, jnp.sum(grad_normed * normed, 0))


def mm(spec, a, b):
    return jnp.einsum(spec, a, b, preferred_element_type=F32)


def body(tokens, w_query, key_weight, value_weight, w_out, gain_attn, gain_ffn, w_router,
         w_gate, w_up, w_down, routes, cotangent):
    T = tokens.shape[0]
    el = w_gate.shape[0]
    nf = lax.axis_size("fsdp")
    nd = lax.axis_size("dp")
    experts = el * nf
    cap = 9 * T * TOP // (8 * experts)
    dp = lax.axis_index("dp")
    fs = lax.axis_index("fsdp")

    packed = jnp.concatenate([w_query, key_weight, value_weight, w_out], 1)
    rows = packed.shape[0] // nd
    mine = lax.dynamic_slice_in_dim(packed, dp * rows, rows, 0)
    full = lax.all_gather(mine, ("fsdp", "dp"), axis=0, tiled=True)
    qkv_full = full[:, : QW + 2 * KW]
    out_full = full[:, QW + 2 * KW:]
    small = jnp.concatenate([w_router, gain_attn[:, None], gain_ffn[:, None]], 1)
    small_full = lax.all_gather(small, "fsdp", axis=0, tiled=True)
    router_full = small_full[:, :experts]
    gain_one = small_full[:, experts].astype(F32)
    gain_two = small_full[:, experts + 1].astype(F32)

    onehot = (routes[:, :, None] == jnp.arange(experts, dtype=jnp.int32)).any(1)
    before = jnp.cumsum(onehot.astype(jnp.int32), 0) - onehot.astype(jnp.int32)
    slots = jnp.where(onehot, before, -1).astype(F32)

    cot_all = lax.all_gather(cotangent, "fsdp", axis=0)

    xf = tokens.astype(F32)
    r1 = rms_scale(xf)
    n1 = xf * r1
    attn_in = (n1 * gain_one).astype(BF)
    proj = jnp.dot(attn_in, qkv_full, preferred_element_type=F32)
    c, s = rope_tables(T)
    q = rotate(proj[:, :QW].reshape(T, QUERY_HEADS, HEAD_SIZE), c, s).astype(BF)
    q = q.reshape(T, KEY_VALUE_HEADS, GROUP, HEAD_SIZE)
    k = rotate(proj[:, QW: QW + KW].reshape(T, KEY_VALUE_HEADS, HEAD_SIZE), c, s).astype(BF)
    v = proj[:, QW + KW:].astype(BF).reshape(T, KEY_VALUE_HEADS, HEAD_SIZE)
    factor = HEAD_SIZE ** (-0.5)
    scores = mm("qgrd,kgd->grqk", q, k) * factor
    keep = jnp.arange(T)[None, :] <= jnp.arange(T)[:, None]
    scores = jnp.where(keep, scores, MASKED)
    top = jnp.max(scores, -1, keepdims=True)
    ex = jnp.exp(scores - top)
    probs = ex / jnp.sum(ex, -1, keepdims=True)
    probs_low = probs.astype(BF)
    mixed = mm("grqk,kgd->qgrd", probs_low, v).reshape(T, QW).astype(BF)
    hidden = xf + jnp.dot(mixed, out_full, preferred_element_type=F32)
    r2 = rms_scale(hidden)
    n2 = hidden * r2
    ffn_in = (n2 * gain_two).astype(BF)
    logits = jnp.dot(ffn_in, router_full, preferred_element_type=F32)
    gates = jnp.where(onehot, logits, MASKED)
    gates = jnp.exp(gates - jnp.max(gates, -1, keepdims=True))
    gates = jnp.where(onehot, gates, 0.0)
    gates = gates / jnp.sum(gates, -1, keepdims=True)

    ffn_all = lax.all_gather(ffn_in, "fsdp", axis=0)
    side = lax.all_gather(jnp.stack([slots.T, gates.T]), "fsdp", axis=0)
    side = lax.dynamic_slice_in_dim(side, fs * el, el, 2)
    slot_l, gate_l = side[:, 0], side[:, 1]
    pick = slot_l[:, :, None, :] == jnp.arange(cap, dtype=F32)[None, None, :, None]
    sel = pick.astype(BF)
    gate_row = jnp.sum(jnp.where(pick, gate_l[:, :, None, :], 0.0), -1, keepdims=True)

    x = mm("nect,ntd->necd", sel, ffn_all).astype(BF)
    g = mm("nect,ntd->necd", sel, cot_all).astype(BF)
    gate_val = mm("necd,edf->necf", x, w_gate)
    up_val = mm("necd,edf->necf", x, w_up)
    sg = jax.nn.sigmoid(gate_val)
    act = gate_val * sg
    hid = act * up_val
    u = mm("necd,efd->necf", g, w_down)
    grad_probs_row = jnp.sum(hid.astype(BF).astype(F32) * u, -1)
    hid_g = (hid * gate_row).astype(BF)
    grad_hid = u * gate_row
    grad_up = (grad_hid * act).astype(BF)
    grad_gate = (grad_hid * up_val * sg * (1.0 + gate_val * (1.0 - sg))).astype(BF)
    out_rows = mm("necf,efd->necd", hid_g, w_down).astype(BF)
    gin_rows = (mm("necf,edf->necd", grad_gate, w_gate) + mm("necf,edf->necd", grad_up, w_up)).astype(BF)
    out_part = mm("nect,necd->ntd", sel, out_rows).astype(BF)
    gin_part = mm("nect,necd->ntd", sel, gin_rows).astype(BF)
    gp_part = jnp.sum(jnp.where(pick, grad_probs_row[..., None], 0.0), 2)
    gp_all = lax.all_to_all(gp_part, "fsdp", split_axis=0, concat_axis=0)
    grad_probs = gp_all.reshape(experts, T).T
    gin_own = lax.psum_scatter(gin_part, "fsdp", scatter_dimension=0, tiled=False)
    out_own = lax.psum_scatter(out_part, "fsdp", scatter_dimension=0, tiled=False)
    term_gate = mm("necd,necf->edf", x, grad_gate)
    term_up = mm("necd,necf->edf", x, grad_up)
    term_down = mm("necf,necd->efd", hid_g, g)
    terms = (term_gate.astype(BF), term_up.astype(BF), term_down.astype(BF))
    terms = lax.psum(terms, "dp")

    output = (hidden + out_own.astype(F32)).astype(BF)
    grad_out = cotangent.astype(F32)
    dot = jnp.sum(grad_probs * gates, -1, keepdims=True)
    grad_logits = (gates * (grad_probs - dot)).astype(BF)
    grad_router = jnp.dot(ffn_in.T, grad_logits, preferred_element_type=F32)
    gffn = gin_own.astype(F32) + jnp.dot(grad_logits, router_full.T, preferred_element_type=F32)
    gh, grad_gain_two = norm_back(gffn, n2, r2, gain_two)
    grad_hidden = grad_out + gh
    branch = grad_hidden.astype(BF)
    grad_out_w = jnp.dot(mixed.T, branch, preferred_element_type=F32)
    gm = jnp.dot(branch, out_full.T, preferred_element_type=F32).astype(BF)
    gm = gm.reshape(T, KEY_VALUE_HEADS, GROUP, HEAD_SIZE)
    gp = mm("qgrd,kgd->grqk", gm, v)
    row = jnp.sum(probs * gp, -1, keepdims=True)
    gs = (probs * (gp - row)).astype(BF)
    gq = mm("grqk,kgd->qgrd", gs, k) * factor
    gk = mm("grqk,qgrd->kgd", gs, q) * factor
    gv = mm("grqk,qgrd->kgd", probs_low, gm)
    gq = rotate(gq.reshape(T, QUERY_HEADS, HEAD_SIZE), c, -s).reshape(T, QW)
    gk = rotate(gk, c, -s).reshape(T, KW)
    gproj = jnp.concatenate([gq, gk, gv.reshape(T, KW)], 1).astype(BF)
    grad_qkv_w = jnp.dot(attn_in.T, gproj, preferred_element_type=F32)
    gattn = jnp.dot(gproj, qkv_full.T, preferred_element_type=F32)
    gt, grad_gain_one = norm_back(gattn, n1, r1, gain_one)
    grad_tokens = (grad_hidden + gt).astype(BF)

    big = jnp.concatenate([grad_qkv_w.astype(BF), grad_out_w.astype(BF)], 1)
    big = lax.psum_scatter(big, ("fsdp", "dp"), scatter_dimension=0, tiled=True)
    big = lax.all_gather(big, "dp", axis=0, tiled=True).astype(F32)
    tiny = jnp.concatenate([grad_router, grad_gain_one[:, None], grad_gain_two[:, None]], 1)
    tiny = lax.psum_scatter(tiny, "fsdp", scatter_dimension=0, tiled=True)
    tiny = lax.psum(tiny, "dp")
    return (
        output,
        grad_tokens,
        big[:, :QW],
        big[:, QW: QW + KW],
        big[:, QW + KW: QW + 2 * KW],
        big[:, QW + 2 * KW:],
        tiny[:, experts],
        tiny[:, experts + 1],
        tiny[:, :experts],
        terms[0].astype(F32),
        terms[1].astype(F32),
        terms[2].astype(F32),
    )


def solution(mesh):
    in_specs = (
        P(("fsdp", "dp"), None),
        P("fsdp", None),
        P("fsdp", None),
        P("fsdp", None),
        P("fsdp", None),
        P("fsdp"),
        P("fsdp"),
        P("fsdp", None),
        P("fsdp", None, None),
        P("fsdp", None, None),
        P("fsdp", None, None),
        P(("fsdp", "dp"), None),
        P(("fsdp", "dp"), None),
    )
    out_specs = (
        P(("fsdp", "dp"), None),
        P(("fsdp", "dp"), None),
        P("fsdp", None),
        P("fsdp", None),
        P("fsdp", None),
        P("fsdp", None),
        P("fsdp"),
        P("fsdp"),
        P("fsdp", None),
        P("fsdp", None, None),
        P("fsdp", None, None),
        P("fsdp", None, None),
    )
    return jax.shard_map(body, mesh=mesh, in_specs=in_specs, out_specs=out_specs, check_vma=False)
```

```python
import functools
import jax
import jax.numpy as jnp
from jax import lax
from jax.experimental import pallas as pl
from jax.experimental.pallas import tpu as pltpu
from jax.sharding import PartitionSpec as P
import numpy as np

MODEL_WIDTH = 1536
QUERY_HEADS = 24
KEY_VALUE_HEADS = 8
HEAD_SIZE = 64
TOP = 8
GROUP = QUERY_HEADS // KEY_VALUE_HEADS
QW = QUERY_HEADS * HEAD_SIZE
KW = KEY_VALUE_HEADS * HEAD_SIZE

EPSILON = 1e-06
ROPE_BASE = 10000.0
MASKED = -1e30
F32 = jnp.float32
BF = jnp.bfloat16


def rope_rows(T):
    half = HEAD_SIZE // 2
    freq = ROPE_BASE ** (-2.0 * np.arange(half, dtype=np.float64) / HEAD_SIZE)
    ang = (np.arange(T, dtype=np.float32)[:, None] * freq.astype(np.float32)[None, :]).astype(np.float32)
    c, s = np.cos(ang), np.sin(ang)
    return (jnp.asarray(np.concatenate([c, c, c, c], 1), F32), jnp.asarray(np.concatenate([-s, s, -s, s], 1), F32))


MESH = pl.DeviceIdType.MESH
VMEM = pltpu.VMEM


def vm():
    return pl.BlockSpec(memory_space=pltpu.VMEM)


def hbm():
    return pl.BlockSpec(memory_space=pl.ANY)


def dot(a, b):
    return lax.dot_general(a, b, (((1,), (0,)), ((), ())), preferred_element_type=F32)


def dot_nt(a, b):
    return lax.dot_general(a, b, (((1,), (1,)), ((), ())), preferred_element_type=F32)


def dot_tn(a, b):
    return lax.dot_general(a, b, (((0,), (0,)), ((), ())), preferred_element_type=F32)


def half_roll(x, first):
    n = x.shape[1]
    h = HEAD_SIZE // 2
    return jnp.where(first, pltpu.roll(x, n - h, axis=1), pltpu.roll(x, h, axis=1))


def greet(nf, nd, f, d):
    barrier = pltpu.get_barrier_semaphore()
    for i in range(1, nf):
        pl.semaphore_signal(barrier, inc=1, device_id=(lax.rem(f + i, nf), d), device_id_type=MESH)
    for i in range(1, nd):
        pl.semaphore_signal(barrier, inc=1, device_id=(f, jnp.bitwise_xor(d, i)), device_id_type=MESH)
    pl.semaphore_wait(barrier, nf + nd - 2)


def head_masks(kblk, lane):
    kf = kblk.astype(F32)
    kr = pltpu.roll(kf, HEAD_SIZE, axis=1)
    low = lane < HEAD_SIZE
    zero = jnp.zeros_like(kf)
    a0 = jnp.where(low, kf, zero).astype(BF)
    a1 = jnp.where(low, zero, kr).astype(BF)
    b0 = jnp.where(low, kr, zero).astype(BF)
    b1 = jnp.where(low, zero, kf).astype(BF)
    return ((a0, a1), (b0, b1))


def front_kernel(nf, nd, experts, tok, pk, small, cot, slots, cosr, sinr,
                 ffn_o, hid_o, gates_o, mix_o, qk_o, v_o, prob_o, wf_o, cot_o, rt_o,
                 wf, sm, attn, rot,
                 s_sm, r_sm, s_z, r_z, s_dp, r_dp, s_sib, r_sib, s_cz, r_cz, s_cs, r_cs, s_loc):
    T, D = tok.shape
    C = nf // 2
    R = pk.shape[0]
    W = pk.shape[1]
    Wq = W // nd
    f = lax.axis_index("fsdp")
    d = lax.axis_index("dp")
    c = f // 2
    k = lax.rem(f, 2)
    sib = f + 1 - 2 * k
    greet(nf, nd, f, d)

    def rows(ff):
        return pl.ds(pl.multiple_of(ff * R, 16), R)

    def cols(dd):
        return pl.ds(pl.multiple_of(dd * Wq, 128), Wq)

    def remote(src, dst, ss, rs, to_f, to_d):
        return pltpu.make_async_remote_copy(src_ref=src, dst_ref=dst, send_sem=ss, recv_sem=rs,
                                            device_id=(to_f, to_d), device_id_type=MESH)

    def src_chip(dr, s):
        return c - s if dr == 0 else c + s

    def has(dr, s):
        return (c - s >= 0) if dr == 0 else (c + s < C)

    def nxt_ok(dr):
        return (c + 1 < C) if dr == 0 else (c - 1 >= 0)

    def nxt_f(dr):
        return f + 2 if dr == 0 else f - 2

    def wz(dr, s, own):
        ff = 2 * src_chip(dr, s - 1) + k
        dst = wf.at[rows(ff), cols(d)]
        src = pk.at[:, cols(d)] if own else dst
        return remote(src, dst, s_z.at[dr, s - 1], r_z.at[dr, s - 1], nxt_f(dr), d)

    def wz_in(dr, s):
        ff = 2 * src_chip(dr, s) + k
        blk = wf.at[rows(ff), cols(d)]
        return remote(blk, blk, s_z.at[dr, s - 1], r_z.at[dr, s - 1], f, d)

    own_small = pltpu.make_async_copy(small, sm.at[f], s_loc.at[0])
    own_small.start()
    sm_copies = []
    for i in range(1, nf):
        cp = remote(small, sm.at[f], s_sm.at[i - 1], r_sm.at[i - 1], lax.rem(f + i, nf), d)
        cp.start()
        sm_copies.append(cp)
    for dr in range(2):
        @pl.when(nxt_ok(dr))
        def _():
            wz(dr, 1, True).start()
    sib_own = remote(pk, wf.at[rows(f)], s_sib.at[0, 0], r_sib.at[0, 0], sib, d)
    sib_own.start()
    own_w = pltpu.make_async_copy(pk, wf.at[rows(f)], s_loc.at[1])
    own_w.start()
    own_c = pltpu.make_async_copy(cot, cot_o.at[f], s_loc.at[2])
    own_c.start()
    sib_c = remote(cot, cot_o.at[f], s_cs.at[0, 0], r_cs.at[0, 0], sib, d)

    def dp_copy(dr, s, i):
        ff = 2 * src_chip(dr, s) + k
        blk = wf.at[rows(ff), cols(d)]
        return remote(blk, blk, s_dp.at[dr, s - 1, i - 1], r_dp.at[dr, s - 1, i - 1], f, jnp.bitwise_xor(d, i))

    def dp_in(dr, s, i):
        ff = 2 * src_chip(dr, s) + k
        blk = wf.at[rows(ff), cols(jnp.bitwise_xor(d, i))]
        return remote(blk, blk, s_dp.at[dr, s - 1, i - 1], r_dp.at[dr, s - 1, i - 1], f, d)

    def sib_copy(dr, s):
        blk = wf.at[rows(2 * src_chip(dr, s) + k)]
        return remote(blk, blk, s_sib.at[dr, s], r_sib.at[dr, s], sib, d)

    def sib_in(dr, s):
        blk = wf.at[rows(2 * src_chip(dr, s) + 1 - k)]
        return remote(blk, blk, s_sib.at[dr, s], r_sib.at[dr, s], sib, d)

    def cz(dr, s, own):
        ff = 2 * src_chip(dr, s - 1) + k
        src = cot if own else cot_o.at[ff]
        return remote(src, cot_o.at[ff], s_cz.at[dr, s - 1], r_cz.at[dr, s - 1], nxt_f(dr), d)

    def cz_in(dr, s):
        ff = 2 * src_chip(dr, s) + k
        return remote(cot_o.at[ff], cot_o.at[ff], s_cz.at[dr, s - 1], r_cz.at[dr, s - 1], f, d)

    def cs(dr, s):
        ff = 2 * src_chip(dr, s) + k
        return remote(cot_o.at[ff], cot_o.at[ff], s_cs.at[dr, s], r_cs.at[dr, s], sib, d)

    def cs_in(dr, s):
        ff = 2 * src_chip(dr, s) + 1 - k
        return remote(cot_o.at[ff], cot_o.at[ff], s_cs.at[dr, s], r_cs.at[dr, s], sib, d)

    for s in range(1, C):
        for dr in range(2):
            @pl.when(has(dr, s))
            def _():
                wz_in(dr, s).wait_recv()
                if s < C - 1:
                    @pl.when(nxt_ok(dr))
                    def _():
                        wz(dr, s + 1, False).start()
                for i in range(1, nd):
                    dp_copy(dr, s, i).start()
    for dr in range(2):
        @pl.when(nxt_ok(dr))
        def _():
            cz(dr, 1, True).start()
    sib_c.start()

    own_small.wait()
    for cp in sm_copies:
        cp.wait()
    Ds = small.shape[1]
    rt = jnp.concatenate([sm[i] for i in range(nf)], axis=1)
    rt_o[...] = rt
    gains = rt[experts:experts + 2].astype(F32)
    gain_one, gain_two = gains[0:1], gains[1:2]
    xf = tok[...].astype(F32)
    r1 = lax.rsqrt(jnp.mean(xf * xf, -1, keepdims=True) + EPSILON)
    attn[...] = (xf * r1 * gain_one).astype(BF)

    for s in range(1, C):
        for dr in range(2):
            @pl.when(has(dr, s))
            def _():
                for i in range(1, nd):
                    dp_in(dr, s, i).wait_recv()
                sib_copy(dr, s).start()
        for dr in range(2):
            if s < C - 1:
                pass

    def cot_step(s):
        for dr in range(2):
            @pl.when(has(dr, s))
            def _():
                cz_in(dr, s).wait_recv()
                if s < C - 1:
                    @pl.when(nxt_ok(dr))
                    def _():
                        cz(dr, s + 1, False).start()
                cs(dr, s).start()

    cot_step(1)
    sib_own.wait()
    own_w.wait()
    for s in range(1, C):
        for dr in range(2):
            @pl.when(has(dr, s))
            def _():
                sib_in(dr, s).wait_recv()
    out_w = pltpu.make_async_copy(wf, wf_o, s_loc.at[3])
    out_w.start()

    first = lax.rem(lax.broadcasted_iota(jnp.int32, (T, 256), 1), HEAD_SIZE) < HEAD_SIZE // 2
    cs_t = jnp.concatenate([cosr[...], cosr[...]], 1)
    sn_t = jnp.concatenate([sinr[...], sinr[...]], 1)
    nqk = (QW + KW) // 256

    @pl.loop(0, nqk)
    def _(i):
        col = pl.ds(pl.multiple_of(i * 256, 256), 256)
        x = dot(attn[...], wf[:, col])
        qk_o[:, col] = (x * cs_t + half_roll(x, first) * sn_t).astype(BF)

    @pl.loop(0, KW // 256)
    def _(i):
        col = pl.ds(pl.multiple_of(QW + KW + i * 256, 256), 256)
        v_o[:, pl.ds(pl.multiple_of(i * 256, 256), 256)] = dot(attn[...], wf[:, col]).astype(BF)

    for s in range(2, min(C, 3)):
        cot_step(s)

    factor = HEAD_SIZE ** (-0.5)
    lane = lax.broadcasted_iota(jnp.int32, (T, 128), 1)
    keep = lax.broadcasted_iota(jnp.int32, (T, T), 1) <= lax.broadcasted_iota(jnp.int32, (T, T), 0)

    @pl.loop(0, KEY_VALUE_HEADS // 2)
    def _(i):
        kc = pl.ds(pl.multiple_of(QW + i * 128, 128), 128)
        kh = head_masks(qk_o[:, kc], lane)
        vh = head_masks(v_o[:, pl.ds(pl.multiple_of(i * 128, 128), 128)], lane)
        for p in range(GROUP):
            qc = pl.ds(pl.multiple_of((i * GROUP + p) * 128, 128), 128)
            q = qk_o[:, qc]
            acc = None
            for half in range(2):
                g = (2 * p + half) // GROUP
                sc = dot_nt(q, kh[g][half]) * factor
                sc = jnp.where(keep, sc, MASKED)
                ex = jnp.exp(sc - jnp.max(sc, -1, keepdims=True))
                pr = (ex / jnp.sum(ex, -1, keepdims=True)).astype(BF)
                prob_o[i * 2 * GROUP + 2 * p + half] = pr
                term = dot(pr, vh[g][half])
                acc = term if acc is None else acc + term
            mix_o[:, qc] = acc.astype(BF)

    for s in range(3, C):
        cot_step(s)

    @pl.loop(0, D // 256)
    def _(i):
        col = pl.ds(pl.multiple_of(i * 256, 256), 256)
        wc = pl.ds(pl.multiple_of(QW + 2 * KW + i * 256, 256), 256)
        hid_o[:, col] = tok[:, col].astype(F32) + dot(mix_o[...], wf[:, wc])

    hidden = hid_o[...]
    r2 = lax.rsqrt(jnp.mean(hidden * hidden, -1, keepdims=True) + EPSILON)
    ffn_o[...] = (hidden * r2 * gain_two).astype(BF)
    logits = dot_nt(rt_o[...], ffn_o[...])[0:experts]
    named = slots[...] >= 0.0
    logits = jnp.where(named, logits, MASKED)
    ex = jnp.where(named, jnp.exp(logits - jnp.max(logits, 0, keepdims=True)), 0.0)
    gates_o[...] = ex / jnp.sum(ex, 0, keepdims=True)

    own_c.wait()
    sib_c.wait()
    out_w.wait()
    for dr in range(2):
        for s in range(1, C):
            @pl.when(has(dr, s))
            def _():
                cs_in(dr, s).wait_recv()
                cs(dr, s).wait_send()
                sib_copy(dr, s).wait_send()
                for i in range(1, nd):
                    dp_copy(dr, s, i).wait_send()

            @pl.when(nxt_ok(dr) & (has(dr, s - 1) if s > 1 else True))
            def _():
                wz(dr, s, s == 1).wait_send()
                cz(dr, s, s == 1).wait_send()


def front(nf, nd, experts, tok, pk, small, cot, slots, cosr, sinr):
    T, D = tok.shape
    C = nf // 2
    W = pk.shape[1]
    out = [
        (T, D, BF, 0), (T, D, F32, 0), (experts, T, F32, 0), (T, QW, BF, 0), (T, QW + KW, BF, 0),
        (T, KW, BF, 0), (QUERY_HEADS, T, T, BF, 0), (D, W, BF, 1), (nf, T, D, BF, 1),
        (small.shape[0], D, BF, 0),
    ]
    dma = pltpu.SemaphoreType.DMA
    return pl.pallas_call(
        functools.partial(front_kernel, nf, nd, experts),
        out_shape=[jax.ShapeDtypeStruct(o[:-2], o[-2]) for o in out],
        in_specs=[vm()] * 7,
        out_specs=[hbm() if o[-1] else vm() for o in out],
        scratch_shapes=[
            VMEM((D, W), BF),
            VMEM((nf,) + small.shape, BF),
            VMEM((T, D), BF),
            VMEM((8, 128), F32),
            dma((nf,)), dma((nf,)),
            dma((2, C)), dma((2, C)),
            dma((2, C, nd)), dma((2, C, nd)),
            dma((2, C)), dma((2, C)),
            dma((2, C)), dma((2, C)),
            dma((2, C)), dma((2, C)),
            dma((4,)),
        ],
        compiler_params=pltpu.CompilerParams(collective_id=1, has_side_effects=True,
                                             vmem_limit_bytes=60 * 2 ** 20),
        cost_estimate=pl.CostEstimate(flops=4_000_000_000, bytes_accessed=60_000_000, transcendentals=2_000_000),
        name="front",
    )(tok, pk, small, cot, slots, cosr, sinr)


def rope_tables(sequence_length):
    half_size = HEAD_SIZE // 2
    positions = jnp.arange(sequence_length, dtype=F32)
    frequency = ROPE_BASE ** (-2.0 * jnp.arange(half_size, dtype=F32) / HEAD_SIZE)
    angles = positions[:, None] * frequency[None, :]
    return (jnp.cos(angles)[:, None, :], jnp.sin(angles)[:, None, :])


def rotate(values, c, s):
    h = values.shape[-1] // 2
    a, b = values[..., :h], values[..., h:]
    return jnp.concatenate([a * c - b * s, a * s + b * c], -1)


def rms_scale(values):
    return lax.rsqrt(jnp.mean(values * values, -1, keepdims=True) + EPSILON)


def norm_back(grad_normed, normed, inv_rms, gain_vec):
    scaled = grad_normed * gain_vec
    grad_input = inv_rms * (scaled - normed * jnp.mean(scaled * normed, -1, keepdims=True))
    return (grad_input, jnp.sum(grad_normed * normed, 0))


def mm(spec, a, b):
    return jnp.einsum(spec, a, b, preferred_element_type=F32)


def body(tokens, w_query, key_weight, value_weight, w_out, gain_attn, gain_ffn, w_router,
         w_gate, w_up, w_down, routes, cotangent):
    T = tokens.shape[0]
    el = w_gate.shape[0]
    nf = lax.axis_size("fsdp")
    nd = lax.axis_size("dp")
    experts = el * nf
    cap = 9 * T * TOP // (8 * experts)
    dp = lax.axis_index("dp")
    fs = lax.axis_index("fsdp")

    packed = jnp.concatenate([w_query, key_weight, value_weight, w_out], 1)
    pad = -(experts + 2) % 16
    small = jnp.concatenate([w_router, gain_attn[:, None], gain_ffn[:, None],
                             jnp.zeros((w_router.shape[0], pad), BF)], 1).T
    onehot = (routes[:, :, None] == jnp.arange(experts, dtype=jnp.int32)).any(1)
    before = jnp.cumsum(onehot.astype(jnp.int32), 0) - onehot.astype(jnp.int32)
    slots = jnp.where(onehot, before, -1).astype(F32)
    cosr, sinr = rope_rows(T)
    ffn_in, hidden, gates_t, mixed, qk, v2, probs_low, full, cot_all, rt = front(
        nf, nd, experts, tokens, packed, small, cotangent, slots.T, cosr, sinr)
    gates = gates_t.T
    qkv_full = full[:, : QW + 2 * KW]
    out_full = full[:, QW + 2 * KW:]
    router_full = rt[:experts].T
    gain_one = rt[experts].astype(F32)
    gain_two = rt[experts + 1].astype(F32)
    xf = tokens.astype(F32)
    r1 = rms_scale(xf)
    n1 = xf * r1
    attn_in = (n1 * gain_one).astype(BF)
    c, s = rope_tables(T)
    q = qk[:, :QW].reshape(T, KEY_VALUE_HEADS, GROUP, HEAD_SIZE)
    k = qk[:, QW:].reshape(T, KEY_VALUE_HEADS, HEAD_SIZE)
    v = v2.reshape(T, KEY_VALUE_HEADS, HEAD_SIZE)
    factor = HEAD_SIZE ** (-0.5)
    probs_low = probs_low.reshape(KEY_VALUE_HEADS, GROUP, T, T)
    probs = probs_low.astype(F32)
    r2 = rms_scale(hidden)
    n2 = hidden * r2

    ffn_all = lax.all_gather(ffn_in, "fsdp", axis=0)
    side = lax.all_gather(jnp.stack([slots.T, gates.T]), "fsdp", axis=0)
    side = lax.dynamic_slice_in_dim(side, fs * el, el, 2)
    slot_l, gate_l = side[:, 0], side[:, 1]
    pick = slot_l[:, :, None, :] == jnp.arange(cap, dtype=F32)[None, None, :, None]
    sel = pick.astype(BF)
    gate_row = jnp.sum(jnp.where(pick, gate_l[:, :, None, :], 0.0), -1, keepdims=True)

    x = mm("nect,ntd->necd", sel, ffn_all).astype(BF)
    g = mm("nect,ntd->necd", sel, cot_all).astype(BF)
    gate_val = mm("necd,edf->necf", x, w_gate)
    up_val = mm("necd,edf->necf", x, w_up)
    sg = jax.nn.sigmoid(gate_val)
    act = gate_val * sg
    hid = act * up_val
    u = mm("necd,efd->necf", g, w_down)
    grad_probs_row = jnp.sum(hid.astype(BF).astype(F32) * u, -1)
    hid_g = (hid * gate_row).astype(BF)
    grad_hid = u * gate_row
    grad_up = (grad_hid * act).astype(BF)
    grad_gate = (grad_hid * up_val * sg * (1.0 + gate_val * (1.0 - sg))).astype(BF)
    out_rows = mm("necf,efd->necd", hid_g, w_down).astype(BF)
    gin_rows = (mm("necf,edf->necd", grad_gate, w_gate) + mm("necf,edf->necd", grad_up, w_up)).astype(BF)
    out_part = mm("nect,necd->ntd", sel, out_rows).astype(BF)
    gin_part = mm("nect,necd->ntd", sel, gin_rows).astype(BF)
    gp_part = jnp.sum(jnp.where(pick, grad_probs_row[..., None], 0.0), 2)
    gp_all = lax.all_to_all(gp_part, "fsdp", split_axis=0, concat_axis=0)
    grad_probs = gp_all.reshape(experts, T).T
    gin_own = lax.psum_scatter(gin_part, "fsdp", scatter_dimension=0, tiled=False)
    out_own = lax.psum_scatter(out_part, "fsdp", scatter_dimension=0, tiled=False)
    term_gate = mm("necd,necf->edf", x, grad_gate)
    term_up = mm("necd,necf->edf", x, grad_up)
    term_down = mm("necf,necd->efd", hid_g, g)
    terms = (term_gate.astype(BF), term_up.astype(BF), term_down.astype(BF))
    terms = lax.psum(terms, "dp")

    output = (hidden + out_own.astype(F32)).astype(BF)
    grad_out = cotangent.astype(F32)
    dot = jnp.sum(grad_probs * gates, -1, keepdims=True)
    grad_logits = (gates * (grad_probs - dot)).astype(BF)
    grad_router = jnp.dot(ffn_in.T, grad_logits, preferred_element_type=F32)
    gffn = gin_own.astype(F32) + jnp.dot(grad_logits, router_full.T, preferred_element_type=F32)
    gh, grad_gain_two = norm_back(gffn, n2, r2, gain_two)
    grad_hidden = grad_out + gh
    branch = grad_hidden.astype(BF)
    grad_out_w = jnp.dot(mixed.T, branch, preferred_element_type=F32)
    gm = jnp.dot(branch, out_full.T, preferred_element_type=F32).astype(BF)
    gm = gm.reshape(T, KEY_VALUE_HEADS, GROUP, HEAD_SIZE)
    gp = mm("qgrd,kgd->grqk", gm, v)
    row = jnp.sum(probs * gp, -1, keepdims=True)
    gs = (probs * (gp - row)).astype(BF)
    gq = mm("grqk,kgd->qgrd", gs, k) * factor
    gk = mm("grqk,qgrd->kgd", gs, q) * factor
    gv = mm("grqk,qgrd->kgd", probs_low, gm)
    gq = rotate(gq.reshape(T, QUERY_HEADS, HEAD_SIZE), c, -s).reshape(T, QW)
    gk = rotate(gk, c, -s).reshape(T, KW)
    gproj = jnp.concatenate([gq, gk, gv.reshape(T, KW)], 1).astype(BF)
    grad_qkv_w = jnp.dot(attn_in.T, gproj, preferred_element_type=F32)
    gattn = jnp.dot(gproj, qkv_full.T, preferred_element_type=F32)
    gt, grad_gain_one = norm_back(gattn, n1, r1, gain_one)
    grad_tokens = (grad_hidden + gt).astype(BF)

    big = jnp.concatenate([grad_qkv_w.astype(BF), grad_out_w.astype(BF)], 1)
    big = lax.psum_scatter(big, ("fsdp", "dp"), scatter_dimension=0, tiled=True)
    big = lax.all_gather(big, "dp", axis=0, tiled=True).astype(F32)
    tiny = jnp.concatenate([grad_router, grad_gain_one[:, None], grad_gain_two[:, None]], 1)
    tiny = lax.psum_scatter(tiny, "fsdp", scatter_dimension=0, tiled=True)
    tiny = lax.psum(tiny, "dp")
    return (
        output,
        grad_tokens,
        big[:, :QW],
        big[:, QW: QW + KW],
        big[:, QW + KW: QW + 2 * KW],
        big[:, QW + 2 * KW:],
        tiny[:, experts],
        tiny[:, experts + 1],
        tiny[:, :experts],
        terms[0].astype(F32),
        terms[1].astype(F32),
        terms[2].astype(F32),
    )


def solution(mesh):
    in_specs = (
        P(("fsdp", "dp"), None),
        P("fsdp", None),
        P("fsdp", None),
        P("fsdp", None),
        P("fsdp", None),
        P("fsdp"),
        P("fsdp"),
        P("fsdp", None),
        P("fsdp", None, None),
        P("fsdp", None, None),
        P("fsdp", None, None),
        P(("fsdp", "dp"), None),
        P(("fsdp", "dp"), None),
    )
    out_specs = (
        P(("fsdp", "dp"), None),
        P(("fsdp", "dp"), None),
        P("fsdp", None),
        P("fsdp", None),
        P("fsdp", None),
        P("fsdp", None),
        P("fsdp"),
        P("fsdp"),
        P("fsdp", None),
        P("fsdp", None, None),
        P("fsdp", None, None),
        P("fsdp", None, None),
    )
    return jax.shard_map(body, mesh=mesh, in_specs=in_specs, out_specs=out_specs, check_vma=False)
```

```python
import functools
import jax
import jax.numpy as jnp
from jax import lax
from jax.experimental import pallas as pl
from jax.experimental.pallas import tpu as pltpu
from jax.sharding import PartitionSpec as P
import numpy as np

MODEL_WIDTH = 1536
QUERY_HEADS = 24
KEY_VALUE_HEADS = 8
HEAD_SIZE = 64
TOP = 8
GROUP = QUERY_HEADS // KEY_VALUE_HEADS
QW = QUERY_HEADS * HEAD_SIZE
KW = KEY_VALUE_HEADS * HEAD_SIZE

EPSILON = 1e-06
ROPE_BASE = 10000.0
MASKED = -1e30
F32 = jnp.float32
BF = jnp.bfloat16


def rope_rows(T):
    half = HEAD_SIZE // 2
    freq = ROPE_BASE ** (-2.0 * np.arange(half, dtype=np.float64) / HEAD_SIZE)
    ang = (np.arange(T, dtype=np.float32)[:, None] * freq.astype(np.float32)[None, :]).astype(np.float32)
    c, s = np.cos(ang), np.sin(ang)
    return (jnp.asarray(np.concatenate([c, c, c, c], 1), F32), jnp.asarray(np.concatenate([-s, s, -s, s], 1), F32))


MESH = pl.DeviceIdType.MESH
VMEM = pltpu.VMEM


def vm():
    return pl.BlockSpec(memory_space=pltpu.VMEM)


def hbm():
    return pl.BlockSpec(memory_space=pl.ANY)


def dot(a, b):
    return lax.dot_general(a, b, (((1,), (0,)), ((), ())), preferred_element_type=F32)


def dot_nt(a, b):
    return lax.dot_general(a, b, (((1,), (1,)), ((), ())), preferred_element_type=F32)


def dot_tn(a, b):
    return lax.dot_general(a, b, (((0,), (0,)), ((), ())), preferred_element_type=F32)


def half_roll(x, first):
    n = x.shape[1]
    h = HEAD_SIZE // 2
    return jnp.where(first, pltpu.roll(x, n - h, axis=1), pltpu.roll(x, h, axis=1))


def greet(nf, nd, f, d):
    barrier = pltpu.get_barrier_semaphore()
    for i in range(1, nf):
        pl.semaphore_signal(barrier, inc=1, device_id=(lax.rem(f + i, nf), d), device_id_type=MESH)
    for i in range(1, nd):
        pl.semaphore_signal(barrier, inc=1, device_id=(f, jnp.bitwise_xor(d, i)), device_id_type=MESH)
    pl.semaphore_wait(barrier, nf + nd - 2)


def head_masks(kblk, lane):
    kf = kblk.astype(F32)
    kr = pltpu.roll(kf, HEAD_SIZE, axis=1)
    low = lane < HEAD_SIZE
    zero = jnp.zeros_like(kf)
    a0 = jnp.where(low, kf, zero).astype(BF)
    a1 = jnp.where(low, zero, kr).astype(BF)
    b0 = jnp.where(low, kr, zero).astype(BF)
    b1 = jnp.where(low, zero, kf).astype(BF)
    return ((a0, a1), (b0, b1))


def front_kernel(nf, nd, experts, tok, pk, small, cot, slots, cosr, sinr,
                 ffn_o, hid_o, gates_o, mix_o, qk_o, v_o, prob_o, wf_o, cot_o, rt_o,
                 wf, sm, attn, rot,
                 s_sm, r_sm, s_z, r_z, s_dp, r_dp, s_sib, r_sib, s_cz, r_cz, s_cs, r_cs, s_loc):
    T, D = tok.shape
    C = nf // 2
    R = pk.shape[0]
    W = pk.shape[1]
    Wq = W // nd
    f = lax.axis_index("fsdp")
    d = lax.axis_index("dp")
    c = f // 2
    k = lax.rem(f, 2)
    sib = f + 1 - 2 * k
    greet(nf, nd, f, d)

    def rows(ff):
        return pl.ds(pl.multiple_of(ff * R, 16), R)

    def cols(dd):
        return pl.ds(pl.multiple_of(dd * Wq, 128), Wq)

    def remote(src, dst, ss, rs, to_f, to_d):
        return pltpu.make_async_remote_copy(src_ref=src, dst_ref=dst, send_sem=ss, recv_sem=rs,
                                            device_id=(to_f, to_d), device_id_type=MESH)

    def src_chip(dr, s):
        return c - s if dr == 0 else c + s

    def has(dr, s):
        return (c - s >= 0) if dr == 0 else (c + s < C)

    def nxt_ok(dr):
        return (c + 1 < C) if dr == 0 else (c - 1 >= 0)

    def nxt_f(dr):
        return f + 2 if dr == 0 else f - 2

    def wz(dr, s, own):
        ff = 2 * src_chip(dr, s - 1) + k
        dst = wf.at[rows(ff), cols(d)]
        src = pk.at[:, cols(d)] if own else dst
        return remote(src, dst, s_z.at[dr, s - 1], r_z.at[dr, s - 1], nxt_f(dr), d)

    def wz_in(dr, s):
        ff = 2 * src_chip(dr, s) + k
        blk = wf.at[rows(ff), cols(d)]
        return remote(blk, blk, s_z.at[dr, s - 1], r_z.at[dr, s - 1], f, d)

    own_small = pltpu.make_async_copy(small, sm.at[f], s_loc.at[0])
    own_small.start()
    sm_copies = []
    for i in range(1, nf):
        cp = remote(small, sm.at[f], s_sm.at[i - 1], r_sm.at[i - 1], lax.rem(f + i, nf), d)
        cp.start()
        sm_copies.append(cp)
    for dr in range(2):
        @pl.when(nxt_ok(dr))
        def _():
            wz(dr, 1, True).start()
    sib_own = remote(pk, wf.at[rows(f)], s_sib.at[0, 0], r_sib.at[0, 0], sib, d)
    sib_own.start()
    own_w = pltpu.make_async_copy(pk, wf.at[rows(f)], s_loc.at[1])
    own_w.start()
    own_c = pltpu.make_async_copy(cot, cot_o.at[f], s_loc.at[2])
    own_c.start()
    sib_c = remote(cot, cot_o.at[f], s_cs.at[0, 0], r_cs.at[0, 0], sib, d)

    def dp_copy(dr, s, i):
        ff = 2 * src_chip(dr, s) + k
        blk = wf.at[rows(ff), cols(d)]
        return remote(blk, blk, s_dp.at[dr, s - 1, i - 1], r_dp.at[dr, s - 1, i - 1], f, jnp.bitwise_xor(d, i))

    def dp_in(dr, s, i):
        ff = 2 * src_chip(dr, s) + k
        blk = wf.at[rows(ff), cols(jnp.bitwise_xor(d, i))]
        return remote(blk, blk, s_dp.at[dr, s - 1, i - 1], r_dp.at[dr, s - 1, i - 1], f, d)

    def sib_copy(dr, s):
        blk = wf.at[rows(2 * src_chip(dr, s) + k)]
        return remote(blk, blk, s_sib.at[dr, s], r_sib.at[dr, s], sib, d)

    def sib_in(dr, s):
        blk = wf.at[rows(2 * src_chip(dr, s) + 1 - k)]
        return remote(blk, blk, s_sib.at[dr, s], r_sib.at[dr, s], sib, d)

    def cz(dr, s, own):
        ff = 2 * src_chip(dr, s - 1) + k
        src = cot if own else cot_o.at[ff]
        return remote(src, cot_o.at[ff], s_cz.at[dr, s - 1], r_cz.at[dr, s - 1], nxt_f(dr), d)

    def cz_in(dr, s):
        ff = 2 * src_chip(dr, s) + k
        return remote(cot_o.at[ff], cot_o.at[ff], s_cz.at[dr, s - 1], r_cz.at[dr, s - 1], f, d)

    def cs(dr, s):
        ff = 2 * src_chip(dr, s) + k
        return remote(cot_o.at[ff], cot_o.at[ff], s_cs.at[dr, s], r_cs.at[dr, s], sib, d)

    def cs_in(dr, s):
        ff = 2 * src_chip(dr, s) + 1 - k
        return remote(cot_o.at[ff], cot_o.at[ff], s_cs.at[dr, s], r_cs.at[dr, s], sib, d)

    for s in range(1, C):
        for dr in range(2):
            @pl.when(has(dr, s))
            def _():
                wz_in(dr, s).wait_recv()
                if s < C - 1:
                    @pl.when(nxt_ok(dr))
                    def _():
                        wz(dr, s + 1, False).start()
                for i in range(1, nd):
                    dp_copy(dr, s, i).start()
    for dr in range(2):
        @pl.when(nxt_ok(dr))
        def _():
            cz(dr, 1, True).start()
    sib_c.start()

    own_small.wait()
    for cp in sm_copies:
        cp.wait()
    Ds = small.shape[1]
    rt = jnp.concatenate([sm[i] for i in range(nf)], axis=1)
    rt_o[...] = rt
    gains = rt[experts:experts + 2].astype(F32)
    gain_one, gain_two = gains[0:1], gains[1:2]
    xf = tok[...].astype(F32)
    r1 = lax.rsqrt(jnp.mean(xf * xf, -1, keepdims=True) + EPSILON)
    attn[...] = (xf * r1 * gain_one).astype(BF)

    for s in range(1, C):
        for dr in range(2):
            @pl.when(has(dr, s))
            def _():
                for i in range(1, nd):
                    dp_in(dr, s, i).wait_recv()
                sib_copy(dr, s).start()
        for dr in range(2):
            if s < C - 1:
                pass

    def cot_step(s):
        for dr in range(2):
            @pl.when(has(dr, s))
            def _():
                cz_in(dr, s).wait_recv()
                if s < C - 1:
                    @pl.when(nxt_ok(dr))
                    def _():
                        cz(dr, s + 1, False).start()
                cs(dr, s).start()

    cot_step(1)
    sib_own.wait()
    own_w.wait()
    for s in range(1, C):
        for dr in range(2):
            @pl.when(has(dr, s))
            def _():
                sib_in(dr, s).wait_recv()
    out_w = pltpu.make_async_copy(wf, wf_o, s_loc.at[3])
    out_w.start()

    first = lax.rem(lax.broadcasted_iota(jnp.int32, (T, 256), 1), HEAD_SIZE) < HEAD_SIZE // 2
    cs_t = jnp.concatenate([cosr[...], cosr[...]], 1)
    sn_t = jnp.concatenate([sinr[...], sinr[...]], 1)
    nqk = (QW + KW) // 256

    @pl.loop(0, nqk)
    def _(i):
        col = pl.ds(pl.multiple_of(i * 256, 256), 256)
        x = dot(attn[...], wf[:, col])
        qk_o[:, col] = (x * cs_t + half_roll(x, first) * sn_t).astype(BF)

    @pl.loop(0, KW // 256)
    def _(i):
        col = pl.ds(pl.multiple_of(QW + KW + i * 256, 256), 256)
        v_o[:, pl.ds(pl.multiple_of(i * 256, 256), 256)] = dot(attn[...], wf[:, col]).astype(BF)

    for s in range(2, min(C, 3)):
        cot_step(s)

    factor = HEAD_SIZE ** (-0.5)
    lane = lax.broadcasted_iota(jnp.int32, (T, 128), 1)
    keep = lax.broadcasted_iota(jnp.int32, (T, T), 1) <= lax.broadcasted_iota(jnp.int32, (T, T), 0)

    @pl.loop(0, KEY_VALUE_HEADS // 2)
    def _(i):
        kc = pl.ds(pl.multiple_of(QW + i * 128, 128), 128)
        kh = head_masks(qk_o[:, kc], lane)
        vh = head_masks(v_o[:, pl.ds(pl.multiple_of(i * 128, 128), 128)], lane)
        for p in range(GROUP):
            qc = pl.ds(pl.multiple_of((i * GROUP + p) * 128, 128), 128)
            q = qk_o[:, qc]
            acc = None
            for half in range(2):
                g = (2 * p + half) // GROUP
                sc = dot_nt(q, kh[g][half]) * factor
                sc = jnp.where(keep, sc, MASKED)
                ex = jnp.exp(sc - jnp.max(sc, -1, keepdims=True))
                pr = (ex / jnp.sum(ex, -1, keepdims=True)).astype(BF)
                prob_o[i * 2 * GROUP + 2 * p + half] = pr
                term = dot(pr, vh[g][half])
                acc = term if acc is None else acc + term
            mix_o[:, qc] = acc.astype(BF)

    for s in range(3, C):
        cot_step(s)

    @pl.loop(0, D // 256)
    def _(i):
        col = pl.ds(pl.multiple_of(i * 256, 256), 256)
        wc = pl.ds(pl.multiple_of(QW + 2 * KW + i * 256, 256), 256)
        hid_o[:, col] = tok[:, col].astype(F32) + dot(mix_o[...], wf[:, wc])

    hidden = hid_o[...]
    r2 = lax.rsqrt(jnp.mean(hidden * hidden, -1, keepdims=True) + EPSILON)
    ffn_o[...] = (hidden * r2 * gain_two).astype(BF)
    logits = dot_nt(rt_o[...], ffn_o[...])[0:experts]
    named = slots[...] >= 0.0
    logits = jnp.where(named, logits, MASKED)
    ex = jnp.where(named, jnp.exp(logits - jnp.max(logits, 0, keepdims=True)), 0.0)
    gates_o[...] = ex / jnp.sum(ex, 0, keepdims=True)

    own_c.wait()
    sib_c.wait()
    out_w.wait()
    for dr in range(2):
        for s in range(1, C):
            @pl.when(has(dr, s))
            def _():
                cs_in(dr, s).wait_recv()
                cs(dr, s).wait_send()
                sib_copy(dr, s).wait_send()
                for i in range(1, nd):
                    dp_copy(dr, s, i).wait_send()

            @pl.when(nxt_ok(dr) & (has(dr, s - 1) if s > 1 else True))
            def _():
                wz(dr, s, s == 1).wait_send()
                cz(dr, s, s == 1).wait_send()


def front(nf, nd, experts, tok, pk, small, cot, slots, cosr, sinr):
    T, D = tok.shape
    C = nf // 2
    W = pk.shape[1]
    out = [
        (T, D, BF, 0), (T, D, F32, 0), (experts, T, F32, 0), (T, QW, BF, 0), (T, QW + KW, BF, 0),
        (T, KW, BF, 0), (QUERY_HEADS, T, T, BF, 0), (D, W, BF, 1), (nf, T, D, BF, 1),
        (small.shape[0], D, BF, 0),
    ]
    dma = pltpu.SemaphoreType.DMA
    return pl.pallas_call(
        functools.partial(front_kernel, nf, nd, experts),
        out_shape=[jax.ShapeDtypeStruct(o[:-2], o[-2]) for o in out],
        in_specs=[vm()] * 7,
        out_specs=[hbm() if o[-1] else vm() for o in out],
        scratch_shapes=[
            VMEM((D, W), BF),
            VMEM((nf,) + small.shape, BF),
            VMEM((T, D), BF),
            VMEM((8, 128), F32),
            dma((nf,)), dma((nf,)),
            dma((2, C)), dma((2, C)),
            dma((2, C, nd)), dma((2, C, nd)),
            dma((2, C)), dma((2, C)),
            dma((2, C)), dma((2, C)),
            dma((2, C)), dma((2, C)),
            dma((4,)),
        ],
        compiler_params=pltpu.CompilerParams(collective_id=1, has_side_effects=True,
                                             vmem_limit_bytes=60 * 2 ** 20),
        cost_estimate=pl.CostEstimate(flops=4_000_000_000, bytes_accessed=60_000_000, transcendentals=2_000_000),
        name="front",
    )(tok, pk, small, cot, slots, cosr, sinr)


def visit(c, C, j):
    both = jnp.minimum(c, C - 1 - c)
    near = j <= 2 * both
    dist = jnp.where(near, (j + 1) // 2, j - both)
    down = jnp.where(near, lax.rem(j, 2) == 0, c < C - 1 - c)
    chip = jnp.where(down, c + dist, c - dist)
    return chip, jnp.where(down, 1, 0), dist


def experts_kernel(nf, el, cap, capp, ffn, cot_a, side, wg_h, wu_h, wd_h,
                   out_o, gin_o, gp_o, t1_o, t2_o,
                   wg, wu, wd, fa, sd, cotb, xs, gs, hs, hgs, orb, irb, st_o, st_i, st1, st2,
                   s_sd, r_sd, s_z, r_z, s_sib, r_sib, s_w, s_loc, s_t):
    T, D = ffn.shape
    FFW = wg.shape[2]
    C = nf // 2
    B = 2 * capp
    f = lax.axis_index("fsdp")
    d = lax.axis_index("dp")
    c = f // 2
    k = lax.rem(f, 2)
    sib = f + 1 - 2 * k
    greet(nf, 1, f, d)

    def remote(src, dst, ss, rs, to_f):
        return pltpu.make_async_remote_copy(src_ref=src, dst_ref=dst, send_sem=ss, recv_sem=rs,
                                            device_id=(to_f, d), device_id_type=MESH)

    def chip_at(dr, s):
        return jnp.where(dr == 0, c - s, c + s)

    def has(dr, s):
        at = chip_at(dr, s)
        return (at >= 0) & (at < C)

    def nxt_ok(dr):
        return (c + 1 < C) if dr == 0 else (c - 1 >= 0)

    def nxt_f(dr):
        return f + 2 if dr == 0 else f - 2

    def z_out(dr, s):
        ff = 2 * chip_at(dr, s - 1) + k
        return remote(fa.at[ff], fa.at[ff], s_z.at[dr, s - 1], r_z.at[dr, s - 1], nxt_f(dr))

    def z_own(dr):
        return remote(ffn, fa.at[f], s_z.at[dr, 0], r_z.at[dr, 0], nxt_f(dr))

    def z_in(dr, s):
        ff = 2 * chip_at(dr, s) + k
        return remote(fa.at[ff], fa.at[ff], s_z.at[dr, s - 1], r_z.at[dr, s - 1], f)

    def sib_out(dr, s):
        ff = 2 * chip_at(dr, s) + k
        return remote(fa.at[ff], fa.at[ff], s_sib.at[dr, s], r_sib.at[dr, s], sib)

    def sib_in(dr, s):
        ff = 2 * chip_at(dr, s) + 1 - k
        return remote(fa.at[ff], fa.at[ff], s_sib.at[dr, s], r_sib.at[dr, s], f)

    for dr in range(2):
        @pl.when(nxt_ok(dr))
        def _():
            z_own(dr).start()
    sib_own = remote(ffn, fa.at[f], s_sib.at[1, 0], r_sib.at[1, 0], sib)
    sib_own.start()
    own = pltpu.make_async_copy(ffn, fa.at[f], s_loc.at[0])
    own.start()
    own_sd = pltpu.make_async_copy(side.at[f], sd.at[f], s_loc.at[1])
    own_sd.start()
    sd_copies = []
    for i in range(1, nf):
        to = lax.rem(f + i, nf)
        cp = remote(side.at[to], sd.at[f], s_sd.at[i - 1], r_sd.at[i - 1], to)
        cp.start()
        sd_copies.append(cp)
    w_copies = []
    for i, (src, dst) in enumerate(((wg_h, wg), (wu_h, wu), (wd_h, wd))):
        cp = pltpu.make_async_copy(src, dst, s_w.at[i])
        cp.start()
        w_copies.append(cp)
    own.wait()
    own_sd.wait()
    for cp in sd_copies:
        cp.wait()
    for cp in w_copies:
        cp.wait()

    row_ids = lax.broadcasted_iota(jnp.int32, (capp, T), 0).astype(F32)

    @pl.loop(0, C)
    def _(j):
        b, dr_b, dist_b = visit(c, C, j)
        cot_cp = pltpu.make_async_copy(cot_a.at[pl.ds(2 * b, 2)], cotb, s_loc.at[2])
        cot_cp.start()

        @pl.when(j >= 1)
        def _():
            for dr in range(2):
                @pl.when(has(dr, j))
                def _():
                    z_in(dr, j).wait_recv()

                    @pl.when(nxt_ok(dr) & (j < C - 1))
                    def _():
                        z_out(dr, j + 1).start()
                    sib_out(dr, j).start()
        sib_in(dr_b, dist_b).wait_recv()
        cot_cp.wait()

        base = pl.multiple_of(b * B, 16)
        gate_rows = [[None, None] for _ in range(el)]
        picks = []
        for kk in range(2):
            s = 2 * b + kk
            parts = []
            for e in range(el):
                hit = row_ids == sd[s, e:e + 1, :]
                gate_rows[e][kk] = jnp.sum(jnp.where(hit, sd[s, el + e:el + e + 1, :], 0.0), -1, keepdims=True)
                parts.append(jnp.where(hit, 1.0, 0.0).astype(BF))
            p2 = jnp.concatenate(parts, 0)
            picks.append(p2)
            for n in range(0, D, 512):
                xv = dot(p2, fa[s, :, n:n + 512]).astype(BF)
                gv_ = dot(p2, cotb[kk, :, n:n + 512]).astype(BF)
                for e in range(el):
                    at = pl.ds(pl.multiple_of(base + kk * capp, 16), capp)
                    xs[e, at, n:n + 512] = xv[e * capp:(e + 1) * capp]
                    gs[e, at, n:n + 512] = gv_[e * capp:(e + 1) * capp]
        here = pl.ds(base, B)
        gp_rows = []
        for e in range(el):
            gate_row = jnp.concatenate(gate_rows[e], 0)
            gpr = jnp.zeros((B, 1), F32)
            for n in range(0, FFW, 256):
                gv = dot(xs[e, here, :], wg[e, :, n:n + 256])
                uv = dot(xs[e, here, :], wu[e, :, n:n + 256])
                u = dot_nt(gs[e, here, :], wd[e, n:n + 256, :])
                sg = 1.0 / (1.0 + jnp.exp(-gv))
                act = gv * sg
                hid = act * uv
                gpr = gpr + jnp.sum(hid * u, -1, keepdims=True)
                hgs[e, here, n:n + 256] = (hid * gate_row).astype(BF)
                gh = u * gate_row
                hs[e, here, n:n + 256] = (gh * uv * (sg * (1.0 + gv * (1.0 - sg)))).astype(BF)
                hs[e, here, FFW + n:FFW + n + 256] = (gh * act).astype(BF)
            gp_rows.append(gpr)
            for n in range(0, D, 512):
                orow = dot(hgs[e, here, :], wd[e, :, n:n + 512]).astype(BF)
                irow = (dot_nt(hs[e, here, 0:FFW], wg[e, n:n + 512, :])
                        + dot_nt(hs[e, here, FFW:2 * FFW], wu[e, n:n + 512, :])).astype(BF)
                for kk in range(2):
                    orb[kk, e * capp:(e + 1) * capp, n:n + 512] = orow[kk * capp:(kk + 1) * capp]
                    irb[kk, e * capp:(e + 1) * capp, n:n + 512] = irow[kk * capp:(kk + 1) * capp]

        def back(bb):
            return (pltpu.make_async_copy(st_o, out_o.at[pl.ds(2 * bb, 2)], s_loc.at[3]),
                    pltpu.make_async_copy(st_i, gin_o.at[pl.ds(2 * bb, 2)], s_loc.at[4]))

        @pl.when(j >= 1)
        def _():
            for cp in back(0):
                cp.wait()
        for kk in range(2):
            s = 2 * b + kk
            for e in range(el):
                hit = picks[kk][e * capp:(e + 1) * capp].astype(F32)
                gp_o[s, e:e + 1, :] = jnp.sum(hit * gp_rows[e][kk * capp:(kk + 1) * capp], 0, keepdims=True)
            for n in range(0, D, 512):
                st_o[kk, :, n:n + 512] = dot_tn(picks[kk], orb[kk, :, n:n + 512]).astype(BF)
                st_i[kk, :, n:n + 512] = dot_tn(picks[kk], irb[kk, :, n:n + 512]).astype(BF)
        for cp in back(b):
            cp.start()

    n1 = D // 256
    n2 = FFW // 256

    def t1_copy(e, i):
        return pltpu.make_async_copy(st1.at[lax.rem(i, 2)], t1_o.at[e, pl.ds(pl.multiple_of(i * 256, 256), 256)],
                                     s_t.at[0, lax.rem(i, 2)])

    def t2_copy(e, i):
        return pltpu.make_async_copy(st2.at[lax.rem(i, 2)], t2_o.at[e, pl.ds(pl.multiple_of(i * 256, 256), 256)],
                                     s_t.at[1, lax.rem(i, 2)])

    for e in range(el):
        @pl.loop(0, n1)
        def _(i):
            @pl.when(i >= 2)
            def _():
                t1_copy(e, i).wait()
            col = pl.ds(pl.multiple_of(i * 256, 256), 256)
            st1[lax.rem(i, 2)] = dot_tn(xs[e, :, col], hs[e]).astype(BF)
            t1_copy(e, i).start()

        @pl.loop(0, n2)
        def _(i):
            @pl.when(i >= 2)
            def _():
                t2_copy(e, i).wait()
            col = pl.ds(pl.multiple_of(i * 256, 256), 256)
            st2[lax.rem(i, 2)] = dot_tn(hgs[e, :, col], gs[e]).astype(BF)
            t2_copy(e, i).start()
        for i in range(2):
            t1_copy(e, i).wait()
            t2_copy(e, i).wait()

    pltpu.make_async_copy(st_o, out_o.at[pl.ds(0, 2)], s_loc.at[3]).wait()
    pltpu.make_async_copy(st_i, gin_o.at[pl.ds(0, 2)], s_loc.at[4]).wait()
    sib_own.wait_send()
    for dr in range(2):
        for s in range(1, C):
            @pl.when(has(dr, s))
            def _():
                sib_out(dr, s).wait_send()
        for s in range(1, C):
            @pl.when(nxt_ok(dr) & has(dr, s - 1))
            def _():
                z_out(dr, s).wait_send()


def experts_call(nf, cap, ffn_in, cot_all, side, w_gate, w_up, w_down):
    T, D = ffn_in.shape
    el, _, FFW = w_gate.shape
    capp = cap + (-cap % 16)
    C = nf // 2
    rows = C * 2 * capp
    dma = pltpu.SemaphoreType.DMA
    out = [((nf, T, D), BF, 1), ((nf, T, D), BF, 1), ((nf, el, T), F32, 0),
           ((el, D, 2 * FFW), BF, 1), ((el, FFW, D), BF, 1)]
    return pl.pallas_call(
        functools.partial(experts_kernel, nf, el, cap, capp),
        out_shape=[jax.ShapeDtypeStruct(o[0], o[1]) for o in out],
        in_specs=[vm(), hbm(), vm(), hbm(), hbm(), hbm()],
        out_specs=[hbm() if o[2] else vm() for o in out],
        scratch_shapes=[
            VMEM((el, D, FFW), BF), VMEM((el, D, FFW), BF), VMEM((el, FFW, D), BF),
            VMEM((nf, T, D), BF), VMEM(side.shape, F32), VMEM((2, T, D), BF),
            VMEM((el, rows, D), BF), VMEM((el, rows, D), BF),
            VMEM((el, rows, 2 * FFW), BF), VMEM((el, rows, FFW), BF),
            VMEM((2, el * capp, D), BF), VMEM((2, el * capp, D), BF),
            VMEM((2, T, D), BF), VMEM((2, T, D), BF),
            VMEM((2, 256, 2 * FFW), BF), VMEM((2, 256, D), BF),
            dma((nf,)), dma((nf,)),
            dma((2, C)), dma((2, C)), dma((2, C)), dma((2, C)),
            dma((3,)), dma((5,)), dma((2, 2)),
        ],
        compiler_params=pltpu.CompilerParams(collective_id=2, has_side_effects=True,
                                             vmem_limit_bytes=62 * 2 ** 20),
        cost_estimate=pl.CostEstimate(flops=40_000_000_000, bytes_accessed=60_000_000, transcendentals=2_000_000),
        name="experts",
    )(ffn_in, cot_all, side, w_gate, w_up, w_down)


def add_blocks(dst, srcs, extra=None):
    @pl.loop(0, dst.shape[0] // 16)
    def _(i):
        at = pl.ds(pl.multiple_of(i * 16, 16), 16)
        total = srcs[0][at, :].astype(F32)
        for s in srcs[1:]:
            total = total + s[at, :].astype(F32)
        dst[at, :] = total.astype(dst.dtype)


class Line:
    def __init__(self, nf, f, d, acc, give, sib, rcv, stage, sems, stage_sem, credit=None):
        self.nf, self.f, self.d = nf, f, d
        self.C = nf // 2
        self.c, self.k = f // 2, lax.rem(f, 2)
        self.acc, self.give, self.sib, self.rcv, self.stage = acc, give, sib, rcv, stage
        self.s_sib, self.r_sib, self.s_z, self.r_z = sems
        self.stage_sem, self.credit = stage_sem, credit

    def remote(self, src, dst, ss, rs, to):
        return pltpu.make_async_remote_copy(src_ref=src, dst_ref=dst, send_sem=ss, recv_sem=rs,
                                            device_id=(to, self.d), device_id_type=MESH)

    def dest(self, dr, s):
        i = s - 1 - (self.C - 1 - self.c) if dr == 0 else s - 1 - self.c
        room = self.c if dr == 0 else self.C - 1 - self.c
        chip = i if dr == 0 else self.C - 1 - i
        return jnp.clip(chip, 0, self.C - 1), (i >= 0) & (i < room), i == 0

    def sib_copy(self, chip):
        return self.remote(self.give(chip), self.sib(chip), self.s_sib.at[chip], self.r_sib.at[chip],
                           self.f + 1 - 2 * self.k)

    def z_copy(self, dr, s, chip):
        return self.remote(self.acc(chip), self.rcv(dr, s - 1), self.s_z.at[dr, s - 1], self.r_z.at[dr, s - 1],
                           self.f - 2 if dr == 0 else self.f + 2)

    def z_in(self, dr, s):
        return self.remote(self.rcv(dr, s - 1), self.rcv(dr, s - 1), self.s_z.at[dr, s - 1], self.r_z.at[dr, s - 1],
                           self.f)

    def start_sib(self):
        if self.credit is not None:
            pl.semaphore_wait(self.credit.at[2], 1)
        for s in range(1, self.C):
            for dr in range(2):
                chip, ok, _ = self.dest(dr, s)

                @pl.when(ok)
                def _():
                    self.sib_copy(chip).start()
        self.sib_copy(self.c).start()

    def gather(self, chip, srcs):
        acc = self.acc(chip)
        if self.stage is None:
            add_blocks(acc, [acc] + srcs)
            return
        for s in srcs:
            cp = pltpu.make_async_copy(s, self.stage, self.stage_sem)
            cp.start()
            cp.wait()
            add_blocks(acc, [acc, self.stage])

    def step(self, s):
        for dr in range(2):
            chip, ok, opening = self.dest(dr, s)
            begins = (self.c == self.C - 1) if dr == 0 else (self.c == 0)

            @pl.when(ok)
            def _():
                self.sib_copy(chip).wait_recv()

                @pl.when(begins)
                def _():
                    self.gather(chip, [self.sib(chip)])
                if s > 1:
                    @pl.when(jnp.logical_not(begins))
                    def _():
                        self.z_in(dr, s - 1).wait_recv()
                        self.gather(chip, [self.sib(chip), self.rcv(dr, s - 2)])
                if self.credit is not None:
                    @pl.when(opening)
                    def _():
                        pl.semaphore_wait(self.credit.at[dr], 1)
                self.z_copy(dr, s, chip).start()

    def last(self):
        self.sib_copy(self.c).wait_recv()
        mid = (self.c > 0) & (self.c < self.C - 1)
        s = self.C - 1
        for dr in range(2):
            @pl.when((self.c < self.C - 1) if dr == 0 else (self.c > 0))
            def _():
                self.z_in(dr, s).wait_recv()

        @pl.when(mid)
        def _():
            self.gather(self.c, [self.sib(self.c), self.rcv(0, s - 1), self.rcv(1, s - 1)])

        @pl.when(self.c == 0)
        def _():
            self.gather(self.c, [self.sib(self.c), self.rcv(0, s - 1)])

        @pl.when(self.c == self.C - 1)
        def _():
            self.gather(self.c, [self.sib(self.c), self.rcv(1, s - 1)])

    def sent(self):
        self.sib_copy(self.c).wait_send()
        for s in range(1, self.C):
            for dr in range(2):
                chip, ok, _ = self.dest(dr, s)

                @pl.when(ok)
                def _():
                    self.sib_copy(chip).wait_send()
                    self.z_copy(dr, s, chip).wait_send()

    def free(self, credit):
        def tell(i, to):
            pl.semaphore_signal(credit.at[i], inc=1, device_id=(to, self.d), device_id_type=MESH)

        tell(2, self.f + 1 - 2 * self.k)

        @pl.when(self.c < self.C - 1)
        def _():
            tell(0, self.f + 2)

        @pl.when(self.c > 0)
        def _():
            tell(1, self.f - 2)


class Cube:
    def __init__(self, nd, f, d, flip, lanes, size, own, land, total, out, sems):
        m = nd.bit_length() - 1
        self.bits = list(range(m))[::-1] if flip else list(range(m))
        self.f, self.d, self.lanes = f, d, lanes
        self.own, self.land, self.total, self.out = own, land, total, out
        self.ss, self.rs = sems
        self.m = m
        self.low, self.length = [0], [size]
        for b in self.bits:
            half = self.length[-1] // 2
            side = lax.rem(d // (1 << b), 2)
            self.low.append(self.low[-1] + side * half)
            self.length.append(half)

    def cut(self, ref, at, n):
        if self.lanes:
            return ref.at[:, pl.ds(pl.multiple_of(at, 128), n)]
        return ref.at[pl.ds(pl.multiple_of(at, 16), n)]

    def remote(self, src, dst, i, to_bit):
        return pltpu.make_async_remote_copy(src_ref=src, dst_ref=dst, send_sem=self.ss.at[i], recv_sem=self.rs.at[i],
                                            device_id=(self.f, jnp.bitwise_xor(self.d, 1 << to_bit)),
                                            device_id_type=MESH)

    def level(self, i):
        if i == 0:
            return self.own, 0
        if i == self.m:
            return self.out, 0
        return self.total(i - 1), self.low[i]

    def down(self, i):
        ref, base = self.level(i)
        half = self.length[i + 1]
        other = 2 * self.low[i] + half - self.low[i + 1]
        return self.remote(self.cut(ref, other - base, half), self.land(i), i, self.bits[i])

    def merge(self, i, add):
        self.down(i).wait_recv()
        ref, base = self.level(i)
        dst, dbase = self.level(i + 1)
        half = self.length[i + 1]
        low = self.low[i + 1]
        add(self.cut(dst, low - dbase, half), self.cut(ref, low - base, half), self.land(i))

    def up(self, i):
        blk = self.cut(self.out, self.low[i + 1], self.length[i + 1])
        return self.remote(blk, blk, self.m + i, self.bits[i])

    def up_in(self, i):
        half = self.length[i + 1]
        other = 2 * self.low[i] + half - self.low[i + 1]
        blk = self.cut(self.out, other, half)
        return self.remote(blk, blk, self.m + i, self.bits[i])

    def sent(self):
        for i in range(self.m):
            self.down(i).wait_send()
            self.up(i).wait_send()


def pipe_add(dst, a, b):
    n, w = dst.shape
    tile = 32
    spec = pl.BlockSpec((tile, w), lambda i: (i, 0))

    def inner(a_ref, b_ref, o_ref):
        o_ref[...] = (a_ref[...].astype(F32) + b_ref[...].astype(F32)).astype(o_ref.dtype)

    pltpu.emit_pipeline(inner, grid=(n // tile,), in_specs=[spec, spec], out_specs=[spec])(a, b, dst)


def back_kernel(nf, nd, el, land_hbm, *refs):
    m = nd.bit_length() - 1
    it = iter(refs)

    def take(n):
        return [next(it) for _ in range(n)]

    (gin_p, out_p, gp_p, t1, t2, tok_h, cot_h, hid_h, ffn_h, gates, mix_h, qk_h, v_h, prob_h, wf_h, rt,
     cosr, sinr) = take(18)
    out_o, gt_o, sh_o, sm_o, t1_o, t2_o = take(6)
    l1 = take(m)
    l2 = take(m)
    a1 = take(m - 1)
    a2 = take(m - 1)
    sib, rcv, sibq, rcvq = take(4)
    (acc, wb, wg, tok, cot, hid, ffn, mix, qk, v, prob, branch, gh, ga, gproj, gpb, smg, smr, smd, shb, sms) = take(21)
    attn, gm = ffn, mix
    shl = take(m)
    stage, stageq = take(2)
    (s_load, s_acc, s_gp, r_gp, s_sib, r_sib, s_z, r_z, s_cube, r_cube, s_sc, r_sc, s_sm, r_sm, s_sd, r_sd,
     s_stage, s_prob, cred) = take(19)

    T, D = tok.shape
    R = wg.shape[0] // nf
    W = wg.shape[1]
    E = gates.shape[0]
    C = nf // 2
    f = lax.axis_index("fsdp")
    d = lax.axis_index("dp")
    c = f // 2
    k = lax.rem(f, 2)
    QV = QW + 2 * KW
    greet(nf, nd, f, d)

    def remote(src, dst, ss, rs, to_f, to_d):
        return pltpu.make_async_remote_copy(src_ref=src, dst_ref=dst, send_sem=ss, recv_sem=rs,
                                            device_id=(to_f, to_d), device_id_type=MESH)

    def rows(ff):
        return pl.ds(pl.multiple_of(ff * R, 16), R)

    st = stage if land_hbm else None
    stq = stageq if land_hbm else None

    def sems(i):
        return (s_sib.at[i], r_sib.at[i], s_z.at[i], r_z.at[i])

    gin_line = Line(nf, f, d, lambda ch: acc.at[ch], lambda ch: gin_p.at[2 * ch + 1 - k], lambda ch: sib.at[ch],
                    lambda dr, s: rcv.at[dr, s], st, sems(0), s_stage)
    wo_cols = pl.ds(QV, D)
    o_line = Line(nf, f, d, lambda ch: wg.at[rows(2 * ch + k), wo_cols], lambda ch: wg.at[rows(2 * ch + 1 - k), wo_cols],
                  lambda ch: sib.at[ch, 0:R], lambda dr, s: rcv.at[dr, s, 0:R],
                  stage.at[0:R] if land_hbm else None, sems(1), s_stage, cred.at[0])
    q_cols = pl.ds(0, QV)
    q_line = Line(nf, f, d, lambda ch: wg.at[rows(2 * ch + k), q_cols], lambda ch: wg.at[rows(2 * ch + 1 - k), q_cols],
                  lambda ch: sibq.at[ch], lambda dr, s: rcvq.at[dr, s], stq, sems(2), s_stage)
    out_line = Line(nf, f, d, lambda ch: acc.at[ch], lambda ch: out_p.at[2 * ch + 1 - k], lambda ch: sib.at[ch],
                    lambda dr, s: rcv.at[dr, s], st, sems(3), s_stage, cred.at[1])

    def acc_loads(src):
        return [pltpu.make_async_copy(src.at[2 * ch + k], acc.at[ch], s_acc.at[ch]) for ch in range(C)]

    gp_copies = []
    for i in range(1, nf):
        to = lax.rem(f + i, nf)
        cp = remote(gp_p.at[to], gpb.at[f], s_gp.at[i - 1], r_gp.at[i - 1], to, d)
        cp.start()
        gp_copies.append(cp)
    loads = acc_loads(gin_p)
    for cp in loads:
        cp.start()
    gin_line.start_sib()
    cubes = []
    for e in range(el):
        for j, (src, out, ls, ts, size) in enumerate(((t1, t1_o, l1, a1, D), (t2, t2_o, l2, a2, t2.shape[1]))):
            cube = Cube(nd, f, d, e >= el // 2, False, size, src.at[e],
                        functools.partial(lambda ls, e, i: ls[i].at[e], ls, e),
                        functools.partial(lambda ts, e, i: ts[i].at[e], ts, e), out.at[e],
                        (s_cube.at[2 * e + j], r_cube.at[2 * e + j]))
            cubes.append(cube)
    for cube in cubes:
        cube.down(0).start()
    own_gp = pltpu.make_async_copy(gp_p.at[f], gpb.at[f], s_load.at[0])
    own_gp.start()
    wo = pltpu.make_async_copy(wf_h.at[:, QV:QV + D], wb.at[:, 0:D], s_load.at[1])
    wo.start()
    others = [(tok_h, tok), (cot_h, cot), (hid_h, hid), (ffn_h, ffn), (mix_h, mix), (qk_h, qk), (v_h, v)]
    more = [pltpu.make_async_copy(a, b, s_load.at[2 + i]) for i, (a, b) in enumerate(others)]
    for cp in more:
        cp.start()

    def prob_load(i):
        at = pl.ds(i * 2 * GROUP, 2 * GROUP)
        return pltpu.make_async_copy(prob_h.at[at], prob.at[lax.rem(i, 2)], s_prob.at[lax.rem(i, 2)])

    prob_load(0).start()
    for cp in loads:
        cp.wait()

    for s in range(1, C):
        gin_line.step(s)
    for cp in more:
        cp.wait()
    own_gp.wait()
    for cp in gp_copies:
        cp.wait()
    gin_line.last()
    gin_line.free(cred.at[0])

    gains = rt[E:E + 2].astype(F32)
    gain_one, gain_two = gains[0:1], gains[1:2]
    gpt = jnp.concatenate([gpb[i] for i in range(nf)], 0)
    gates_v = gates[...]
    gl = (gates_v * (gpt - jnp.sum(gpt * gates_v, 0, keepdims=True))).astype(BF)
    for n in range(0, D, 512):
        sms[0:E, n:n + 512] = dot(gl, ffn[:, n:n + 512])
    for n in range(0, D, 512):
        ga[:, n:n + 512] = dot_tn(gl, rt[0:E, n:n + 512])
    sms[E:, :] = jnp.zeros((sms.shape[0] - E, D), F32)
    TR = 32

    @pl.loop(0, T // TR)
    def _(i):
        at = pl.ds(pl.multiple_of(i * TR, TR), TR)
        h = hid[at, :]
        r2 = lax.rsqrt(jnp.mean(h * h, -1, keepdims=True) + EPSILON)
        n2 = h * r2
        gf = acc[c, at, :].astype(F32) + ga[at, :]
        sms[E + 1:E + 2, :] += jnp.sum(gf * n2, 0, keepdims=True)
        g2 = gf * gain_two
        x = cot[at, :].astype(F32) + r2 * (g2 - n2 * jnp.mean(g2 * n2, -1, keepdims=True))
        gh[at, :] = x
        branch[at, :] = x.astype(BF)

    @pl.loop(0, QW // 256)
    def _(i):
        at = pl.ds(pl.multiple_of(i * 256, 256), 256)
        wg[at, QV:QV + D] = dot_tn(mix[:, at], branch[...]).astype(BF)
    o_line.start_sib()
    o_line.step(1)
    gin_line.sent()
    wo.wait()

    @pl.loop(0, QW // 256)
    def _(i):
        at = pl.ds(pl.multiple_of(i * 256, 256), 256)
        gm[:, at] = dot_nt(branch[...], wb[at, 0:D]).astype(BF)
    wq = pltpu.make_async_copy(wf_h.at[:, 0:QV], wb, s_load.at[1])
    wq.start()
    for cube in cubes:
        cube.merge(0, pipe_add)
    for cube in cubes:
        cube.down(1).start() if m > 1 else cube.up(0).start()

    factor = HEAD_SIZE ** (-0.5)
    lane = lax.broadcasted_iota(jnp.int32, (T, 128), 1)
    low = lane < HEAD_SIZE
    first = lax.rem(lane, HEAD_SIZE) < HEAD_SIZE // 2

    def unrotate(x):
        return x * cosr[...] - half_roll(x, first) * sinr[...]

    @pl.loop(0, KEY_VALUE_HEADS // 2)
    def _(i):
        @pl.when(i + 1 < KEY_VALUE_HEADS // 2)
        def _():
            prob_load(i + 1).start()
        prob_load(i).wait()
        slot = lax.rem(i, 2)
        kcol = pl.ds(pl.multiple_of(i * 128, 128), 128)
        kh = head_masks(qk[:, pl.ds(pl.multiple_of(QW + i * 128, 128), 128)], lane)
        vh = head_masks(v[:, kcol], lane)
        gk = [[None, None], [None, None]]
        gv = [[None, None], [None, None]]
        for p in range(GROUP):
            qc = pl.ds(pl.multiple_of((i * GROUP + p) * 128, 128), 128)
            q = qk[:, qc]
            g = gm[:, qc]
            gq = None
            for half in range(2):
                kv = (2 * p + half) // GROUP
                pr = prob[slot, 2 * p + half]
                prf = pr.astype(F32)
                gp = dot_nt(g, vh[kv][half])
                gs = (prf * (gp - jnp.sum(prf * gp, -1, keepdims=True))).astype(BF)
                term = dot(gs, kh[kv][half])
                gq = term if gq is None else gq + term
                tk = dot_tn(gs, q)
                tv = dot_tn(pr, g)
                gk[kv][half] = tk if gk[kv][half] is None else gk[kv][half] + tk
                gv[kv][half] = tv if gv[kv][half] is None else gv[kv][half] + tv
            gproj[:, qc] = unrotate(gq * factor).astype(BF)

        def join(x):
            a = jnp.where(low, x[0][0] + pltpu.roll(x[0][1], HEAD_SIZE, axis=1), 0.0)
            b = jnp.where(low, 0.0, pltpu.roll(x[1][0], HEAD_SIZE, axis=1) + x[1][1])
            return a + b

        gproj[:, pl.ds(pl.multiple_of(QW + i * 128, 128), 128)] = unrotate(join(gk) * factor).astype(BF)
        gproj[:, pl.ds(pl.multiple_of(QW + KW + i * 128, 128), 128)] = join(gv).astype(BF)

    if C > 2:
        o_line.step(2)
    @pl.loop(0, T // TR)
    def _(i):
        at = pl.ds(pl.multiple_of(i * TR, TR), TR)
        x = tok[at, :].astype(F32)
        r1 = lax.rsqrt(jnp.mean(x * x, -1, keepdims=True) + EPSILON)
        attn[at, :] = (x * r1 * gain_one).astype(BF)

    @pl.loop(0, D // 256)
    def _(i):
        at = pl.ds(pl.multiple_of(i * 256, 256), 256)
        for n in range(0, QV, 512):
            wg[at, n:n + 512] = dot_tn(attn[:, at], gproj[:, n:n + 512]).astype(BF)
    q_line.start_sib()
    for s in range(3, C):
        o_line.step(s)
    q_line.step(1)
    if m > 1:
        for cube in cubes:
            cube.merge(1, pipe_add)
        for cube in cubes:
            cube.down(2).start() if m > 2 else cube.up(1).start()
    wq.wait()

    @pl.loop(0, D // 256)
    def _(i):
        at = pl.ds(pl.multiple_of(i * 256, 256), 256)
        ga[:, at] = dot_nt(gproj[...], wb[at, :])

    @pl.loop(0, T // TR)
    def _(i):
        at = pl.ds(pl.multiple_of(i * TR, TR), TR)
        x = tok[at, :].astype(F32)
        r1 = lax.rsqrt(jnp.mean(x * x, -1, keepdims=True) + EPSILON)
        n1 = x * r1
        gat = ga[at, :]
        sms[E:E + 1, :] += jnp.sum(gat * n1, 0, keepdims=True)
        g1 = gat * gain_one
        gt_o[at, :] = (gh[at, :] + r1 * (g1 - n1 * jnp.mean(g1 * n1, -1, keepdims=True))).astype(BF)

    small = sms[...]
    for i in range(nf):
        smg[i] = small[:, i * R:(i + 1) * R]
    sm_copies = []
    for i in range(1, nf):
        to = lax.rem(f + i, nf)
        cp = remote(smg.at[to], smr.at[f], s_sm.at[i - 1], r_sm.at[i - 1], to, d)
        cp.start()
        sm_copies.append(cp)
    smr_own = pltpu.make_async_copy(smg.at[f], smr.at[f], s_load.at[0])
    smr_own.start()

    o_line.last()
    o_line.free(cred.at[1])
    if C > 2:
        q_line.step(2)
    o_line.sent()
    out_loads = acc_loads(out_p)
    for cp in out_loads:
        cp.start()
    smr_own.wait()
    for cp in sm_copies:
        cp.wait()
    total = smr[0]
    for i in range(1, nf):
        total = total + smr[i]
    smd[0] = total
    sd_copies = []
    for i in range(1, nd):
        cp = remote(smd.at[0], smd.at[i], s_sd.at[i - 1], r_sd.at[i - 1], f, jnp.bitwise_xor(d, i))
        cp.start()
        sd_copies.append(cp)
    for s in range(3, C):
        q_line.step(s)
    out_line.start_sib()
    for cp in out_loads:
        cp.wait()
    if m > 2:
        for i in range(2, m):
            for cube in cubes:
                cube.merge(i, pipe_add)
            for cube in cubes:
                cube.down(i + 1).start() if i + 1 < m else cube.up(m - 1).start()
    for i in range(m - 1, 0, -1):
        for cube in cubes:
            cube.up_in(i).wait_recv()
        for cube in cubes:
            cube.up(i - 1).start()
    out_line.step(1)
    q_line.last()

    own = wg.at[rows(f)]
    add_blocks(shb, [own])
    half = W // 2
    shards = []
    for h in range(2):
        shards.append(Cube(nd, f, d, h == 1, True, half, shb.at[:, h * half:(h + 1) * half],
                           functools.partial(lambda h, i: shl[i].at[h], h),
                           functools.partial(lambda h, i: shb.at[:, h * half:(h + 1) * half], h),
                           sh_o.at[:, h * half:(h + 1) * half], (s_sc.at[h], r_sc.at[h])))

    def level(self, i):
        return (self.own, 0) if i < self.m else (self.out, 0)

    for cube in shards:
        cube.level = functools.partial(level, cube)
        cube.down(0).start()

    def vadd(dst, a, b):
        add_blocks(dst, [a, b])

    if C > 2:
        out_line.step(2)
    for i in range(m):
        for cube in shards:
            cube.merge(i, vadd)
        for cube in shards:
            cube.down(i + 1).start() if i + 1 < m else cube.up(i).start()
    for s in range(3, C):
        out_line.step(s)
    for i in range(m - 1, 0, -1):
        for cube in shards:
            cube.up_in(i).wait_recv()
        for cube in shards:
            cube.up(i - 1).start()
    for cp in sd_copies:
        cp.wait()
    total = smd[0]
    for i in range(1, nd):
        total = total + smd[i]
    sm_o[...] = total
    out_line.last()

    @pl.loop(0, T // TR)
    def _(i):
        at = pl.ds(pl.multiple_of(i * TR, TR), TR)
        out_o[at, :] = (hid[at, :] + acc[c, at, :].astype(F32)).astype(BF)


    q_line.sent()
    out_line.sent()
    for cube in cubes + shards:
        cube.up_in(0).wait_recv()
        cube.sent()


def back(nf, nd, el, args):
    gin, t1, t2 = args[0], args[3], args[4]
    _, T, D = gin.shape
    E = args[9].shape[0]
    W = args[14].shape[1]
    R = D // nf
    C = nf // 2
    m = nd.bit_length() - 1
    QV = QW + 2 * KW
    FFW = t2.shape[1]
    SR = E + 2 + (-(E + 2) % 8)
    land_hbm = C > 4
    s = jax.ShapeDtypeStruct
    out_shape = [s((T, D), BF), s((T, D), BF), s((R, W), BF), s((SR, R), F32), s(t1.shape, BF), s(t2.shape, BF)]
    out_specs = [vm(), vm(), vm(), vm(), hbm(), hbm()]
    extra = [(el, D >> (i + 1), t1.shape[2]) for i in range(m)] + [(el, FFW >> (i + 1), D) for i in range(m)]
    extra += [(el, D >> (i + 1), t1.shape[2]) for i in range(m - 1)] + [(el, FFW >> (i + 1), D) for i in range(m - 1)]
    lands = [(C, T, D), (2, C - 1, T, D), (C, R, QV), (2, C - 1, R, QV)]
    scratch = []
    if land_hbm:
        extra += lands
    else:
        scratch += [VMEM(x, BF) for x in lands]
    out_shape += [s(x, BF) for x in extra]
    out_specs += [hbm()] * len(extra)
    dma = pltpu.SemaphoreType.DMA
    scratch += [
        VMEM((C, T, D), BF), VMEM((D, QV), BF), VMEM((D, W), BF),
        VMEM((T, D), BF), VMEM((T, D), BF), VMEM((T, D), F32), VMEM((T, D), BF), VMEM((T, QW), BF),
        VMEM((T, QW + KW), BF), VMEM((T, KW), BF), VMEM((2, 2 * GROUP, T, T), BF),
        VMEM((T, D), BF), VMEM((T, D), F32), VMEM((T, D), F32), VMEM((T, QV), BF),
        VMEM((nf, el, T), F32), VMEM((nf, SR, R), F32), VMEM((nf, SR, R), F32), VMEM((nd, SR, R), F32), VMEM((R, W), BF),
        VMEM((SR, D), F32),
    ]
    scratch += [VMEM((2, R, W >> (i + 2)), BF) for i in range(m)]
    scratch += [VMEM((T, D) if land_hbm else (16, 128), BF), VMEM((R, QV) if land_hbm else (16, 128), BF)]
    scratch += [
        dma((10,)), dma((C,)), dma((nf,)), dma((nf,)),
        dma((4, C)), dma((4, C)), dma((4, 2, C)), dma((4, 2, C)),
        dma((2 * el, 2 * m)), dma((2 * el, 2 * m)), dma((2, 2 * m)), dma((2, 2 * m)),
        dma((nf,)), dma((nf,)), dma((nd,)), dma((nd,)), dma(()), dma((2,)),
        pltpu.SemaphoreType.REGULAR((2, 3)),
    ]
    inner = [hbm(), hbm(), vm(), hbm(), hbm(), hbm(), hbm(), hbm(), hbm(), vm(), hbm(), hbm(), hbm(), hbm(), hbm(), vm(),
             vm(), vm()]
    return pl.pallas_call(
        functools.partial(back_kernel, nf, nd, el, land_hbm),
        out_shape=out_shape,
        in_specs=inner,
        out_specs=out_specs,
        scratch_shapes=scratch,
        compiler_params=pltpu.CompilerParams(collective_id=3, has_side_effects=True,
                                             vmem_limit_bytes=63 * 2 ** 20),
        cost_estimate=pl.CostEstimate(flops=8_000_000_000, bytes_accessed=90_000_000, transcendentals=100_000),
        name="back",
    )(*args)[:6]


def body(tokens, w_query, key_weight, value_weight, w_out, gain_attn, gain_ffn, w_router,
         w_gate, w_up, w_down, routes, cotangent):
    T = tokens.shape[0]
    el = w_gate.shape[0]
    ff = w_gate.shape[2]
    nf = lax.axis_size("fsdp")
    nd = lax.axis_size("dp")
    experts = el * nf
    cap = 9 * T * TOP // (8 * experts)

    packed = jnp.concatenate([w_query, key_weight, value_weight, w_out], 1)
    pad = -(experts + 2) % 16
    small = jnp.concatenate([w_router, gain_attn[:, None], gain_ffn[:, None],
                             jnp.zeros((w_router.shape[0], pad), BF)], 1).T
    onehot = (routes[:, :, None] == jnp.arange(experts, dtype=jnp.int32)).any(1).astype(BF)
    earlier = (jnp.arange(T)[:, None] < jnp.arange(T)[None, :]).astype(BF)
    before = lax.dot_general(onehot, earlier, (((0,), (0,)), ((), ())), preferred_element_type=F32)
    slots = jnp.where(onehot.T > 0, before, -1.0)
    cosr, sinr = rope_rows(T)
    ffn_in, hidden, gates, mixed, qk, v, probs, full, cot_all, rt = front(
        nf, nd, experts, tokens, packed, small, cotangent, slots, cosr, sinr)
    side = jnp.concatenate([slots.reshape(nf, el, T), gates.reshape(nf, el, T)], 1)
    out_part, gin_part, gp_part, t1, t2 = experts_call(nf, cap, ffn_in, cot_all, side, w_gate, w_up, w_down)
    output, grad_tokens, shard, smalls, t1, t2 = back(nf, nd, el, (
        gin_part, out_part, gp_part, t1, t2, tokens, cotangent, hidden, ffn_in, gates, mixed, qk, v, probs, full, rt,
        cosr, sinr))
    big = shard.astype(F32)
    return (
        output,
        grad_tokens,
        big[:, :QW],
        big[:, QW: QW + KW],
        big[:, QW + KW: QW + 2 * KW],
        big[:, QW + 2 * KW:],
        smalls[experts],
        smalls[experts + 1],
        smalls[:experts].T,
        t1[:, :, :ff].astype(F32),
        t1[:, :, ff:].astype(F32),
        t2.astype(F32),
    )


def solution(mesh):
    in_specs = (
        P(("fsdp", "dp"), None),
        P("fsdp", None),
        P("fsdp", None),
        P("fsdp", None),
        P("fsdp", None),
        P("fsdp"),
        P("fsdp"),
        P("fsdp", None),
        P("fsdp", None, None),
        P("fsdp", None, None),
        P("fsdp", None, None),
        P(("fsdp", "dp"), None),
        P(("fsdp", "dp"), None),
    )
    out_specs = (
        P(("fsdp", "dp"), None),
        P(("fsdp", "dp"), None),
        P("fsdp", None),
        P("fsdp", None),
        P("fsdp", None),
        P("fsdp", None),
        P("fsdp"),
        P("fsdp"),
        P("fsdp", None),
        P("fsdp", None, None),
        P("fsdp", None, None),
        P("fsdp", None, None),
    )
    return jax.shard_map(body, mesh=mesh, in_specs=in_specs, out_specs=out_specs, check_vma=False)
```

```python
import functools
import jax
import jax.numpy as jnp
from jax import lax
from jax.experimental import pallas as pl
from jax.experimental.pallas import tpu as pltpu
from jax.sharding import PartitionSpec as P
import numpy as np

MODEL_WIDTH = 1536
QUERY_HEADS = 24
KEY_VALUE_HEADS = 8
HEAD_SIZE = 64
TOP = 8
GROUP = QUERY_HEADS // KEY_VALUE_HEADS
QW = QUERY_HEADS * HEAD_SIZE
KW = KEY_VALUE_HEADS * HEAD_SIZE

EPSILON = 1e-06
ROPE_BASE = 10000.0
MASKED = -1e30
F32 = jnp.float32
BF = jnp.bfloat16


def rope_rows(T):
    half = HEAD_SIZE // 2
    freq = ROPE_BASE ** (-2.0 * np.arange(half, dtype=np.float64) / HEAD_SIZE)
    ang = (np.arange(T, dtype=np.float32)[:, None] * freq.astype(np.float32)[None, :]).astype(np.float32)
    c, s = np.cos(ang), np.sin(ang)
    return (jnp.asarray(np.concatenate([c, c, c, c], 1), F32), jnp.asarray(np.concatenate([-s, s, -s, s], 1), F32))


MESH = pl.DeviceIdType.MESH
VMEM = pltpu.VMEM


def vm():
    return pl.BlockSpec(memory_space=pltpu.VMEM)


def hbm():
    return pl.BlockSpec(memory_space=pl.ANY)


def dot(a, b):
    return lax.dot_general(a, b, (((1,), (0,)), ((), ())), preferred_element_type=F32)


def dot_nt(a, b):
    return lax.dot_general(a, b, (((1,), (1,)), ((), ())), preferred_element_type=F32)


def dot_tn(a, b):
    return lax.dot_general(a, b, (((0,), (0,)), ((), ())), preferred_element_type=F32)


def half_roll(x, first):
    n = x.shape[1]
    h = HEAD_SIZE // 2
    return jnp.where(first, pltpu.roll(x, n - h, axis=1), pltpu.roll(x, h, axis=1))


def greet(nf, nd, f, d):
    barrier = pltpu.get_barrier_semaphore()
    for i in range(1, nf):
        pl.semaphore_signal(barrier, inc=1, device_id=(lax.rem(f + i, nf), d), device_id_type=MESH)
    for i in range(1, nd):
        pl.semaphore_signal(barrier, inc=1, device_id=(f, jnp.bitwise_xor(d, i)), device_id_type=MESH)
    pl.semaphore_wait(barrier, nf + nd - 2)


def head_masks(kblk, lane):
    kf = kblk.astype(F32)
    kr = pltpu.roll(kf, HEAD_SIZE, axis=1)
    low = lane < HEAD_SIZE
    zero = jnp.zeros_like(kf)
    a0 = jnp.where(low, kf, zero).astype(BF)
    a1 = jnp.where(low, zero, kr).astype(BF)
    b0 = jnp.where(low, kr, zero).astype(BF)
    b1 = jnp.where(low, zero, kf).astype(BF)
    return ((a0, a1), (b0, b1))


def front_kernel(nf, nd, experts, tok, wq, wk, wv, wo, small, cot, slots, cosr, sinr,
                 ffn_o, hid_o, gates_o, mix_o, qk_o, v_o, prob_o, wf_o, cot_o, rt_o,
                 wf, sm, attn, rot,
                 s_sm, r_sm, s_z, r_z, s_dp, r_dp, s_sib, r_sib, s_cz, r_cz, s_cs, r_cs, s_loc, s_w):
    T, D = tok.shape
    C = nf // 2
    R = wq.shape[0]
    W = wf.shape[1]
    WA = 3 * W // 4
    parts = ((0, WA), (WA, W - WA))
    f = lax.axis_index("fsdp")
    d = lax.axis_index("dp")
    c = f // 2
    k = lax.rem(f, 2)
    sib = f + 1 - 2 * k
    greet(nf, nd, f, d)

    def rows(ff):
        return pl.ds(pl.multiple_of(ff * R, 16), R)

    def cols(dd, g):
        at, n = parts[g]
        return pl.ds(pl.multiple_of(at + dd * (n // nd), 128), n // nd)

    def remote(src, dst, ss, rs, to_f, to_d):
        return pltpu.make_async_remote_copy(src_ref=src, dst_ref=dst, send_sem=ss, recv_sem=rs,
                                            device_id=(to_f, to_d), device_id_type=MESH)

    def src_chip(dr, s):
        return c - s if dr == 0 else c + s

    def has(dr, s):
        return (c - s >= 0) if dr == 0 else (c + s < C)

    def nxt_ok(dr):
        return (c + 1 < C) if dr == 0 else (c - 1 >= 0)

    def nxt_f(dr):
        return f + 2 if dr == 0 else f - 2

    def wz(dr, s, g):
        blk = wf.at[rows(2 * src_chip(dr, s - 1) + k), cols(d, g)]
        return remote(blk, blk, s_z.at[g, dr, s - 1], r_z.at[g, dr, s - 1], nxt_f(dr), d)

    def wz_in(dr, s, g):
        blk = wf.at[rows(2 * src_chip(dr, s) + k), cols(d, g)]
        return remote(blk, blk, s_z.at[g, dr, s - 1], r_z.at[g, dr, s - 1], f, d)

    at = 0
    w_own = []
    for i, w in enumerate((wq, wk, wv, wo)):
        w_own.append(pltpu.make_async_copy(w, wf.at[rows(f), at:at + w.shape[1]], s_w.at[i]))
        at += w.shape[1]
    for cp in w_own:
        cp.start()
    for cp in w_own:
        cp.wait()
    for g in range(2):
        for dr in range(2):
            @pl.when(nxt_ok(dr))
            def _():
                wz(dr, 1, g).start()

    own_small = pltpu.make_async_copy(small, sm.at[f], s_loc.at[0])
    own_small.start()
    sm_copies = []
    for i in range(1, nf):
        cp = remote(small, sm.at[f], s_sm.at[i - 1], r_sm.at[i - 1], lax.rem(f + i, nf), d)
        cp.start()
        sm_copies.append(cp)
    sib_own = remote(wf.at[rows(f)], wf.at[rows(f)], s_sib.at[0, 0, 0], r_sib.at[0, 0, 0], sib, d)
    sib_own.start()
    own_c = pltpu.make_async_copy(cot, cot_o.at[f], s_loc.at[2])
    own_c.start()
    sib_c = remote(cot, cot_o.at[f], s_cs.at[0, 0], r_cs.at[0, 0], sib, d)

    def dp_copy(dr, s, g, i):
        blk = wf.at[rows(2 * src_chip(dr, s) + k), cols(d, g)]
        return remote(blk, blk, s_dp.at[g, dr, s - 1, i - 1], r_dp.at[g, dr, s - 1, i - 1], f, jnp.bitwise_xor(d, i))

    def dp_in(dr, s, g, i):
        blk = wf.at[rows(2 * src_chip(dr, s) + k), cols(jnp.bitwise_xor(d, i), g)]
        return remote(blk, blk, s_dp.at[g, dr, s - 1, i - 1], r_dp.at[g, dr, s - 1, i - 1], f, d)

    def sib_copy(dr, s, g):
        at, n = parts[g]
        blk = wf.at[rows(2 * src_chip(dr, s) + k), at:at + n]
        return remote(blk, blk, s_sib.at[g, dr, s], r_sib.at[g, dr, s], sib, d)

    def sib_in(dr, s, g):
        at, n = parts[g]
        blk = wf.at[rows(2 * src_chip(dr, s) + 1 - k), at:at + n]
        return remote(blk, blk, s_sib.at[g, dr, s], r_sib.at[g, dr, s], sib, d)

    def cz(dr, s, own):
        ff = 2 * src_chip(dr, s - 1) + k
        src = cot if own else cot_o.at[ff]
        return remote(src, cot_o.at[ff], s_cz.at[dr, s - 1], r_cz.at[dr, s - 1], nxt_f(dr), d)

    def cz_in(dr, s):
        ff = 2 * src_chip(dr, s) + k
        return remote(cot_o.at[ff], cot_o.at[ff], s_cz.at[dr, s - 1], r_cz.at[dr, s - 1], f, d)

    def cs(dr, s):
        ff = 2 * src_chip(dr, s) + k
        return remote(cot_o.at[ff], cot_o.at[ff], s_cs.at[dr, s], r_cs.at[dr, s], sib, d)

    def cs_in(dr, s):
        ff = 2 * src_chip(dr, s) + 1 - k
        return remote(cot_o.at[ff], cot_o.at[ff], s_cs.at[dr, s], r_cs.at[dr, s], sib, d)

    for s in range(1, C):
        for g in range(2):
            for dr in range(2):
                @pl.when(has(dr, s))
                def _():
                    wz_in(dr, s, g).wait_recv()
                    if s < C - 1:
                        @pl.when(nxt_ok(dr))
                        def _():
                            wz(dr, s + 1, g).start()
                    if g == 0:
                        for i in range(1, nd):
                            dp_copy(dr, s, g, i).start()
    for dr in range(2):
        @pl.when(nxt_ok(dr))
        def _():
            cz(dr, 1, True).start()
    sib_c.start()
    for s in range(1, C):
        for dr in range(2):
            @pl.when(has(dr, s))
            def _():
                for i in range(1, nd):
                    dp_copy(dr, s, 1, i).start()

    def group_in(s, g):
        for dr in range(2):
            @pl.when(has(dr, s))
            def _():
                for i in range(1, nd):
                    dp_in(dr, s, g, i).wait_recv()
                sib_copy(dr, s, g).start()

    def cores_in(g):
        for s in range(1, C):
            for dr in range(2):
                @pl.when(has(dr, s))
                def _():
                    sib_in(dr, s, g).wait_recv()

    own_small.wait()
    for cp in sm_copies:
        cp.wait()
    Ds = small.shape[1]
    rt = jnp.concatenate([sm[i] for i in range(nf)], axis=1)
    rt_o[...] = rt
    gains = rt[experts:experts + 2].astype(F32)
    gain_one, gain_two = gains[0:1], gains[1:2]
    xf = tok[...].astype(F32)
    r1 = lax.rsqrt(jnp.mean(xf * xf, -1, keepdims=True) + EPSILON)
    attn[...] = (xf * r1 * gain_one).astype(BF)

    def cot_step(s):
        for dr in range(2):
            @pl.when(has(dr, s))
            def _():
                cz_in(dr, s).wait_recv()
                if s < C - 1:
                    @pl.when(nxt_ok(dr))
                    def _():
                        cz(dr, s + 1, False).start()
                cs(dr, s).start()

    for s in range(1, C - 1):
        group_in(s, 0)
    cot_step(1)
    group_in(C - 1, 0)
    sib_own.wait()
    cores_in(0)

    first = lax.rem(lax.broadcasted_iota(jnp.int32, (T, 256), 1), HEAD_SIZE) < HEAD_SIZE // 2
    cs_t = jnp.concatenate([cosr[...], cosr[...]], 1)
    sn_t = jnp.concatenate([sinr[...], sinr[...]], 1)
    nqk = (QW + KW) // 256

    @pl.loop(0, nqk)
    def _(i):
        col = pl.ds(pl.multiple_of(i * 256, 256), 256)
        x = dot(attn[...], wf[:, col])
        qk_o[:, col] = (x * cs_t + half_roll(x, first) * sn_t).astype(BF)

    @pl.loop(0, KW // 256)
    def _(i):
        col = pl.ds(pl.multiple_of(QW + KW + i * 256, 256), 256)
        v_o[:, pl.ds(pl.multiple_of(i * 256, 256), 256)] = dot(attn[...], wf[:, col]).astype(BF)

    for s in range(2, min(C, 3)):
        cot_step(s)

    factor = HEAD_SIZE ** (-0.5)
    lane = lax.broadcasted_iota(jnp.int32, (T, 128), 1)
    keep = lax.broadcasted_iota(jnp.int32, (T, T), 1) <= lax.broadcasted_iota(jnp.int32, (T, T), 0)

    @pl.loop(0, KEY_VALUE_HEADS // 2)
    def _(i):
        kc = pl.ds(pl.multiple_of(QW + i * 128, 128), 128)
        kh = head_masks(qk_o[:, kc], lane)
        vh = head_masks(v_o[:, pl.ds(pl.multiple_of(i * 128, 128), 128)], lane)
        for p in range(GROUP):
            qc = pl.ds(pl.multiple_of((i * GROUP + p) * 128, 128), 128)
            q = qk_o[:, qc]
            acc = None
            for half in range(2):
                g = (2 * p + half) // GROUP
                sc = dot_nt(q, kh[g][half]) * factor
                sc = jnp.where(keep, sc, MASKED)
                ex = jnp.exp(sc - jnp.max(sc, -1, keepdims=True))
                pr = (ex / jnp.sum(ex, -1, keepdims=True)).astype(BF)
                prob_o[i * 2 * GROUP + 2 * p + half] = pr
                term = dot(pr, vh[g][half])
                acc = term if acc is None else acc + term
            mix_o[:, qc] = acc.astype(BF)

    for s in range(1, C):
        group_in(s, 1)
    cores_in(1)
    out_w = pltpu.make_async_copy(wf, wf_o, s_loc.at[3])
    out_w.start()

    @pl.loop(0, D // 256)
    def _(i):
        col = pl.ds(pl.multiple_of(i * 256, 256), 256)
        wc = pl.ds(pl.multiple_of(QW + 2 * KW + i * 256, 256), 256)
        hid_o[:, col] = tok[:, col].astype(F32) + dot(mix_o[...], wf[:, wc])

    hidden = hid_o[...]
    r2 = lax.rsqrt(jnp.mean(hidden * hidden, -1, keepdims=True) + EPSILON)
    ffn_o[...] = (hidden * r2 * gain_two).astype(BF)
    logits = dot_nt(rt_o[...], ffn_o[...])[0:experts]
    named = slots[...] >= 0.0
    logits = jnp.where(named, logits, MASKED)
    ex = jnp.where(named, jnp.exp(logits - jnp.max(logits, 0, keepdims=True)), 0.0)
    gates_o[...] = ex / jnp.sum(ex, 0, keepdims=True)

    for s in range(3, C):
        cot_step(s)
    own_c.wait()
    sib_c.wait()
    out_w.wait()
    for dr in range(2):
        for s in range(1, C):
            @pl.when(has(dr, s))
            def _():
                cs_in(dr, s).wait_recv()
                cs(dr, s).wait_send()
                for g in range(2):
                    sib_copy(dr, s, g).wait_send()
                    for i in range(1, nd):
                        dp_copy(dr, s, g, i).wait_send()

            @pl.when(nxt_ok(dr) & (has(dr, s - 1) if s > 1 else True))
            def _():
                for g in range(2):
                    wz(dr, s, g).wait_send()
                cz(dr, s, s == 1).wait_send()


def front(nf, nd, experts, tok, ws, small, cot, slots, cosr, sinr):
    T, D = tok.shape
    C = nf // 2
    W = sum(w.shape[1] for w in ws)
    out = [
        (T, D, BF, 0), (T, D, F32, 0), (experts, T, F32, 0), (T, QW, BF, 0), (T, QW + KW, BF, 0),
        (T, KW, BF, 0), (QUERY_HEADS, T, T, BF, 0), (D, W, BF, 1), (nf, T, D, BF, 1),
        (small.shape[0], D, BF, 0),
    ]
    dma = pltpu.SemaphoreType.DMA
    return pl.pallas_call(
        functools.partial(front_kernel, nf, nd, experts),
        out_shape=[jax.ShapeDtypeStruct(o[:-2], o[-2]) for o in out],
        in_specs=[vm()] + [hbm()] * 4 + [vm()] * 5,
        out_specs=[hbm() if o[-1] else vm() for o in out],
        scratch_shapes=[
            VMEM((D, W), BF),
            VMEM((nf,) + small.shape, BF),
            VMEM((T, D), BF),
            VMEM((8, 128), F32),
            dma((nf,)), dma((nf,)),
            dma((2, 2, C)), dma((2, 2, C)),
            dma((2, 2, C, nd)), dma((2, 2, C, nd)),
            dma((2, 2, C)), dma((2, 2, C)),
            dma((2, C)), dma((2, C)),
            dma((2, C)), dma((2, C)),
            dma((4,)), dma((4,)),
        ],
        compiler_params=pltpu.CompilerParams(collective_id=1, has_side_effects=True,
                                             vmem_limit_bytes=60 * 2 ** 20),
        cost_estimate=pl.CostEstimate(flops=4_000_000_000, bytes_accessed=60_000_000, transcendentals=2_000_000),
        name="front",
    )(tok, *ws, small, cot, slots, cosr, sinr)


def add_blocks(dst, srcs, extra=None):
    @pl.loop(0, dst.shape[0] // 16)
    def _(i):
        at = pl.ds(pl.multiple_of(i * 16, 16), 16)
        total = srcs[0][at, :].astype(F32)
        for s in srcs[1:]:
            total = total + s[at, :].astype(F32)
        dst[at, :] = total.astype(dst.dtype)


class Line:
    def __init__(self, nf, f, d, acc, give, sib, rcv, stage, sems, stage_sem, credit=None):
        self.nf, self.f, self.d = nf, f, d
        self.C = nf // 2
        self.c, self.k = f // 2, lax.rem(f, 2)
        self.acc, self.give, self.sib, self.rcv, self.stage = acc, give, sib, rcv, stage
        self.s_sib, self.r_sib, self.s_z, self.r_z = sems
        self.stage_sem, self.credit = stage_sem, credit

    def remote(self, src, dst, ss, rs, to):
        return pltpu.make_async_remote_copy(src_ref=src, dst_ref=dst, send_sem=ss, recv_sem=rs,
                                            device_id=(to, self.d), device_id_type=MESH)

    def dest(self, dr, s):
        i = s - 1 - (self.C - 1 - self.c) if dr == 0 else s - 1 - self.c
        room = self.c if dr == 0 else self.C - 1 - self.c
        chip = i if dr == 0 else self.C - 1 - i
        return jnp.clip(chip, 0, self.C - 1), (i >= 0) & (i < room), i == 0

    def sib_copy(self, chip):
        return self.remote(self.give(chip), self.sib(chip), self.s_sib.at[chip], self.r_sib.at[chip],
                           self.f + 1 - 2 * self.k)

    def z_copy(self, dr, s, chip):
        return self.remote(self.acc(chip), self.rcv(dr, s - 1), self.s_z.at[dr, s - 1], self.r_z.at[dr, s - 1],
                           self.f - 2 if dr == 0 else self.f + 2)

    def z_in(self, dr, s):
        return self.remote(self.rcv(dr, s - 1), self.rcv(dr, s - 1), self.s_z.at[dr, s - 1], self.r_z.at[dr, s - 1],
                           self.f)

    def start_sib(self):
        if self.credit is not None:
            pl.semaphore_wait(self.credit.at[2], 1)
        for s in range(1, self.C):
            for dr in range(2):
                chip, ok, _ = self.dest(dr, s)

                @pl.when(ok)
                def _():
                    self.sib_copy(chip).start()
        self.sib_copy(self.c).start()

    def gather(self, chip, srcs):
        acc = self.acc(chip)
        if self.stage is None:
            add_blocks(acc, [acc] + srcs)
            return
        for s in srcs:
            cp = pltpu.make_async_copy(s, self.stage, self.stage_sem)
            cp.start()
            cp.wait()
            add_blocks(acc, [acc, self.stage])

    def step(self, s):
        for dr in range(2):
            chip, ok, opening = self.dest(dr, s)
            begins = (self.c == self.C - 1) if dr == 0 else (self.c == 0)

            @pl.when(ok)
            def _():
                self.sib_copy(chip).wait_recv()

                @pl.when(begins)
                def _():
                    self.gather(chip, [self.sib(chip)])
                if s > 1:
                    @pl.when(jnp.logical_not(begins))
                    def _():
                        self.z_in(dr, s - 1).wait_recv()
                        self.gather(chip, [self.sib(chip), self.rcv(dr, s - 2)])
                if self.credit is not None:
                    @pl.when(opening)
                    def _():
                        pl.semaphore_wait(self.credit.at[dr], 1)
                self.z_copy(dr, s, chip).start()

    def last(self):
        self.sib_copy(self.c).wait_recv()
        mid = (self.c > 0) & (self.c < self.C - 1)
        s = self.C - 1
        for dr in range(2):
            @pl.when((self.c < self.C - 1) if dr == 0 else (self.c > 0))
            def _():
                self.z_in(dr, s).wait_recv()

        @pl.when(mid)
        def _():
            self.gather(self.c, [self.sib(self.c), self.rcv(0, s - 1), self.rcv(1, s - 1)])

        @pl.when(self.c == 0)
        def _():
            self.gather(self.c, [self.sib(self.c), self.rcv(0, s - 1)])

        @pl.when(self.c == self.C - 1)
        def _():
            self.gather(self.c, [self.sib(self.c), self.rcv(1, s - 1)])

    def sent(self):
        self.sib_copy(self.c).wait_send()
        for s in range(1, self.C):
            for dr in range(2):
                chip, ok, _ = self.dest(dr, s)

                @pl.when(ok)
                def _():
                    self.sib_copy(chip).wait_send()
                    self.z_copy(dr, s, chip).wait_send()

    def free(self, credit):
        def tell(i, to):
            pl.semaphore_signal(credit.at[i], inc=1, device_id=(to, self.d), device_id_type=MESH)

        tell(2, self.f + 1 - 2 * self.k)

        @pl.when(self.c < self.C - 1)
        def _():
            tell(0, self.f + 2)

        @pl.when(self.c > 0)
        def _():
            tell(1, self.f - 2)


class Cube:
    def __init__(self, nd, f, d, flip, lanes, size, own, land, total, out, sems):
        m = nd.bit_length() - 1
        self.bits = list(range(m))[::-1] if flip else list(range(m))
        self.f, self.d, self.lanes = f, d, lanes
        self.own, self.land, self.total, self.out = own, land, total, out
        self.ss, self.rs = sems
        self.m = m
        self.low, self.length = [0], [size]
        for b in self.bits:
            half = self.length[-1] // 2
            side = lax.rem(d // (1 << b), 2)
            self.low.append(self.low[-1] + side * half)
            self.length.append(half)

    def cut(self, ref, at, n):
        if self.lanes:
            return ref.at[:, pl.ds(pl.multiple_of(at, 128), n)]
        return ref.at[pl.ds(pl.multiple_of(at, 16), n)]

    def remote(self, src, dst, i, to_bit):
        return pltpu.make_async_remote_copy(src_ref=src, dst_ref=dst, send_sem=self.ss.at[i], recv_sem=self.rs.at[i],
                                            device_id=(self.f, jnp.bitwise_xor(self.d, 1 << to_bit)),
                                            device_id_type=MESH)

    def level(self, i):
        if i == 0:
            return self.own, 0
        if i == self.m:
            return self.out, 0
        return self.total(i - 1), self.low[i]

    def down(self, i):
        ref, base = self.level(i)
        half = self.length[i + 1]
        other = 2 * self.low[i] + half - self.low[i + 1]
        return self.remote(self.cut(ref, other - base, half), self.land(i), i, self.bits[i])

    def merge(self, i, add):
        self.down(i).wait_recv()
        self.fold(i, add)

    def fold(self, i, add):
        ref, base = self.level(i)
        dst, dbase = self.level(i + 1)
        half = self.length[i + 1]
        low = self.low[i + 1]
        add(self.cut(dst, low - dbase, half), self.cut(ref, low - base, half), self.land(i))

    def up(self, i):
        blk = self.cut(self.out, self.low[i + 1], self.length[i + 1])
        return self.remote(blk, blk, self.m + i, self.bits[i])

    def up_in(self, i):
        half = self.length[i + 1]
        other = 2 * self.low[i] + half - self.low[i + 1]
        blk = self.cut(self.out, other, half)
        return self.remote(blk, blk, self.m + i, self.bits[i])

    def sent(self, first=0):
        for i in range(self.m):
            if i >= first:
                self.down(i).wait_send()
            self.up(i).wait_send()


def pipe_add(dst, a, b):
    n, w = dst.shape
    tile = 128 if n % 128 == 0 else 64
    spec = pl.BlockSpec((tile, w), lambda i: (i, 0))

    def inner(a_ref, b_ref, o_ref):
        o_ref[...] = (a_ref[...].astype(F32) + b_ref[...].astype(F32)).astype(o_ref.dtype)

    pltpu.emit_pipeline(inner, grid=(n // tile,), in_specs=[spec, spec], out_specs=[spec])(a, b, dst)

def visit(c, C, j):
    both = jnp.minimum(c, C - 1 - c)
    near = j <= 2 * both
    dist = jnp.where(near, (j + 1) // 2, j - both)
    down = jnp.where(near, lax.rem(j, 2) == 0, c < C - 1 - c)
    chip = jnp.where(down, c + dist, c - dist)
    return chip, jnp.where(down, 1, 0), dist


def term_cubes(nd, el, f, d, t1, t2, out1, out2, l1, l2, a1, a2, sems):
    cubes = []
    for e in range(el):
        for j, (src, out, ls, ts) in enumerate(((t1, out1, l1, a1), (t2, out2, l2, a2))):
            pick = functools.partial(lambda refs, e, i: refs[i].at[e], ls, e)
            tot = functools.partial(lambda refs, e, i: refs[i].at[e], ts, e)
            cubes.append(Cube(nd, f, d, (e + j) % 2 == 1, False, src.shape[1], src.at[e], pick, tot,
                              None if out is None else out.at[e], (sems[0].at[2 * e + j], sems[1].at[2 * e + j])))
    return cubes


def experts_kernel(nf, nd, el, cap, capp, land_hbm, ffn, cot_a, side, wg_h, wu_h, wd_h,
                   out_o, gin_o, gp_o, t1_o, t2_o, l1, l2, sib_l, rcv_l, acc,
                   wg, wu, wd, fa, sd, cotb, xs, gs, hs, hgs, orb, irb, st_o, give, st1, st2, stage,
                   s_sd, r_sd, s_z, r_z, s_sib, r_sib, s_w, s_loc, s_t, s_ls, r_ls, s_lz, r_lz, s_st, s_cube, r_cube):
    T, D = ffn.shape
    FFW = wg.shape[2]
    C = nf // 2
    B = 2 * capp
    f = lax.axis_index("fsdp")
    d = lax.axis_index("dp")
    c = f // 2
    k = lax.rem(f, 2)
    sib = f + 1 - 2 * k
    greet(nf, nd, f, d)

    def remote(src, dst, ss, rs, to_f):
        return pltpu.make_async_remote_copy(src_ref=src, dst_ref=dst, send_sem=ss, recv_sem=rs,
                                            device_id=(to_f, d), device_id_type=MESH)

    def chip_at(dr, s):
        return jnp.where(dr == 0, c - s, c + s)

    def has(dr, s):
        at = chip_at(dr, s)
        return (at >= 0) & (at < C)

    def nxt_ok(dr):
        return (c + 1 < C) if dr == 0 else (c - 1 >= 0)

    def nxt_f(dr):
        return f + 2 if dr == 0 else f - 2

    def z_out(dr, s):
        ff = 2 * chip_at(dr, s - 1) + k
        return remote(fa.at[ff], fa.at[ff], s_z.at[dr, s - 1], r_z.at[dr, s - 1], nxt_f(dr))

    def z_own(dr):
        return remote(ffn, fa.at[f], s_z.at[dr, 0], r_z.at[dr, 0], nxt_f(dr))

    def z_in(dr, s):
        ff = 2 * chip_at(dr, s) + k
        return remote(fa.at[ff], fa.at[ff], s_z.at[dr, s - 1], r_z.at[dr, s - 1], f)

    def sib_out(dr, s):
        ff = 2 * chip_at(dr, s) + k
        return remote(fa.at[ff], fa.at[ff], s_sib.at[dr, s], r_sib.at[dr, s], sib)

    def sib_in(dr, s):
        ff = 2 * chip_at(dr, s) + 1 - k
        return remote(fa.at[ff], fa.at[ff], s_sib.at[dr, s], r_sib.at[dr, s], f)

    line = Line(nf, f, d, lambda ch: acc.at[ch], lambda ch: give.at[0], lambda ch: sib_l.at[ch],
                lambda dr, s: rcv_l.at[dr, s], stage if land_hbm else None, (s_ls, r_ls, s_lz, r_lz), s_st)

    def handed(chip, slot):
        return remote(give.at[slot], sib_l.at[chip], s_ls.at[chip], r_ls.at[chip], sib)

    for dr in range(2):
        @pl.when(nxt_ok(dr))
        def _():
            z_own(dr).start()
    sib_own = remote(ffn, fa.at[f], s_sib.at[1, 0], r_sib.at[1, 0], sib)
    sib_own.start()
    own = pltpu.make_async_copy(ffn, fa.at[f], s_loc.at[0])
    own.start()
    own_sd = pltpu.make_async_copy(side.at[f], sd.at[f], s_loc.at[1])
    own_sd.start()
    sd_copies = []
    for i in range(1, nf):
        to = lax.rem(f + i, nf)
        cp = remote(side.at[to], sd.at[f], s_sd.at[i - 1], r_sd.at[i - 1], to)
        cp.start()
        sd_copies.append(cp)
    w_copies = []
    for i, (src, dst) in enumerate(((wg_h, wg), (wu_h, wu), (wd_h, wd))):
        cp = pltpu.make_async_copy(src, dst, s_w.at[i])
        cp.start()
        w_copies.append(cp)
    own.wait()
    own_sd.wait()
    for cp in sd_copies:
        cp.wait()
    for cp in w_copies:
        cp.wait()

    row_ids = lax.broadcasted_iota(jnp.int32, (capp, T), 0).astype(F32)

    @pl.loop(0, C)
    def _(j):
        b, dr_b, dist_b = visit(c, C, j)
        cot_cp = pltpu.make_async_copy(cot_a.at[pl.ds(2 * b, 2)], cotb, s_loc.at[2])
        cot_cp.start()

        @pl.when(j >= 1)
        def _():
            for dr in range(2):
                @pl.when(has(dr, j))
                def _():
                    z_in(dr, j).wait_recv()

                    @pl.when(nxt_ok(dr) & (j < C - 1))
                    def _():
                        z_out(dr, j + 1).start()
                    sib_out(dr, j).start()
        sib_in(dr_b, dist_b).wait_recv()
        cot_cp.wait()

        base = pl.multiple_of(b * B, 16)
        gate_rows = [[None, None] for _ in range(el)]
        picks = []
        for kk in range(2):
            s = 2 * b + kk
            parts = []
            for e in range(el):
                hit = row_ids == sd[s, e:e + 1, :]
                gate_rows[e][kk] = jnp.sum(jnp.where(hit, sd[s, el + e:el + e + 1, :], 0.0), -1, keepdims=True)
                parts.append(jnp.where(hit, 1.0, 0.0).astype(BF))
            p2 = jnp.concatenate(parts, 0)
            picks.append(p2)
            for n in range(0, D, 512):
                xv = dot(p2, fa[s, :, n:n + 512]).astype(BF)
                gv_ = dot(p2, cotb[kk, :, n:n + 512]).astype(BF)
                for e in range(el):
                    at = pl.ds(pl.multiple_of(base + kk * capp, 16), capp)
                    xs[e, at, n:n + 512] = xv[e * capp:(e + 1) * capp]
                    gs[e, at, n:n + 512] = gv_[e * capp:(e + 1) * capp]
        here = pl.ds(base, B)
        gp_rows = []
        for e in range(el):
            gate_row = jnp.concatenate(gate_rows[e], 0)
            gpr = jnp.zeros((B, 1), F32)
            for n in range(0, FFW, 256):
                gv = dot(xs[e, here, :], wg[e, :, n:n + 256])
                uv = dot(xs[e, here, :], wu[e, :, n:n + 256])
                u = dot_nt(gs[e, here, :], wd[e, n:n + 256, :])
                sg = 1.0 / (1.0 + jnp.exp(-gv))
                act = gv * sg
                hid = act * uv
                gpr = gpr + jnp.sum(hid * u, -1, keepdims=True)
                hgs[e, here, n:n + 256] = (hid * gate_row).astype(BF)
                gh = u * gate_row
                hs[e, here, n:n + 256] = (gh * uv * (sg * (1.0 + gv * (1.0 - sg)))).astype(BF)
                hs[e, here, FFW + n:FFW + n + 256] = (gh * act).astype(BF)
            gp_rows.append(gpr)
            for n in range(0, D, 512):
                orow = dot(hgs[e, here, :], wd[e, :, n:n + 512]).astype(BF)
                irow = (dot_nt(hs[e, here, 0:FFW], wg[e, n:n + 512, :])
                        + dot_nt(hs[e, here, FFW:2 * FFW], wu[e, n:n + 512, :])).astype(BF)
                for kk in range(2):
                    orb[kk, e * capp:(e + 1) * capp, n:n + 512] = orow[kk * capp:(kk + 1) * capp]
                    irb[kk, e * capp:(e + 1) * capp, n:n + 512] = irow[kk * capp:(kk + 1) * capp]

        @pl.when(j >= 2)
        def _():
            before, _, _ = visit(c, C, j - 2)
            handed(before, lax.rem(j, 2)).wait_send()
        for kk in range(2):
            s = 2 * b + kk

            def combine(dst):
                for n in range(0, D, 512):
                    dst[:, n:n + 512] = dot_tn(picks[kk], irb[kk, :, n:n + 512]).astype(BF)

            @pl.when(k == kk)
            def _():
                combine(acc.at[b])

            @pl.when(k != kk)
            def _():
                combine(give.at[lax.rem(j, 2)])
                handed(b, lax.rem(j, 2)).start()

        def back(bb):
            return pltpu.make_async_copy(st_o, out_o.at[pl.ds(2 * bb, 2)], s_loc.at[3])

        @pl.when(j >= 1)
        def _():
            back(0).wait()
        for kk in range(2):
            s = 2 * b + kk
            for e in range(el):
                hit = picks[kk][e * capp:(e + 1) * capp].astype(F32)
                gp_o[s, e:e + 1, :] = jnp.sum(hit * gp_rows[e][kk * capp:(kk + 1) * capp], 0, keepdims=True)
            for n in range(0, D, 512):
                st_o[kk, :, n:n + 512] = dot_tn(picks[kk], orb[kk, :, n:n + 512]).astype(BF)
        back(b).start()

    line.step(1)

    n1 = D // 256
    n2 = FFW // 256

    def t1_copy(e, i):
        return pltpu.make_async_copy(st1.at[lax.rem(i, 2)], t1_o.at[e, pl.ds(pl.multiple_of(i * 256, 256), 256)],
                                     s_t.at[0, lax.rem(i, 2)])

    def t2_copy(e, i):
        return pltpu.make_async_copy(st2.at[lax.rem(i, 2)], t2_o.at[e, pl.ds(pl.multiple_of(i * 256, 256), 256)],
                                     s_t.at[1, lax.rem(i, 2)])

    cubes = term_cubes(nd, el, f, d, t1_o, t2_o, None, None, [l1], [l2], [], [], (s_cube, r_cube))
    for e in range(el):
        @pl.loop(0, n1)
        def _(i):
            @pl.when(i >= 2)
            def _():
                t1_copy(e, i).wait()
            col = pl.ds(pl.multiple_of(i * 256, 256), 256)
            st1[lax.rem(i, 2)] = dot_tn(xs[e, :, col], hs[e]).astype(BF)
            t1_copy(e, i).start()

        for i in range(2):
            t1_copy(e, i).wait()
        cubes[2 * e].down(0).start()

        @pl.loop(0, n2)
        def _(i):
            @pl.when(i >= 2)
            def _():
                t2_copy(e, i).wait()
            col = pl.ds(pl.multiple_of(i * 256, 256), 256)
            st2[lax.rem(i, 2)] = dot_tn(hgs[e, :, col], gs[e]).astype(BF)
            t2_copy(e, i).start()
        for i in range(2):
            t2_copy(e, i).wait()
        cubes[2 * e + 1].down(0).start()
        if e < C - 2:
            line.step(e + 2)

    for s in range(el + 2, C):
        line.step(s)
    for s in range(C - 2, el):
        pass
    line.last()
    gin_o[...] = acc[c]

    pltpu.make_async_copy(st_o, out_o.at[pl.ds(0, 2)], s_loc.at[3]).wait()
    for j in range(max(C - 2, 0), C):
        chip, _, _ = visit(c, C, j)
        handed(chip, j % 2).wait_send()
    for s in range(1, C):
        for dr in range(2):
            chip, ok, _ = line.dest(dr, s)

            @pl.when(ok)
            def _():
                line.z_copy(dr, s, chip).wait_send()
    for cube in cubes:
        cube.down(0).wait()
    sib_own.wait_send()
    for dr in range(2):
        for s in range(1, C):
            @pl.when(has(dr, s))
            def _():
                sib_out(dr, s).wait_send()
        for s in range(1, C):
            @pl.when(nxt_ok(dr) & has(dr, s - 1))
            def _():
                z_out(dr, s).wait_send()


def experts_call(nf, nd, cap, ffn_in, cot_all, side, w_gate, w_up, w_down):
    T, D = ffn_in.shape
    el, _, FFW = w_gate.shape
    capp = cap + (-cap % 16)
    C = nf // 2
    rows = C * 2 * capp
    land_hbm = C > 4
    dma = pltpu.SemaphoreType.DMA
    out = [((nf, T, D), BF, 1), ((T, D), BF, 0), ((nf, el, T), F32, 0),
           ((el, D, 2 * FFW), BF, 1), ((el, FFW, D), BF, 1),
           ((el, D // 2, 2 * FFW), BF, 1), ((el, FFW // 2, D), BF, 1)]
    lands = [(C, T, D), (2, C - 1, T, D)]
    scratch = []
    if land_hbm:
        out += [(x, BF, 1) for x in lands]
    else:
        scratch += [VMEM(x, BF) for x in lands]
    scratch += [
        VMEM((C, T, D), BF),
        VMEM((el, D, FFW), BF), VMEM((el, D, FFW), BF), VMEM((el, FFW, D), BF),
        VMEM((nf, T, D), BF), VMEM(side.shape, F32), VMEM((2, T, D), BF),
        VMEM((el, rows, D), BF), VMEM((el, rows, D), BF),
        VMEM((el, rows, 2 * FFW), BF), VMEM((el, rows, FFW), BF),
        VMEM((2, el * capp, D), BF), VMEM((2, el * capp, D), BF),
        VMEM((2, T, D), BF), VMEM((2, T, D), BF),
        VMEM((2, 256, 2 * FFW), BF), VMEM((2, 256, D), BF),
        VMEM((T, D) if land_hbm else (16, 128), BF),
        dma((nf,)), dma((nf,)),
        dma((2, C)), dma((2, C)), dma((2, C)), dma((2, C)),
        dma((3,)), dma((5,)), dma((2, 2)),
        dma((C,)), dma((C,)), dma((2, C)), dma((2, C)), dma(()),
        dma((2 * el, 2 * (nd.bit_length() - 1))), dma((2 * el, 2 * (nd.bit_length() - 1))),
    ]
    return pl.pallas_call(
        functools.partial(experts_kernel, nf, nd, el, cap, capp, land_hbm),
        out_shape=[jax.ShapeDtypeStruct(o[0], o[1]) for o in out],
        in_specs=[vm(), hbm(), vm(), hbm(), hbm(), hbm()],
        out_specs=[hbm() if o[2] else vm() for o in out],
        scratch_shapes=scratch,
        compiler_params=pltpu.CompilerParams(collective_id=2, has_side_effects=True,
                                             vmem_limit_bytes=63 * 2 ** 20),
        cost_estimate=pl.CostEstimate(flops=40_000_000_000, bytes_accessed=60_000_000, transcendentals=2_000_000),
        name="experts",
    )(ffn_in, cot_all, side, w_gate, w_up, w_down)[:7]


def back_kernel(nf, nd, el, land_hbm, *refs):
    m = nd.bit_length() - 1
    it = iter(refs)

    def take(n):
        return [next(it) for _ in range(n)]

    (gin, out_p, gp_p, t1, t2, f1, f2, tok_h, cot_h, hid_h, ffn_h, gates, mix_h, qk_h, v_h, prob_h, wf_h, rt,
     cosr, sinr) = take(20)
    out_o, gt_o, sh_o, sm_o, t1_o, t2_o = take(6)
    l1 = [f1] + take(m - 1)
    l2 = [f2] + take(m - 1)
    a1 = take(m - 1)
    a2 = take(m - 1)
    sib, rcv, sibq, rcvq = take(4)
    (acc, wb, wg, tok, cot, hid, ffn, mix, qk, v, prob, branch, gh, ga, gproj, gpb, smg, smr, smd, shb, sms) = take(21)
    attn, gm = ffn, mix
    shl = take(m)
    stage, stageq = take(2)
    (s_load, s_acc, s_gp, r_gp, s_sib, r_sib, s_z, r_z, s_cube, r_cube, s_sc, r_sc, s_sm, r_sm, s_sd, r_sd,
     s_stage, s_prob, cred) = take(19)

    T, D = tok.shape
    R = wg.shape[0] // nf
    W = wg.shape[1]
    E = gates.shape[0]
    C = nf // 2
    f = lax.axis_index("fsdp")
    d = lax.axis_index("dp")
    c = f // 2
    k = lax.rem(f, 2)
    QV = QW + 2 * KW
    greet(nf, nd, f, d)

    def remote(src, dst, ss, rs, to_f, to_d):
        return pltpu.make_async_remote_copy(src_ref=src, dst_ref=dst, send_sem=ss, recv_sem=rs,
                                            device_id=(to_f, to_d), device_id_type=MESH)

    def rows(ff):
        return pl.ds(pl.multiple_of(ff * R, 16), R)

    st = stage if land_hbm else None
    stq = stageq if land_hbm else None

    def sems(i):
        return (s_sib.at[i], r_sib.at[i], s_z.at[i], r_z.at[i])

    wo_cols = pl.ds(QV, D)
    o_line = Line(nf, f, d, lambda ch: wg.at[rows(2 * ch + k), wo_cols], lambda ch: wg.at[rows(2 * ch + 1 - k), wo_cols],
                  lambda ch: sib.at[ch, 0:R], lambda dr, s: rcv.at[dr, s, 0:R],
                  stage.at[0:R] if land_hbm else None, sems(1), s_stage)
    q_cols = pl.ds(0, QV)
    q_line = Line(nf, f, d, lambda ch: wg.at[rows(2 * ch + k), q_cols], lambda ch: wg.at[rows(2 * ch + 1 - k), q_cols],
                  lambda ch: sibq.at[ch], lambda dr, s: rcvq.at[dr, s], stq, sems(2), s_stage)
    out_line = Line(nf, f, d, lambda ch: acc.at[ch], lambda ch: out_p.at[2 * ch + 1 - k], lambda ch: sib.at[ch],
                    lambda dr, s: rcv.at[dr, s], st, sems(3), s_stage, cred)

    def acc_loads(src):
        return [pltpu.make_async_copy(src.at[2 * ch + k], acc.at[ch], s_acc.at[ch]) for ch in range(C)]

    gp_copies = []
    for i in range(1, nf):
        to = lax.rem(f + i, nf)
        cp = remote(gp_p.at[to], gpb.at[f], s_gp.at[i - 1], r_gp.at[i - 1], to, d)
        cp.start()
        gp_copies.append(cp)
    out_loads = acc_loads(out_p)
    for cp in out_loads:
        cp.start()
    cubes = term_cubes(nd, el, f, d, t1, t2, t1_o, t2_o, l1, l2, a1, a2, (s_cube, r_cube))
    own_gp = pltpu.make_async_copy(gp_p.at[f], gpb.at[f], s_load.at[0])
    own_gp.start()
    wo = pltpu.make_async_copy(wf_h.at[:, QV:QV + D], wb.at[:, 0:D], s_load.at[1])
    wo.start()
    others = [(tok_h, tok), (cot_h, cot), (hid_h, hid), (ffn_h, ffn), (mix_h, mix), (qk_h, qk), (v_h, v)]
    more = [pltpu.make_async_copy(a, b, s_load.at[2 + i]) for i, (a, b) in enumerate(others)]
    for cp in more:
        cp.start()

    def prob_load(i):
        at = pl.ds(i * 2 * GROUP, 2 * GROUP)
        return pltpu.make_async_copy(prob_h.at[at], prob.at[lax.rem(i, 2)], s_prob.at[lax.rem(i, 2)])

    prob_load(0).start()
    for i in range(0, 1):
        for cube in cubes:
            cube.fold(i, pipe_add)
            cube.down(i + 1).start() if m > 1 else cube.up(0).start()
    for cp in more:
        cp.wait()
    own_gp.wait()
    for cp in gp_copies:
        cp.wait()

    gains = rt[E:E + 2].astype(F32)
    gain_one, gain_two = gains[0:1], gains[1:2]
    gpt = jnp.concatenate([gpb[i] for i in range(nf)], 0)
    gates_v = gates[...]
    gl = (gates_v * (gpt - jnp.sum(gpt * gates_v, 0, keepdims=True))).astype(BF)
    for n in range(0, D, 512):
        sms[0:E, n:n + 512] = dot(gl, ffn[:, n:n + 512])
    for n in range(0, D, 512):
        ga[:, n:n + 512] = dot_tn(gl, rt[0:E, n:n + 512])
    sms[E:, :] = jnp.zeros((sms.shape[0] - E, D), F32)
    TR = 32

    @pl.loop(0, T // TR)
    def _(i):
        at = pl.ds(pl.multiple_of(i * TR, TR), TR)
        h = hid[at, :]
        r2 = lax.rsqrt(jnp.mean(h * h, -1, keepdims=True) + EPSILON)
        n2 = h * r2
        gf = gin[at, :].astype(F32) + ga[at, :]
        sms[E + 1:E + 2, :] += jnp.sum(gf * n2, 0, keepdims=True)
        g2 = gf * gain_two
        x = cot[at, :].astype(F32) + r2 * (g2 - n2 * jnp.mean(g2 * n2, -1, keepdims=True))
        gh[at, :] = x
        branch[at, :] = x.astype(BF)

    @pl.loop(0, QW // 256)
    def _(i):
        at = pl.ds(pl.multiple_of(i * 256, 256), 256)
        wg[at, QV:QV + D] = dot_tn(mix[:, at], branch[...]).astype(BF)
    o_line.start_sib()
    o_line.step(1)
    wo.wait()

    @pl.loop(0, QW // 256)
    def _(i):
        at = pl.ds(pl.multiple_of(i * 256, 256), 256)
        gm[:, at] = dot_nt(branch[...], wb[at, 0:D]).astype(BF)
    wq = pltpu.make_async_copy(wf_h.at[:, 0:QV], wb, s_load.at[1])
    wq.start()
    factor = HEAD_SIZE ** (-0.5)
    lane = lax.broadcasted_iota(jnp.int32, (T, 128), 1)
    low = lane < HEAD_SIZE
    first = lax.rem(lane, HEAD_SIZE) < HEAD_SIZE // 2

    def unrotate(x):
        return x * cosr[...] - half_roll(x, first) * sinr[...]

    @pl.loop(0, KEY_VALUE_HEADS // 2)
    def _(i):
        @pl.when(i + 1 < KEY_VALUE_HEADS // 2)
        def _():
            prob_load(i + 1).start()
        prob_load(i).wait()
        slot = lax.rem(i, 2)
        kcol = pl.ds(pl.multiple_of(i * 128, 128), 128)
        kh = head_masks(qk[:, pl.ds(pl.multiple_of(QW + i * 128, 128), 128)], lane)
        vh = head_masks(v[:, kcol], lane)
        gk = [[None, None], [None, None]]
        gv = [[None, None], [None, None]]
        for p in range(GROUP):
            qc = pl.ds(pl.multiple_of((i * GROUP + p) * 128, 128), 128)
            q = qk[:, qc]
            g = gm[:, qc]
            gq = None
            for half in range(2):
                kv = (2 * p + half) // GROUP
                pr = prob[slot, 2 * p + half]
                prf = pr.astype(F32)
                gp = dot_nt(g, vh[kv][half])
                gs = (prf * (gp - jnp.sum(prf * gp, -1, keepdims=True))).astype(BF)
                term = dot(gs, kh[kv][half])
                gq = term if gq is None else gq + term
                tk = dot_tn(gs, q)
                tv = dot_tn(pr, g)
                gk[kv][half] = tk if gk[kv][half] is None else gk[kv][half] + tk
                gv[kv][half] = tv if gv[kv][half] is None else gv[kv][half] + tv
            gproj[:, qc] = unrotate(gq * factor).astype(BF)

        def join(x):
            a = jnp.where(low, x[0][0] + pltpu.roll(x[0][1], HEAD_SIZE, axis=1), 0.0)
            b = jnp.where(low, 0.0, pltpu.roll(x[1][0], HEAD_SIZE, axis=1) + x[1][1])
            return a + b

        gproj[:, pl.ds(pl.multiple_of(QW + i * 128, 128), 128)] = unrotate(join(gk) * factor).astype(BF)
        gproj[:, pl.ds(pl.multiple_of(QW + KW + i * 128, 128), 128)] = join(gv).astype(BF)

        if C > 2:
            @pl.when(i == 1)
            def _():
                o_line.step(2)

    if m > 1:
        for cube in cubes:
            cube.merge(1, pipe_add)
            cube.down(2).start() if m > 2 else cube.up(1).start()
    @pl.loop(0, T // TR)
    def _(i):
        at = pl.ds(pl.multiple_of(i * TR, TR), TR)
        x = tok[at, :].astype(F32)
        r1 = lax.rsqrt(jnp.mean(x * x, -1, keepdims=True) + EPSILON)
        attn[at, :] = (x * r1 * gain_one).astype(BF)

    @pl.loop(0, D // 256)
    def _(i):
        at = pl.ds(pl.multiple_of(i * 256, 256), 256)
        for n in range(0, QV, 512):
            wg[at, n:n + 512] = dot_tn(attn[:, at], gproj[:, n:n + 512]).astype(BF)
    q_line.start_sib()
    for s in range(3, C):
        o_line.step(s)
    q_line.step(1)
    wq.wait()

    @pl.loop(0, D // 256)
    def _(i):
        at = pl.ds(pl.multiple_of(i * 256, 256), 256)
        ga[:, at] = dot_nt(gproj[...], wb[at, :])

    @pl.loop(0, T // TR)
    def _(i):
        at = pl.ds(pl.multiple_of(i * TR, TR), TR)
        x = tok[at, :].astype(F32)
        r1 = lax.rsqrt(jnp.mean(x * x, -1, keepdims=True) + EPSILON)
        n1 = x * r1
        gat = ga[at, :]
        sms[E:E + 1, :] += jnp.sum(gat * n1, 0, keepdims=True)
        g1 = gat * gain_one
        gt_o[at, :] = (gh[at, :] + r1 * (g1 - n1 * jnp.mean(g1 * n1, -1, keepdims=True))).astype(BF)

    small = sms[...]
    for i in range(nf):
        smg[i] = small[:, i * R:(i + 1) * R]
    sm_copies = []
    for i in range(1, nf):
        to = lax.rem(f + i, nf)
        cp = remote(smg.at[to], smr.at[f], s_sm.at[i - 1], r_sm.at[i - 1], to, d)
        cp.start()
        sm_copies.append(cp)
    smr_own = pltpu.make_async_copy(smg.at[f], smr.at[f], s_load.at[0])
    smr_own.start()

    o_line.last()
    o_line.free(cred)
    if m > 2:
        for i in range(2, m):
            for cube in cubes:
                cube.merge(i, pipe_add)
                cube.down(i + 1).start() if i + 1 < m else cube.up(m - 1).start()
    for i in range(m - 1, 0, -1):
        for cube in cubes:
            cube.up_in(i).wait_recv()
            cube.up(i - 1).start()
    if C > 2:
        q_line.step(2)
    o_line.sent()
    for cp in out_loads:
        cp.wait()
    smr_own.wait()
    for cp in sm_copies:
        cp.wait()
    total = smr[0]
    for i in range(1, nf):
        total = total + smr[i]
    smd[0] = total
    sd_copies = []
    for i in range(1, nd):
        cp = remote(smd.at[0], smd.at[i], s_sd.at[i - 1], r_sd.at[i - 1], f, jnp.bitwise_xor(d, i))
        cp.start()
        sd_copies.append(cp)
    for s in range(3, C):
        q_line.step(s)
    out_line.start_sib()
    out_line.step(1)
    q_line.last()

    own = wg.at[rows(f)]
    add_blocks(shb, [own])
    half = W // 2
    shards = []
    for h in range(2):
        shards.append(Cube(nd, f, d, h == 1, True, half, shb.at[:, h * half:(h + 1) * half],
                           functools.partial(lambda h, i: shl[i].at[h], h),
                           functools.partial(lambda h, i: shb.at[:, h * half:(h + 1) * half], h),
                           sh_o.at[:, h * half:(h + 1) * half], (s_sc.at[h], r_sc.at[h])))

    def level(self, i):
        return (self.own, 0) if i < self.m else (self.out, 0)

    for cube in shards:
        cube.level = functools.partial(level, cube)
        cube.down(0).start()

    def vadd(dst, a, b):
        add_blocks(dst, [a, b])

    if C > 2:
        out_line.step(2)
    for i in range(m):
        for cube in shards:
            cube.merge(i, vadd)
        for cube in shards:
            cube.down(i + 1).start() if i + 1 < m else cube.up(i).start()
    for s in range(3, C):
        out_line.step(s)
    for i in range(m - 1, 0, -1):
        for cube in shards:
            cube.up_in(i).wait_recv()
        for cube in shards:
            cube.up(i - 1).start()
    for cp in sd_copies:
        cp.wait()
    total = smd[0]
    for i in range(1, nd):
        total = total + smd[i]
    sm_o[...] = total
    out_line.last()

    @pl.loop(0, T // TR)
    def _(i):
        at = pl.ds(pl.multiple_of(i * TR, TR), TR)
        out_o[at, :] = (hid[at, :] + acc[c, at, :].astype(F32)).astype(BF)


    q_line.sent()
    out_line.sent()
    for cube in cubes:
        cube.up_in(0).wait_recv()
        cube.sent(1)
    for cube in shards:
        cube.up_in(0).wait_recv()
        cube.sent()


def back(nf, nd, el, args):
    gin, t1, t2 = args[0], args[3], args[4]
    T, D = gin.shape
    E = args[11].shape[0]
    W = args[16].shape[1]
    R = D // nf
    C = nf // 2
    m = nd.bit_length() - 1
    QV = QW + 2 * KW
    FFW = t2.shape[1]
    SR = E + 2 + (-(E + 2) % 8)
    land_hbm = C > 4
    s = jax.ShapeDtypeStruct
    out_shape = [s((T, D), BF), s((T, D), BF), s((R, W), BF), s((SR, R), F32), s(t1.shape, BF), s(t2.shape, BF)]
    out_specs = [vm(), vm(), vm(), vm(), hbm(), hbm()]
    extra = [(el, D >> (i + 1), t1.shape[2]) for i in range(1, m)] + [(el, FFW >> (i + 1), D) for i in range(1, m)]
    extra += [(el, D >> (i + 1), t1.shape[2]) for i in range(m - 1)] + [(el, FFW >> (i + 1), D) for i in range(m - 1)]
    lands = [(C, T, D), (2, C - 1, T, D), (C, R, QV), (2, C - 1, R, QV)]
    scratch = []
    if land_hbm:
        extra += lands
    else:
        scratch += [VMEM(x, BF) for x in lands]
    out_shape += [s(x, BF) for x in extra]
    out_specs += [hbm()] * len(extra)
    dma = pltpu.SemaphoreType.DMA
    scratch += [
        VMEM((C, T, D), BF), VMEM((D, QV), BF), VMEM((D, W), BF),
        VMEM((T, D), BF), VMEM((T, D), BF), VMEM((T, D), F32), VMEM((T, D), BF), VMEM((T, QW), BF),
        VMEM((T, QW + KW), BF), VMEM((T, KW), BF), VMEM((2, 2 * GROUP, T, T), BF),
        VMEM((T, D), BF), VMEM((T, D), F32), VMEM((T, D), F32), VMEM((T, QV), BF),
        VMEM((nf, el, T), F32), VMEM((nf, SR, R), F32), VMEM((nf, SR, R), F32), VMEM((nd, SR, R), F32), VMEM((R, W), BF),
        VMEM((SR, D), F32),
    ]
    scratch += [VMEM((2, R, W >> (i + 2)), BF) for i in range(m)]
    scratch += [VMEM((T, D) if land_hbm else (16, 128), BF), VMEM((R, QV) if land_hbm else (16, 128), BF)]
    scratch += [
        dma((10,)), dma((C,)), dma((nf,)), dma((nf,)),
        dma((4, C)), dma((4, C)), dma((4, 2, C)), dma((4, 2, C)),
        dma((2 * el, 2 * m)), dma((2 * el, 2 * m)), dma((2, 2 * m)), dma((2, 2 * m)),
        dma((nf,)), dma((nf,)), dma((nd,)), dma((nd,)), dma(()), dma((2,)),
        pltpu.SemaphoreType.REGULAR((3,)),
    ]
    inner = [vm(), hbm(), vm(), hbm(), hbm(), hbm(), hbm(), hbm(), hbm(), hbm(), hbm(), vm(), hbm(), hbm(), hbm(), hbm(), hbm(), vm(),
             vm(), vm()]
    return pl.pallas_call(
        functools.partial(back_kernel, nf, nd, el, land_hbm),
        out_shape=out_shape,
        in_specs=inner,
        out_specs=out_specs,
        scratch_shapes=scratch,
        compiler_params=pltpu.CompilerParams(collective_id=3, has_side_effects=True,
                                             vmem_limit_bytes=63 * 2 ** 20),
        cost_estimate=pl.CostEstimate(flops=8_000_000_000, bytes_accessed=90_000_000, transcendentals=100_000),
        name="back",
    )(*args)[:6]


def body(tokens, w_query, key_weight, value_weight, w_out, gain_attn, gain_ffn, w_router,
         w_gate, w_up, w_down, routes, cotangent):
    T = tokens.shape[0]
    el = w_gate.shape[0]
    ff = w_gate.shape[2]
    nf = lax.axis_size("fsdp")
    nd = lax.axis_size("dp")
    experts = el * nf
    cap = 9 * T * TOP // (8 * experts)

    pad = -(experts + 2) % 16
    small = jnp.concatenate([w_router, gain_attn[:, None], gain_ffn[:, None],
                             jnp.zeros((w_router.shape[0], pad), BF)], 1).T
    onehot = (routes[:, :, None] == jnp.arange(experts, dtype=jnp.int32)).any(1).astype(BF)
    earlier = (jnp.arange(T)[:, None] < jnp.arange(T)[None, :]).astype(BF)
    before = lax.dot_general(onehot, earlier, (((0,), (0,)), ((), ())), preferred_element_type=F32)
    slots = jnp.where(onehot.T > 0, before, -1.0)
    cosr, sinr = rope_rows(T)
    ffn_in, hidden, gates, mixed, qk, v, probs, full, cot_all, rt = front(
        nf, nd, experts, tokens, (w_query, key_weight, value_weight, w_out), small, cotangent, slots, cosr, sinr)
    side = jnp.concatenate([slots.reshape(nf, el, T), gates.reshape(nf, el, T)], 1)
    out_part, gin, gp_part, t1, t2, f1, f2 = experts_call(nf, nd, cap, ffn_in, cot_all, side, w_gate, w_up, w_down)
    output, grad_tokens, shard, smalls, t1, t2 = back(nf, nd, el, (
        gin, out_part, gp_part, t1, t2, f1, f2, tokens, cotangent, hidden, ffn_in, gates, mixed, qk, v, probs, full, rt,
        cosr, sinr))
    big = shard.astype(F32)
    return (
        output,
        grad_tokens,
        big[:, :QW],
        big[:, QW: QW + KW],
        big[:, QW + KW: QW + 2 * KW],
        big[:, QW + 2 * KW:],
        smalls[experts],
        smalls[experts + 1],
        smalls[:experts].T,
        t1[:, :, :ff].astype(F32),
        t1[:, :, ff:].astype(F32),
        t2.astype(F32),
    )


def solution(mesh):
    in_specs = (
        P(("fsdp", "dp"), None),
        P("fsdp", None),
        P("fsdp", None),
        P("fsdp", None),
        P("fsdp", None),
        P("fsdp"),
        P("fsdp"),
        P("fsdp", None),
        P("fsdp", None, None),
        P("fsdp", None, None),
        P("fsdp", None, None),
        P(("fsdp", "dp"), None),
        P(("fsdp", "dp"), None),
    )
    out_specs = (
        P(("fsdp", "dp"), None),
        P(("fsdp", "dp"), None),
        P("fsdp", None),
        P("fsdp", None),
        P("fsdp", None),
        P("fsdp", None),
        P("fsdp"),
        P("fsdp"),
        P("fsdp", None),
        P("fsdp", None, None),
        P("fsdp", None, None),
        P("fsdp", None, None),
    )
    return jax.shard_map(body, mesh=mesh, in_specs=in_specs, out_specs=out_specs, check_vma=False)
```

```python
import functools
import jax
import jax.numpy as jnp
from jax import lax
from jax.experimental import pallas as pl
from jax.experimental.pallas import tpu as pltpu
from jax.sharding import PartitionSpec as P
import numpy as np

MODEL_WIDTH = 1536
QUERY_HEADS = 24
KEY_VALUE_HEADS = 8
HEAD_SIZE = 64
TOP = 8
GROUP = QUERY_HEADS // KEY_VALUE_HEADS
QW = QUERY_HEADS * HEAD_SIZE
KW = KEY_VALUE_HEADS * HEAD_SIZE

EPSILON = 1e-06
ROPE_BASE = 10000.0
MASKED = -1e30
F32 = jnp.float32
BF = jnp.bfloat16


def rope_rows(T):
    half = HEAD_SIZE // 2
    freq = ROPE_BASE ** (-2.0 * np.arange(half, dtype=np.float64) / HEAD_SIZE)
    ang = (np.arange(T, dtype=np.float32)[:, None] * freq.astype(np.float32)[None, :]).astype(np.float32)
    c, s = np.cos(ang), np.sin(ang)
    return (jnp.asarray(np.concatenate([c, c, c, c], 1), F32), jnp.asarray(np.concatenate([-s, s, -s, s], 1), F32))


MESH = pl.DeviceIdType.MESH
VMEM = pltpu.VMEM


def vm():
    return pl.BlockSpec(memory_space=pltpu.VMEM)


def hbm():
    return pl.BlockSpec(memory_space=pl.ANY)


def dot(a, b):
    return lax.dot_general(a, b, (((1,), (0,)), ((), ())), preferred_element_type=F32)


def dot_nt(a, b):
    return lax.dot_general(a, b, (((1,), (1,)), ((), ())), preferred_element_type=F32)


def dot_tn(a, b):
    return lax.dot_general(a, b, (((0,), (0,)), ((), ())), preferred_element_type=F32)


def half_roll(x, first):
    n = x.shape[1]
    h = HEAD_SIZE // 2
    return jnp.where(first, pltpu.roll(x, n - h, axis=1), pltpu.roll(x, h, axis=1))


def greet(nf, nd, f, d):
    barrier = pltpu.get_barrier_semaphore()
    for i in range(1, nf):
        pl.semaphore_signal(barrier, inc=1, device_id=(lax.rem(f + i, nf), d), device_id_type=MESH)
    for i in range(1, nd):
        pl.semaphore_signal(barrier, inc=1, device_id=(f, jnp.bitwise_xor(d, i)), device_id_type=MESH)
    pl.semaphore_wait(barrier, nf + nd - 2)


def head_masks(kblk, lane):
    kf = kblk.astype(F32)
    kr = pltpu.roll(kf, HEAD_SIZE, axis=1)
    low = lane < HEAD_SIZE
    zero = jnp.zeros_like(kf)
    a0 = jnp.where(low, kf, zero).astype(BF)
    a1 = jnp.where(low, zero, kr).astype(BF)
    b0 = jnp.where(low, kr, zero).astype(BF)
    b1 = jnp.where(low, zero, kf).astype(BF)
    return ((a0, a1), (b0, b1))


def front_kernel(nf, nd, experts, tok, wq, wk, wv, wo, small, cot, slots, cosr, sinr,
                 ffn_o, hid_o, gates_o, mix_o, qk_o, v_o, prob_o, wf_o, cot_o, rt_o,
                 wf, sm, attn, rot,
                 s_sm, r_sm, s_z, r_z, s_dp, r_dp, s_sib, r_sib, s_cz, r_cz, s_cs, r_cs, s_loc, s_w):
    T, D = tok.shape
    C = nf // 2
    R = wq.shape[0]
    W = wf.shape[1]
    WA = 3 * W // 4
    parts = ((0, WA), (WA, W - WA))
    f = lax.axis_index("fsdp")
    d = lax.axis_index("dp")
    c = f // 2
    k = lax.rem(f, 2)
    sib = f + 1 - 2 * k
    greet(nf, nd, f, d)

    def rows(ff):
        return pl.ds(pl.multiple_of(ff * R, 16), R)

    def cols(dd, g):
        at, n = parts[g]
        return pl.ds(pl.multiple_of(at + dd * (n // nd), 128), n // nd)

    def remote(src, dst, ss, rs, to_f, to_d):
        return pltpu.make_async_remote_copy(src_ref=src, dst_ref=dst, send_sem=ss, recv_sem=rs,
                                            device_id=(to_f, to_d), device_id_type=MESH)

    def src_chip(dr, s):
        return c - s if dr == 0 else c + s

    def has(dr, s):
        return (c - s >= 0) if dr == 0 else (c + s < C)

    def nxt_ok(dr):
        return (c + 1 < C) if dr == 0 else (c - 1 >= 0)

    def nxt_f(dr):
        return f + 2 if dr == 0 else f - 2

    def wz(dr, s, g):
        blk = wf.at[rows(2 * src_chip(dr, s - 1) + k), cols(d, g)]
        return remote(blk, blk, s_z.at[g, dr, s - 1], r_z.at[g, dr, s - 1], nxt_f(dr), d)

    def wz_in(dr, s, g):
        blk = wf.at[rows(2 * src_chip(dr, s) + k), cols(d, g)]
        return remote(blk, blk, s_z.at[g, dr, s - 1], r_z.at[g, dr, s - 1], f, d)

    halves = (slice(0, D // 2), slice(D // 2, D))

    def cz(dr, s, own, h):
        ff = 2 * src_chip(dr, s - 1) + k
        src = cot.at[:, halves[h]] if own else cot_o.at[ff, :, halves[h]]
        return remote(src, cot_o.at[ff, :, halves[h]], s_cz.at[h, dr, s - 1], r_cz.at[h, dr, s - 1], nxt_f(dr), d)

    def cz_in(dr, s, h):
        blk = cot_o.at[2 * src_chip(dr, s) + k, :, halves[h]]
        return remote(blk, blk, s_cz.at[h, dr, s - 1], r_cz.at[h, dr, s - 1], f, d)

    def cs(dr, s):
        ff = 2 * src_chip(dr, s) + k
        return remote(cot_o.at[ff], cot_o.at[ff], s_cs.at[dr, s], r_cs.at[dr, s], sib, d)

    def cs_in(dr, s):
        ff = 2 * src_chip(dr, s) + 1 - k
        return remote(cot_o.at[ff], cot_o.at[ff], s_cs.at[dr, s], r_cs.at[dr, s], sib, d)

    at = 0
    w_own = []
    for i, w in enumerate((wq, wk, wv, wo)):
        w_own.append(pltpu.make_async_copy(w, wf.at[rows(f), at:at + w.shape[1]], s_w.at[i]))
        at += w.shape[1]
    for cp in w_own:
        cp.start()
    for cp in w_own:
        cp.wait()
    for g in range(2):
        for dr in range(2):
            @pl.when(nxt_ok(dr))
            def _():
                wz(dr, 1, g).start()
    own_small = pltpu.make_async_copy(small, sm.at[f], s_loc.at[0])
    own_small.start()
    sm_copies = []
    for i in range(1, nf):
        cp = remote(small, sm.at[f], s_sm.at[i - 1], r_sm.at[i - 1], lax.rem(f + i, nf), d)
        cp.start()
        sm_copies.append(cp)
    for dr in range(2):
        @pl.when((c if dr == 0 else C - 1 - c) == 0)
        def _():
            for h in range(2):
                cz(dr, 1, True, h).start()
    sib_own = remote(wf.at[rows(f)], wf.at[rows(f)], s_sib.at[0, 0, 0], r_sib.at[0, 0, 0], sib, d)
    sib_own.start()
    own_c = pltpu.make_async_copy(cot, cot_o.at[f], s_loc.at[2])
    own_c.start()
    sib_c = remote(cot, cot_o.at[f], s_cs.at[0, 0], r_cs.at[0, 0], sib, d)

    def dp_copy(dr, s, g, i):
        blk = wf.at[rows(2 * src_chip(dr, s) + k), cols(d, g)]
        return remote(blk, blk, s_dp.at[g, dr, s - 1, i - 1], r_dp.at[g, dr, s - 1, i - 1], f, jnp.bitwise_xor(d, i))

    def dp_in(dr, s, g, i):
        blk = wf.at[rows(2 * src_chip(dr, s) + k), cols(jnp.bitwise_xor(d, i), g)]
        return remote(blk, blk, s_dp.at[g, dr, s - 1, i - 1], r_dp.at[g, dr, s - 1, i - 1], f, d)

    def sib_copy(dr, s, g):
        at, n = parts[g]
        blk = wf.at[rows(2 * src_chip(dr, s) + k), at:at + n]
        return remote(blk, blk, s_sib.at[g, dr, s], r_sib.at[g, dr, s], sib, d)

    def sib_in(dr, s, g):
        at, n = parts[g]
        blk = wf.at[rows(2 * src_chip(dr, s) + 1 - k), at:at + n]
        return remote(blk, blk, s_sib.at[g, dr, s], r_sib.at[g, dr, s], sib, d)

    for s in range(1, C):
        for g in range(2):
            for dr in range(2):
                @pl.when(has(dr, s))
                def _():
                    wz_in(dr, s, g).wait_recv()
                    if s < C - 1:
                        @pl.when(nxt_ok(dr))
                        def _():
                            wz(dr, s + 1, g).start()
                    if g == 0:
                        for i in range(1, nd):
                            dp_copy(dr, s, g, i).start()
        for dr in range(2):
            @pl.when(nxt_ok(dr) & ((c if dr == 0 else C - 1 - c) == s))
            def _():
                for h in range(2):
                    cz(dr, 1, True, h).start()
    sib_c.start()
    for s in range(1, C):
        for dr in range(2):
            @pl.when(has(dr, s))
            def _():
                for i in range(1, nd):
                    dp_copy(dr, s, 1, i).start()

    def group_in(s, g):
        for dr in range(2):
            @pl.when(has(dr, s))
            def _():
                for i in range(1, nd):
                    dp_in(dr, s, g, i).wait_recv()
                sib_copy(dr, s, g).start()

    def cores_in(g):
        for s in range(1, C):
            for dr in range(2):
                @pl.when(has(dr, s))
                def _():
                    sib_in(dr, s, g).wait_recv()

    own_small.wait()
    for cp in sm_copies:
        cp.wait()
    Ds = small.shape[1]
    rt = jnp.concatenate([sm[i] for i in range(nf)], axis=1)
    rt_o[...] = rt
    gains = rt[experts:experts + 2].astype(F32)
    gain_one, gain_two = gains[0:1], gains[1:2]
    xf = tok[...].astype(F32)
    r1 = lax.rsqrt(jnp.mean(xf * xf, -1, keepdims=True) + EPSILON)
    attn[...] = (xf * r1 * gain_one).astype(BF)

    def cot_step(s):
        for dr in range(2):
            @pl.when(has(dr, s))
            def _():
                for h in range(2):
                    cz_in(dr, s, h).wait_recv()
                    if s < C - 1:
                        @pl.when(nxt_ok(dr))
                        def _():
                            cz(dr, s + 1, False, h).start()
                cs(dr, s).start()

    cot_step(1)
    for s in range(1, C - 1):
        group_in(s, 0)
    for s in range(2, min(C, 3)):
        cot_step(s)
    group_in(C - 1, 0)
    sib_own.wait()
    cores_in(0)

    first = lax.rem(lax.broadcasted_iota(jnp.int32, (T, 256), 1), HEAD_SIZE) < HEAD_SIZE // 2
    cs_t = jnp.concatenate([cosr[...], cosr[...]], 1)
    sn_t = jnp.concatenate([sinr[...], sinr[...]], 1)
    nqk = (QW + KW) // 256

    @pl.loop(0, nqk)
    def _(i):
        col = pl.ds(pl.multiple_of(i * 256, 256), 256)
        x = dot(attn[...], wf[:, col])
        qk_o[:, col] = (x * cs_t + half_roll(x, first) * sn_t).astype(BF)

    @pl.loop(0, KW // 256)
    def _(i):
        col = pl.ds(pl.multiple_of(QW + KW + i * 256, 256), 256)
        v_o[:, pl.ds(pl.multiple_of(i * 256, 256), 256)] = dot(attn[...], wf[:, col]).astype(BF)

    factor = HEAD_SIZE ** (-0.5)
    lane = lax.broadcasted_iota(jnp.int32, (T, 128), 1)
    keep = lax.broadcasted_iota(jnp.int32, (T, T), 1) <= lax.broadcasted_iota(jnp.int32, (T, T), 0)

    @pl.loop(0, KEY_VALUE_HEADS // 2)
    def _(i):
        kc = pl.ds(pl.multiple_of(QW + i * 128, 128), 128)
        kh = head_masks(qk_o[:, kc], lane)
        vh = head_masks(v_o[:, pl.ds(pl.multiple_of(i * 128, 128), 128)], lane)
        for p in range(GROUP):
            qc = pl.ds(pl.multiple_of((i * GROUP + p) * 128, 128), 128)
            q = qk_o[:, qc]
            acc = None
            for half in range(2):
                g = (2 * p + half) // GROUP
                sc = dot_nt(q, kh[g][half]) * factor
                sc = jnp.where(keep, sc, MASKED)
                ex = jnp.exp(sc - jnp.max(sc, -1, keepdims=True))
                pr = (ex / jnp.sum(ex, -1, keepdims=True)).astype(BF)
                prob_o[i * 2 * GROUP + 2 * p + half] = pr
                term = dot(pr, vh[g][half])
                acc = term if acc is None else acc + term
            mix_o[:, qc] = acc.astype(BF)

    for s in range(1, C):
        group_in(s, 1)
    cores_in(1)
    out_w = pltpu.make_async_copy(wf, wf_o, s_loc.at[3])
    out_w.start()
    for s in range(3, C):
        cot_step(s)

    @pl.loop(0, D // 256)
    def _(i):
        col = pl.ds(pl.multiple_of(i * 256, 256), 256)
        wc = pl.ds(pl.multiple_of(QW + 2 * KW + i * 256, 256), 256)
        hid_o[:, col] = tok[:, col].astype(F32) + dot(mix_o[...], wf[:, wc])

    hidden = hid_o[...]
    r2 = lax.rsqrt(jnp.mean(hidden * hidden, -1, keepdims=True) + EPSILON)
    ffn_o[...] = (hidden * r2 * gain_two).astype(BF)
    logits = dot_nt(rt_o[...], ffn_o[...])[0:experts]
    named = slots[...] >= 0.0
    logits = jnp.where(named, logits, MASKED)
    ex = jnp.where(named, jnp.exp(logits - jnp.max(logits, 0, keepdims=True)), 0.0)
    gates_o[...] = ex / jnp.sum(ex, 0, keepdims=True)

    own_c.wait()
    sib_c.wait()
    out_w.wait()
    for dr in range(2):
        for s in range(1, C):
            @pl.when(has(dr, s))
            def _():
                cs_in(dr, s).wait_recv()
                cs(dr, s).wait_send()
                for g in range(2):
                    sib_copy(dr, s, g).wait_send()
                    for i in range(1, nd):
                        dp_copy(dr, s, g, i).wait_send()

            @pl.when(nxt_ok(dr) & (has(dr, s - 1) if s > 1 else True))
            def _():
                for g in range(2):
                    wz(dr, s, g).wait_send()
                for h in range(2):
                    cz(dr, s, s == 1, h).wait_send()


def front(nf, nd, experts, tok, ws, small, cot, slots, cosr, sinr):
    T, D = tok.shape
    C = nf // 2
    W = sum(w.shape[1] for w in ws)
    out = [
        (T, D, BF, 0), (T, D, F32, 0), (experts, T, F32, 0), (T, QW, BF, 0), (T, QW + KW, BF, 0),
        (T, KW, BF, 0), (QUERY_HEADS, T, T, BF, 0), (D, W, BF, 1), (nf, T, D, BF, 1),
        (small.shape[0], D, BF, 0),
    ]
    dma = pltpu.SemaphoreType.DMA
    return pl.pallas_call(
        functools.partial(front_kernel, nf, nd, experts),
        out_shape=[jax.ShapeDtypeStruct(o[:-2], o[-2]) for o in out],
        in_specs=[vm()] + [hbm()] * 4 + [vm()] * 5,
        out_specs=[hbm() if o[-1] else vm() for o in out],
        scratch_shapes=[
            VMEM((D, W), BF),
            VMEM((nf,) + small.shape, BF),
            VMEM((T, D), BF),
            VMEM((8, 128), F32),
            dma((nf,)), dma((nf,)),
            dma((2, 2, C)), dma((2, 2, C)),
            dma((2, 2, C, nd)), dma((2, 2, C, nd)),
            dma((2, 2, C)), dma((2, 2, C)),
            dma((2, 2, C)), dma((2, 2, C)),
            dma((2, C)), dma((2, C)),
            dma((4,)), dma((4,)),
        ],
        compiler_params=pltpu.CompilerParams(collective_id=1, has_side_effects=True,
                                             vmem_limit_bytes=60 * 2 ** 20),
        cost_estimate=pl.CostEstimate(flops=4_000_000_000, bytes_accessed=60_000_000, transcendentals=2_000_000),
        name="front",
    )(tok, *ws, small, cot, slots, cosr, sinr)


def add_blocks(dst, srcs, extra=None):
    @pl.loop(0, dst.shape[0] // 16)
    def _(i):
        at = pl.ds(pl.multiple_of(i * 16, 16), 16)
        total = srcs[0][at, :].astype(F32)
        for s in srcs[1:]:
            total = total + s[at, :].astype(F32)
        dst[at, :] = total.astype(dst.dtype)


class Line:
    def __init__(self, nf, f, d, acc, give, sib, rcv, stage, sems, stage_sem):
        self.nf, self.f, self.d = nf, f, d
        self.C = nf // 2
        self.c, self.k = f // 2, lax.rem(f, 2)
        self.acc, self.give, self.sib, self.rcv, self.stage = acc, give, sib, rcv, stage
        self.s_sib, self.r_sib, self.s_z, self.r_z = sems
        self.stage_sem = stage_sem

    def remote(self, src, dst, ss, rs, to):
        return pltpu.make_async_remote_copy(src_ref=src, dst_ref=dst, send_sem=ss, recv_sem=rs,
                                            device_id=(to, self.d), device_id_type=MESH)

    def dest(self, dr, s):
        i = s - 1 - (self.C - 1 - self.c) if dr == 0 else s - 1 - self.c
        room = self.c if dr == 0 else self.C - 1 - self.c
        chip = i if dr == 0 else self.C - 1 - i
        return jnp.clip(chip, 0, self.C - 1), (i >= 0) & (i < room)

    def sib_copy(self, chip):
        return self.remote(self.give(chip), self.sib(chip), self.s_sib.at[chip], self.r_sib.at[chip],
                           self.f + 1 - 2 * self.k)

    def z_copy(self, dr, s, chip):
        return self.remote(self.acc(chip), self.rcv(dr, s - 1), self.s_z.at[dr, s - 1], self.r_z.at[dr, s - 1],
                           self.f - 2 if dr == 0 else self.f + 2)

    def z_in(self, dr, s):
        return self.remote(self.rcv(dr, s - 1), self.rcv(dr, s - 1), self.s_z.at[dr, s - 1], self.r_z.at[dr, s - 1],
                           self.f)

    def start_sib(self):
        for s in range(1, self.C):
            for dr in range(2):
                chip, ok = self.dest(dr, s)

                @pl.when(ok)
                def _():
                    self.sib_copy(chip).start()
        self.sib_copy(self.c).start()

    def gather(self, chip, srcs):
        acc = self.acc(chip)
        if self.stage is None:
            add_blocks(acc, [acc] + srcs)
            return
        for s in srcs:
            cp = pltpu.make_async_copy(s, self.stage, self.stage_sem)
            cp.start()
            cp.wait()
            add_blocks(acc, [acc, self.stage])

    def step(self, s):
        for dr in range(2):
            chip, ok = self.dest(dr, s)
            begins = (self.c == self.C - 1) if dr == 0 else (self.c == 0)

            @pl.when(ok)
            def _():
                other = []
                if self.sib is not None:
                    self.sib_copy(chip).wait_recv()
                    other = [self.sib(chip)]

                    @pl.when(begins)
                    def _():
                        self.gather(chip, other)
                if s > 1:
                    @pl.when(jnp.logical_not(begins))
                    def _():
                        self.z_in(dr, s - 1).wait_recv()
                        self.gather(chip, other + [self.rcv(dr, s - 2)])
                self.z_copy(dr, s, chip).start()

    def last(self):
        other = []
        if self.sib is not None:
            self.sib_copy(self.c).wait_recv()
            other = [self.sib(self.c)]
        mid = (self.c > 0) & (self.c < self.C - 1)
        s = self.C - 1
        for dr in range(2):
            @pl.when((self.c < self.C - 1) if dr == 0 else (self.c > 0))
            def _():
                self.z_in(dr, s).wait_recv()

        @pl.when(mid)
        def _():
            self.gather(self.c, other + [self.rcv(0, s - 1), self.rcv(1, s - 1)])

        @pl.when(self.c == 0)
        def _():
            self.gather(self.c, other + [self.rcv(0, s - 1)])

        @pl.when(self.c == self.C - 1)
        def _():
            self.gather(self.c, other + [self.rcv(1, s - 1)])

    def sent(self):
        if self.acc is None:
            for chip in range(self.C):
                self.sib_copy(chip).wait_send()
            return
        if self.sib is not None:
            self.sib_copy(self.c).wait_send()
        for s in range(1, self.C):
            for dr in range(2):
                chip, ok = self.dest(dr, s)

                @pl.when(ok)
                def _():
                    if self.sib is not None:
                        self.sib_copy(chip).wait_send()
                    self.z_copy(dr, s, chip).wait_send()


class Cube:
    def __init__(self, nd, f, d, flip, lanes, size, own, land, total, out, sems):
        m = nd.bit_length() - 1
        order = [1 << b for b in range(m)]
        if isinstance(flip, bool):
            self.masks = order[::-1] if flip else order
        else:
            self.masks = [jnp.where(flip, b, a) for a, b in zip(order, order[::-1])]
        self.f, self.d, self.lanes = f, d, lanes
        self.own, self.land, self.total, self.out = own, land, total, out
        self.ss, self.rs = sems
        self.m = m
        self.in_place, self.whole = False, True
        self.low, self.length = [0], [size]
        for mask in self.masks:
            half = self.length[-1] // 2
            side = lax.rem(d // mask, 2)
            self.low.append(self.low[-1] + side * half)
            self.length.append(half)

    def cut(self, ref, at, n):
        if self.lanes:
            return ref.at[:, pl.ds(pl.multiple_of(at, 128), n)]
        return ref.at[pl.ds(pl.multiple_of(at, 16), n)]

    def remote(self, src, dst, i, mask):
        return pltpu.make_async_remote_copy(src_ref=src, dst_ref=dst, send_sem=self.ss.at[i], recv_sem=self.rs.at[i],
                                            device_id=(self.f, jnp.bitwise_xor(self.d, mask)),
                                            device_id_type=MESH)

    def level(self, i):
        if i == 0 or (self.in_place and (i < self.m or not self.whole)):
            return self.own, 0
        if i == self.m:
            return self.out, 0
        return self.total(i - 1), self.low[i]

    def down(self, i):
        ref, base = self.level(i)
        half = self.length[i + 1]
        other = 2 * self.low[i] + half - self.low[i + 1]
        return self.remote(self.cut(ref, other - base, half), self.land(i), i, self.masks[i])

    def merge(self, i, add):
        self.down(i).wait_recv()
        self.fold(i, add)

    def fold(self, i, add):
        ref, base = self.level(i)
        dst, dbase = self.level(i + 1)
        half = self.length[i + 1]
        low = self.low[i + 1]
        add(self.cut(dst, low - dbase, half), self.cut(ref, low - base, half), self.land(i))

    def up(self, i):
        blk = self.cut(self.out, self.low[i + 1], self.length[i + 1])
        return self.remote(blk, blk, self.m + i, self.masks[i])

    def up_in(self, i):
        half = self.length[i + 1]
        other = 2 * self.low[i] + half - self.low[i + 1]
        blk = self.cut(self.out, other, half)
        return self.remote(blk, blk, self.m + i, self.masks[i])

    def sent(self, first=0):
        for i in range(self.m):
            if i >= first:
                self.down(i).wait_send()
            self.up(i).wait_send()


def pipe_add(dst, a, b):
    n, w = dst.shape
    tile = 128 if n % 128 == 0 else 64
    spec = pl.BlockSpec((tile, w), lambda i: (i, 0))

    def inner(a_ref, b_ref, o_ref):
        o_ref[...] = (a_ref[...].astype(F32) + b_ref[...].astype(F32)).astype(o_ref.dtype)

    pltpu.emit_pipeline(inner, grid=(n // tile,), in_specs=[spec, spec], out_specs=[spec])(a, b, dst)

def visit(c, C, j):
    both = jnp.minimum(c, C - 1 - c)
    near = j <= 2 * both
    dist = jnp.where(near, (j + 1) // 2, j - both)
    down = jnp.where(near, lax.rem(j, 2) == 0, c < C - 1 - c)
    chip = jnp.where(down, c + dist, c - dist)
    return chip, jnp.where(down, 1, 0), dist


def term_cubes(nd, el, f, d, t1, t2, out1, out2, l1, l2, a1, a2, sems):
    cubes = []
    for e in range(el):
        for j, (src, out, ls, ts) in enumerate(((t1, out1, l1, a1), (t2, out2, l2, a2))):
            pick = functools.partial(lambda refs, e, i: refs[i].at[e], ls, e)
            tot = functools.partial(lambda refs, e, i: refs[i].at[e], ts, e)
            cubes.append(Cube(nd, f, d, (e + j) % 2 == 1, False, src.shape[1], src.at[e], pick, tot,
                              None if out is None else out.at[e], (sems[0].at[2 * e + j], sems[1].at[2 * e + j])))
    return cubes


def experts_kernel(nf, nd, el, cap, capp, land_hbm, ffn, cot_a, side, wg_h, wu_h, wd_h,
                   out_o, gin_o, gp_o, t1_o, t2_o, l1, sib_l, rcv_l, acc,
                   wg, wu, wd, fa, sd, cotb, xs, gs, hs, hgs, orb, irb, st_o, give, st1, st2, stage, us,
                   s_sd, r_sd, s_z, r_z, s_sib, r_sib, s_w, s_loc, s_t, s_ls, r_ls, s_lz, r_lz, s_st, s_cube, r_cube):
    T, D = ffn.shape
    FFW = wg.shape[2]
    C = nf // 2
    B = 2 * capp
    f = lax.axis_index("fsdp")
    d = lax.axis_index("dp")
    c = f // 2
    k = lax.rem(f, 2)
    sib = f + 1 - 2 * k
    greet(nf, nd, f, d)

    def remote(src, dst, ss, rs, to_f):
        return pltpu.make_async_remote_copy(src_ref=src, dst_ref=dst, send_sem=ss, recv_sem=rs,
                                            device_id=(to_f, d), device_id_type=MESH)

    def chip_at(dr, s):
        return jnp.where(dr == 0, c - s, c + s)

    def has(dr, s):
        at = chip_at(dr, s)
        return (at >= 0) & (at < C)

    def nxt_ok(dr):
        return (c + 1 < C) if dr == 0 else (c - 1 >= 0)

    def nxt_f(dr):
        return f + 2 if dr == 0 else f - 2

    halves = (slice(0, D // 2), slice(D // 2, D))

    def z_out(dr, s, h):
        blk = fa.at[2 * chip_at(dr, s - 1) + k, :, halves[h]]
        return remote(blk, blk, s_z.at[h, dr, s - 1], r_z.at[h, dr, s - 1], nxt_f(dr))

    def z_own(dr, h):
        return remote(ffn.at[:, halves[h]], fa.at[f, :, halves[h]], s_z.at[h, dr, 0], r_z.at[h, dr, 0], nxt_f(dr))

    def z_in(dr, s, h):
        blk = fa.at[2 * chip_at(dr, s) + k, :, halves[h]]
        return remote(blk, blk, s_z.at[h, dr, s - 1], r_z.at[h, dr, s - 1], f)

    def sib_out(dr, s):
        ff = 2 * chip_at(dr, s) + k
        return remote(fa.at[ff], fa.at[ff], s_sib.at[dr, s], r_sib.at[dr, s], sib)

    def sib_in(dr, s):
        ff = 2 * chip_at(dr, s) + 1 - k
        return remote(fa.at[ff], fa.at[ff], s_sib.at[dr, s], r_sib.at[dr, s], f)

    lines = [Line(nf, f, d, lambda ch, cut=cut: acc.at[ch, :, cut], lambda ch, cut=cut: give.at[0, :, cut],
                  lambda ch, cut=cut: sib_l.at[ch, :, cut], lambda dr, s, cut=cut: rcv_l.at[dr, s, :, cut],
                  stage.at[:, cut] if land_hbm else None, (s_ls.at[h], r_ls.at[h], s_lz.at[h], r_lz.at[h]), s_st)
             for h, cut in enumerate(halves)]

    def handed(chip, slot, h):
        return remote(give.at[slot, :, halves[h]], sib_l.at[chip, :, halves[h]], s_ls.at[h, chip], r_ls.at[h, chip], sib)

    def reduce_step(s):
        for line in lines:
            line.step(s)

    for h in range(2):
        for dr in range(2):
            @pl.when(nxt_ok(dr))
            def _():
                z_own(dr, h).start()
    sib_own = remote(ffn, fa.at[f], s_sib.at[1, 0], r_sib.at[1, 0], sib)
    sib_own.start()
    own = pltpu.make_async_copy(ffn, fa.at[f], s_loc.at[0])
    own.start()
    own_sd = pltpu.make_async_copy(side.at[f], sd.at[f], s_loc.at[1])
    own_sd.start()
    sd_copies = []
    for i in range(1, nf):
        to = lax.rem(f + i, nf)
        cp = remote(side.at[to], sd.at[f], s_sd.at[i - 1], r_sd.at[i - 1], to)
        cp.start()
        sd_copies.append(cp)
    w_copies = []
    for i, (src, dst) in enumerate(((wg_h, wg), (wu_h, wu), (wd_h, wd))):
        cp = pltpu.make_async_copy(src, dst, s_w.at[i])
        cp.start()
        w_copies.append(cp)
    own.wait()
    own_sd.wait()
    for cp in sd_copies:
        cp.wait()
    for cp in w_copies:
        cp.wait()

    row_ids = lax.broadcasted_iota(jnp.int32, (capp, T), 0).astype(F32)

    @pl.loop(0, C)
    def _(j):
        b, dr_b, dist_b = visit(c, C, j)
        cot_cp = pltpu.make_async_copy(cot_a.at[pl.ds(2 * b, 2)], cotb, s_loc.at[2])
        cot_cp.start()

        base = pl.multiple_of(b * B, 16)
        gate_rows = [[None, None] for _ in range(el)]
        picks = []
        for kk in range(2):
            s = 2 * b + kk
            parts = []
            for e in range(el):
                hit = row_ids == sd[s, e:e + 1, :]
                gate_rows[e][kk] = jnp.sum(jnp.where(hit, sd[s, el + e:el + e + 1, :], 0.0), -1, keepdims=True)
                parts.append(jnp.where(hit, 1.0, 0.0).astype(BF))
            p2 = jnp.concatenate(parts, 0)
            picks.append(p2)
        cot_cp.wait()

        def spread(rows_of, dst):
            for kk in range(2):
                for n in range(0, D, 512):
                    val = dot(picks[kk], rows_of(kk, n)).astype(BF)
                    for e in range(el):
                        at = pl.ds(pl.multiple_of(base + kk * capp, 16), capp)
                        dst[e, at, n:n + 512] = val[e * capp:(e + 1) * capp]

        here = pl.ds(base, B)
        spread(lambda kk, n: cotb[kk, :, n:n + 512], gs)
        for e in range(el):
            for n in range(0, FFW, 256):
                us[e, :, n:n + 256] = dot_nt(gs[e, here, :], wd[e, n:n + 256, :])

        @pl.when(j >= 1)
        def _():
            for dr in range(2):
                @pl.when(has(dr, j))
                def _():
                    for h in range(2):
                        z_in(dr, j, h).wait_recv()

                        @pl.when(nxt_ok(dr) & (j < C - 1))
                        def _():
                            z_out(dr, j + 1, h).start()
                    sib_out(dr, j).start()
        sib_in(dr_b, dist_b).wait_recv()
        spread(lambda kk, n: fa[2 * b + kk, :, n:n + 512], xs)
        gp_rows = []
        for e in range(el):
            gate_row = jnp.concatenate(gate_rows[e], 0)
            gpr = jnp.zeros((B, 1), F32)
            for n in range(0, FFW, 256):
                gv = dot(xs[e, here, :], wg[e, :, n:n + 256])
                uv = dot(xs[e, here, :], wu[e, :, n:n + 256])
                u = us[e, :, n:n + 256]
                sg = 1.0 / (1.0 + jnp.exp(-gv))
                act = gv * sg
                hid = act * uv
                gpr = gpr + jnp.sum(hid * u, -1, keepdims=True)
                hgs[e, here, n:n + 256] = (hid * gate_row).astype(BF)
                gh = u * gate_row
                hs[e, here, n:n + 256] = (gh * uv * (sg * (1.0 + gv * (1.0 - sg)))).astype(BF)
                hs[e, here, FFW + n:FFW + n + 256] = (gh * act).astype(BF)
            gp_rows.append(gpr)
            for n in range(0, D, 512):
                irow = (dot_nt(hs[e, here, 0:FFW], wg[e, n:n + 512, :])
                        + dot_nt(hs[e, here, FFW:2 * FFW], wu[e, n:n + 512, :])).astype(BF)
                for kk in range(2):
                    irb[kk, e * capp:(e + 1) * capp, n:n + 512] = irow[kk * capp:(kk + 1) * capp]

        @pl.when(j >= 2)
        def _():
            before, _, _ = visit(c, C, j - 2)
            for h in range(2):
                handed(before, lax.rem(j, 2), h).wait_send()
        for h in range(2):
            for kk in range(2):
                def combine(dst):
                    cut = halves[h]
                    dst[:, cut] = dot_tn(picks[kk], irb[kk, :, cut]).astype(BF)

                @pl.when(k == kk)
                def _():
                    combine(acc.at[b])

                @pl.when(k != kk)
                def _():
                    combine(give.at[lax.rem(j, 2)])
                    handed(b, lax.rem(j, 2), h).start()

        @pl.when(j == C - 1)
        def _():
            reduce_step(1)
        for e in range(el):
            for n in range(0, D, 512):
                orow = dot(hgs[e, here, :], wd[e, :, n:n + 512]).astype(BF)
                for kk in range(2):
                    orb[kk, e * capp:(e + 1) * capp, n:n + 512] = orow[kk * capp:(kk + 1) * capp]

        def back(bb):
            return pltpu.make_async_copy(st_o, out_o.at[pl.ds(2 * bb, 2)], s_loc.at[3])

        @pl.when(j >= 1)
        def _():
            back(0).wait()
        for kk in range(2):
            s = 2 * b + kk
            for e in range(el):
                hit = picks[kk][e * capp:(e + 1) * capp].astype(F32)
                gp_o[s, e:e + 1, :] = jnp.sum(hit * gp_rows[e][kk * capp:(kk + 1) * capp], 0, keepdims=True)
            for n in range(0, D, 512):
                st_o[kk, :, n:n + 512] = dot_tn(picks[kk], orb[kk, :, n:n + 512]).astype(BF)
        back(b).start()

    n1 = D // 256
    n2 = FFW // 256

    def t1_copy(e, i):
        return pltpu.make_async_copy(st1.at[lax.rem(i, 2)], t1_o.at[e, pl.ds(pl.multiple_of(i * 256, 256), 256)],
                                     s_t.at[0, lax.rem(i, 2)])

    def t2_copy(e, i):
        return pltpu.make_async_copy(st2.at[lax.rem(i, 2)], t2_o.at[e, pl.ds(pl.multiple_of(i * 256, 256), 256)],
                                     s_t.at[1, lax.rem(i, 2)])

    cubes = term_cubes(nd, el, f, d, t1_o, t2_o, None, None, [l1], None, [], [], (s_cube, r_cube))
    for e in range(el):
        @pl.loop(0, n1)
        def _(i):
            @pl.when(i >= 2)
            def _():
                t1_copy(e, i).wait()
            col = pl.ds(pl.multiple_of(i * 256, 256), 256)
            st1[lax.rem(i, 2)] = dot_tn(xs[e, :, col], hs[e]).astype(BF)
            t1_copy(e, i).start()

        for i in range(2):
            t1_copy(e, i).wait()
        cubes[2 * e].down(0).start()
        if e == el - 1 and C > 2:
            reduce_step(2)

        @pl.loop(0, n2)
        def _(i):
            @pl.when(i >= 2)
            def _():
                t2_copy(e, i).wait()
            col = pl.ds(pl.multiple_of(i * 256, 256), 256)
            st2[lax.rem(i, 2)] = dot_tn(hgs[e, :, col], gs[e]).astype(BF)
            t2_copy(e, i).start()
        for i in range(2):
            t2_copy(e, i).wait()

    for s in range(3, C):
        reduce_step(s)
    for line in lines:
        line.last()
    gin_o[...] = acc[c]

    pltpu.make_async_copy(st_o, out_o.at[pl.ds(0, 2)], s_loc.at[3]).wait()
    for j in range(max(C - 2, 0), C):
        chip, _, _ = visit(c, C, j)
        for h in range(2):
            handed(chip, j % 2, h).wait_send()
    for line in lines:
        for s in range(1, C):
            for dr in range(2):
                chip, ok = line.dest(dr, s)

                @pl.when(ok)
                def _():
                    line.z_copy(dr, s, chip).wait_send()
    for cube in cubes[::2]:
        cube.down(0).wait()
    sib_own.wait_send()
    for dr in range(2):
        for s in range(1, C):
            @pl.when(has(dr, s))
            def _():
                sib_out(dr, s).wait_send()
        for s in range(1, C):
            @pl.when(nxt_ok(dr) & has(dr, s - 1))
            def _():
                for h in range(2):
                    z_out(dr, s, h).wait_send()


def experts_call(nf, nd, cap, ffn_in, cot_all, side, w_gate, w_up, w_down):
    T, D = ffn_in.shape
    el, _, FFW = w_gate.shape
    capp = cap + (-cap % 16)
    C = nf // 2
    rows = C * 2 * capp
    land_hbm = C > 4
    dma = pltpu.SemaphoreType.DMA
    out = [((nf, T, D), BF, 1), ((T, D), BF, 0), ((nf, el, T), F32, 0),
           ((el, D, 2 * FFW), BF, 1), ((el, FFW, D), BF, 1),
           ((el, D // 2, 2 * FFW), BF, 1)]
    lands = [(C, T, D), (2, C - 1, T, D)]
    scratch = []
    if land_hbm:
        out += [(x, BF, 1) for x in lands]
    else:
        scratch += [VMEM(x, BF) for x in lands]
    scratch += [
        VMEM((C, T, D), BF),
        VMEM((el, D, FFW), BF), VMEM((el, D, FFW), BF), VMEM((el, FFW, D), BF),
        VMEM((nf, T, D), BF), VMEM(side.shape, F32), VMEM((2, T, D), BF),
        VMEM((el, rows, D), BF), VMEM((el, rows, D), BF),
        VMEM((el, rows, 2 * FFW), BF), VMEM((el, rows, FFW), BF),
        VMEM((2, el * capp, D), BF), VMEM((2, el * capp, D), BF),
        VMEM((2, T, D), BF), VMEM((2, T, D), BF),
        VMEM((2, 256, 2 * FFW), BF), VMEM((2, 256, D), BF),
        VMEM((T, D) if land_hbm else (16, 128), BF),
        VMEM((el, 2 * capp, FFW), F32),
        dma((nf,)), dma((nf,)),
        dma((2, 2, C)), dma((2, 2, C)), dma((2, C)), dma((2, C)),
        dma((3,)), dma((5,)), dma((2, 2)),
        dma((2, C)), dma((2, C)), dma((2, 2, C)), dma((2, 2, C)), dma(()),
        dma((2 * el, 2 * (nd.bit_length() - 1))), dma((2 * el, 2 * (nd.bit_length() - 1))),
    ]
    return pl.pallas_call(
        functools.partial(experts_kernel, nf, nd, el, cap, capp, land_hbm),
        out_shape=[jax.ShapeDtypeStruct(o[0], o[1]) for o in out],
        in_specs=[vm(), hbm(), vm(), hbm(), hbm(), hbm()],
        out_specs=[hbm() if o[2] else vm() for o in out],
        scratch_shapes=scratch,
        compiler_params=pltpu.CompilerParams(collective_id=2, has_side_effects=True,
                                             vmem_limit_bytes=63 * 2 ** 20),
        cost_estimate=pl.CostEstimate(flops=40_000_000_000, bytes_accessed=60_000_000, transcendentals=2_000_000),
        name="experts",
    )(ffn_in, cot_all, side, w_gate, w_up, w_down)[:6]


def back_kernel(nf, nd, el, land_hbm, split, *refs):
    m = nd.bit_length() - 1
    it = iter(refs)

    def take(n):
        return [next(it) for _ in range(n)]

    (gin, out_p, gp_p, t1, t2, f1, tok_h, cot_h, hid_h, ffn_h, gates, mix_h, qk_h, v_h, prob_h, wf_h, rt,
     cosr, sinr) = take(19)
    out_o, gt_o, sh_o, sm_o, t1_o, t2_o = take(6)
    l1 = [f1] + take(m - 1)
    l2 = take(m)
    a1 = take(m - 1)
    a2 = take(m - 1)
    sibo, rcvo, sib, rcv, sibq, rcvq = take(6)
    (acc, wb, wg, tok, cot, hid, ffn, mix, qk, v, prob, branch, gh, ga, gproj, gpb, smg, smr, smd, sms) = take(20)
    attn, gm = ffn, mix
    shl = take(m)
    if split:
        xo = next(it)
        xol = take(m)
    stage, stageq = take(2)
    (s_load, s_acc, s_gp, r_gp, s_sib, r_sib, s_z, r_z, s_cube, r_cube, s_sc, r_sc, s_sm, r_sm, s_sd, r_sd,
     s_stage, s_prob) = take(18)

    T, D = tok.shape
    R = wg.shape[0] // nf
    W = wg.shape[1]
    E = gates.shape[0]
    C = nf // 2
    f = lax.axis_index("fsdp")
    d = lax.axis_index("dp")
    c = f // 2
    k = lax.rem(f, 2)
    QV = QW + 2 * KW
    greet(nf, nd, f, d)

    def remote(src, dst, ss, rs, to_f, to_d):
        return pltpu.make_async_remote_copy(src_ref=src, dst_ref=dst, send_sem=ss, recv_sem=rs,
                                            device_id=(to_f, to_d), device_id_type=MESH)

    def rows(ff):
        return pl.ds(pl.multiple_of(ff * R, 16), R)


    def sems(i):
        return (s_sib.at[i], r_sib.at[i], s_z.at[i], r_z.at[i])

    def halves_of(first, n, sb, rc, sg, ids):
        res = []
        for h in range(2):
            at = first + h * (n // 2)
            cut, loc = pl.ds(at, n // 2), pl.ds(h * (n // 2), n // 2)
            res.append(Line(nf, f, d, lambda ch, cut=cut: wg.at[rows(2 * ch + k), cut],
                            lambda ch, cut=cut: wg.at[rows(2 * ch + 1 - k), cut],
                            lambda ch, loc=loc: sb.at[ch, :, loc], lambda dr, s, loc=loc: rc.at[dr, s, :, loc],
                            sg.at[:, loc] if land_hbm else None, sems(ids[h]), s_stage))
        return res

    if split:
        o_lines = []
        pair = Line(nf, f, d, None, lambda ch: wg.at[rows(2 * ch + 1 - k), QV:QV + D], lambda ch: sib.at[ch], None, None,
                    sems(0), s_stage)
        o_cubes = []
        for h in range(2):
            top = h * (C * R // 2)
            cube = Cube(nd, f, d, h == 1, True, D, xo.at[top:top + C * R // 2],
                        functools.partial(lambda h, i: xol[i].at[h], h), None, None, (s_sc.at[h], r_sc.at[h]))
            cube.in_place, cube.whole = True, False
            o_cubes.append(cube)
        o_low = [cube.low[m] for cube in o_cubes]

        def o_block(ch):
            low = pl.multiple_of(jnp.where(ch < C // 2, o_low[0], o_low[1]), 128)
            return xo.at[pl.ds(pl.multiple_of(ch * R, 16), R), pl.ds(low, D >> m)]

        o_line = Line(nf, f, d, o_block, None, None, lambda dr, s: rcv.at[dr, s], None, sems(1), s_stage)
        o_up = Cube(nd, f, d, c >= C // 2, True, D, None, None, None, sh_o.at[:, QV:QV + D], (s_sc.at[2], r_sc.at[2]))
    else:
        o_lines = halves_of(QV, D, sib, rcv, stage.at[0:R], (0, 1))
    q_lines = halves_of(0, QV, sibq, rcvq, stageq, (2, 4))
    out_line = Line(nf, f, d, lambda ch: acc.at[ch], lambda ch: out_p.at[2 * ch + 1 - k], lambda ch: sibo.at[ch],
                    lambda dr, s: rcvo.at[dr, s], stage, sems(3), s_stage)

    def acc_loads(src):
        return [pltpu.make_async_copy(src.at[2 * ch + k], acc.at[ch], s_acc.at[ch]) for ch in range(C)]

    gp_copies = []
    for i in range(1, nf):
        to = lax.rem(f + i, nf)
        cp = remote(gp_p.at[to], gpb.at[f], s_gp.at[i - 1], r_gp.at[i - 1], to, d)
        cp.start()
        gp_copies.append(cp)
    out_line.start_sib()
    out_loads = acc_loads(out_p)
    for cp in out_loads:
        cp.start()
    cubes = term_cubes(nd, el, f, d, t1, t2, t1_o, t2_o, l1, l2, a1, a2, (s_cube, r_cube))
    first_terms, second_terms = cubes[::2], cubes[1::2]
    for cube in second_terms:
        cube.down(0).start()
    own_gp = pltpu.make_async_copy(gp_p.at[f], gpb.at[f], s_load.at[0])
    own_gp.start()
    wo = pltpu.make_async_copy(wf_h.at[:, QV:QV + D], wb.at[:, 0:D], s_load.at[1])
    wo.start()
    others = [(tok_h, tok), (cot_h, cot), (hid_h, hid), (ffn_h, ffn), (mix_h, mix), (qk_h, qk), (v_h, v)]
    more = [pltpu.make_async_copy(a, b, s_load.at[2 + i]) for i, (a, b) in enumerate(others)]
    for cp in more:
        cp.start()

    def prob_load(i):
        at = pl.ds(i * 2 * GROUP, 2 * GROUP)
        return pltpu.make_async_copy(prob_h.at[at], prob.at[lax.rem(i, 2)], s_prob.at[lax.rem(i, 2)])

    prob_load(0).start()

    def onward(cube, i):
        cube.down(i + 1).start() if i + 1 < m else cube.up(i).start()

    def chain(group, start, add):
        def merged(i):
            for cube in group:
                cube.merge(i, add)
                onward(cube, i)

        def raised(i):
            for cube in group:
                cube.up_in(i).wait_recv()
                cube.up(i - 1).start()

        return ([functools.partial(merged, i) for i in range(start, m)]
                + [functools.partial(raised, i) for i in range(m - 1, 0, -1)])

    def vadd(dst, a, b):
        add_blocks(dst, [a, b])

    def run(steps, n=1):
        for _ in range(min(n, len(steps))):
            steps.pop(0)()

    steps1, steps2 = chain(first_terms, 1, pipe_add), chain(second_terms, 1, pipe_add)
    for cube in first_terms:
        cube.fold(0, pipe_add)
        onward(cube, 0)
    for cp in out_loads:
        cp.wait()
    out_line.step(1)
    for cp in more:
        cp.wait()
    own_gp.wait()
    for cp in gp_copies:
        cp.wait()

    gains = rt[E:E + 2].astype(F32)
    gain_one, gain_two = gains[0:1], gains[1:2]
    gpt = jnp.concatenate([gpb[i] for i in range(nf)], 0)
    gates_v = gates[...]
    gl = (gates_v * (gpt - jnp.sum(gpt * gates_v, 0, keepdims=True))).astype(BF)
    for n in range(0, D, 512):
        sms[0:E, n:n + 512] = dot(gl, ffn[:, n:n + 512])
    for n in range(0, D, 512):
        ga[:, n:n + 512] = dot_tn(gl, rt[0:E, n:n + 512])
    sms[E:, :] = jnp.zeros((sms.shape[0] - E, D), F32)
    TR = 32

    @pl.loop(0, T // TR)
    def _(i):
        at = pl.ds(pl.multiple_of(i * TR, TR), TR)
        h = hid[at, :]
        r2 = lax.rsqrt(jnp.mean(h * h, -1, keepdims=True) + EPSILON)
        n2 = h * r2
        gf = gin[at, :].astype(F32) + ga[at, :]
        sms[E + 1:E + 2, :] += jnp.sum(gf * n2, 0, keepdims=True)
        g2 = gf * gain_two
        x = cot[at, :].astype(F32) + r2 * (g2 - n2 * jnp.mean(g2 * n2, -1, keepdims=True))
        gh[at, :] = x
        branch[at, :] = x.astype(BF)

    @pl.loop(0, QW // 256)
    def _(i):
        at = pl.ds(pl.multiple_of(i * 256, 256), 256)
        wg[at, QV:QV + D] = dot_tn(mix[:, at], branch[...]).astype(BF)
    if split:
        pair.start_sib()
        if C > 2:
            out_line.step(2)
    else:
        for line in o_lines:
            line.start_sib()
        for line in o_lines:
            line.step(1)
    wo.wait()

    @pl.loop(0, QW // 256)
    def _(i):
        at = pl.ds(pl.multiple_of(i * 256, 256), 256)
        gm[:, at] = dot_nt(branch[...], wb[at, 0:D]).astype(BF)
    wq = pltpu.make_async_copy(wf_h.at[:, 0:QV], wb, s_load.at[1])
    wq.start()
    if split:
        for ch in range(C):
            pair.sib_copy(ch).wait_recv()
            add_blocks(xo.at[ch * R:(ch + 1) * R], [wg.at[rows(2 * ch + k), QV:QV + D], sib.at[ch]])
        for cube in o_cubes:
            cube.down(0).start()
    for cube in second_terms:
        cube.merge(0, pipe_add)
        onward(cube, 0)
    factor = HEAD_SIZE ** (-0.5)
    lane = lax.broadcasted_iota(jnp.int32, (T, 128), 1)
    low = lane < HEAD_SIZE
    first = lax.rem(lane, HEAD_SIZE) < HEAD_SIZE // 2

    def unrotate(x):
        return x * cosr[...] - half_roll(x, first) * sinr[...]

    @pl.loop(0, KEY_VALUE_HEADS // 2)
    def _(i):
        @pl.when(i + 1 < KEY_VALUE_HEADS // 2)
        def _():
            prob_load(i + 1).start()
        prob_load(i).wait()
        slot = lax.rem(i, 2)
        kcol = pl.ds(pl.multiple_of(i * 128, 128), 128)
        kh = head_masks(qk[:, pl.ds(pl.multiple_of(QW + i * 128, 128), 128)], lane)
        vh = head_masks(v[:, kcol], lane)
        gk = [[None, None], [None, None]]
        gv = [[None, None], [None, None]]
        for p in range(GROUP):
            qc = pl.ds(pl.multiple_of((i * GROUP + p) * 128, 128), 128)
            q = qk[:, qc]
            g = gm[:, qc]
            gq = None
            for half in range(2):
                kv = (2 * p + half) // GROUP
                pr = prob[slot, 2 * p + half]
                prf = pr.astype(F32)
                gp = dot_nt(g, vh[kv][half])
                gs = (prf * (gp - jnp.sum(prf * gp, -1, keepdims=True))).astype(BF)
                term = dot(gs, kh[kv][half])
                gq = term if gq is None else gq + term
                tk = dot_tn(gs, q)
                tv = dot_tn(pr, g)
                gk[kv][half] = tk if gk[kv][half] is None else gk[kv][half] + tk
                gv[kv][half] = tv if gv[kv][half] is None else gv[kv][half] + tv
            gproj[:, qc] = unrotate(gq * factor).astype(BF)

        def join(x):
            a = jnp.where(low, x[0][0] + pltpu.roll(x[0][1], HEAD_SIZE, axis=1), 0.0)
            b = jnp.where(low, 0.0, pltpu.roll(x[1][0], HEAD_SIZE, axis=1) + x[1][1])
            return a + b

        gproj[:, pl.ds(pl.multiple_of(QW + i * 128, 128), 128)] = unrotate(join(gk) * factor).astype(BF)
        gproj[:, pl.ds(pl.multiple_of(QW + KW + i * 128, 128), 128)] = join(gv).astype(BF)

        if C > 2:
            @pl.when(i == 1)
            def _():
                for line in o_lines:
                    line.step(2)


    def o_merge(i):
        for cube in o_cubes:
            cube.merge(i, vadd)
            if i + 1 < m:
                cube.down(i + 1).start()

    @pl.loop(0, T // TR)
    def _(i):
        at = pl.ds(pl.multiple_of(i * TR, TR), TR)
        x = tok[at, :].astype(F32)
        r1 = lax.rsqrt(jnp.mean(x * x, -1, keepdims=True) + EPSILON)
        attn[at, :] = (x * r1 * gain_one).astype(BF)

    @pl.loop(0, D // 256)
    def _(i):
        at = pl.ds(pl.multiple_of(i * 256, 256), 256)
        for n in range(0, QV, 512):
            wg[at, n:n + 512] = dot_tn(attn[:, at], gproj[:, n:n + 512]).astype(BF)
    for line in q_lines:
        line.start_sib()
    for s in range(3, C):
        for line in o_lines:
            line.step(s)
    for line in q_lines:
        line.step(1)
    run(steps1)
    run(steps2)
    if split:
        o_merge(0)
    wq.wait()

    @pl.loop(0, D // 256)
    def _(i):
        at = pl.ds(pl.multiple_of(i * 256, 256), 256)
        ga[:, at] = dot_nt(gproj[...], wb[at, :])

    @pl.loop(0, T // TR)
    def _(i):
        at = pl.ds(pl.multiple_of(i * TR, TR), TR)
        x = tok[at, :].astype(F32)
        r1 = lax.rsqrt(jnp.mean(x * x, -1, keepdims=True) + EPSILON)
        n1 = x * r1
        gat = ga[at, :]
        sms[E:E + 1, :] += jnp.sum(gat * n1, 0, keepdims=True)
        g1 = gat * gain_one
        gt_o[at, :] = (gh[at, :] + r1 * (g1 - n1 * jnp.mean(g1 * n1, -1, keepdims=True))).astype(BF)

    small = sms[...]
    for i in range(nf):
        smg[i] = small[:, i * R:(i + 1) * R]
    sm_copies = []
    for i in range(1, nf):
        to = lax.rem(f + i, nf)
        cp = remote(smg.at[to], smr.at[f], s_sm.at[i - 1], r_sm.at[i - 1], to, d)
        cp.start()
        sm_copies.append(cp)
    smr_own = pltpu.make_async_copy(smg.at[f], smr.at[f], s_load.at[0])
    smr_own.start()

    for line in o_lines:
        line.last()
    late = []
    width = QV if split else W
    for h in range(2):
        top = h * (R // 2)
        own = wg.at[pl.ds(pl.multiple_of(f * R + top, 16), R // 2), 0:width]
        cube = Cube(nd, f, d, h == 1, True, width, own, functools.partial(lambda h, i: shl[i].at[h], h),
                    None, sh_o.at[top:top + R // 2, 0:width], (s_sc.at[3 + h], r_sc.at[3 + h]))
        cube.in_place = True
        late.append(cube)
    steps_l = chain(late, 0, vadd)
    run(steps1)
    run(steps2)
    if C > 2:
        for line in q_lines:
            line.step(2)
    if split:
        for i in range(1, m):
            o_merge(i)
        o_line.step(1)
    if split:
        if C > 2:
            o_line.step(2)
        pair.sent()
    for line in o_lines:
        line.sent()
    smr_own.wait()
    for cp in sm_copies:
        cp.wait()
    total = smr[0]
    for i in range(1, nf):
        total = total + smr[i]
    smd[0] = total
    sd_copies = []
    for i in range(1, nd):
        cp = remote(smd.at[0], smd.at[i], s_sd.at[i - 1], r_sd.at[i - 1], f, jnp.bitwise_xor(d, i))
        cp.start()
        sd_copies.append(cp)
    for s in range(3, C):
        for line in q_lines:
            line.step(s)
    if not split and C > 2:
        out_line.step(2)
    run(steps1, len(steps1))
    run(steps2, len(steps2))
    if split:
        for s in range(3, C):
            o_line.step(s)
        o_line.last()
        add_blocks(sh_o.at[:, pl.ds(pl.multiple_of(QV + o_up.low[m], 128), D >> m)], [o_block(c)])
        o_up.up(m - 1).start()
    for line in q_lines:
        line.last()
    for cube in late:
        cube.down(0).start()
    for s in range(3, C):
        out_line.step(s)
    if split:
        for i in range(m - 1, 0, -1):
            o_up.up_in(i).wait_recv()
            o_up.up(i - 1).start()
    run(steps_l, len(steps_l))
    for cp in sd_copies:
        cp.wait()
    total = smd[0]
    for i in range(1, nd):
        total = total + smd[i]
    sm_o[...] = total
    out_line.last()

    @pl.loop(0, T // TR)
    def _(i):
        at = pl.ds(pl.multiple_of(i * TR, TR), TR)
        out_o[at, :] = (hid[at, :] + acc[c, at, :].astype(F32)).astype(BF)


    for line in q_lines:
        line.sent()
    out_line.sent()
    for i, cube in enumerate(cubes):
        cube.up_in(0).wait_recv()
        cube.sent(1 - i % 2)
    if split:
        o_up.up_in(0).wait_recv()
        o_line.sent()
        for i in range(m):
            o_up.up(i).wait_send()
            for cube in o_cubes:
                cube.down(i).wait_send()
    for cube in late:
        cube.up_in(0).wait_recv()
        cube.sent()


def back(nf, nd, el, args):
    gin, t1, t2 = args[0], args[3], args[4]
    T, D = gin.shape
    E = args[10].shape[0]
    W = args[15].shape[1]
    R = D // nf
    C = nf // 2
    m = nd.bit_length() - 1
    QV = QW + 2 * KW
    FFW = t2.shape[1]
    SR = E + 2 + (-(E + 2) % 8)
    land_hbm = C > 4
    s = jax.ShapeDtypeStruct
    out_shape = [s((T, D), BF), s((T, D), BF), s((R, W), BF), s((SR, R), F32), s(t1.shape, BF), s(t2.shape, BF)]
    out_specs = [vm(), vm(), vm(), vm(), hbm(), hbm()]
    extra = [(el, D >> (i + 1), t1.shape[2]) for i in range(1, m)] + [(el, FFW >> (i + 1), D) for i in range(m)]
    extra += [(el, D >> (i + 1), t1.shape[2]) for i in range(m - 1)] + [(el, FFW >> (i + 1), D) for i in range(m - 1)]
    extra += [(C, T, D), (2, C - 1, T, D)]
    split = not land_hbm and (D >> m) % 128 == 0 and (QV >> m) % 128 == 0
    lands = [(C, R, D), (2, C - 1, R, D >> m if split else D), (C, R, QV), (2, C - 1, R, QV)]
    scratch = []
    if land_hbm:
        extra += lands
    else:
        scratch += [VMEM(x, BF) for x in lands]
    out_shape += [s(x, BF) for x in extra]
    out_specs += [hbm()] * len(extra)
    dma = pltpu.SemaphoreType.DMA
    scratch += [
        VMEM((C, T, D), BF), VMEM((D, QV), BF), VMEM((D, W), BF),
        VMEM((T, D), BF), VMEM((T, D), BF), VMEM((T, D), F32), VMEM((T, D), BF), VMEM((T, QW), BF),
        VMEM((T, QW + KW), BF), VMEM((T, KW), BF), VMEM((2, 2 * GROUP, T, T), BF),
        VMEM((T, D), BF), VMEM((T, D), F32), VMEM((T, D), F32), VMEM((T, QV), BF),
        VMEM((nf, el, T), F32), VMEM((nf, SR, R), F32), VMEM((nf, SR, R), F32), VMEM((nd, SR, R), F32),
        VMEM((SR, D), F32),
    ]
    scratch += [VMEM((2, R // 2, (QV if split else W) >> (i + 1)), BF) for i in range(m)]
    if split:
        scratch += [VMEM((C * R, D), BF)] + [VMEM((2, C * R // 2, D >> (i + 1)), BF) for i in range(m)]
    scratch += [VMEM((T, D), BF), VMEM((R, QV) if land_hbm else (16, 128), BF)]
    scratch += [
        dma((10,)), dma((C,)), dma((nf,)), dma((nf,)),
        dma((5, C)), dma((5, C)), dma((5, 2, C)), dma((5, 2, C)),
        dma((2 * el, 2 * m)), dma((2 * el, 2 * m)), dma((5, 2 * m)), dma((5, 2 * m)),
        dma((nf,)), dma((nf,)), dma((nd,)), dma((nd,)), dma(()), dma((2,)),
    ]
    inner = [vm(), hbm(), vm(), hbm(), hbm(), hbm(), hbm(), hbm(), hbm(), hbm(), vm(), hbm(), hbm(), hbm(), hbm(), hbm(), vm(),
             vm(), vm()]
    return pl.pallas_call(
        functools.partial(back_kernel, nf, nd, el, land_hbm, split),
        out_shape=out_shape,
        in_specs=inner,
        out_specs=out_specs,
        scratch_shapes=scratch,
        compiler_params=pltpu.CompilerParams(collective_id=3, has_side_effects=True,
                                             vmem_limit_bytes=63 * 2 ** 20),
        cost_estimate=pl.CostEstimate(flops=8_000_000_000, bytes_accessed=90_000_000, transcendentals=100_000),
        name="back",
    )(*args)[:6]


def body(tokens, w_query, key_weight, value_weight, w_out, gain_attn, gain_ffn, w_router,
         w_gate, w_up, w_down, routes, cotangent):
    T = tokens.shape[0]
    el = w_gate.shape[0]
    nf = lax.axis_size("fsdp")
    nd = lax.axis_size("dp")
    experts = el * nf
    cap = 9 * T * TOP // (8 * experts)

    pad = -(experts + 2) % 16
    small = jnp.concatenate([w_router, gain_attn[:, None], gain_ffn[:, None],
                             jnp.zeros((w_router.shape[0], pad), BF)], 1).T
    onehot = (routes[:, :, None] == jnp.arange(experts, dtype=jnp.int32)).any(1).astype(BF)
    earlier = (jnp.arange(T)[:, None] < jnp.arange(T)[None, :]).astype(BF)
    before = lax.dot_general(onehot, earlier, (((0,), (0,)), ((), ())), preferred_element_type=F32)
    slots = jnp.where(onehot.T > 0, before, -1.0)
    cosr, sinr = rope_rows(T)
    ffn_in, hidden, gates, mixed, qk, v, probs, full, cot_all, rt = front(
        nf, nd, experts, tokens, (w_query, key_weight, value_weight, w_out), small, cotangent, slots, cosr, sinr)
    side = jnp.concatenate([slots.reshape(nf, el, T), gates.reshape(nf, el, T)], 1)
    out_part, gin, gp_part, t1, t2, f1 = experts_call(nf, nd, cap, ffn_in, cot_all, side, w_gate, w_up, w_down)
    output, grad_tokens, shard, smalls, t1, t2 = back(nf, nd, el, (
        gin, out_part, gp_part, t1, t2, f1, tokens, cotangent, hidden, ffn_in, gates, mixed, qk, v, probs, full, rt,
        cosr, sinr))
    big = shard.astype(F32)
    ff = w_gate.shape[2]
    return (
        output,
        grad_tokens,
        big[:, :QW],
        big[:, QW: QW + KW],
        big[:, QW + KW: QW + 2 * KW],
        big[:, QW + 2 * KW:],
        smalls[experts],
        smalls[experts + 1],
        smalls[:experts].T,
        t1[:, :, :ff].astype(F32),
        t1[:, :, ff:].astype(F32),
        t2.astype(F32),
    )


def solution(mesh):
    in_specs = (
        P(("fsdp", "dp"), None),
        P("fsdp", None),
        P("fsdp", None),
        P("fsdp", None),
        P("fsdp", None),
        P("fsdp"),
        P("fsdp"),
        P("fsdp", None),
        P("fsdp", None, None),
        P("fsdp", None, None),
        P("fsdp", None, None),
        P(("fsdp", "dp"), None),
        P(("fsdp", "dp"), None),
    )
    out_specs = (
        P(("fsdp", "dp"), None),
        P(("fsdp", "dp"), None),
        P("fsdp", None),
        P("fsdp", None),
        P("fsdp", None),
        P("fsdp", None),
        P("fsdp"),
        P("fsdp"),
        P("fsdp", None),
        P("fsdp", None, None),
        P("fsdp", None, None),
        P("fsdp", None, None),
    )
    return jax.shard_map(body, mesh=mesh, in_specs=in_specs, out_specs=out_specs, check_vma=False)
```

```python
import functools
import jax
import jax.numpy as jnp
from jax import lax
from jax.experimental import pallas as pl
from jax.experimental.pallas import tpu as pltpu
from jax.sharding import PartitionSpec as P
import numpy as np

MODEL_WIDTH = 1536
QUERY_HEADS = 24
KEY_VALUE_HEADS = 8
HEAD_SIZE = 64
TOP = 8
GROUP = QUERY_HEADS // KEY_VALUE_HEADS
QW = QUERY_HEADS * HEAD_SIZE
KW = KEY_VALUE_HEADS * HEAD_SIZE

EPSILON = 1e-06
ROPE_BASE = 10000.0
MASKED = -1e30
F32 = jnp.float32
BF = jnp.bfloat16


def rope_rows(T):
    half = HEAD_SIZE // 2
    freq = ROPE_BASE ** (-2.0 * np.arange(half, dtype=np.float64) / HEAD_SIZE)
    ang = (np.arange(T, dtype=np.float32)[:, None] * freq.astype(np.float32)[None, :]).astype(np.float32)
    c, s = np.cos(ang), np.sin(ang)
    return (jnp.asarray(np.concatenate([c, c, c, c], 1), F32), jnp.asarray(np.concatenate([-s, s, -s, s], 1), F32))


MESH = pl.DeviceIdType.MESH
VMEM = pltpu.VMEM


def vm():
    return pl.BlockSpec(memory_space=pltpu.VMEM)


def hbm():
    return pl.BlockSpec(memory_space=pl.ANY)


def dot(a, b):
    return lax.dot_general(a, b, (((1,), (0,)), ((), ())), preferred_element_type=F32)


def dot_nt(a, b):
    return lax.dot_general(a, b, (((1,), (1,)), ((), ())), preferred_element_type=F32)


def dot_tn(a, b):
    return lax.dot_general(a, b, (((0,), (0,)), ((), ())), preferred_element_type=F32)


def half_roll(x, first):
    n = x.shape[1]
    h = HEAD_SIZE // 2
    return jnp.where(first, pltpu.roll(x, n - h, axis=1), pltpu.roll(x, h, axis=1))


def greet(nf, nd, f, d):
    barrier = pltpu.get_barrier_semaphore()
    for i in range(1, nf):
        pl.semaphore_signal(barrier, inc=1, device_id=(lax.rem(f + i, nf), d), device_id_type=MESH)
    for i in range(1, nd):
        pl.semaphore_signal(barrier, inc=1, device_id=(f, jnp.bitwise_xor(d, i)), device_id_type=MESH)
    pl.semaphore_wait(barrier, nf + nd - 2)


def head_masks(kblk, lane):
    kf = kblk.astype(F32)
    kr = pltpu.roll(kf, HEAD_SIZE, axis=1)
    low = lane < HEAD_SIZE
    zero = jnp.zeros_like(kf)
    a0 = jnp.where(low, kf, zero).astype(BF)
    a1 = jnp.where(low, zero, kr).astype(BF)
    b0 = jnp.where(low, kr, zero).astype(BF)
    b1 = jnp.where(low, zero, kf).astype(BF)
    return ((a0, a1), (b0, b1))


def front_kernel(nf, nd, experts, tok, wq, wk, wv, wo, small, cot, slots, cosr, sinr,
                 ffn_o, hid_o, gates_o, mix_o, qk_o, v_o, prob_o, wf_o, cot_o, rt_o,
                 wf, sm, attn, rot,
                 s_sm, r_sm, s_z, r_z, s_dp, r_dp, s_sib, r_sib, s_cz, r_cz, s_cs, r_cs, s_loc, s_w):
    T, D = tok.shape
    C = nf // 2
    R = wq.shape[0]
    W = wf.shape[1]
    WA = 3 * W // 4
    parts = ((0, WA), (WA, W - WA))
    f = lax.axis_index("fsdp")
    d = lax.axis_index("dp")
    c = f // 2
    k = lax.rem(f, 2)
    sib = f + 1 - 2 * k
    greet(nf, nd, f, d)

    def rows(ff):
        return pl.ds(pl.multiple_of(ff * R, 16), R)

    def cols(dd, g):
        at, n = parts[g]
        return pl.ds(pl.multiple_of(at + dd * (n // nd), 128), n // nd)

    def remote(src, dst, ss, rs, to_f, to_d):
        return pltpu.make_async_remote_copy(src_ref=src, dst_ref=dst, send_sem=ss, recv_sem=rs,
                                            device_id=(to_f, to_d), device_id_type=MESH)

    def src_chip(dr, s):
        return c - s if dr == 0 else c + s

    def has(dr, s):
        return (c - s >= 0) if dr == 0 else (c + s < C)

    def nxt_ok(dr):
        return (c + 1 < C) if dr == 0 else (c - 1 >= 0)

    def nxt_f(dr):
        return f + 2 if dr == 0 else f - 2

    def wz(dr, s, g):
        blk = wf.at[rows(2 * src_chip(dr, s - 1) + k), cols(d, g)]
        return remote(blk, blk, s_z.at[g, dr, s - 1], r_z.at[g, dr, s - 1], nxt_f(dr), d)

    def wz_in(dr, s, g):
        blk = wf.at[rows(2 * src_chip(dr, s) + k), cols(d, g)]
        return remote(blk, blk, s_z.at[g, dr, s - 1], r_z.at[g, dr, s - 1], f, d)

    halves = (slice(0, D // 2), slice(D // 2, D))

    def cz(dr, s, own, h):
        ff = 2 * src_chip(dr, s - 1) + k
        src = cot.at[:, halves[h]] if own else cot_o.at[ff, :, halves[h]]
        return remote(src, cot_o.at[ff, :, halves[h]], s_cz.at[h, dr, s - 1], r_cz.at[h, dr, s - 1], nxt_f(dr), d)

    def cz_in(dr, s, h):
        blk = cot_o.at[2 * src_chip(dr, s) + k, :, halves[h]]
        return remote(blk, blk, s_cz.at[h, dr, s - 1], r_cz.at[h, dr, s - 1], f, d)

    def cs(dr, s):
        ff = 2 * src_chip(dr, s) + k
        return remote(cot_o.at[ff], cot_o.at[ff], s_cs.at[dr, s], r_cs.at[dr, s], sib, d)

    def cs_in(dr, s):
        ff = 2 * src_chip(dr, s) + 1 - k
        return remote(cot_o.at[ff], cot_o.at[ff], s_cs.at[dr, s], r_cs.at[dr, s], sib, d)

    at = 0
    w_own = []
    for i, w in enumerate((wq, wk, wv, wo)):
        w_own.append(pltpu.make_async_copy(w, wf.at[rows(f), at:at + w.shape[1]], s_w.at[i]))
        at += w.shape[1]
    for cp in w_own:
        cp.start()
    for cp in w_own:
        cp.wait()
    for g in range(2):
        for dr in range(2):
            @pl.when(nxt_ok(dr))
            def _():
                wz(dr, 1, g).start()
    own_small = pltpu.make_async_copy(small, sm.at[f], s_loc.at[0])
    own_small.start()
    sm_copies = []
    for i in range(1, nf):
        cp = remote(small, sm.at[f], s_sm.at[i - 1], r_sm.at[i - 1], lax.rem(f + i, nf), d)
        cp.start()
        sm_copies.append(cp)
    for dr in range(2):
        @pl.when((c if dr == 0 else C - 1 - c) == 0)
        def _():
            for h in range(2):
                cz(dr, 1, True, h).start()
    sib_own = remote(wf.at[rows(f)], wf.at[rows(f)], s_sib.at[0, 0, 0], r_sib.at[0, 0, 0], sib, d)
    sib_own.start()
    own_c = pltpu.make_async_copy(cot, cot_o.at[f], s_loc.at[2])
    own_c.start()
    sib_c = remote(cot, cot_o.at[f], s_cs.at[0, 0], r_cs.at[0, 0], sib, d)

    def dp_copy(dr, s, g, i):
        blk = wf.at[rows(2 * src_chip(dr, s) + k), cols(d, g)]
        return remote(blk, blk, s_dp.at[g, dr, s - 1, i - 1], r_dp.at[g, dr, s - 1, i - 1], f, jnp.bitwise_xor(d, i))

    def dp_in(dr, s, g, i):
        blk = wf.at[rows(2 * src_chip(dr, s) + k), cols(jnp.bitwise_xor(d, i), g)]
        return remote(blk, blk, s_dp.at[g, dr, s - 1, i - 1], r_dp.at[g, dr, s - 1, i - 1], f, d)

    def sib_copy(dr, s, g):
        at, n = parts[g]
        blk = wf.at[rows(2 * src_chip(dr, s) + k), at:at + n]
        return remote(blk, blk, s_sib.at[g, dr, s], r_sib.at[g, dr, s], sib, d)

    def sib_in(dr, s, g):
        at, n = parts[g]
        blk = wf.at[rows(2 * src_chip(dr, s) + 1 - k), at:at + n]
        return remote(blk, blk, s_sib.at[g, dr, s], r_sib.at[g, dr, s], sib, d)

    for s in range(1, C):
        for g in range(2):
            for dr in range(2):
                @pl.when(has(dr, s))
                def _():
                    wz_in(dr, s, g).wait_recv()
                    if s < C - 1:
                        @pl.when(nxt_ok(dr))
                        def _():
                            wz(dr, s + 1, g).start()
                    if g == 0:
                        for i in range(1, nd):
                            dp_copy(dr, s, g, i).start()
        for dr in range(2):
            @pl.when(nxt_ok(dr) & ((c if dr == 0 else C - 1 - c) == s))
            def _():
                for h in range(2):
                    cz(dr, 1, True, h).start()
    sib_c.start()
    for s in range(1, C):
        for dr in range(2):
            @pl.when(has(dr, s))
            def _():
                for i in range(1, nd):
                    dp_copy(dr, s, 1, i).start()

    def group_in(s, g):
        for dr in range(2):
            @pl.when(has(dr, s))
            def _():
                for i in range(1, nd):
                    dp_in(dr, s, g, i).wait_recv()
                sib_copy(dr, s, g).start()

    def cores_in(g):
        for s in range(1, C):
            for dr in range(2):
                @pl.when(has(dr, s))
                def _():
                    sib_in(dr, s, g).wait_recv()

    own_small.wait()
    for cp in sm_copies:
        cp.wait()
    Ds = small.shape[1]
    rt = jnp.concatenate([sm[i] for i in range(nf)], axis=1)
    rt_o[...] = rt
    gains = rt[experts:experts + 2].astype(F32)
    gain_one, gain_two = gains[0:1], gains[1:2]
    xf = tok[...].astype(F32)
    r1 = lax.rsqrt(jnp.mean(xf * xf, -1, keepdims=True) + EPSILON)
    attn[...] = (xf * r1 * gain_one).astype(BF)

    def cot_step(s):
        for dr in range(2):
            @pl.when(has(dr, s))
            def _():
                for h in range(2):
                    cz_in(dr, s, h).wait_recv()
                    if s < C - 1:
                        @pl.when(nxt_ok(dr))
                        def _():
                            cz(dr, s + 1, False, h).start()
                cs(dr, s).start()

    cot_step(1)
    for s in range(1, C - 1):
        group_in(s, 0)
    group_in(C - 1, 0)
    sib_own.wait()
    cores_in(0)

    first = lax.rem(lax.broadcasted_iota(jnp.int32, (T, 256), 1), HEAD_SIZE) < HEAD_SIZE // 2
    cs_t = jnp.concatenate([cosr[...], cosr[...]], 1)
    sn_t = jnp.concatenate([sinr[...], sinr[...]], 1)
    nqk = (QW + KW) // 256

    @pl.loop(0, nqk)
    def _(i):
        col = pl.ds(pl.multiple_of(i * 256, 256), 256)
        x = dot(attn[...], wf[:, col])
        qk_o[:, col] = (x * cs_t + half_roll(x, first) * sn_t).astype(BF)

    @pl.loop(0, KW // 256)
    def _(i):
        col = pl.ds(pl.multiple_of(QW + KW + i * 256, 256), 256)
        v_o[:, pl.ds(pl.multiple_of(i * 256, 256), 256)] = dot(attn[...], wf[:, col]).astype(BF)

    factor = HEAD_SIZE ** (-0.5)
    lane = lax.broadcasted_iota(jnp.int32, (T, 128), 1)
    keep = lax.broadcasted_iota(jnp.int32, (T, T), 1) <= lax.broadcasted_iota(jnp.int32, (T, T), 0)

    @pl.loop(0, KEY_VALUE_HEADS // 2)
    def _(i):
        if C > 2:
            @pl.when(i == 2)
            def _():
                cot_step(2)
        kc = pl.ds(pl.multiple_of(QW + i * 128, 128), 128)
        kh = head_masks(qk_o[:, kc], lane)
        vh = head_masks(v_o[:, pl.ds(pl.multiple_of(i * 128, 128), 128)], lane)
        for p in range(GROUP):
            qc = pl.ds(pl.multiple_of((i * GROUP + p) * 128, 128), 128)
            q = qk_o[:, qc]
            acc = None
            for half in range(2):
                g = (2 * p + half) // GROUP
                sc = dot_nt(q, kh[g][half]) * factor
                sc = jnp.where(keep, sc, MASKED)
                ex = jnp.exp(sc - jnp.max(sc, -1, keepdims=True))
                pr = (ex / jnp.sum(ex, -1, keepdims=True)).astype(BF)
                prob_o[i * 2 * GROUP + 2 * p + half] = pr
                term = dot(pr, vh[g][half])
                acc = term if acc is None else acc + term
            mix_o[:, qc] = acc.astype(BF)

    for s in range(1, C):
        group_in(s, 1)
    cores_in(1)
    out_w = pltpu.make_async_copy(wf, wf_o, s_loc.at[3])
    out_w.start()

    @pl.loop(0, D // 256)
    def _(i):
        col = pl.ds(pl.multiple_of(i * 256, 256), 256)
        wc = pl.ds(pl.multiple_of(QW + 2 * KW + i * 256, 256), 256)
        hid_o[:, col] = tok[:, col].astype(F32) + dot(mix_o[...], wf[:, wc])

    hidden = hid_o[...]
    r2 = lax.rsqrt(jnp.mean(hidden * hidden, -1, keepdims=True) + EPSILON)
    ffn_o[...] = (hidden * r2 * gain_two).astype(BF)
    logits = dot_nt(rt_o[...], ffn_o[...])[0:experts]
    named = slots[...] >= 0.0
    logits = jnp.where(named, logits, MASKED)
    ex = jnp.where(named, jnp.exp(logits - jnp.max(logits, 0, keepdims=True)), 0.0)
    gates_o[...] = ex / jnp.sum(ex, 0, keepdims=True)

    for s in range(3, C):
        cot_step(s)
    own_c.wait()
    sib_c.wait()
    out_w.wait()
    for dr in range(2):
        for s in range(1, C):
            @pl.when(has(dr, s))
            def _():
                cs_in(dr, s).wait_recv()
                cs(dr, s).wait_send()
                for g in range(2):
                    sib_copy(dr, s, g).wait_send()
                    for i in range(1, nd):
                        dp_copy(dr, s, g, i).wait_send()

            @pl.when(nxt_ok(dr) & (has(dr, s - 1) if s > 1 else True))
            def _():
                for g in range(2):
                    wz(dr, s, g).wait_send()
                for h in range(2):
                    cz(dr, s, s == 1, h).wait_send()


def front(nf, nd, experts, tok, ws, small, cot, slots, cosr, sinr):
    T, D = tok.shape
    C = nf // 2
    W = sum(w.shape[1] for w in ws)
    out = [
        (T, D, BF, 0), (T, D, F32, 0), (experts, T, F32, 0), (T, QW, BF, 0), (T, QW + KW, BF, 0),
        (T, KW, BF, 0), (QUERY_HEADS, T, T, BF, 0), (D, W, BF, 1), (nf, T, D, BF, 1),
        (small.shape[0], D, BF, 0),
    ]
    dma = pltpu.SemaphoreType.DMA
    return pl.pallas_call(
        functools.partial(front_kernel, nf, nd, experts),
        out_shape=[jax.ShapeDtypeStruct(o[:-2], o[-2]) for o in out],
        in_specs=[vm()] + [hbm()] * 4 + [vm()] * 5,
        out_specs=[hbm() if o[-1] else vm() for o in out],
        scratch_shapes=[
            VMEM((D, W), BF),
            VMEM((nf,) + small.shape, BF),
            VMEM((T, D), BF),
            VMEM((8, 128), F32),
            dma((nf,)), dma((nf,)),
            dma((2, 2, C)), dma((2, 2, C)),
            dma((2, 2, C, nd)), dma((2, 2, C, nd)),
            dma((2, 2, C)), dma((2, 2, C)),
            dma((2, 2, C)), dma((2, 2, C)),
            dma((2, C)), dma((2, C)),
            dma((4,)), dma((4,)),
        ],
        compiler_params=pltpu.CompilerParams(collective_id=1, has_side_effects=True,
                                             vmem_limit_bytes=60 * 2 ** 20),
        cost_estimate=pl.CostEstimate(flops=4_000_000_000, bytes_accessed=60_000_000, transcendentals=2_000_000),
        name="front",
    )(tok, *ws, small, cot, slots, cosr, sinr)


def add_blocks(dst, srcs, extra=None):
    @pl.loop(0, dst.shape[0] // 16)
    def _(i):
        at = pl.ds(pl.multiple_of(i * 16, 16), 16)
        total = srcs[0][at, :].astype(F32)
        for s in srcs[1:]:
            total = total + s[at, :].astype(F32)
        dst[at, :] = total.astype(dst.dtype)


class Line:
    def __init__(self, nf, f, d, acc, give, sib, rcv, stage, sems, stage_sem):
        self.nf, self.f, self.d = nf, f, d
        self.C = nf // 2
        self.c, self.k = f // 2, lax.rem(f, 2)
        self.acc, self.give, self.sib, self.rcv, self.stage = acc, give, sib, rcv, stage
        self.s_sib, self.r_sib, self.s_z, self.r_z = sems
        self.stage_sem = stage_sem

    def remote(self, src, dst, ss, rs, to):
        return pltpu.make_async_remote_copy(src_ref=src, dst_ref=dst, send_sem=ss, recv_sem=rs,
                                            device_id=(to, self.d), device_id_type=MESH)

    def dest(self, dr, s):
        i = s - 1 - (self.C - 1 - self.c) if dr == 0 else s - 1 - self.c
        room = self.c if dr == 0 else self.C - 1 - self.c
        chip = i if dr == 0 else self.C - 1 - i
        return jnp.clip(chip, 0, self.C - 1), (i >= 0) & (i < room)

    def sib_copy(self, chip):
        return self.remote(self.give(chip), self.sib(chip), self.s_sib.at[chip], self.r_sib.at[chip],
                           self.f + 1 - 2 * self.k)

    def z_copy(self, dr, s, chip):
        return self.remote(self.acc(chip), self.rcv(dr, s - 1), self.s_z.at[dr, s - 1], self.r_z.at[dr, s - 1],
                           self.f - 2 if dr == 0 else self.f + 2)

    def z_in(self, dr, s):
        return self.remote(self.rcv(dr, s - 1), self.rcv(dr, s - 1), self.s_z.at[dr, s - 1], self.r_z.at[dr, s - 1],
                           self.f)

    def start_sib(self):
        for s in range(1, self.C):
            for dr in range(2):
                chip, ok = self.dest(dr, s)

                @pl.when(ok)
                def _():
                    self.sib_copy(chip).start()
        self.sib_copy(self.c).start()

    def gather(self, chip, srcs):
        acc = self.acc(chip)
        if self.stage is None:
            add_blocks(acc, [acc] + srcs)
            return
        for s in srcs:
            cp = pltpu.make_async_copy(s, self.stage, self.stage_sem)
            cp.start()
            cp.wait()
            add_blocks(acc, [acc, self.stage])

    def step(self, s):
        for dr in range(2):
            chip, ok = self.dest(dr, s)
            begins = (self.c == self.C - 1) if dr == 0 else (self.c == 0)

            @pl.when(ok)
            def _():
                other = []
                if self.sib is not None:
                    self.sib_copy(chip).wait_recv()
                    other = [self.sib(chip)]

                    @pl.when(begins)
                    def _():
                        self.gather(chip, other)
                if s > 1:
                    @pl.when(jnp.logical_not(begins))
                    def _():
                        self.z_in(dr, s - 1).wait_recv()
                        self.gather(chip, other + [self.rcv(dr, s - 2)])
                self.z_copy(dr, s, chip).start()

    def last(self):
        other = []
        if self.sib is not None:
            self.sib_copy(self.c).wait_recv()
            other = [self.sib(self.c)]
        mid = (self.c > 0) & (self.c < self.C - 1)
        s = self.C - 1
        for dr in range(2):
            @pl.when((self.c < self.C - 1) if dr == 0 else (self.c > 0))
            def _():
                self.z_in(dr, s).wait_recv()

        @pl.when(mid)
        def _():
            self.gather(self.c, other + [self.rcv(0, s - 1), self.rcv(1, s - 1)])

        @pl.when(self.c == 0)
        def _():
            self.gather(self.c, other + [self.rcv(0, s - 1)])

        @pl.when(self.c == self.C - 1)
        def _():
            self.gather(self.c, other + [self.rcv(1, s - 1)])

    def sent(self):
        if self.acc is None:
            for chip in range(self.C):
                self.sib_copy(chip).wait_send()
            return
        if self.sib is not None:
            self.sib_copy(self.c).wait_send()
        for s in range(1, self.C):
            for dr in range(2):
                chip, ok = self.dest(dr, s)

                @pl.when(ok)
                def _():
                    if self.sib is not None:
                        self.sib_copy(chip).wait_send()
                    self.z_copy(dr, s, chip).wait_send()


class Cube:
    def __init__(self, nd, f, d, flip, lanes, size, own, land, total, out, sems):
        m = nd.bit_length() - 1
        order = [1 << b for b in range(m)]
        if isinstance(flip, bool):
            self.masks = order[::-1] if flip else order
        else:
            self.masks = [jnp.where(flip, b, a) for a, b in zip(order, order[::-1])]
        self.f, self.d, self.lanes = f, d, lanes
        self.own, self.land, self.total, self.out = own, land, total, out
        self.ss, self.rs = sems
        self.m = m
        self.in_place, self.whole = False, True
        self.low, self.length = [0], [size]
        for mask in self.masks:
            half = self.length[-1] // 2
            side = lax.rem(d // mask, 2)
            self.low.append(self.low[-1] + side * half)
            self.length.append(half)

    def cut(self, ref, at, n):
        if self.lanes:
            return ref.at[:, pl.ds(pl.multiple_of(at, 128), n)]
        return ref.at[pl.ds(pl.multiple_of(at, 16), n)]

    def remote(self, src, dst, i, mask):
        return pltpu.make_async_remote_copy(src_ref=src, dst_ref=dst, send_sem=self.ss.at[i], recv_sem=self.rs.at[i],
                                            device_id=(self.f, jnp.bitwise_xor(self.d, mask)),
                                            device_id_type=MESH)

    def level(self, i):
        if i == 0 or (self.in_place and (i < self.m or not self.whole)):
            return self.own, 0
        if i == self.m:
            return self.out, 0
        return self.total(i - 1), self.low[i]

    def down(self, i):
        ref, base = self.level(i)
        half = self.length[i + 1]
        other = 2 * self.low[i] + half - self.low[i + 1]
        return self.remote(self.cut(ref, other - base, half), self.land(i), i, self.masks[i])

    def merge(self, i, add):
        self.down(i).wait_recv()
        self.fold(i, add)

    def fold(self, i, add):
        ref, base = self.level(i)
        dst, dbase = self.level(i + 1)
        half = self.length[i + 1]
        low = self.low[i + 1]
        add(self.cut(dst, low - dbase, half), self.cut(ref, low - base, half), self.land(i))

    def up(self, i):
        blk = self.cut(self.out, self.low[i + 1], self.length[i + 1])
        return self.remote(blk, blk, self.m + i, self.masks[i])

    def up_in(self, i):
        half = self.length[i + 1]
        other = 2 * self.low[i] + half - self.low[i + 1]
        blk = self.cut(self.out, other, half)
        return self.remote(blk, blk, self.m + i, self.masks[i])

    def sent(self, first=0):
        for i in range(self.m):
            if i >= first:
                self.down(i).wait_send()
            self.up(i).wait_send()


def pipe_add(dst, a, b):
    n, w = dst.shape
    tile = next(t for t in (256, 192, 128, 64) if n % t == 0 and t * w <= 256 * 1024)
    spec = pl.BlockSpec((tile, w), lambda i: (i, 0))

    def inner(a_ref, b_ref, o_ref):
        o_ref[...] = (a_ref[...].astype(F32) + b_ref[...].astype(F32)).astype(o_ref.dtype)

    pltpu.emit_pipeline(inner, grid=(n // tile,), in_specs=[spec, spec], out_specs=[spec])(a, b, dst)

def visit(c, C, j):
    both = jnp.minimum(c, C - 1 - c)
    near = j <= 2 * both
    dist = jnp.where(near, (j + 1) // 2, j - both)
    down = jnp.where(near, lax.rem(j, 2) == 0, c < C - 1 - c)
    chip = jnp.where(down, c + dist, c - dist)
    return chip, jnp.where(down, 1, 0), dist


def term_cubes(nd, el, f, d, t1, t2, out1, out2, l1, l2, a1, a2, sems):
    cubes = []
    for e in range(el):
        for j, (src, out, ls, ts) in enumerate(((t1, out1, l1, a1), (t2, out2, l2, a2))):
            pick = functools.partial(lambda refs, e, i: refs[i].at[e], ls, e)
            tot = functools.partial(lambda refs, e, i: refs[i].at[e], ts, e)
            cubes.append(Cube(nd, f, d, (e + j) % 2 == 1, False, src.shape[1], src.at[e], pick, tot,
                              None if out is None else out.at[e], (sems[0].at[2 * e + j], sems[1].at[2 * e + j])))
    return cubes


def experts_kernel(nf, nd, el, cap, capp, land_hbm, ffn, cot_a, side, wg_h, wu_h, wd_h,
                   out_o, gin_o, gp_o, t1_o, t2_o, l1, sib_l, rcv_l, acc,
                   wg, wu, wd, fa, sd, cotb, xs, gs, hs, hgs, orb, irb, st_o, give, st1, st2, stage, us,
                   s_sd, r_sd, s_z, r_z, s_sib, r_sib, s_w, s_loc, s_t, s_ls, r_ls, s_lz, r_lz, s_st, s_cube, r_cube):
    T, D = ffn.shape
    FFW = wg.shape[2]
    C = nf // 2
    B = 2 * capp
    f = lax.axis_index("fsdp")
    d = lax.axis_index("dp")
    c = f // 2
    k = lax.rem(f, 2)
    sib = f + 1 - 2 * k
    greet(nf, nd, f, d)

    def remote(src, dst, ss, rs, to_f):
        return pltpu.make_async_remote_copy(src_ref=src, dst_ref=dst, send_sem=ss, recv_sem=rs,
                                            device_id=(to_f, d), device_id_type=MESH)

    def chip_at(dr, s):
        return jnp.where(dr == 0, c - s, c + s)

    def has(dr, s):
        at = chip_at(dr, s)
        return (at >= 0) & (at < C)

    def nxt_ok(dr):
        return (c + 1 < C) if dr == 0 else (c - 1 >= 0)

    def nxt_f(dr):
        return f + 2 if dr == 0 else f - 2

    halves = (slice(0, D // 2), slice(D // 2, D))

    def z_out(dr, s, h):
        blk = fa.at[2 * chip_at(dr, s - 1) + k, :, halves[h]]
        return remote(blk, blk, s_z.at[h, dr, s - 1], r_z.at[h, dr, s - 1], nxt_f(dr))

    def z_own(dr, h):
        return remote(ffn.at[:, halves[h]], fa.at[f, :, halves[h]], s_z.at[h, dr, 0], r_z.at[h, dr, 0], nxt_f(dr))

    def z_in(dr, s, h):
        blk = fa.at[2 * chip_at(dr, s) + k, :, halves[h]]
        return remote(blk, blk, s_z.at[h, dr, s - 1], r_z.at[h, dr, s - 1], f)

    def sib_out(dr, s):
        ff = 2 * chip_at(dr, s) + k
        return remote(fa.at[ff], fa.at[ff], s_sib.at[dr, s], r_sib.at[dr, s], sib)

    def sib_in(dr, s):
        ff = 2 * chip_at(dr, s) + 1 - k
        return remote(fa.at[ff], fa.at[ff], s_sib.at[dr, s], r_sib.at[dr, s], f)

    lines = [Line(nf, f, d, lambda ch, cut=cut: acc.at[ch, :, cut], lambda ch, cut=cut: give.at[0, :, cut],
                  lambda ch, cut=cut: sib_l.at[ch, :, cut], lambda dr, s, cut=cut: rcv_l.at[dr, s, :, cut],
                  stage.at[:, cut] if land_hbm else None, (s_ls.at[h], r_ls.at[h], s_lz.at[h], r_lz.at[h]), s_st)
             for h, cut in enumerate(halves)]

    def handed(chip, slot, h):
        return remote(give.at[slot, :, halves[h]], sib_l.at[chip, :, halves[h]], s_ls.at[h, chip], r_ls.at[h, chip], sib)

    def reduce_step(s):
        for line in lines:
            line.step(s)

    for h in range(2):
        for dr in range(2):
            @pl.when(nxt_ok(dr))
            def _():
                z_own(dr, h).start()
    sib_own = remote(ffn, fa.at[f], s_sib.at[1, 0], r_sib.at[1, 0], sib)
    sib_own.start()
    own = pltpu.make_async_copy(ffn, fa.at[f], s_loc.at[0])
    own.start()
    own_sd = pltpu.make_async_copy(side.at[f], sd.at[f], s_loc.at[1])
    own_sd.start()
    sd_copies = []
    for i in range(1, nf):
        to = lax.rem(f + i, nf)
        cp = remote(side.at[to], sd.at[f], s_sd.at[i - 1], r_sd.at[i - 1], to)
        cp.start()
        sd_copies.append(cp)
    w_copies = []
    for i, (src, dst) in enumerate(((wg_h, wg), (wu_h, wu), (wd_h, wd))):
        cp = pltpu.make_async_copy(src, dst, s_w.at[i])
        cp.start()
        w_copies.append(cp)
    own.wait()
    own_sd.wait()
    for cp in sd_copies:
        cp.wait()
    for cp in w_copies:
        cp.wait()

    row_ids = lax.broadcasted_iota(jnp.int32, (capp, T), 0).astype(F32)

    @pl.loop(0, C)
    def _(j):
        b, dr_b, dist_b = visit(c, C, j)
        cot_cp = pltpu.make_async_copy(cot_a.at[pl.ds(2 * b, 2)], cotb, s_loc.at[2])
        cot_cp.start()

        base = pl.multiple_of(b * B, 16)
        gate_rows = [[None, None] for _ in range(el)]
        picks = []
        for kk in range(2):
            s = 2 * b + kk
            parts = []
            for e in range(el):
                hit = row_ids == sd[s, e:e + 1, :]
                gate_rows[e][kk] = jnp.sum(jnp.where(hit, sd[s, el + e:el + e + 1, :], 0.0), -1, keepdims=True)
                parts.append(jnp.where(hit, 1.0, 0.0).astype(BF))
            p2 = jnp.concatenate(parts, 0)
            picks.append(p2)
        cot_cp.wait()

        def spread(rows_of, dst):
            for kk in range(2):
                for n in range(0, D, 512):
                    val = dot(picks[kk], rows_of(kk, n)).astype(BF)
                    for e in range(el):
                        at = pl.ds(pl.multiple_of(base + kk * capp, 16), capp)
                        dst[e, at, n:n + 512] = val[e * capp:(e + 1) * capp]

        here = pl.ds(base, B)
        spread(lambda kk, n: cotb[kk, :, n:n + 512], gs)
        for e in range(el):
            for n in range(0, FFW, 256):
                us[e, :, n:n + 256] = dot_nt(gs[e, here, :], wd[e, n:n + 256, :])

        @pl.when(j >= 1)
        def _():
            for dr in range(2):
                @pl.when(has(dr, j))
                def _():
                    for h in range(2):
                        z_in(dr, j, h).wait_recv()

                        @pl.when(nxt_ok(dr) & (j < C - 1))
                        def _():
                            z_out(dr, j + 1, h).start()
                    sib_out(dr, j).start()
        sib_in(dr_b, dist_b).wait_recv()
        spread(lambda kk, n: fa[2 * b + kk, :, n:n + 512], xs)
        gp_rows = []
        for e in range(el):
            gate_row = jnp.concatenate(gate_rows[e], 0)
            gpr = jnp.zeros((B, 1), F32)
            for n in range(0, FFW, 256):
                gv = dot(xs[e, here, :], wg[e, :, n:n + 256])
                uv = dot(xs[e, here, :], wu[e, :, n:n + 256])
                u = us[e, :, n:n + 256]
                sg = 1.0 / (1.0 + jnp.exp(-gv))
                act = gv * sg
                hid = act * uv
                gpr = gpr + jnp.sum(hid * u, -1, keepdims=True)
                hgs[e, here, n:n + 256] = (hid * gate_row).astype(BF)
                gh = u * gate_row
                hs[e, here, n:n + 256] = (gh * uv * (sg * (1.0 + gv * (1.0 - sg)))).astype(BF)
                hs[e, here, FFW + n:FFW + n + 256] = (gh * act).astype(BF)
            gp_rows.append(gpr)
            for n in range(0, D, 512):
                irow = (dot_nt(hs[e, here, 0:FFW], wg[e, n:n + 512, :])
                        + dot_nt(hs[e, here, FFW:2 * FFW], wu[e, n:n + 512, :])).astype(BF)
                for kk in range(2):
                    irb[kk, e * capp:(e + 1) * capp, n:n + 512] = irow[kk * capp:(kk + 1) * capp]

        @pl.when(j >= 2)
        def _():
            before, _, _ = visit(c, C, j - 2)
            for h in range(2):
                handed(before, lax.rem(j, 2), h).wait_send()
        for h in range(2):
            for kk in range(2):
                def combine(dst):
                    cut = halves[h]
                    dst[:, cut] = dot_tn(picks[kk], irb[kk, :, cut]).astype(BF)

                @pl.when(k == kk)
                def _():
                    combine(acc.at[b])

                @pl.when(k != kk)
                def _():
                    combine(give.at[lax.rem(j, 2)])
                    handed(b, lax.rem(j, 2), h).start()

        @pl.when(j == C - 1)
        def _():
            reduce_step(1)
        for e in range(el):
            for n in range(0, D, 512):
                orow = dot(hgs[e, here, :], wd[e, :, n:n + 512]).astype(BF)
                for kk in range(2):
                    orb[kk, e * capp:(e + 1) * capp, n:n + 512] = orow[kk * capp:(kk + 1) * capp]

        def back(bb):
            return pltpu.make_async_copy(st_o, out_o.at[pl.ds(2 * bb, 2)], s_loc.at[3])

        @pl.when(j >= 1)
        def _():
            back(0).wait()
        for kk in range(2):
            s = 2 * b + kk
            for e in range(el):
                hit = picks[kk][e * capp:(e + 1) * capp].astype(F32)
                gp_o[s, e:e + 1, :] = jnp.sum(hit * gp_rows[e][kk * capp:(kk + 1) * capp], 0, keepdims=True)
            for n in range(0, D, 512):
                st_o[kk, :, n:n + 512] = dot_tn(picks[kk], orb[kk, :, n:n + 512]).astype(BF)
        back(b).start()

    n1 = D // 256
    n2 = FFW // 256

    def t1_copy(e, i):
        return pltpu.make_async_copy(st1.at[lax.rem(i, 2)], t1_o.at[e, pl.ds(pl.multiple_of(i * 256, 256), 256)],
                                     s_t.at[0, lax.rem(i, 2)])

    def t2_copy(e, i):
        return pltpu.make_async_copy(st2.at[lax.rem(i, 2)], t2_o.at[e, pl.ds(pl.multiple_of(i * 256, 256), 256)],
                                     s_t.at[1, lax.rem(i, 2)])

    cubes = term_cubes(nd, el, f, d, t1_o, t2_o, None, None, [l1], None, [], [], (s_cube, r_cube))
    for e in range(el):
        @pl.loop(0, n1)
        def _(i):
            @pl.when(i >= 2)
            def _():
                t1_copy(e, i).wait()
            col = pl.ds(pl.multiple_of(i * 256, 256), 256)
            st1[lax.rem(i, 2)] = dot_tn(xs[e, :, col], hs[e]).astype(BF)
            t1_copy(e, i).start()

        for i in range(2):
            t1_copy(e, i).wait()
        cubes[2 * e].down(0).start()
        if e == el - 1 and C > 2:
            reduce_step(2)

        @pl.loop(0, n2)
        def _(i):
            @pl.when(i >= 2)
            def _():
                t2_copy(e, i).wait()
            col = pl.ds(pl.multiple_of(i * 256, 256), 256)
            st2[lax.rem(i, 2)] = dot_tn(hgs[e, :, col], gs[e]).astype(BF)
            t2_copy(e, i).start()
        for i in range(2):
            t2_copy(e, i).wait()

    for s in range(3, C):
        reduce_step(s)
    for line in lines:
        line.last()
    gin_o[...] = acc[c]

    pltpu.make_async_copy(st_o, out_o.at[pl.ds(0, 2)], s_loc.at[3]).wait()
    for j in range(max(C - 2, 0), C):
        chip, _, _ = visit(c, C, j)
        for h in range(2):
            handed(chip, j % 2, h).wait_send()
    for line in lines:
        for s in range(1, C):
            for dr in range(2):
                chip, ok = line.dest(dr, s)

                @pl.when(ok)
                def _():
                    line.z_copy(dr, s, chip).wait_send()
    for cube in cubes[::2]:
        cube.down(0).wait()
    sib_own.wait_send()
    for dr in range(2):
        for s in range(1, C):
            @pl.when(has(dr, s))
            def _():
                sib_out(dr, s).wait_send()
        for s in range(1, C):
            @pl.when(nxt_ok(dr) & has(dr, s - 1))
            def _():
                for h in range(2):
                    z_out(dr, s, h).wait_send()


def experts_call(nf, nd, cap, ffn_in, cot_all, side, w_gate, w_up, w_down):
    T, D = ffn_in.shape
    el, _, FFW = w_gate.shape
    capp = cap + (-cap % 16)
    C = nf // 2
    rows = C * 2 * capp
    land_hbm = C > 4
    dma = pltpu.SemaphoreType.DMA
    out = [((nf, T, D), BF, 1), ((T, D), BF, 0), ((nf, el, T), F32, 0),
           ((el, D, 2 * FFW), BF, 1), ((el, FFW, D), BF, 1),
           ((el, D // 2, 2 * FFW), BF, 1)]
    lands = [(C, T, D), (2, C - 1, T, D)]
    scratch = []
    if land_hbm:
        out += [(x, BF, 1) for x in lands]
    else:
        scratch += [VMEM(x, BF) for x in lands]
    scratch += [
        VMEM((C, T, D), BF),
        VMEM((el, D, FFW), BF), VMEM((el, D, FFW), BF), VMEM((el, FFW, D), BF),
        VMEM((nf, T, D), BF), VMEM(side.shape, F32), VMEM((2, T, D), BF),
        VMEM((el, rows, D), BF), VMEM((el, rows, D), BF),
        VMEM((el, rows, 2 * FFW), BF), VMEM((el, rows, FFW), BF),
        VMEM((2, el * capp, D), BF), VMEM((2, el * capp, D), BF),
        VMEM((2, T, D), BF), VMEM((2, T, D), BF),
        VMEM((2, 256, 2 * FFW), BF), VMEM((2, 256, D), BF),
        VMEM((T, D) if land_hbm else (16, 128), BF),
        VMEM((el, 2 * capp, FFW), F32),
        dma((nf,)), dma((nf,)),
        dma((2, 2, C)), dma((2, 2, C)), dma((2, C)), dma((2, C)),
        dma((3,)), dma((5,)), dma((2, 2)),
        dma((2, C)), dma((2, C)), dma((2, 2, C)), dma((2, 2, C)), dma(()),
        dma((2 * el, 2 * (nd.bit_length() - 1))), dma((2 * el, 2 * (nd.bit_length() - 1))),
    ]
    return pl.pallas_call(
        functools.partial(experts_kernel, nf, nd, el, cap, capp, land_hbm),
        out_shape=[jax.ShapeDtypeStruct(o[0], o[1]) for o in out],
        in_specs=[vm(), hbm(), vm(), hbm(), hbm(), hbm()],
        out_specs=[hbm() if o[2] else vm() for o in out],
        scratch_shapes=scratch,
        compiler_params=pltpu.CompilerParams(collective_id=2, has_side_effects=True,
                                             vmem_limit_bytes=63 * 2 ** 20),
        cost_estimate=pl.CostEstimate(flops=40_000_000_000, bytes_accessed=60_000_000, transcendentals=2_000_000),
        name="experts",
    )(ffn_in, cot_all, side, w_gate, w_up, w_down)[:6]


def back_kernel(nf, nd, el, land_hbm, split, *refs):
    m = nd.bit_length() - 1
    it = iter(refs)

    def take(n):
        return [next(it) for _ in range(n)]

    (gin, out_p, gp_p, t1, t2, f1, tok_h, cot_h, hid_h, ffn_h, gates, mix_h, qk_h, v_h, prob_h, wf_h, rt,
     cosr, sinr) = take(19)
    out_o, gt_o, sh_o, sm_o, t1_o, t2_o = take(6)
    l1 = [f1] + take(m - 1)
    l2 = take(m)
    a1 = take(m - 1)
    a2 = take(m - 1)
    sibo, rcvo, sib, rcv, sibq, rcvq = take(6)
    (acc, wb, wg, tok, cot, hid, ffn, mix, qk, v, prob, branch, gh, ga, gproj, gpb, smg, smr, smd, sms) = take(20)
    attn, gm = ffn, mix
    shl = take(m * (2 if split else 1))
    if split:
        xo = next(it)
        xol = take(m)
    stage, stageq = take(2)
    (s_load, s_acc, s_gp, r_gp, s_sib, r_sib, s_z, r_z, s_cube, r_cube, s_sc, r_sc, s_sm, r_sm, s_sd, r_sd,
     s_stage, s_prob) = take(18)

    T, D = tok.shape
    R = wg.shape[0] // nf
    W = wg.shape[1]
    E = gates.shape[0]
    C = nf // 2
    f = lax.axis_index("fsdp")
    d = lax.axis_index("dp")
    c = f // 2
    k = lax.rem(f, 2)
    QV = QW + 2 * KW
    QZ, OW = QV, D
    greet(nf, nd, f, d)

    def remote(src, dst, ss, rs, to_f, to_d):
        return pltpu.make_async_remote_copy(src_ref=src, dst_ref=dst, send_sem=ss, recv_sem=rs,
                                            device_id=(to_f, to_d), device_id_type=MESH)

    def rows(ff):
        return pl.ds(pl.multiple_of(ff * R, 16), R)


    def sems(i):
        return (s_sib.at[i], r_sib.at[i], s_z.at[i], r_z.at[i])

    def lines_of(first, cuts, sb, rc, sg, ids):
        res = []
        for h, (top, n) in enumerate(cuts):
            cut, loc = pl.ds(first + top, n), pl.ds(top, n)
            res.append(Line(nf, f, d, lambda ch, cut=cut: wg.at[rows(2 * ch + k), cut],
                            lambda ch, cut=cut: wg.at[rows(2 * ch + 1 - k), cut],
                            lambda ch, loc=loc: sb.at[ch, :, loc], lambda dr, s, loc=loc: rc.at[dr, s, :, loc],
                            sg.at[:, loc] if land_hbm else None, sems(ids[h]), s_stage))
        return res

    if split:
        o_lines = []
        pair = Line(nf, f, d, None, lambda ch: wg.at[rows(2 * ch + 1 - k), QZ:W], lambda ch: sib.at[ch], None, None,
                    sems(0), s_stage)
        o_cubes = []
        for h in range(2):
            top = h * (C * R // 2)
            cube = Cube(nd, f, d, h == 1, True, OW, xo.at[top:top + C * R // 2],
                        functools.partial(lambda h, i: xol[i].at[h], h), None, None, (s_sc.at[h], r_sc.at[h]))
            cube.in_place, cube.whole = True, False
            o_cubes.append(cube)
        o_low = [cube.low[m] for cube in o_cubes]

        def o_block(ch):
            low = pl.multiple_of(jnp.where(ch < C // 2, o_low[0], o_low[1]), 128)
            return xo.at[pl.ds(pl.multiple_of(ch * R, 16), R), pl.ds(low, OW >> m)]

        o_line = Line(nf, f, d, o_block, None, None, lambda dr, s: rcv.at[dr, s], None, sems(1), s_stage)
        o_up = Cube(nd, f, d, c >= C // 2, True, OW, None, None, None, sh_o.at[:, QZ:W], (s_sc.at[2], r_sc.at[2]))
    else:
        o_lines = lines_of(QV, ((0, D // 2), (D // 2, D // 2)), sib, rcv, stage.at[0:R], (0, 1))
    q_cuts = ((0, QW), (QW, 2 * KW))
    q_lines = lines_of(0, q_cuts, sibq, rcvq, stageq, (2, 4))
    out_line = Line(nf, f, d, lambda ch: acc.at[ch], lambda ch: out_p.at[2 * ch + 1 - k], lambda ch: sibo.at[ch],
                    lambda dr, s: rcvo.at[dr, s], stage, sems(3), s_stage)

    def acc_loads(src):
        return [pltpu.make_async_copy(src.at[2 * ch + k], acc.at[ch], s_acc.at[ch]) for ch in range(C)]

    gp_copies = []
    for i in range(1, nf):
        to = lax.rem(f + i, nf)
        cp = remote(gp_p.at[to], gpb.at[f], s_gp.at[i - 1], r_gp.at[i - 1], to, d)
        cp.start()
        gp_copies.append(cp)
    out_line.start_sib()
    out_loads = acc_loads(out_p)
    for cp in out_loads:
        cp.start()
    cubes = term_cubes(nd, el, f, d, t1, t2, t1_o, t2_o, l1, l2, a1, a2, (s_cube, r_cube))
    first_terms, second_terms = cubes[::2], cubes[1::2]
    for cube in second_terms:
        cube.down(0).start()
    own_gp = pltpu.make_async_copy(gp_p.at[f], gpb.at[f], s_load.at[0])
    own_gp.start()
    wo = pltpu.make_async_copy(wf_h.at[:, QV:QV + D], wb.at[:, 0:D], s_load.at[1])
    wo.start()
    others = [(tok_h, tok), (cot_h, cot), (hid_h, hid), (ffn_h, ffn), (mix_h, mix), (qk_h, qk), (v_h, v)]
    more = [pltpu.make_async_copy(a, b, s_load.at[2 + i]) for i, (a, b) in enumerate(others)]
    for cp in more:
        cp.start()

    def prob_load(i):
        at = pl.ds(i * 2 * GROUP, 2 * GROUP)
        return pltpu.make_async_copy(prob_h.at[at], prob.at[lax.rem(i, 2)], s_prob.at[lax.rem(i, 2)])

    prob_load(0).start()

    def onward(cube, i):
        cube.down(i + 1).start() if i + 1 < m else cube.up(i).start()

    def chain(group, start, add):
        def merged(i):
            for cube in group:
                cube.merge(i, add)
                onward(cube, i)

        def raised(i):
            for cube in group:
                cube.up_in(i).wait_recv()
                cube.up(i - 1).start()

        return ([functools.partial(merged, i) for i in range(start, m)]
                + [functools.partial(raised, i) for i in range(m - 1, 0, -1)])

    def vadd(dst, a, b):
        add_blocks(dst, [a, b])

    def run(steps, n=1):
        for _ in range(min(n, len(steps))):
            steps.pop(0)()

    steps1, steps2 = chain(first_terms, 1, pipe_add), chain(second_terms, 0, pipe_add)
    for cube in first_terms:
        cube.fold(0, pipe_add)
        onward(cube, 0)
    for cp in out_loads:
        cp.wait()
    out_line.step(1)
    for cp in more:
        cp.wait()
    own_gp.wait()
    for cp in gp_copies:
        cp.wait()

    gains = rt[E:E + 2].astype(F32)
    gain_one, gain_two = gains[0:1], gains[1:2]
    gpt = jnp.concatenate([gpb[i] for i in range(nf)], 0)
    gates_v = gates[...]
    gl = (gates_v * (gpt - jnp.sum(gpt * gates_v, 0, keepdims=True))).astype(BF)
    for n in range(0, D, 512):
        sms[0:E, n:n + 512] = dot(gl, ffn[:, n:n + 512])
    for n in range(0, D, 512):
        ga[:, n:n + 512] = dot_tn(gl, rt[0:E, n:n + 512])
    sms[E:, :] = jnp.zeros((sms.shape[0] - E, D), F32)
    TR = 32

    @pl.loop(0, T // TR)
    def _(i):
        at = pl.ds(pl.multiple_of(i * TR, TR), TR)
        h = hid[at, :]
        r2 = lax.rsqrt(jnp.mean(h * h, -1, keepdims=True) + EPSILON)
        n2 = h * r2
        gf = gin[at, :].astype(F32) + ga[at, :]
        sms[E + 1:E + 2, :] += jnp.sum(gf * n2, 0, keepdims=True)
        g2 = gf * gain_two
        x = cot[at, :].astype(F32) + r2 * (g2 - n2 * jnp.mean(g2 * n2, -1, keepdims=True))
        gh[at, :] = x
        branch[at, :] = x.astype(BF)

    @pl.loop(0, QW // 256)
    def _(i):
        at = pl.ds(pl.multiple_of(i * 256, 256), 256)
        wg[at, QV:QV + D] = dot_tn(mix[:, at], branch[...]).astype(BF)
    if split:
        pair.start_sib()
        if C > 2:
            out_line.step(2)
    else:
        for line in o_lines:
            line.start_sib()
        for line in o_lines:
            line.step(1)
    wo.wait()

    @pl.loop(0, QW // 256)
    def _(i):
        at = pl.ds(pl.multiple_of(i * 256, 256), 256)
        gm[:, at] = dot_nt(branch[...], wb[at, 0:D]).astype(BF)
    wq = pltpu.make_async_copy(wf_h.at[:, 0:QV], wb, s_load.at[1])
    wq.start()
    if split:
        for ch in range(C):
            pair.sib_copy(ch).wait_recv()
            add_blocks(xo.at[ch * R:(ch + 1) * R], [wg.at[rows(2 * ch + k), QZ:W], sib.at[ch]])
        for cube in o_cubes:
            cube.down(0).start()
    run(steps2)
    factor = HEAD_SIZE ** (-0.5)
    lane = lax.broadcasted_iota(jnp.int32, (T, 128), 1)
    low = lane < HEAD_SIZE
    first = lax.rem(lane, HEAD_SIZE) < HEAD_SIZE // 2

    def unrotate(x):
        return x * cosr[...] - half_roll(x, first) * sinr[...]

    @pl.loop(0, KEY_VALUE_HEADS // 2)
    def _(i):
        @pl.when(i + 1 < KEY_VALUE_HEADS // 2)
        def _():
            prob_load(i + 1).start()
        prob_load(i).wait()
        slot = lax.rem(i, 2)
        kcol = pl.ds(pl.multiple_of(i * 128, 128), 128)
        kh = head_masks(qk[:, pl.ds(pl.multiple_of(QW + i * 128, 128), 128)], lane)
        vh = head_masks(v[:, kcol], lane)
        gk = [[None, None], [None, None]]
        gv = [[None, None], [None, None]]
        for p in range(GROUP):
            qc = pl.ds(pl.multiple_of((i * GROUP + p) * 128, 128), 128)
            q = qk[:, qc]
            g = gm[:, qc]
            gq = None
            for half in range(2):
                kv = (2 * p + half) // GROUP
                pr = prob[slot, 2 * p + half]
                prf = pr.astype(F32)
                gp = dot_nt(g, vh[kv][half])
                gs = (prf * (gp - jnp.sum(prf * gp, -1, keepdims=True))).astype(BF)
                term = dot(gs, kh[kv][half])
                gq = term if gq is None else gq + term
                tk = dot_tn(gs, q)
                tv = dot_tn(pr, g)
                gk[kv][half] = tk if gk[kv][half] is None else gk[kv][half] + tk
                gv[kv][half] = tv if gv[kv][half] is None else gv[kv][half] + tv
            gproj[:, qc] = unrotate(gq * factor).astype(BF)

        def join(x):
            a = jnp.where(low, x[0][0] + pltpu.roll(x[0][1], HEAD_SIZE, axis=1), 0.0)
            b = jnp.where(low, 0.0, pltpu.roll(x[1][0], HEAD_SIZE, axis=1) + x[1][1])
            return a + b

        gproj[:, pl.ds(pl.multiple_of(QW + i * 128, 128), 128)] = unrotate(join(gk) * factor).astype(BF)
        gproj[:, pl.ds(pl.multiple_of(QW + KW + i * 128, 128), 128)] = join(gv).astype(BF)

        if C > 2:
            @pl.when(i == 1)
            def _():
                for line in o_lines:
                    line.step(2)


    def o_merge(i):
        for cube in o_cubes:
            cube.merge(i, vadd)
            if i + 1 < m:
                cube.down(i + 1).start()

    @pl.loop(0, T // TR)
    def _(i):
        at = pl.ds(pl.multiple_of(i * TR, TR), TR)
        x = tok[at, :].astype(F32)
        r1 = lax.rsqrt(jnp.mean(x * x, -1, keepdims=True) + EPSILON)
        attn[at, :] = (x * r1 * gain_one).astype(BF)

    for line, (top, width) in zip(q_lines, q_cuts):
        @pl.loop(0, D // 256)
        def _(i):
            at = pl.ds(pl.multiple_of(i * 256, 256), 256)
            for n in range(top, top + width, 512):
                wg[at, n:n + 512] = dot_tn(attn[:, at], gproj[:, n:n + 512]).astype(BF)
        line.start_sib()
        if line is q_lines[0]:
            for s in range(3, C):
                for other in o_lines:
                    other.step(s)
        line.step(1)
    run(steps1)
    run(steps2)
    if split:
        o_merge(0)
    wq.wait()

    @pl.loop(0, D // 256)
    def _(i):
        at = pl.ds(pl.multiple_of(i * 256, 256), 256)
        ga[:, at] = dot_nt(gproj[...], wb[at, :])

    @pl.loop(0, T // TR)
    def _(i):
        at = pl.ds(pl.multiple_of(i * TR, TR), TR)
        x = tok[at, :].astype(F32)
        r1 = lax.rsqrt(jnp.mean(x * x, -1, keepdims=True) + EPSILON)
        n1 = x * r1
        gat = ga[at, :]
        sms[E:E + 1, :] += jnp.sum(gat * n1, 0, keepdims=True)
        g1 = gat * gain_one
        gt_o[at, :] = (gh[at, :] + r1 * (g1 - n1 * jnp.mean(g1 * n1, -1, keepdims=True))).astype(BF)

    small = sms[...]
    for i in range(nf):
        smg[i] = small[:, i * R:(i + 1) * R]
    sm_copies = []
    for i in range(1, nf):
        to = lax.rem(f + i, nf)
        cp = remote(smg.at[to], smr.at[f], s_sm.at[i - 1], r_sm.at[i - 1], to, d)
        cp.start()
        sm_copies.append(cp)
    smr_own = pltpu.make_async_copy(smg.at[f], smr.at[f], s_load.at[0])
    smr_own.start()

    for line in o_lines:
        line.last()
    lates = []
    for g, (left, width) in enumerate(q_cuts if split else ((0, W),)):
        late = []
        for h in range(2):
            top = h * (R // 2)
            own = wg.at[pl.ds(pl.multiple_of(f * R + top, 16), R // 2), left:left + width]
            cube = Cube(nd, f, d, h == 1, True, width, own, functools.partial(lambda g, h, i: shl[g * m + i].at[h], g, h),
                        None, sh_o.at[top:top + R // 2, left:left + width], (s_sc.at[3 + 2 * g + h], r_sc.at[3 + 2 * g + h]))
            cube.in_place = True
            late.append(cube)
        lates.append(late)
    steps_l = [chain(late, 0, vadd) for late in lates]
    run(steps1)
    run(steps2)
    if C > 2:
        for line in q_lines:
            line.step(2)
    if split:
        for i in range(1, m):
            o_merge(i)
        o_line.step(1)
    if split:
        if C > 2:
            o_line.step(2)
        pair.sent()
    for line in o_lines:
        line.sent()
    smr_own.wait()
    for cp in sm_copies:
        cp.wait()
    total = smr[0]
    for i in range(1, nf):
        total = total + smr[i]
    smd[0] = total
    sd_copies = []
    for i in range(1, nd):
        cp = remote(smd.at[0], smd.at[i], s_sd.at[i - 1], r_sd.at[i - 1], f, jnp.bitwise_xor(d, i))
        cp.start()
        sd_copies.append(cp)
    for s in range(3, C):
        for line in q_lines:
            line.step(s)
    if not split and C > 2:
        out_line.step(2)
    run(steps1, len(steps1))
    run(steps2, len(steps2))
    if split:
        for s in range(3, C):
            o_line.step(s)
        o_line.last()
        add_blocks(sh_o.at[:, pl.ds(pl.multiple_of(QZ + o_up.low[m], 128), OW >> m)], [o_block(c)])
        o_up.up(m - 1).start()
    for g, line in enumerate(q_lines):
        line.last()
        if split or line is q_lines[-1]:
            for cube in lates[g if split else 0]:
                cube.down(0).start()
    for s in range(3, C):
        out_line.step(s)
    if split:
        for i in range(m - 1, 0, -1):
            o_up.up_in(i).wait_recv()
            o_up.up(i - 1).start()
    while steps_l[-1]:
        for steps in steps_l:
            run(steps)
    for cp in sd_copies:
        cp.wait()
    total = smd[0]
    for i in range(1, nd):
        total = total + smd[i]
    sm_o[...] = total
    out_line.last()

    @pl.loop(0, T // TR)
    def _(i):
        at = pl.ds(pl.multiple_of(i * TR, TR), TR)
        out_o[at, :] = (hid[at, :] + acc[c, at, :].astype(F32)).astype(BF)


    for line in q_lines:
        line.sent()
    out_line.sent()
    for i, cube in enumerate(cubes):
        cube.up_in(0).wait_recv()
        cube.sent(1 - i % 2)
    if split:
        o_up.up_in(0).wait_recv()
        o_line.sent()
        for i in range(m):
            o_up.up(i).wait_send()
            for cube in o_cubes:
                cube.down(i).wait_send()
    for cube in [cube for late in lates for cube in late]:
        cube.up_in(0).wait_recv()
        cube.sent()


def back(nf, nd, el, args):
    gin, t1, t2 = args[0], args[3], args[4]
    T, D = gin.shape
    E = args[10].shape[0]
    W = args[15].shape[1]
    R = D // nf
    C = nf // 2
    m = nd.bit_length() - 1
    QV = QW + 2 * KW
    FFW = t2.shape[1]
    SR = E + 2 + (-(E + 2) % 8)
    land_hbm = C > 4
    s = jax.ShapeDtypeStruct
    out_shape = [s((T, D), BF), s((T, D), BF), s((R, W), BF), s((SR, R), F32), s(t1.shape, BF), s(t2.shape, BF)]
    out_specs = [vm(), vm(), vm(), vm(), hbm(), hbm()]
    extra = [(el, D >> (i + 1), t1.shape[2]) for i in range(1, m)] + [(el, FFW >> (i + 1), D) for i in range(m)]
    extra += [(el, D >> (i + 1), t1.shape[2]) for i in range(m - 1)] + [(el, FFW >> (i + 1), D) for i in range(m - 1)]
    extra += [(C, T, D), (2, C - 1, T, D)]
    QZ, OW = QV, D
    split = not land_hbm and (OW >> m) % 128 == 0 and (QW >> m) % 128 == 0 and (2 * KW >> m) % 128 == 0
    lands = [(C, R, OW), (2, C - 1, R, OW >> m if split else D), (C, R, QZ), (2, C - 1, R, QZ)]
    scratch = []
    if land_hbm:
        extra += lands
    else:
        scratch += [VMEM(x, BF) for x in lands]
    out_shape += [s(x, BF) for x in extra]
    out_specs += [hbm()] * len(extra)
    dma = pltpu.SemaphoreType.DMA
    scratch += [
        VMEM((C, T, D), BF), VMEM((D, QV), BF), VMEM((D, W), BF),
        VMEM((T, D), BF), VMEM((T, D), BF), VMEM((T, D), F32), VMEM((T, D), BF), VMEM((T, QW), BF),
        VMEM((T, QW + KW), BF), VMEM((T, KW), BF), VMEM((2, 2 * GROUP, T, T), BF),
        VMEM((T, D), BF), VMEM((T, D), F32), VMEM((T, D), F32), VMEM((T, QV), BF),
        VMEM((nf, el, T), F32), VMEM((nf, SR, R), F32), VMEM((nf, SR, R), F32), VMEM((nd, SR, R), F32),
        VMEM((SR, D), F32),
    ]
    for n in ((QW, 2 * KW) if split else (W,)):
        scratch += [VMEM((2, R // 2, n >> (i + 1)), BF) for i in range(m)]
    if split:
        scratch += [VMEM((C * R, OW), BF)] + [VMEM((2, C * R // 2, OW >> (i + 1)), BF) for i in range(m)]
    scratch += [VMEM((T, D), BF), VMEM((R, QV) if land_hbm else (16, 128), BF)]
    scratch += [
        dma((10,)), dma((C,)), dma((nf,)), dma((nf,)),
        dma((5, C)), dma((5, C)), dma((5, 2, C)), dma((5, 2, C)),
        dma((2 * el, 2 * m)), dma((2 * el, 2 * m)), dma((7, 2 * m)), dma((7, 2 * m)),
        dma((nf,)), dma((nf,)), dma((nd,)), dma((nd,)), dma(()), dma((2,)),
    ]
    inner = [vm(), hbm(), vm(), hbm(), hbm(), hbm(), hbm(), hbm(), hbm(), hbm(), vm(), hbm(), hbm(), hbm(), hbm(), hbm(), vm(),
             vm(), vm()]
    return pl.pallas_call(
        functools.partial(back_kernel, nf, nd, el, land_hbm, split),
        out_shape=out_shape,
        in_specs=inner,
        out_specs=out_specs,
        scratch_shapes=scratch,
        compiler_params=pltpu.CompilerParams(collective_id=3, has_side_effects=True,
                                             vmem_limit_bytes=63 * 2 ** 20),
        cost_estimate=pl.CostEstimate(flops=8_000_000_000, bytes_accessed=90_000_000, transcendentals=100_000),
        name="back",
    )(*args)[:6]


def body(tokens, w_query, key_weight, value_weight, w_out, gain_attn, gain_ffn, w_router,
         w_gate, w_up, w_down, routes, cotangent):
    T = tokens.shape[0]
    el = w_gate.shape[0]
    nf = lax.axis_size("fsdp")
    nd = lax.axis_size("dp")
    experts = el * nf
    cap = 9 * T * TOP // (8 * experts)

    pad = -(experts + 2) % 16
    small = jnp.concatenate([w_router, gain_attn[:, None], gain_ffn[:, None],
                             jnp.zeros((w_router.shape[0], pad), BF)], 1).T
    onehot = (routes[:, :, None] == jnp.arange(experts, dtype=jnp.int32)).any(1).astype(BF)
    earlier = (jnp.arange(T)[:, None] < jnp.arange(T)[None, :]).astype(BF)
    before = lax.dot_general(onehot, earlier, (((0,), (0,)), ((), ())), preferred_element_type=F32)
    slots = jnp.where(onehot.T > 0, before, -1.0)
    cosr, sinr = rope_rows(T)
    ffn_in, hidden, gates, mixed, qk, v, probs, full, cot_all, rt = front(
        nf, nd, experts, tokens, (w_query, key_weight, value_weight, w_out), small, cotangent, slots, cosr, sinr)
    side = jnp.concatenate([slots.reshape(nf, el, T), gates.reshape(nf, el, T)], 1)
    out_part, gin, gp_part, t1, t2, f1 = experts_call(nf, nd, cap, ffn_in, cot_all, side, w_gate, w_up, w_down)
    output, grad_tokens, shard, smalls, t1, t2 = back(nf, nd, el, (
        gin, out_part, gp_part, t1, t2, f1, tokens, cotangent, hidden, ffn_in, gates, mixed, qk, v, probs, full, rt,
        cosr, sinr))
    big = shard.astype(F32)
    ff = w_gate.shape[2]
    return (
        output,
        grad_tokens,
        big[:, :QW],
        big[:, QW: QW + KW],
        big[:, QW + KW: QW + 2 * KW],
        big[:, QW + 2 * KW:],
        smalls[experts],
        smalls[experts + 1],
        smalls[:experts].T,
        t1[:, :, :ff].astype(F32),
        t1[:, :, ff:].astype(F32),
        t2.astype(F32),
    )


def solution(mesh):
    in_specs = (
        P(("fsdp", "dp"), None),
        P("fsdp", None),
        P("fsdp", None),
        P("fsdp", None),
        P("fsdp", None),
        P("fsdp"),
        P("fsdp"),
        P("fsdp", None),
        P("fsdp", None, None),
        P("fsdp", None, None),
        P("fsdp", None, None),
        P(("fsdp", "dp"), None),
        P(("fsdp", "dp"), None),
    )
    out_specs = (
        P(("fsdp", "dp"), None),
        P(("fsdp", "dp"), None),
        P("fsdp", None),
        P("fsdp", None),
        P("fsdp", None),
        P("fsdp", None),
        P("fsdp"),
        P("fsdp"),
        P("fsdp", None),
        P("fsdp", None, None),
        P("fsdp", None, None),
        P("fsdp", None, None),
    )
    return jax.shard_map(body, mesh=mesh, in_specs=in_specs, out_specs=out_specs, check_vma=False)
```

```python
import functools
import jax
import jax.numpy as jnp
from jax import lax
from jax.experimental import pallas as pl
from jax.experimental.pallas import tpu as pltpu
from jax.sharding import PartitionSpec as P
import numpy as np

MODEL_WIDTH = 1536
QUERY_HEADS = 24
KEY_VALUE_HEADS = 8
HEAD_SIZE = 64
TOP = 8
GROUP = QUERY_HEADS // KEY_VALUE_HEADS
QW = QUERY_HEADS * HEAD_SIZE
KW = KEY_VALUE_HEADS * HEAD_SIZE

EPSILON = 1e-06
ROPE_BASE = 10000.0
MASKED = -1e30
F32 = jnp.float32
BF = jnp.bfloat16


def rope_rows(T):
    half = HEAD_SIZE // 2
    freq = ROPE_BASE ** (-2.0 * np.arange(half, dtype=np.float64) / HEAD_SIZE)
    ang = (np.arange(T, dtype=np.float32)[:, None] * freq.astype(np.float32)[None, :]).astype(np.float32)
    c, s = np.cos(ang), np.sin(ang)
    return (jnp.asarray(np.concatenate([c, c, c, c], 1), F32), jnp.asarray(np.concatenate([-s, s, -s, s], 1), F32))


MESH = pl.DeviceIdType.MESH
VMEM = pltpu.VMEM


def vm():
    return pl.BlockSpec(memory_space=pltpu.VMEM)


def hbm():
    return pl.BlockSpec(memory_space=pl.ANY)


def dot(a, b):
    return lax.dot_general(a, b, (((1,), (0,)), ((), ())), preferred_element_type=F32)


def dot_nt(a, b):
    return lax.dot_general(a, b, (((1,), (1,)), ((), ())), preferred_element_type=F32)


def dot_tn(a, b):
    return lax.dot_general(a, b, (((0,), (0,)), ((), ())), preferred_element_type=F32)


def half_roll(x, first):
    n = x.shape[1]
    h = HEAD_SIZE // 2
    return jnp.where(first, pltpu.roll(x, n - h, axis=1), pltpu.roll(x, h, axis=1))


def greet(nf, nd, f, d):
    barrier = pltpu.get_barrier_semaphore()
    for i in range(1, nf):
        pl.semaphore_signal(barrier, inc=1, device_id=(lax.rem(f + i, nf), d), device_id_type=MESH)
    for i in range(1, nd):
        pl.semaphore_signal(barrier, inc=1, device_id=(f, jnp.bitwise_xor(d, i)), device_id_type=MESH)
    pl.semaphore_wait(barrier, nf + nd - 2)


def head_masks(kblk, lane):
    kf = kblk.astype(F32)
    kr = pltpu.roll(kf, HEAD_SIZE, axis=1)
    low = lane < HEAD_SIZE
    zero = jnp.zeros_like(kf)
    a0 = jnp.where(low, kf, zero).astype(BF)
    a1 = jnp.where(low, zero, kr).astype(BF)
    b0 = jnp.where(low, kr, zero).astype(BF)
    b1 = jnp.where(low, zero, kf).astype(BF)
    return ((a0, a1), (b0, b1))


def front_kernel(nf, nd, experts, tok, wq, wk, wv, wo, small, cot, slots, cosr, sinr,
                 ffn_o, hid_o, gates_o, side_o, mix_o, qk_o, v_o, prob_o, wf_o, cot_o, rt_o,
                 wf, sm, attn, rot,
                 s_sm, r_sm, s_z, r_z, s_dp, r_dp, s_sib, r_sib, s_cz, r_cz, s_cs, r_cs, s_loc, s_w):
    T, D = tok.shape
    C = nf // 2
    R = wq.shape[0]
    W = wf.shape[1]
    WA = 3 * W // 4
    parts = ((0, WA), (WA, W - WA))
    f = lax.axis_index("fsdp")
    d = lax.axis_index("dp")
    c = f // 2
    k = lax.rem(f, 2)
    sib = f + 1 - 2 * k
    greet(nf, nd, f, d)

    def rows(ff):
        return pl.ds(pl.multiple_of(ff * R, 16), R)

    def cols(dd, g):
        at, n = parts[g]
        return pl.ds(pl.multiple_of(at + dd * (n // nd), 128), n // nd)

    def remote(src, dst, ss, rs, to_f, to_d):
        return pltpu.make_async_remote_copy(src_ref=src, dst_ref=dst, send_sem=ss, recv_sem=rs,
                                            device_id=(to_f, to_d), device_id_type=MESH)

    def src_chip(dr, s):
        return c - s if dr == 0 else c + s

    def has(dr, s):
        return (c - s >= 0) if dr == 0 else (c + s < C)

    def nxt_ok(dr):
        return (c + 1 < C) if dr == 0 else (c - 1 >= 0)

    def nxt_f(dr):
        return f + 2 if dr == 0 else f - 2

    def wz(dr, s, g):
        blk = wf.at[rows(2 * src_chip(dr, s - 1) + k), cols(d, g)]
        return remote(blk, blk, s_z.at[g, dr, s - 1], r_z.at[g, dr, s - 1], nxt_f(dr), d)

    def wz_in(dr, s, g):
        blk = wf.at[rows(2 * src_chip(dr, s) + k), cols(d, g)]
        return remote(blk, blk, s_z.at[g, dr, s - 1], r_z.at[g, dr, s - 1], f, d)

    halves = (slice(0, D // 2), slice(D // 2, D))

    def cz(dr, s, own, h):
        ff = 2 * src_chip(dr, s - 1) + k
        src = cot.at[:, halves[h]] if own else cot_o.at[ff, :, halves[h]]
        return remote(src, cot_o.at[ff, :, halves[h]], s_cz.at[h, dr, s - 1], r_cz.at[h, dr, s - 1], nxt_f(dr), d)

    def cz_in(dr, s, h):
        blk = cot_o.at[2 * src_chip(dr, s) + k, :, halves[h]]
        return remote(blk, blk, s_cz.at[h, dr, s - 1], r_cz.at[h, dr, s - 1], f, d)

    def cs(dr, s):
        ff = 2 * src_chip(dr, s) + k
        return remote(cot_o.at[ff], cot_o.at[ff], s_cs.at[dr, s], r_cs.at[dr, s], sib, d)

    def cs_in(dr, s):
        ff = 2 * src_chip(dr, s) + 1 - k
        return remote(cot_o.at[ff], cot_o.at[ff], s_cs.at[dr, s], r_cs.at[dr, s], sib, d)

    at = 0
    w_own = []
    for i, w in enumerate((wq, wk, wv, wo)):
        w_own.append(pltpu.make_async_copy(w, wf.at[rows(f), at:at + w.shape[1]], s_w.at[i]))
        at += w.shape[1]
    for cp in w_own:
        cp.start()
    for cp in w_own:
        cp.wait()
    for g in range(2):
        for dr in range(2):
            @pl.when(nxt_ok(dr))
            def _():
                wz(dr, 1, g).start()
    own_small = pltpu.make_async_copy(small, sm.at[f], s_loc.at[0])
    own_small.start()
    sm_copies = []
    for i in range(1, nf):
        cp = remote(small, sm.at[f], s_sm.at[i - 1], r_sm.at[i - 1], lax.rem(f + i, nf), d)
        cp.start()
        sm_copies.append(cp)
    for dr in range(2):
        @pl.when((c if dr == 0 else C - 1 - c) == 0)
        def _():
            for h in range(2):
                cz(dr, 1, True, h).start()
    sib_own = remote(wf.at[rows(f)], wf.at[rows(f)], s_sib.at[0, 0, 0], r_sib.at[0, 0, 0], sib, d)
    sib_own.start()
    own_c = pltpu.make_async_copy(cot, cot_o.at[f], s_loc.at[2])
    own_c.start()
    sib_c = remote(cot, cot_o.at[f], s_cs.at[0, 0], r_cs.at[0, 0], sib, d)

    def dp_copy(dr, s, g, i):
        blk = wf.at[rows(2 * src_chip(dr, s) + k), cols(d, g)]
        return remote(blk, blk, s_dp.at[g, dr, s - 1, i - 1], r_dp.at[g, dr, s - 1, i - 1], f, jnp.bitwise_xor(d, i))

    def dp_in(dr, s, g, i):
        blk = wf.at[rows(2 * src_chip(dr, s) + k), cols(jnp.bitwise_xor(d, i), g)]
        return remote(blk, blk, s_dp.at[g, dr, s - 1, i - 1], r_dp.at[g, dr, s - 1, i - 1], f, d)

    def sib_copy(dr, s, g):
        at, n = parts[g]
        blk = wf.at[rows(2 * src_chip(dr, s) + k), at:at + n]
        return remote(blk, blk, s_sib.at[g, dr, s], r_sib.at[g, dr, s], sib, d)

    def sib_in(dr, s, g):
        at, n = parts[g]
        blk = wf.at[rows(2 * src_chip(dr, s) + 1 - k), at:at + n]
        return remote(blk, blk, s_sib.at[g, dr, s], r_sib.at[g, dr, s], sib, d)

    for s in range(1, C):
        for g in range(2):
            for dr in range(2):
                @pl.when(has(dr, s))
                def _():
                    wz_in(dr, s, g).wait_recv()
                    if s < C - 1:
                        @pl.when(nxt_ok(dr))
                        def _():
                            wz(dr, s + 1, g).start()
                    if g == 0:
                        for i in range(1, nd):
                            dp_copy(dr, s, g, i).start()
        for dr in range(2):
            @pl.when(nxt_ok(dr) & ((c if dr == 0 else C - 1 - c) == s))
            def _():
                for h in range(2):
                    cz(dr, 1, True, h).start()
    sib_c.start()
    for s in range(1, C):
        for dr in range(2):
            @pl.when(has(dr, s))
            def _():
                for i in range(1, nd):
                    dp_copy(dr, s, 1, i).start()

    def group_in(s, g):
        for dr in range(2):
            @pl.when(has(dr, s))
            def _():
                for i in range(1, nd):
                    dp_in(dr, s, g, i).wait_recv()
                sib_copy(dr, s, g).start()

    def cores_in(g):
        for s in range(1, C):
            for dr in range(2):
                @pl.when(has(dr, s))
                def _():
                    sib_in(dr, s, g).wait_recv()

    own_small.wait()
    for cp in sm_copies:
        cp.wait()
    Ds = small.shape[1]
    rt = jnp.concatenate([sm[i] for i in range(nf)], axis=1)
    rt_o[...] = rt
    gains = rt[experts:experts + 2].astype(F32)
    gain_one, gain_two = gains[0:1], gains[1:2]
    xf = tok[...].astype(F32)
    r1 = lax.rsqrt(jnp.mean(xf * xf, -1, keepdims=True) + EPSILON)
    attn[...] = (xf * r1 * gain_one).astype(BF)

    def cot_step(s):
        for dr in range(2):
            @pl.when(has(dr, s))
            def _():
                for h in range(2):
                    cz_in(dr, s, h).wait_recv()
                    if s < C - 1:
                        @pl.when(nxt_ok(dr))
                        def _():
                            cz(dr, s + 1, False, h).start()
                cs(dr, s).start()

    cot_step(1)
    for s in range(1, C - 1):
        group_in(s, 0)
    group_in(C - 1, 0)
    sib_own.wait()
    cores_in(0)

    first = lax.rem(lax.broadcasted_iota(jnp.int32, (T, 256), 1), HEAD_SIZE) < HEAD_SIZE // 2
    cs_t = jnp.concatenate([cosr[...], cosr[...]], 1)
    sn_t = jnp.concatenate([sinr[...], sinr[...]], 1)
    nqk = (QW + KW) // 256

    @pl.loop(0, nqk)
    def _(i):
        col = pl.ds(pl.multiple_of(i * 256, 256), 256)
        x = dot(attn[...], wf[:, col])
        qk_o[:, col] = (x * cs_t + half_roll(x, first) * sn_t).astype(BF)

    @pl.loop(0, KW // 256)
    def _(i):
        col = pl.ds(pl.multiple_of(QW + KW + i * 256, 256), 256)
        v_o[:, pl.ds(pl.multiple_of(i * 256, 256), 256)] = dot(attn[...], wf[:, col]).astype(BF)

    factor = HEAD_SIZE ** (-0.5)
    lane = lax.broadcasted_iota(jnp.int32, (T, 128), 1)
    keep = lax.broadcasted_iota(jnp.int32, (T, T), 1) <= lax.broadcasted_iota(jnp.int32, (T, T), 0)

    @pl.loop(0, KEY_VALUE_HEADS // 2)
    def _(i):
        if C > 2:
            @pl.when(i == 2)
            def _():
                cot_step(2)
        kc = pl.ds(pl.multiple_of(QW + i * 128, 128), 128)
        kh = head_masks(qk_o[:, kc], lane)
        vh = head_masks(v_o[:, pl.ds(pl.multiple_of(i * 128, 128), 128)], lane)
        for p in range(GROUP):
            qc = pl.ds(pl.multiple_of((i * GROUP + p) * 128, 128), 128)
            q = qk_o[:, qc]
            acc = None
            for half in range(2):
                g = (2 * p + half) // GROUP
                sc = dot_nt(q, kh[g][half]) * factor
                sc = jnp.where(keep, sc, MASKED)
                ex = jnp.exp(sc - jnp.max(sc, -1, keepdims=True))
                pr = (ex / jnp.sum(ex, -1, keepdims=True)).astype(BF)
                prob_o[i * 2 * GROUP + 2 * p + half] = pr
                term = dot(pr, vh[g][half])
                acc = term if acc is None else acc + term
            mix_o[:, qc] = acc.astype(BF)

    for s in range(1, C):
        group_in(s, 1)
    cores_in(1)
    out_w = pltpu.make_async_copy(wf, wf_o, s_loc.at[3])
    out_w.start()

    @pl.loop(0, D // 256)
    def _(i):
        col = pl.ds(pl.multiple_of(i * 256, 256), 256)
        wc = pl.ds(pl.multiple_of(QW + 2 * KW + i * 256, 256), 256)
        hid_o[:, col] = tok[:, col].astype(F32) + dot(mix_o[...], wf[:, wc])

    hidden = hid_o[...]
    r2 = lax.rsqrt(jnp.mean(hidden * hidden, -1, keepdims=True) + EPSILON)
    ffn_o[...] = (hidden * r2 * gain_two).astype(BF)
    logits = dot_nt(rt_o[...], ffn_o[...])[0:experts]
    named = slots[...] >= 0.0
    logits = jnp.where(named, logits, MASKED)
    ex = jnp.where(named, jnp.exp(logits - jnp.max(logits, 0, keepdims=True)), 0.0)
    gates = ex / jnp.sum(ex, 0, keepdims=True)
    gates_o[...] = gates
    el = experts // nf
    for i in range(nf):
        side_o[i, 0:el] = slots[i * el:(i + 1) * el, :]
        side_o[i, el:2 * el] = gates[i * el:(i + 1) * el]

    for s in range(3, C):
        cot_step(s)
    own_c.wait()
    sib_c.wait()
    out_w.wait()
    for dr in range(2):
        for s in range(1, C):
            @pl.when(has(dr, s))
            def _():
                cs_in(dr, s).wait_recv()
                cs(dr, s).wait_send()
                for g in range(2):
                    sib_copy(dr, s, g).wait_send()
                    for i in range(1, nd):
                        dp_copy(dr, s, g, i).wait_send()

            @pl.when(nxt_ok(dr) & (has(dr, s - 1) if s > 1 else True))
            def _():
                for g in range(2):
                    wz(dr, s, g).wait_send()
                for h in range(2):
                    cz(dr, s, s == 1, h).wait_send()


def front(nf, nd, experts, tok, ws, small, cot, slots, cosr, sinr):
    T, D = tok.shape
    C = nf // 2
    W = sum(w.shape[1] for w in ws)
    out = [
        (T, D, BF, 0), (T, D, F32, 0), (experts, T, F32, 0), (nf, 2 * experts // nf, T, F32, 0), (T, QW, BF, 0), (T, QW + KW, BF, 0),
        (T, KW, BF, 0), (QUERY_HEADS, T, T, BF, 0), (D, W, BF, 1), (nf, T, D, BF, 1),
        (small.shape[0], D, BF, 0),
    ]
    dma = pltpu.SemaphoreType.DMA
    return pl.pallas_call(
        functools.partial(front_kernel, nf, nd, experts),
        out_shape=[jax.ShapeDtypeStruct(o[:-2], o[-2]) for o in out],
        in_specs=[vm()] + [hbm()] * 4 + [vm()] * 5,
        out_specs=[hbm() if o[-1] else vm() for o in out],
        scratch_shapes=[
            VMEM((D, W), BF),
            VMEM((nf,) + small.shape, BF),
            VMEM((T, D), BF),
            VMEM((8, 128), F32),
            dma((nf,)), dma((nf,)),
            dma((2, 2, C)), dma((2, 2, C)),
            dma((2, 2, C, nd)), dma((2, 2, C, nd)),
            dma((2, 2, C)), dma((2, 2, C)),
            dma((2, 2, C)), dma((2, 2, C)),
            dma((2, C)), dma((2, C)),
            dma((4,)), dma((4,)),
        ],
        compiler_params=pltpu.CompilerParams(collective_id=1, has_side_effects=True,
                                             vmem_limit_bytes=60 * 2 ** 20),
        cost_estimate=pl.CostEstimate(flops=4_000_000_000, bytes_accessed=60_000_000, transcendentals=2_000_000),
        name="front",
    )(tok, *ws, small, cot, slots, cosr, sinr)


def add_blocks(dst, srcs, extra=None):
    @pl.loop(0, dst.shape[0] // 16)
    def _(i):
        at = pl.ds(pl.multiple_of(i * 16, 16), 16)
        total = srcs[0][at, :].astype(F32)
        for s in srcs[1:]:
            total = total + s[at, :].astype(F32)
        dst[at, :] = total.astype(dst.dtype)


class Line:
    def __init__(self, nf, f, d, acc, give, sib, rcv, stage, sems, stage_sem):
        self.nf, self.f, self.d = nf, f, d
        self.C = nf // 2
        self.c, self.k = f // 2, lax.rem(f, 2)
        self.acc, self.give, self.sib, self.rcv, self.stage = acc, give, sib, rcv, stage
        self.s_sib, self.r_sib, self.s_z, self.r_z = sems
        self.stage_sem = stage_sem

    def remote(self, src, dst, ss, rs, to):
        return pltpu.make_async_remote_copy(src_ref=src, dst_ref=dst, send_sem=ss, recv_sem=rs,
                                            device_id=(to, self.d), device_id_type=MESH)

    def dest(self, dr, s):
        i = s - 1 - (self.C - 1 - self.c) if dr == 0 else s - 1 - self.c
        room = self.c if dr == 0 else self.C - 1 - self.c
        chip = i if dr == 0 else self.C - 1 - i
        return jnp.clip(chip, 0, self.C - 1), (i >= 0) & (i < room)

    def sib_copy(self, chip):
        return self.remote(self.give(chip), self.sib(chip), self.s_sib.at[chip], self.r_sib.at[chip],
                           self.f + 1 - 2 * self.k)

    def z_copy(self, dr, s, chip):
        return self.remote(self.acc(chip), self.rcv(dr, s - 1), self.s_z.at[dr, s - 1], self.r_z.at[dr, s - 1],
                           self.f - 2 if dr == 0 else self.f + 2)

    def z_in(self, dr, s):
        return self.remote(self.rcv(dr, s - 1), self.rcv(dr, s - 1), self.s_z.at[dr, s - 1], self.r_z.at[dr, s - 1],
                           self.f)

    def start_sib(self):
        for s in range(1, self.C):
            for dr in range(2):
                chip, ok = self.dest(dr, s)

                @pl.when(ok)
                def _():
                    self.sib_copy(chip).start()
        self.sib_copy(self.c).start()

    def gather(self, chip, srcs):
        acc = self.acc(chip)
        if self.stage is None:
            add_blocks(acc, [acc] + srcs)
            return
        for s in srcs:
            cp = pltpu.make_async_copy(s, self.stage, self.stage_sem)
            cp.start()
            cp.wait()
            add_blocks(acc, [acc, self.stage])

    def step(self, s):
        for dr in range(2):
            chip, ok = self.dest(dr, s)
            begins = (self.c == self.C - 1) if dr == 0 else (self.c == 0)

            @pl.when(ok)
            def _():
                other = []
                if self.sib is not None:
                    self.sib_copy(chip).wait_recv()
                    other = [self.sib(chip)]

                    @pl.when(begins)
                    def _():
                        self.gather(chip, other)
                if s > 1:
                    @pl.when(jnp.logical_not(begins))
                    def _():
                        self.z_in(dr, s - 1).wait_recv()
                        self.gather(chip, other + [self.rcv(dr, s - 2)])
                self.z_copy(dr, s, chip).start()

    def last(self):
        other = []
        if self.sib is not None:
            self.sib_copy(self.c).wait_recv()
            other = [self.sib(self.c)]
        mid = (self.c > 0) & (self.c < self.C - 1)
        s = self.C - 1
        for dr in range(2):
            @pl.when((self.c < self.C - 1) if dr == 0 else (self.c > 0))
            def _():
                self.z_in(dr, s).wait_recv()

        @pl.when(mid)
        def _():
            self.gather(self.c, other + [self.rcv(0, s - 1), self.rcv(1, s - 1)])

        @pl.when(self.c == 0)
        def _():
            self.gather(self.c, other + [self.rcv(0, s - 1)])

        @pl.when(self.c == self.C - 1)
        def _():
            self.gather(self.c, other + [self.rcv(1, s - 1)])

    def sent(self):
        if self.acc is None:
            for chip in range(self.C):
                self.sib_copy(chip).wait_send()
            return
        if self.sib is not None:
            self.sib_copy(self.c).wait_send()
        for s in range(1, self.C):
            for dr in range(2):
                chip, ok = self.dest(dr, s)

                @pl.when(ok)
                def _():
                    if self.sib is not None:
                        self.sib_copy(chip).wait_send()
                    self.z_copy(dr, s, chip).wait_send()


class Cube:
    def __init__(self, nd, f, d, flip, lanes, size, own, land, total, out, sems):
        m = nd.bit_length() - 1
        order = [1 << b for b in range(m)]
        if isinstance(flip, bool):
            self.masks = order[::-1] if flip else order
        else:
            self.masks = [jnp.where(flip, b, a) for a, b in zip(order, order[::-1])]
        self.f, self.d, self.lanes = f, d, lanes
        self.own, self.land, self.total, self.out = own, land, total, out
        self.ss, self.rs = sems
        self.m = m
        self.in_place, self.whole = False, True
        self.low, self.length = [0], [size]
        for mask in self.masks:
            half = self.length[-1] // 2
            side = lax.rem(d // mask, 2)
            self.low.append(self.low[-1] + side * half)
            self.length.append(half)

    def cut(self, ref, at, n):
        if self.lanes:
            return ref.at[:, pl.ds(pl.multiple_of(at, 128), n)]
        return ref.at[pl.ds(pl.multiple_of(at, 16), n)]

    def remote(self, src, dst, i, mask):
        return pltpu.make_async_remote_copy(src_ref=src, dst_ref=dst, send_sem=self.ss.at[i], recv_sem=self.rs.at[i],
                                            device_id=(self.f, jnp.bitwise_xor(self.d, mask)),
                                            device_id_type=MESH)

    def level(self, i):
        if i == 0 or (self.in_place and (i < self.m or not self.whole)):
            return self.own, 0
        if i == self.m:
            return self.out, 0
        return self.total(i - 1), self.low[i]

    def down(self, i):
        ref, base = self.level(i)
        half = self.length[i + 1]
        other = 2 * self.low[i] + half - self.low[i + 1]
        return self.remote(self.cut(ref, other - base, half), self.land(i), i, self.masks[i])

    def merge(self, i, add):
        self.down(i).wait_recv()
        self.fold(i, add)

    def fold(self, i, add):
        ref, base = self.level(i)
        dst, dbase = self.level(i + 1)
        half = self.length[i + 1]
        low = self.low[i + 1]
        add(self.cut(dst, low - dbase, half), self.cut(ref, low - base, half), self.land(i))

    def up(self, i):
        blk = self.cut(self.out, self.low[i + 1], self.length[i + 1])
        return self.remote(blk, blk, self.m + i, self.masks[i])

    def up_in(self, i):
        half = self.length[i + 1]
        other = 2 * self.low[i] + half - self.low[i + 1]
        blk = self.cut(self.out, other, half)
        return self.remote(blk, blk, self.m + i, self.masks[i])

    def sent(self, first=0):
        for i in range(self.m):
            if i >= first:
                self.down(i).wait_send()
            self.up(i).wait_send()


def pipe_add(dst, a, b):
    n, w = dst.shape
    tile = next(t for t in (256, 192, 128, 64) if n % t == 0 and t * w <= 256 * 1024)
    spec = pl.BlockSpec((tile, w), lambda i: (i, 0))

    def inner(a_ref, b_ref, o_ref):
        o_ref[...] = (a_ref[...].astype(F32) + b_ref[...].astype(F32)).astype(o_ref.dtype)

    pltpu.emit_pipeline(inner, grid=(n // tile,), in_specs=[spec, spec], out_specs=[spec])(a, b, dst)

def visit(c, C, j):
    both = jnp.minimum(c, C - 1 - c)
    near = j <= 2 * both
    dist = jnp.where(near, (j + 1) // 2, j - both)
    down = jnp.where(near, lax.rem(j, 2) == 0, c < C - 1 - c)
    chip = jnp.where(down, c + dist, c - dist)
    return chip, jnp.where(down, 1, 0), dist


def term_cubes(nd, el, f, d, t1, t2, out1, out2, l1, l2, a1, a2, sems):
    cubes = []
    for e in range(el):
        for j, (src, out, ls, ts) in enumerate(((t1, out1, l1, a1), (t2, out2, l2, a2))):
            pick = functools.partial(lambda refs, e, i: refs[i].at[e], ls, e)
            tot = functools.partial(lambda refs, e, i: refs[i].at[e], ts, e)
            cubes.append(Cube(nd, f, d, (e + j) % 2 == 1, False, src.shape[1], src.at[e], pick, tot,
                              None if out is None else out.at[e], (sems[0].at[2 * e + j], sems[1].at[2 * e + j])))
    return cubes


def experts_kernel(nf, nd, el, cap, capp, land_hbm, ffn, cot_a, side, wg_h, wu_h, wd_h,
                   out_o, gin_o, gp_o, t1_o, t2_o, l1, sib_l, rcv_l, acc,
                   wg, wu, wd, fa, sd, cotb, xs, gs, hs, hgs, orb, irb, st_o, give, st1, st2, stage, us,
                   s_sd, r_sd, s_z, r_z, s_sib, r_sib, s_w, s_loc, s_t, s_ls, r_ls, s_lz, r_lz, s_st, s_cube, r_cube):
    T, D = ffn.shape
    FFW = wg.shape[2]
    C = nf // 2
    B = 2 * capp
    f = lax.axis_index("fsdp")
    d = lax.axis_index("dp")
    c = f // 2
    k = lax.rem(f, 2)
    sib = f + 1 - 2 * k
    greet(nf, nd, f, d)

    def remote(src, dst, ss, rs, to_f):
        return pltpu.make_async_remote_copy(src_ref=src, dst_ref=dst, send_sem=ss, recv_sem=rs,
                                            device_id=(to_f, d), device_id_type=MESH)

    def chip_at(dr, s):
        return jnp.where(dr == 0, c - s, c + s)

    def has(dr, s):
        at = chip_at(dr, s)
        return (at >= 0) & (at < C)

    def nxt_ok(dr):
        return (c + 1 < C) if dr == 0 else (c - 1 >= 0)

    def nxt_f(dr):
        return f + 2 if dr == 0 else f - 2

    halves = (slice(0, D // 2), slice(D // 2, D))

    def z_out(dr, s, h):
        blk = fa.at[2 * chip_at(dr, s - 1) + k, :, halves[h]]
        return remote(blk, blk, s_z.at[h, dr, s - 1], r_z.at[h, dr, s - 1], nxt_f(dr))

    def z_own(dr, h):
        return remote(ffn.at[:, halves[h]], fa.at[f, :, halves[h]], s_z.at[h, dr, 0], r_z.at[h, dr, 0], nxt_f(dr))

    def z_in(dr, s, h):
        blk = fa.at[2 * chip_at(dr, s) + k, :, halves[h]]
        return remote(blk, blk, s_z.at[h, dr, s - 1], r_z.at[h, dr, s - 1], f)

    def sib_out(dr, s):
        ff = 2 * chip_at(dr, s) + k
        return remote(fa.at[ff], fa.at[ff], s_sib.at[dr, s], r_sib.at[dr, s], sib)

    def sib_in(dr, s):
        ff = 2 * chip_at(dr, s) + 1 - k
        return remote(fa.at[ff], fa.at[ff], s_sib.at[dr, s], r_sib.at[dr, s], f)

    lines = [Line(nf, f, d, lambda ch, cut=cut: acc.at[ch, :, cut], lambda ch, cut=cut: give.at[0, :, cut],
                  lambda ch, cut=cut: sib_l.at[ch, :, cut], lambda dr, s, cut=cut: rcv_l.at[dr, s, :, cut],
                  stage.at[:, cut] if land_hbm else None, (s_ls.at[h], r_ls.at[h], s_lz.at[h], r_lz.at[h]), s_st)
             for h, cut in enumerate(halves)]

    def handed(chip, slot, h):
        return remote(give.at[slot, :, halves[h]], sib_l.at[chip, :, halves[h]], s_ls.at[h, chip], r_ls.at[h, chip], sib)

    def reduce_step(s):
        for line in lines:
            line.step(s)

    for h in range(2):
        for dr in range(2):
            @pl.when(nxt_ok(dr))
            def _():
                z_own(dr, h).start()
    sib_own = remote(ffn, fa.at[f], s_sib.at[1, 0], r_sib.at[1, 0], sib)
    sib_own.start()
    own = pltpu.make_async_copy(ffn, fa.at[f], s_loc.at[0])
    own.start()
    own_sd = pltpu.make_async_copy(side.at[f], sd.at[f], s_loc.at[1])
    own_sd.start()
    sd_copies = []
    for i in range(1, nf):
        to = lax.rem(f + i, nf)
        cp = remote(side.at[to], sd.at[f], s_sd.at[i - 1], r_sd.at[i - 1], to)
        cp.start()
        sd_copies.append(cp)
    w_copies = []
    for i, (src, dst) in enumerate(((wg_h, wg), (wu_h, wu), (wd_h, wd))):
        cp = pltpu.make_async_copy(src, dst, s_w.at[i])
        cp.start()
        w_copies.append(cp)
    own.wait()
    own_sd.wait()
    for cp in sd_copies:
        cp.wait()
    for cp in w_copies:
        cp.wait()

    n1 = D // 256
    n2 = FFW // 256
    cubes = term_cubes(nd, el, f, d, t1_o, t2_o, None, None, [l1], None, [], [], (s_cube, r_cube))

    def t1_copy(e, i):
        return pltpu.make_async_copy(st1.at[lax.rem(i, 2)], t1_o.at[e, pl.ds(pl.multiple_of(i * 256, 256), 256)],
                                     s_t.at[0, lax.rem(i, 2)])

    def t2_copy(e, i):
        return pltpu.make_async_copy(st2.at[lax.rem(i, 2)], t2_o.at[e, pl.ds(pl.multiple_of(i * 256, 256), 256)],
                                     s_t.at[1, lax.rem(i, 2)])

    def t1_terms(e):
        @pl.loop(0, n1)
        def _(i):
            @pl.when(i >= 2)
            def _():
                t1_copy(e, i).wait()
            col = pl.ds(pl.multiple_of(i * 256, 256), 256)
            st1[lax.rem(i, 2)] = dot_tn(xs[e, :, col], hs[e]).astype(BF)
            t1_copy(e, i).start()

        for i in range(2):
            t1_copy(e, i).wait()
        cubes[2 * e].down(0).start()

    def t2_terms(e):
        @pl.loop(0, n2)
        def _(i):
            @pl.when(i >= 2)
            def _():
                t2_copy(e, i).wait()
            col = pl.ds(pl.multiple_of(i * 256, 256), 256)
            st2[lax.rem(i, 2)] = dot_tn(hgs[e, :, col], gs[e]).astype(BF)
            t2_copy(e, i).start()

        for i in range(2):
            t2_copy(e, i).wait()

    row_ids = lax.broadcasted_iota(jnp.int32, (capp, T), 0).astype(F32)

    @pl.loop(0, C)
    def _(j):
        b, dr_b, dist_b = visit(c, C, j)
        cot_cp = pltpu.make_async_copy(cot_a.at[pl.ds(2 * b, 2)], cotb, s_loc.at[2])
        cot_cp.start()

        base = pl.multiple_of(b * B, 16)
        gate_rows = [[None, None] for _ in range(el)]
        picks = []
        for kk in range(2):
            s = 2 * b + kk
            parts = []
            for e in range(el):
                hit = row_ids == sd[s, e:e + 1, :]
                gate_rows[e][kk] = jnp.sum(jnp.where(hit, sd[s, el + e:el + e + 1, :], 0.0), -1, keepdims=True)
                parts.append(jnp.where(hit, 1.0, 0.0).astype(BF))
            p2 = jnp.concatenate(parts, 0)
            picks.append(p2)
        cot_cp.wait()

        def spread(rows_of, dst):
            for kk in range(2):
                for n in range(0, D, 512):
                    val = dot(picks[kk], rows_of(kk, n)).astype(BF)
                    for e in range(el):
                        at = pl.ds(pl.multiple_of(base + kk * capp, 16), capp)
                        dst[e, at, n:n + 512] = val[e * capp:(e + 1) * capp]

        here = pl.ds(base, B)
        spread(lambda kk, n: cotb[kk, :, n:n + 512], gs)
        for e in range(el):
            for n in range(0, FFW, 256):
                us[e, :, n:n + 256] = dot_nt(gs[e, here, :], wd[e, n:n + 256, :])

        @pl.when(j >= 1)
        def _():
            for dr in range(2):
                @pl.when(has(dr, j))
                def _():
                    for h in range(2):
                        z_in(dr, j, h).wait_recv()

                        @pl.when(nxt_ok(dr) & (j < C - 1))
                        def _():
                            z_out(dr, j + 1, h).start()
                    sib_out(dr, j).start()
        sib_in(dr_b, dist_b).wait_recv()
        spread(lambda kk, n: fa[2 * b + kk, :, n:n + 512], xs)
        gp_rows = []
        for e in range(el):
            gate_row = jnp.concatenate(gate_rows[e], 0)
            gpr = jnp.zeros((B, 1), F32)
            for n in range(0, FFW, 256):
                gv = dot(xs[e, here, :], wg[e, :, n:n + 256])
                uv = dot(xs[e, here, :], wu[e, :, n:n + 256])
                u = us[e, :, n:n + 256]
                sg = 1.0 / (1.0 + jnp.exp(-gv))
                act = gv * sg
                hid = act * uv
                gpr = gpr + jnp.sum(hid * u, -1, keepdims=True)
                hgs[e, here, n:n + 256] = (hid * gate_row).astype(BF)
                gh = u * gate_row
                hs[e, here, n:n + 256] = (gh * uv * (sg * (1.0 + gv * (1.0 - sg)))).astype(BF)
                hs[e, here, FFW + n:FFW + n + 256] = (gh * act).astype(BF)
            gp_rows.append(gpr)
            for n in range(0, D, 512):
                irow = (dot_nt(hs[e, here, 0:FFW], wg[e, n:n + 512, :])
                        + dot_nt(hs[e, here, FFW:2 * FFW], wu[e, n:n + 512, :])).astype(BF)
                for kk in range(2):
                    irb[kk, e * capp:(e + 1) * capp, n:n + 512] = irow[kk * capp:(kk + 1) * capp]

        @pl.when(j >= 2)
        def _():
            before, _, _ = visit(c, C, j - 2)
            for h in range(2):
                handed(before, lax.rem(j, 2), h).wait_send()
        for h in range(2):
            for kk in range(2):
                def combine(dst):
                    cut = halves[h]
                    dst[:, cut] = dot_tn(picks[kk], irb[kk, :, cut]).astype(BF)

                @pl.when(k == kk)
                def _():
                    combine(acc.at[b])

                @pl.when(k != kk)
                def _():
                    combine(give.at[lax.rem(j, 2)])
                    handed(b, lax.rem(j, 2), h).start()

        @pl.when(j == C - 1)
        def _():
            reduce_step(1)
            for e in range(el):
                t1_terms(e)
        for e in range(el):
            for n in range(0, D, 512):
                orow = dot(hgs[e, here, :], wd[e, :, n:n + 512]).astype(BF)
                for kk in range(2):
                    orb[kk, e * capp:(e + 1) * capp, n:n + 512] = orow[kk * capp:(kk + 1) * capp]

        def back(bb):
            return pltpu.make_async_copy(st_o, out_o.at[pl.ds(2 * bb, 2)], s_loc.at[3])

        @pl.when(j >= 1)
        def _():
            back(0).wait()
        for kk in range(2):
            s = 2 * b + kk
            for e in range(el):
                hit = picks[kk][e * capp:(e + 1) * capp].astype(F32)
                gp_o[s, e:e + 1, :] = jnp.sum(hit * gp_rows[e][kk * capp:(kk + 1) * capp], 0, keepdims=True)
            for n in range(0, D, 512):
                st_o[kk, :, n:n + 512] = dot_tn(picks[kk], orb[kk, :, n:n + 512]).astype(BF)
        back(b).start()

    if C > 2:
        reduce_step(2)
    for e in range(el):
        t2_terms(e)
    for s in range(3, C):
        reduce_step(s)
    for line in lines:
        line.last()
    gin_o[...] = acc[c]

    pltpu.make_async_copy(st_o, out_o.at[pl.ds(0, 2)], s_loc.at[3]).wait()
    for j in range(max(C - 2, 0), C):
        chip, _, _ = visit(c, C, j)
        for h in range(2):
            handed(chip, j % 2, h).wait_send()
    for line in lines:
        for s in range(1, C):
            for dr in range(2):
                chip, ok = line.dest(dr, s)

                @pl.when(ok)
                def _():
                    line.z_copy(dr, s, chip).wait_send()
    for cube in cubes[::2]:
        cube.down(0).wait()
    sib_own.wait_send()
    for dr in range(2):
        for s in range(1, C):
            @pl.when(has(dr, s))
            def _():
                sib_out(dr, s).wait_send()
        for s in range(1, C):
            @pl.when(nxt_ok(dr) & has(dr, s - 1))
            def _():
                for h in range(2):
                    z_out(dr, s, h).wait_send()


def experts_call(nf, nd, cap, ffn_in, cot_all, side, w_gate, w_up, w_down):
    T, D = ffn_in.shape
    el, _, FFW = w_gate.shape
    capp = cap + (-cap % 16)
    C = nf // 2
    rows = C * 2 * capp
    land_hbm = C > 4
    dma = pltpu.SemaphoreType.DMA
    out = [((nf, T, D), BF, 1), ((T, D), BF, 0), ((nf, el, T), F32, 0),
           ((el, D, 2 * FFW), BF, 1), ((el, FFW, D), BF, 1),
           ((el, D // 2, 2 * FFW), BF, 1)]
    lands = [(C, T, D), (2, C - 1, T, D)]
    scratch = []
    if land_hbm:
        out += [(x, BF, 1) for x in lands]
    else:
        scratch += [VMEM(x, BF) for x in lands]
    scratch += [
        VMEM((C, T, D), BF),
        VMEM((el, D, FFW), BF), VMEM((el, D, FFW), BF), VMEM((el, FFW, D), BF),
        VMEM((nf, T, D), BF), VMEM(side.shape, F32), VMEM((2, T, D), BF),
        VMEM((el, rows, D), BF), VMEM((el, rows, D), BF),
        VMEM((el, rows, 2 * FFW), BF), VMEM((el, rows, FFW), BF),
        VMEM((2, el * capp, D), BF), VMEM((2, el * capp, D), BF),
        VMEM((2, T, D), BF), VMEM((2, T, D), BF),
        VMEM((2, 256, 2 * FFW), BF), VMEM((2, 256, D), BF),
        VMEM((T, D) if land_hbm else (16, 128), BF),
        VMEM((el, 2 * capp, FFW), F32),
        dma((nf,)), dma((nf,)),
        dma((2, 2, C)), dma((2, 2, C)), dma((2, C)), dma((2, C)),
        dma((3,)), dma((5,)), dma((2, 2)),
        dma((2, C)), dma((2, C)), dma((2, 2, C)), dma((2, 2, C)), dma(()),
        dma((2 * el, 2 * (nd.bit_length() - 1))), dma((2 * el, 2 * (nd.bit_length() - 1))),
    ]
    return pl.pallas_call(
        functools.partial(experts_kernel, nf, nd, el, cap, capp, land_hbm),
        out_shape=[jax.ShapeDtypeStruct(o[0], o[1]) for o in out],
        in_specs=[vm(), hbm(), vm(), hbm(), hbm(), hbm()],
        out_specs=[hbm() if o[2] else vm() for o in out],
        scratch_shapes=scratch,
        compiler_params=pltpu.CompilerParams(collective_id=2, has_side_effects=True,
                                             vmem_limit_bytes=63 * 2 ** 20),
        cost_estimate=pl.CostEstimate(flops=40_000_000_000, bytes_accessed=60_000_000, transcendentals=2_000_000),
        name="experts",
    )(ffn_in, cot_all, side, w_gate, w_up, w_down)[:6]


def back_kernel(nf, nd, el, land_hbm, split, *refs):
    m = nd.bit_length() - 1
    it = iter(refs)

    def take(n):
        return [next(it) for _ in range(n)]

    (gin, out_p, gp_p, t1, t2, f1, tok_h, cot_h, hid_h, ffn_h, gates, mix_h, qk_h, v_h, prob_h, wf_h, rt,
     cosr, sinr) = take(19)
    out_o, gt_o, sh_o, sm_o, t1_o, t2_o = take(6)
    l1 = [f1] + take(m - 1)
    l2 = take(m)
    a1 = take(m - 1)
    a2 = take(m - 1)
    sibo, rcvo, sib, rcv, sibq, rcvq = take(6)
    (acc, wb, wg, tok, cot, hid, ffn, mix, qk, v, prob, branch, gh, ga, gproj, gpb, smg, smr, smd, sms) = take(20)
    attn, gm = ffn, mix
    shl = take(m * (2 if split else 1))
    if split:
        xo = next(it)
        xol = take(m)
    stage, stageq = take(2)
    (s_load, s_acc, s_gp, r_gp, s_sib, r_sib, s_z, r_z, s_cube, r_cube, s_sc, r_sc, s_sm, r_sm, s_sd, r_sd,
     s_stage, s_prob) = take(18)

    T, D = tok.shape
    R = wg.shape[0] // nf
    W = wg.shape[1]
    E = gates.shape[0]
    C = nf // 2
    f = lax.axis_index("fsdp")
    d = lax.axis_index("dp")
    c = f // 2
    k = lax.rem(f, 2)
    QV = QW + 2 * KW
    QZ, OW = QV, D
    greet(nf, nd, f, d)

    def remote(src, dst, ss, rs, to_f, to_d):
        return pltpu.make_async_remote_copy(src_ref=src, dst_ref=dst, send_sem=ss, recv_sem=rs,
                                            device_id=(to_f, to_d), device_id_type=MESH)

    def rows(ff):
        return pl.ds(pl.multiple_of(ff * R, 16), R)


    def sems(i):
        return (s_sib.at[i], r_sib.at[i], s_z.at[i], r_z.at[i])

    def lines_of(first, cuts, sb, rc, sg, ids):
        res = []
        for h, (top, n) in enumerate(cuts):
            cut, loc = pl.ds(first + top, n), pl.ds(top, n)
            res.append(Line(nf, f, d, lambda ch, cut=cut: wg.at[rows(2 * ch + k), cut],
                            lambda ch, cut=cut: wg.at[rows(2 * ch + 1 - k), cut],
                            lambda ch, loc=loc: sb.at[ch, :, loc], lambda dr, s, loc=loc: rc.at[dr, s, :, loc],
                            sg.at[:, loc] if land_hbm else None, sems(ids[h]), s_stage))
        return res

    if split:
        o_lines = []
        pair = Line(nf, f, d, None, lambda ch: wg.at[rows(2 * ch + 1 - k), QZ:W], lambda ch: sib.at[ch], None, None,
                    sems(0), s_stage)
        o_cubes = []
        for h in range(2):
            top = h * (C * R // 2)
            cube = Cube(nd, f, d, h == 1, True, OW, xo.at[top:top + C * R // 2],
                        functools.partial(lambda h, i: xol[i].at[h], h), None, None, (s_sc.at[h], r_sc.at[h]))
            cube.in_place, cube.whole = True, False
            o_cubes.append(cube)
        o_low = [cube.low[m] for cube in o_cubes]

        def o_block(ch):
            low = pl.multiple_of(jnp.where(ch < C // 2, o_low[0], o_low[1]), 128)
            return xo.at[pl.ds(pl.multiple_of(ch * R, 16), R), pl.ds(low, OW >> m)]

        o_line = Line(nf, f, d, o_block, None, None, lambda dr, s: rcv.at[dr, s], None, sems(1), s_stage)
        o_up = Cube(nd, f, d, c >= C // 2, True, OW, None, None, None, sh_o.at[:, QZ:W], (s_sc.at[2], r_sc.at[2]))
    else:
        o_lines = lines_of(QV, ((0, D // 2), (D // 2, D // 2)), sib, rcv, stage.at[0:R], (0, 1))
    q_cuts = ((0, QW), (QW, 2 * KW))
    q_lines = lines_of(0, q_cuts, sibq, rcvq, stageq, (2, 4))
    out_line = Line(nf, f, d, lambda ch: acc.at[ch], lambda ch: out_p.at[2 * ch + 1 - k], lambda ch: sibo.at[ch],
                    lambda dr, s: rcvo.at[dr, s], stage, sems(3), s_stage)

    def acc_loads(src):
        return [pltpu.make_async_copy(src.at[2 * ch + k], acc.at[ch], s_acc.at[ch]) for ch in range(C)]

    gp_copies = []
    for i in range(1, nf):
        to = lax.rem(f + i, nf)
        cp = remote(gp_p.at[to], gpb.at[f], s_gp.at[i - 1], r_gp.at[i - 1], to, d)
        cp.start()
        gp_copies.append(cp)
    out_line.start_sib()
    out_loads = acc_loads(out_p)
    for cp in out_loads:
        cp.start()
    cubes = term_cubes(nd, el, f, d, t1, t2, t1_o, t2_o, l1, l2, a1, a2, (s_cube, r_cube))
    first_terms, second_terms = cubes[::2], cubes[1::2]
    for cube in second_terms:
        cube.down(0).start()
    own_gp = pltpu.make_async_copy(gp_p.at[f], gpb.at[f], s_load.at[0])
    own_gp.start()
    wo = pltpu.make_async_copy(wf_h.at[:, QV:QV + D], wb.at[:, 0:D], s_load.at[1])
    wo.start()
    others = [(tok_h, tok), (cot_h, cot), (hid_h, hid), (ffn_h, ffn), (mix_h, mix), (qk_h, qk), (v_h, v)]
    more = [pltpu.make_async_copy(a, b, s_load.at[2 + i]) for i, (a, b) in enumerate(others)]
    for cp in more:
        cp.start()

    def prob_load(i):
        at = pl.ds(i * 2 * GROUP, 2 * GROUP)
        return pltpu.make_async_copy(prob_h.at[at], prob.at[lax.rem(i, 2)], s_prob.at[lax.rem(i, 2)])

    prob_load(0).start()

    def onward(cube, i):
        cube.down(i + 1).start() if i + 1 < m else cube.up(i).start()

    def chain(group, start, add):
        def merged(i):
            for cube in group:
                cube.merge(i, add)
                onward(cube, i)

        def raised(i):
            for cube in group:
                cube.up_in(i).wait_recv()
                cube.up(i - 1).start()

        return ([functools.partial(merged, i) for i in range(start, m)]
                + [functools.partial(raised, i) for i in range(m - 1, 0, -1)])

    def vadd(dst, a, b):
        add_blocks(dst, [a, b])

    def run(steps, n=1):
        for _ in range(min(n, len(steps))):
            steps.pop(0)()

    steps1, steps2 = chain(first_terms, 1, pipe_add), chain(second_terms, 0, pipe_add)
    for cube in first_terms:
        cube.fold(0, pipe_add)
        onward(cube, 0)
    for cp in out_loads:
        cp.wait()
    out_line.step(1)
    for cp in more:
        cp.wait()
    own_gp.wait()
    for cp in gp_copies:
        cp.wait()

    gains = rt[E:E + 2].astype(F32)
    gain_one, gain_two = gains[0:1], gains[1:2]
    gpt = jnp.concatenate([gpb[i] for i in range(nf)], 0)
    gates_v = gates[...]
    gl = (gates_v * (gpt - jnp.sum(gpt * gates_v, 0, keepdims=True))).astype(BF)
    for n in range(0, D, 512):
        sms[0:E, n:n + 512] = dot(gl, ffn[:, n:n + 512])
    for n in range(0, D, 512):
        ga[:, n:n + 512] = dot_tn(gl, rt[0:E, n:n + 512])
    sms[E:, :] = jnp.zeros((sms.shape[0] - E, D), F32)
    TR = 32

    @pl.loop(0, T // TR)
    def _(i):
        at = pl.ds(pl.multiple_of(i * TR, TR), TR)
        h = hid[at, :]
        r2 = lax.rsqrt(jnp.mean(h * h, -1, keepdims=True) + EPSILON)
        n2 = h * r2
        gf = gin[at, :].astype(F32) + ga[at, :]
        sms[E + 1:E + 2, :] += jnp.sum(gf * n2, 0, keepdims=True)
        g2 = gf * gain_two
        x = cot[at, :].astype(F32) + r2 * (g2 - n2 * jnp.mean(g2 * n2, -1, keepdims=True))
        gh[at, :] = x
        branch[at, :] = x.astype(BF)

    @pl.loop(0, QW // 256)
    def _(i):
        at = pl.ds(pl.multiple_of(i * 256, 256), 256)
        wg[at, QV:QV + D] = dot_tn(mix[:, at], branch[...]).astype(BF)
    if split:
        pair.start_sib()
        if C > 2:
            out_line.step(2)
    else:
        for line in o_lines:
            line.start_sib()
        for line in o_lines:
            line.step(1)
    wo.wait()

    @pl.loop(0, QW // 256)
    def _(i):
        at = pl.ds(pl.multiple_of(i * 256, 256), 256)
        gm[:, at] = dot_nt(branch[...], wb[at, 0:D]).astype(BF)
    wq = pltpu.make_async_copy(wf_h.at[:, 0:QV], wb, s_load.at[1])
    wq.start()
    if split:
        for ch in range(C):
            pair.sib_copy(ch).wait_recv()
            add_blocks(xo.at[ch * R:(ch + 1) * R], [wg.at[rows(2 * ch + k), QZ:W], sib.at[ch]])
        for cube in o_cubes:
            cube.down(0).start()
    run(steps2)
    factor = HEAD_SIZE ** (-0.5)
    lane = lax.broadcasted_iota(jnp.int32, (T, 128), 1)
    low = lane < HEAD_SIZE
    first = lax.rem(lane, HEAD_SIZE) < HEAD_SIZE // 2

    def unrotate(x):
        return x * cosr[...] - half_roll(x, first) * sinr[...]

    @pl.loop(0, KEY_VALUE_HEADS // 2)
    def _(i):
        @pl.when(i + 1 < KEY_VALUE_HEADS // 2)
        def _():
            prob_load(i + 1).start()
        prob_load(i).wait()
        slot = lax.rem(i, 2)
        kcol = pl.ds(pl.multiple_of(i * 128, 128), 128)
        kh = head_masks(qk[:, pl.ds(pl.multiple_of(QW + i * 128, 128), 128)], lane)
        vh = head_masks(v[:, kcol], lane)
        gk = [[None, None], [None, None]]
        gv = [[None, None], [None, None]]
        for p in range(GROUP):
            qc = pl.ds(pl.multiple_of((i * GROUP + p) * 128, 128), 128)
            q = qk[:, qc]
            g = gm[:, qc]
            gq = None
            for half in range(2):
                kv = (2 * p + half) // GROUP
                pr = prob[slot, 2 * p + half]
                prf = pr.astype(F32)
                gp = dot_nt(g, vh[kv][half])
                gs = (prf * (gp - jnp.sum(prf * gp, -1, keepdims=True))).astype(BF)
                term = dot(gs, kh[kv][half])
                gq = term if gq is None else gq + term
                tk = dot_tn(gs, q)
                tv = dot_tn(pr, g)
                gk[kv][half] = tk if gk[kv][half] is None else gk[kv][half] + tk
                gv[kv][half] = tv if gv[kv][half] is None else gv[kv][half] + tv
            gproj[:, qc] = unrotate(gq * factor).astype(BF)

        def join(x):
            a = jnp.where(low, x[0][0] + pltpu.roll(x[0][1], HEAD_SIZE, axis=1), 0.0)
            b = jnp.where(low, 0.0, pltpu.roll(x[1][0], HEAD_SIZE, axis=1) + x[1][1])
            return a + b

        gproj[:, pl.ds(pl.multiple_of(QW + i * 128, 128), 128)] = unrotate(join(gk) * factor).astype(BF)
        gproj[:, pl.ds(pl.multiple_of(QW + KW + i * 128, 128), 128)] = join(gv).astype(BF)

        if C > 2:
            @pl.when(i == 1)
            def _():
                for line in o_lines:
                    line.step(2)


    def o_merge(i):
        for cube in o_cubes:
            cube.merge(i, vadd)
            if i + 1 < m:
                cube.down(i + 1).start()

    @pl.loop(0, T // TR)
    def _(i):
        at = pl.ds(pl.multiple_of(i * TR, TR), TR)
        x = tok[at, :].astype(F32)
        r1 = lax.rsqrt(jnp.mean(x * x, -1, keepdims=True) + EPSILON)
        attn[at, :] = (x * r1 * gain_one).astype(BF)

    for line, (top, width) in zip(q_lines, q_cuts):
        @pl.loop(0, D // 256)
        def _(i):
            at = pl.ds(pl.multiple_of(i * 256, 256), 256)
            for n in range(top, top + width, 512):
                wg[at, n:n + 512] = dot_tn(attn[:, at], gproj[:, n:n + 512]).astype(BF)
        line.start_sib()
        if line is q_lines[0]:
            for s in range(3, C):
                for other in o_lines:
                    other.step(s)
        line.step(1)
    run(steps1)
    run(steps2)
    if split:
        o_merge(0)
    wq.wait()

    @pl.loop(0, D // 256)
    def _(i):
        at = pl.ds(pl.multiple_of(i * 256, 256), 256)
        ga[:, at] = dot_nt(gproj[...], wb[at, :])

    @pl.loop(0, T // TR)
    def _(i):
        at = pl.ds(pl.multiple_of(i * TR, TR), TR)
        x = tok[at, :].astype(F32)
        r1 = lax.rsqrt(jnp.mean(x * x, -1, keepdims=True) + EPSILON)
        n1 = x * r1
        gat = ga[at, :]
        sms[E:E + 1, :] += jnp.sum(gat * n1, 0, keepdims=True)
        g1 = gat * gain_one
        gt_o[at, :] = (gh[at, :] + r1 * (g1 - n1 * jnp.mean(g1 * n1, -1, keepdims=True))).astype(BF)

    small = sms[...]
    for i in range(nf):
        smg[i] = small[:, i * R:(i + 1) * R]
    sm_copies = []
    for i in range(1, nf):
        to = lax.rem(f + i, nf)
        cp = remote(smg.at[to], smr.at[f], s_sm.at[i - 1], r_sm.at[i - 1], to, d)
        cp.start()
        sm_copies.append(cp)
    smr_own = pltpu.make_async_copy(smg.at[f], smr.at[f], s_load.at[0])
    smr_own.start()

    for line in o_lines:
        line.last()
    lates = []
    for g, (left, width) in enumerate(q_cuts if split else ((0, W),)):
        late = []
        for h in range(2):
            top = h * (R // 2)
            own = wg.at[pl.ds(pl.multiple_of(f * R + top, 16), R // 2), left:left + width]
            cube = Cube(nd, f, d, h == 1, True, width, own, functools.partial(lambda g, h, i: shl[g * m + i].at[h], g, h),
                        None, sh_o.at[top:top + R // 2, left:left + width], (s_sc.at[3 + 2 * g + h], r_sc.at[3 + 2 * g + h]))
            cube.in_place = True
            late.append(cube)
        lates.append(late)
    steps_l = [chain(late, 0, vadd) for late in lates]
    run(steps1)
    run(steps2)
    if C > 2:
        for line in q_lines:
            line.step(2)
    if split:
        for i in range(1, m):
            o_merge(i)
        o_line.step(1)
    if split:
        if C > 2:
            o_line.step(2)
        pair.sent()
    for line in o_lines:
        line.sent()
    smr_own.wait()
    for cp in sm_copies:
        cp.wait()
    total = smr[0]
    for i in range(1, nf):
        total = total + smr[i]
    smd[0] = total
    sd_copies = []
    for i in range(1, nd):
        cp = remote(smd.at[0], smd.at[i], s_sd.at[i - 1], r_sd.at[i - 1], f, jnp.bitwise_xor(d, i))
        cp.start()
        sd_copies.append(cp)
    for s in range(3, C):
        for line in q_lines:
            line.step(s)
    if not split and C > 2:
        out_line.step(2)
    run(steps1, len(steps1))
    run(steps2, len(steps2))
    if split:
        for s in range(3, C):
            o_line.step(s)
        o_line.last()
        add_blocks(sh_o.at[:, pl.ds(pl.multiple_of(QZ + o_up.low[m], 128), OW >> m)], [o_block(c)])
        o_up.up(m - 1).start()
    for g, line in enumerate(q_lines):
        line.last()
        if split or line is q_lines[-1]:
            for cube in lates[g if split else 0]:
                cube.down(0).start()
    for s in range(3, C):
        out_line.step(s)
    if split:
        for i in range(m - 1, 0, -1):
            o_up.up_in(i).wait_recv()
            o_up.up(i - 1).start()
    while steps_l[-1]:
        for steps in steps_l:
            run(steps)
    for cp in sd_copies:
        cp.wait()
    total = smd[0]
    for i in range(1, nd):
        total = total + smd[i]
    sm_o[...] = total
    out_line.last()

    @pl.loop(0, T // TR)
    def _(i):
        at = pl.ds(pl.multiple_of(i * TR, TR), TR)
        out_o[at, :] = (hid[at, :] + acc[c, at, :].astype(F32)).astype(BF)


    for line in q_lines:
        line.sent()
    out_line.sent()
    for i, cube in enumerate(cubes):
        cube.up_in(0).wait_recv()
        cube.sent(1 - i % 2)
    if split:
        o_up.up_in(0).wait_recv()
        o_line.sent()
        for i in range(m):
            o_up.up(i).wait_send()
            for cube in o_cubes:
                cube.down(i).wait_send()
    for cube in [cube for late in lates for cube in late]:
        cube.up_in(0).wait_recv()
        cube.sent()


def back(nf, nd, el, args):
    gin, t1, t2 = args[0], args[3], args[4]
    T, D = gin.shape
    E = args[10].shape[0]
    W = args[15].shape[1]
    R = D // nf
    C = nf // 2
    m = nd.bit_length() - 1
    QV = QW + 2 * KW
    FFW = t2.shape[1]
    SR = E + 2 + (-(E + 2) % 8)
    land_hbm = C > 4
    s = jax.ShapeDtypeStruct
    out_shape = [s((T, D), BF), s((T, D), BF), s((R, W), BF), s((SR, R), F32), s(t1.shape, BF), s(t2.shape, BF)]
    out_specs = [vm(), vm(), vm(), vm(), hbm(), hbm()]
    extra = [(el, D >> (i + 1), t1.shape[2]) for i in range(1, m)] + [(el, FFW >> (i + 1), D) for i in range(m)]
    extra += [(el, D >> (i + 1), t1.shape[2]) for i in range(m - 1)] + [(el, FFW >> (i + 1), D) for i in range(m - 1)]
    extra += [(C, T, D), (2, C - 1, T, D)]
    QZ, OW = QV, D
    split = not land_hbm and (OW >> m) % 128 == 0 and (QW >> m) % 128 == 0 and (2 * KW >> m) % 128 == 0
    lands = [(C, R, OW), (2, C - 1, R, OW >> m if split else D), (C, R, QZ), (2, C - 1, R, QZ)]
    scratch = []
    if land_hbm:
        extra += lands
    else:
        scratch += [VMEM(x, BF) for x in lands]
    out_shape += [s(x, BF) for x in extra]
    out_specs += [hbm()] * len(extra)
    dma = pltpu.SemaphoreType.DMA
    scratch += [
        VMEM((C, T, D), BF), VMEM((D, QV), BF), VMEM((D, W), BF),
        VMEM((T, D), BF), VMEM((T, D), BF), VMEM((T, D), F32), VMEM((T, D), BF), VMEM((T, QW), BF),
        VMEM((T, QW + KW), BF), VMEM((T, KW), BF), VMEM((2, 2 * GROUP, T, T), BF),
        VMEM((T, D), BF), VMEM((T, D), F32), VMEM((T, D), F32), VMEM((T, QV), BF),
        VMEM((nf, el, T), F32), VMEM((nf, SR, R), F32), VMEM((nf, SR, R), F32), VMEM((nd, SR, R), F32),
        VMEM((SR, D), F32),
    ]
    for n in ((QW, 2 * KW) if split else (W,)):
        scratch += [VMEM((2, R // 2, n >> (i + 1)), BF) for i in range(m)]
    if split:
        scratch += [VMEM((C * R, OW), BF)] + [VMEM((2, C * R // 2, OW >> (i + 1)), BF) for i in range(m)]
    scratch += [VMEM((T, D), BF), VMEM((R, QV) if land_hbm else (16, 128), BF)]
    scratch += [
        dma((10,)), dma((C,)), dma((nf,)), dma((nf,)),
        dma((5, C)), dma((5, C)), dma((5, 2, C)), dma((5, 2, C)),
        dma((2 * el, 2 * m)), dma((2 * el, 2 * m)), dma((7, 2 * m)), dma((7, 2 * m)),
        dma((nf,)), dma((nf,)), dma((nd,)), dma((nd,)), dma(()), dma((2,)),
    ]
    inner = [vm(), hbm(), vm(), hbm(), hbm(), hbm(), hbm(), hbm(), hbm(), hbm(), vm(), hbm(), hbm(), hbm(), hbm(), hbm(), vm(),
             vm(), vm()]
    return pl.pallas_call(
        functools.partial(back_kernel, nf, nd, el, land_hbm, split),
        out_shape=out_shape,
        in_specs=inner,
        out_specs=out_specs,
        scratch_shapes=scratch,
        compiler_params=pltpu.CompilerParams(collective_id=3, has_side_effects=True,
                                             vmem_limit_bytes=63 * 2 ** 20),
        cost_estimate=pl.CostEstimate(flops=8_000_000_000, bytes_accessed=90_000_000, transcendentals=100_000),
        name="back",
    )(*args)[:6]


def body(tokens, w_query, key_weight, value_weight, w_out, gain_attn, gain_ffn, w_router,
         w_gate, w_up, w_down, routes, cotangent):
    T = tokens.shape[0]
    el = w_gate.shape[0]
    nf = lax.axis_size("fsdp")
    nd = lax.axis_size("dp")
    experts = el * nf
    cap = 9 * T * TOP // (8 * experts)

    pad = -(experts + 2) % 16
    small = jnp.concatenate([w_router, gain_attn[:, None], gain_ffn[:, None],
                             jnp.zeros((w_router.shape[0], pad), BF)], 1).T
    onehot = (routes[:, :, None] == jnp.arange(experts, dtype=jnp.int32)).any(1).astype(BF)
    earlier = (jnp.arange(T)[:, None] < jnp.arange(T)[None, :]).astype(BF)
    before = lax.dot_general(onehot, earlier, (((0,), (0,)), ((), ())), preferred_element_type=F32)
    slots = jnp.where(onehot.T > 0, before, -1.0)
    cosr, sinr = rope_rows(T)
    ffn_in, hidden, gates, side, mixed, qk, v, probs, full, cot_all, rt = front(
        nf, nd, experts, tokens, (w_query, key_weight, value_weight, w_out), small, cotangent, slots, cosr, sinr)
    out_part, gin, gp_part, t1, t2, f1 = experts_call(nf, nd, cap, ffn_in, cot_all, side, w_gate, w_up, w_down)
    output, grad_tokens, shard, smalls, t1, t2 = back(nf, nd, el, (
        gin, out_part, gp_part, t1, t2, f1, tokens, cotangent, hidden, ffn_in, gates, mixed, qk, v, probs, full, rt,
        cosr, sinr))
    big = shard.astype(F32)
    ff = w_gate.shape[2]
    return (
        output,
        grad_tokens,
        big[:, :QW],
        big[:, QW: QW + KW],
        big[:, QW + KW: QW + 2 * KW],
        big[:, QW + 2 * KW:],
        smalls[experts],
        smalls[experts + 1],
        smalls[:experts].T,
        t1[:, :, :ff].astype(F32),
        t1[:, :, ff:].astype(F32),
        t2.astype(F32),
    )


def solution(mesh):
    in_specs = (
        P(("fsdp", "dp"), None),
        P("fsdp", None),
        P("fsdp", None),
        P("fsdp", None),
        P("fsdp", None),
        P("fsdp"),
        P("fsdp"),
        P("fsdp", None),
        P("fsdp", None, None),
        P("fsdp", None, None),
        P("fsdp", None, None),
        P(("fsdp", "dp"), None),
        P(("fsdp", "dp"), None),
    )
    out_specs = (
        P(("fsdp", "dp"), None),
        P(("fsdp", "dp"), None),
        P("fsdp", None),
        P("fsdp", None),
        P("fsdp", None),
        P("fsdp", None),
        P("fsdp"),
        P("fsdp"),
        P("fsdp", None),
        P("fsdp", None, None),
        P("fsdp", None, None),
        P("fsdp", None, None),
    )
    return jax.shard_map(body, mesh=mesh, in_specs=in_specs, out_specs=out_specs, check_vma=False)
```

```python
import functools
import jax
import jax.numpy as jnp
from jax import lax
from jax.experimental import pallas as pl
from jax.experimental.pallas import tpu as pltpu
from jax.sharding import PartitionSpec as P
import numpy as np

MODEL_WIDTH = 1536
QUERY_HEADS = 24
KEY_VALUE_HEADS = 8
HEAD_SIZE = 64
TOP = 8
GROUP = QUERY_HEADS // KEY_VALUE_HEADS
QW = QUERY_HEADS * HEAD_SIZE
KW = KEY_VALUE_HEADS * HEAD_SIZE

EPSILON = 1e-06
ROPE_BASE = 10000.0
MASKED = -1e30
F32 = jnp.float32
BF = jnp.bfloat16


def rope_rows(T):
    half = HEAD_SIZE // 2
    freq = ROPE_BASE ** (-2.0 * np.arange(half, dtype=np.float64) / HEAD_SIZE)
    ang = (np.arange(T, dtype=np.float32)[:, None] * freq.astype(np.float32)[None, :]).astype(np.float32)
    c, s = np.cos(ang), np.sin(ang)
    return (jnp.asarray(np.concatenate([c, c, c, c], 1), F32), jnp.asarray(np.concatenate([-s, s, -s, s], 1), F32))


MESH = pl.DeviceIdType.MESH
VMEM = pltpu.VMEM


def vm():
    return pl.BlockSpec(memory_space=pltpu.VMEM)


def hbm():
    return pl.BlockSpec(memory_space=pl.ANY)


def dot(a, b):
    return lax.dot_general(a, b, (((1,), (0,)), ((), ())), preferred_element_type=F32)


def dot_nt(a, b):
    return lax.dot_general(a, b, (((1,), (1,)), ((), ())), preferred_element_type=F32)


def dot_tn(a, b):
    return lax.dot_general(a, b, (((0,), (0,)), ((), ())), preferred_element_type=F32)


def half_roll(x, first):
    n = x.shape[1]
    h = HEAD_SIZE // 2
    return jnp.where(first, pltpu.roll(x, n - h, axis=1), pltpu.roll(x, h, axis=1))


def greet(nf, nd, f, d):
    barrier = pltpu.get_barrier_semaphore()
    for i in range(1, nf):
        pl.semaphore_signal(barrier, inc=1, device_id=(lax.rem(f + i, nf), d), device_id_type=MESH)
    for i in range(1, nd):
        pl.semaphore_signal(barrier, inc=1, device_id=(f, jnp.bitwise_xor(d, i)), device_id_type=MESH)
    pl.semaphore_wait(barrier, nf + nd - 2)


def head_masks(kblk, lane):
    kf = kblk.astype(F32)
    kr = pltpu.roll(kf, HEAD_SIZE, axis=1)
    low = lane < HEAD_SIZE
    zero = jnp.zeros_like(kf)
    a0 = jnp.where(low, kf, zero).astype(BF)
    a1 = jnp.where(low, zero, kr).astype(BF)
    b0 = jnp.where(low, kr, zero).astype(BF)
    b1 = jnp.where(low, zero, kf).astype(BF)
    return ((a0, a1), (b0, b1))


def front_kernel(nf, nd, experts, tok, wq, wk, wv, wo, small, cot, slots, cosr, sinr,
                 ffn_o, hid_o, gates_o, side_o, mix_o, qk_o, v_o, prob_o, wf_o, cot_o, rt_o,
                 wf, sm, attn, rot,
                 s_sm, r_sm, s_z, r_z, s_dp, r_dp, s_sib, r_sib, s_cz, r_cz, s_cs, r_cs, s_loc, s_w):
    T, D = tok.shape
    C = nf // 2
    R = wq.shape[0]
    W = wf.shape[1]
    WA = 3 * W // 4
    parts = ((0, WA), (WA, W - WA))
    f = lax.axis_index("fsdp")
    d = lax.axis_index("dp")
    c = f // 2
    k = lax.rem(f, 2)
    sib = f + 1 - 2 * k
    greet(nf, nd, f, d)

    def rows(ff):
        return pl.ds(pl.multiple_of(ff * R, 16), R)

    def cols(dd, g):
        at, n = parts[g]
        return pl.ds(pl.multiple_of(at + dd * (n // nd), 128), n // nd)

    def remote(src, dst, ss, rs, to_f, to_d):
        return pltpu.make_async_remote_copy(src_ref=src, dst_ref=dst, send_sem=ss, recv_sem=rs,
                                            device_id=(to_f, to_d), device_id_type=MESH)

    def src_chip(dr, s):
        return c - s if dr == 0 else c + s

    def has(dr, s):
        return (c - s >= 0) if dr == 0 else (c + s < C)

    def nxt_ok(dr):
        return (c + 1 < C) if dr == 0 else (c - 1 >= 0)

    def nxt_f(dr):
        return f + 2 if dr == 0 else f - 2

    def wz(dr, s, g):
        blk = wf.at[rows(2 * src_chip(dr, s - 1) + k), cols(d, g)]
        return remote(blk, blk, s_z.at[g, dr, s - 1], r_z.at[g, dr, s - 1], nxt_f(dr), d)

    def wz_in(dr, s, g):
        blk = wf.at[rows(2 * src_chip(dr, s) + k), cols(d, g)]
        return remote(blk, blk, s_z.at[g, dr, s - 1], r_z.at[g, dr, s - 1], f, d)

    halves = (slice(0, D // 2), slice(D // 2, D))

    def cz(dr, s, own, h):
        ff = 2 * src_chip(dr, s - 1) + k
        src = cot.at[:, halves[h]] if own else cot_o.at[ff, :, halves[h]]
        return remote(src, cot_o.at[ff, :, halves[h]], s_cz.at[h, dr, s - 1], r_cz.at[h, dr, s - 1], nxt_f(dr), d)

    def cz_in(dr, s, h):
        blk = cot_o.at[2 * src_chip(dr, s) + k, :, halves[h]]
        return remote(blk, blk, s_cz.at[h, dr, s - 1], r_cz.at[h, dr, s - 1], f, d)

    def cs(dr, s):
        ff = 2 * src_chip(dr, s) + k
        return remote(cot_o.at[ff], cot_o.at[ff], s_cs.at[dr, s], r_cs.at[dr, s], sib, d)

    def cs_in(dr, s):
        ff = 2 * src_chip(dr, s) + 1 - k
        return remote(cot_o.at[ff], cot_o.at[ff], s_cs.at[dr, s], r_cs.at[dr, s], sib, d)

    at = 0
    w_own = []
    for i, w in enumerate((wq, wk, wv, wo)):
        w_own.append(pltpu.make_async_copy(w, wf.at[rows(f), at:at + w.shape[1]], s_w.at[i]))
        at += w.shape[1]
    for cp in w_own:
        cp.start()
    for cp in w_own:
        cp.wait()
    for g in range(2):
        for dr in range(2):
            @pl.when(nxt_ok(dr))
            def _():
                wz(dr, 1, g).start()
    own_small = pltpu.make_async_copy(small, sm.at[f], s_loc.at[0])
    own_small.start()
    sm_copies = []
    for i in range(1, nf):
        cp = remote(small, sm.at[f], s_sm.at[i - 1], r_sm.at[i - 1], lax.rem(f + i, nf), d)
        cp.start()
        sm_copies.append(cp)
    for dr in range(2):
        @pl.when((c if dr == 0 else C - 1 - c) == 0)
        def _():
            for h in range(2):
                cz(dr, 1, True, h).start()
    sib_own = remote(wf.at[rows(f)], wf.at[rows(f)], s_sib.at[0, 0, 0], r_sib.at[0, 0, 0], sib, d)
    sib_own.start()
    own_c = pltpu.make_async_copy(cot, cot_o.at[f], s_loc.at[2])
    own_c.start()
    sib_c = remote(cot, cot_o.at[f], s_cs.at[0, 0], r_cs.at[0, 0], sib, d)

    def dp_copy(dr, s, g, i):
        blk = wf.at[rows(2 * src_chip(dr, s) + k), cols(d, g)]
        return remote(blk, blk, s_dp.at[g, dr, s - 1, i - 1], r_dp.at[g, dr, s - 1, i - 1], f, jnp.bitwise_xor(d, i))

    def dp_in(dr, s, g, i):
        blk = wf.at[rows(2 * src_chip(dr, s) + k), cols(jnp.bitwise_xor(d, i), g)]
        return remote(blk, blk, s_dp.at[g, dr, s - 1, i - 1], r_dp.at[g, dr, s - 1, i - 1], f, d)

    def sib_copy(dr, s, g):
        at, n = parts[g]
        blk = wf.at[rows(2 * src_chip(dr, s) + k), at:at + n]
        return remote(blk, blk, s_sib.at[g, dr, s], r_sib.at[g, dr, s], sib, d)

    def sib_in(dr, s, g):
        at, n = parts[g]
        blk = wf.at[rows(2 * src_chip(dr, s) + 1 - k), at:at + n]
        return remote(blk, blk, s_sib.at[g, dr, s], r_sib.at[g, dr, s], sib, d)

    for s in range(1, C):
        for g in range(2):
            for dr in range(2):
                @pl.when(has(dr, s))
                def _():
                    wz_in(dr, s, g).wait_recv()
                    if s < C - 1:
                        @pl.when(nxt_ok(dr))
                        def _():
                            wz(dr, s + 1, g).start()
                    if g == 0:
                        for i in range(1, nd):
                            dp_copy(dr, s, g, i).start()
        for dr in range(2):
            @pl.when(nxt_ok(dr) & ((c if dr == 0 else C - 1 - c) == s))
            def _():
                for h in range(2):
                    cz(dr, 1, True, h).start()
    sib_c.start()
    for s in range(1, C):
        for dr in range(2):
            @pl.when(has(dr, s))
            def _():
                for i in range(1, nd):
                    dp_copy(dr, s, 1, i).start()

    def group_in(s, g):
        for dr in range(2):
            @pl.when(has(dr, s))
            def _():
                for i in range(1, nd):
                    dp_in(dr, s, g, i).wait_recv()
                sib_copy(dr, s, g).start()

    def cores_in(g):
        for s in range(1, C):
            for dr in range(2):
                @pl.when(has(dr, s))
                def _():
                    sib_in(dr, s, g).wait_recv()

    own_small.wait()
    for cp in sm_copies:
        cp.wait()
    Ds = small.shape[1]
    rt = jnp.concatenate([sm[i] for i in range(nf)], axis=1)
    rt_o[...] = rt
    gains = rt[experts:experts + 2].astype(F32)
    gain_one, gain_two = gains[0:1], gains[1:2]
    xf = tok[...].astype(F32)
    r1 = lax.rsqrt(jnp.mean(xf * xf, -1, keepdims=True) + EPSILON)
    attn[...] = (xf * r1 * gain_one).astype(BF)

    def cot_step(s):
        for dr in range(2):
            @pl.when(has(dr, s))
            def _():
                for h in range(2):
                    cz_in(dr, s, h).wait_recv()
                    if s < C - 1:
                        @pl.when(nxt_ok(dr))
                        def _():
                            cz(dr, s + 1, False, h).start()
                cs(dr, s).start()

    cot_step(1)
    for s in range(1, C - 1):
        group_in(s, 0)
    group_in(C - 1, 0)
    sib_own.wait()
    cores_in(0)

    first = lax.rem(lax.broadcasted_iota(jnp.int32, (T, 256), 1), HEAD_SIZE) < HEAD_SIZE // 2
    cs_t = jnp.concatenate([cosr[...], cosr[...]], 1)
    sn_t = jnp.concatenate([sinr[...], sinr[...]], 1)
    nqk = (QW + KW) // 256

    @pl.loop(0, nqk)
    def _(i):
        col = pl.ds(pl.multiple_of(i * 256, 256), 256)
        x = dot(attn[...], wf[:, col])
        qk_o[:, col] = (x * cs_t + half_roll(x, first) * sn_t).astype(BF)

    @pl.loop(0, KW // 256)
    def _(i):
        col = pl.ds(pl.multiple_of(QW + KW + i * 256, 256), 256)
        v_o[:, pl.ds(pl.multiple_of(i * 256, 256), 256)] = dot(attn[...], wf[:, col]).astype(BF)

    factor = HEAD_SIZE ** (-0.5)
    lane = lax.broadcasted_iota(jnp.int32, (T, 128), 1)
    keep = lax.broadcasted_iota(jnp.int32, (T, T), 1) <= lax.broadcasted_iota(jnp.int32, (T, T), 0)

    @pl.loop(0, KEY_VALUE_HEADS // 2)
    def _(i):
        if C > 2:
            @pl.when(i == 2)
            def _():
                cot_step(2)
        kc = pl.ds(pl.multiple_of(QW + i * 128, 128), 128)
        kh = head_masks(qk_o[:, kc], lane)
        vh = head_masks(v_o[:, pl.ds(pl.multiple_of(i * 128, 128), 128)], lane)
        for p in range(GROUP):
            qc = pl.ds(pl.multiple_of((i * GROUP + p) * 128, 128), 128)
            q = qk_o[:, qc]
            acc = None
            for half in range(2):
                g = (2 * p + half) // GROUP
                sc = dot_nt(q, kh[g][half]) * factor
                sc = jnp.where(keep, sc, MASKED)
                ex = jnp.exp(sc - jnp.max(sc, -1, keepdims=True))
                pr = (ex / jnp.sum(ex, -1, keepdims=True)).astype(BF)
                prob_o[i * 2 * GROUP + 2 * p + half] = pr
                term = dot(pr, vh[g][half])
                acc = term if acc is None else acc + term
            mix_o[:, qc] = acc.astype(BF)

    for s in range(1, C):
        group_in(s, 1)
    cores_in(1)
    out_w = pltpu.make_async_copy(wf, wf_o, s_loc.at[3])
    out_w.start()

    @pl.loop(0, D // 256)
    def _(i):
        col = pl.ds(pl.multiple_of(i * 256, 256), 256)
        wc = pl.ds(pl.multiple_of(QW + 2 * KW + i * 256, 256), 256)
        hid_o[:, col] = tok[:, col].astype(F32) + dot(mix_o[...], wf[:, wc])

    hidden = hid_o[...]
    r2 = lax.rsqrt(jnp.mean(hidden * hidden, -1, keepdims=True) + EPSILON)
    ffn_o[...] = (hidden * r2 * gain_two).astype(BF)
    logits = dot_nt(rt_o[...], ffn_o[...])[0:experts]
    named = slots[...] >= 0.0
    logits = jnp.where(named, logits, MASKED)
    ex = jnp.where(named, jnp.exp(logits - jnp.max(logits, 0, keepdims=True)), 0.0)
    gates = ex / jnp.sum(ex, 0, keepdims=True)
    gates_o[...] = gates
    el = experts // nf
    for i in range(nf):
        side_o[i, 0:el] = slots[i * el:(i + 1) * el, :]
        side_o[i, el:2 * el] = gates[i * el:(i + 1) * el]

    for s in range(3, C):
        cot_step(s)
    own_c.wait()
    sib_c.wait()
    out_w.wait()
    for dr in range(2):
        for s in range(1, C):
            @pl.when(has(dr, s))
            def _():
                cs_in(dr, s).wait_recv()
                cs(dr, s).wait_send()
                for g in range(2):
                    sib_copy(dr, s, g).wait_send()
                    for i in range(1, nd):
                        dp_copy(dr, s, g, i).wait_send()

            @pl.when(nxt_ok(dr) & (has(dr, s - 1) if s > 1 else True))
            def _():
                for g in range(2):
                    wz(dr, s, g).wait_send()
                for h in range(2):
                    cz(dr, s, s == 1, h).wait_send()


def front(nf, nd, experts, tok, ws, small, cot, slots, cosr, sinr):
    T, D = tok.shape
    C = nf // 2
    W = sum(w.shape[1] for w in ws)
    out = [
        (T, D, BF, 0), (T, D, F32, 0), (experts, T, F32, 0), (nf, 2 * experts // nf, T, F32, 0), (T, QW, BF, 0), (T, QW + KW, BF, 0),
        (T, KW, BF, 0), (QUERY_HEADS, T, T, BF, 0), (D, W, BF, 1), (nf, T, D, BF, 1),
        (small.shape[0], D, BF, 0),
    ]
    dma = pltpu.SemaphoreType.DMA
    return pl.pallas_call(
        functools.partial(front_kernel, nf, nd, experts),
        out_shape=[jax.ShapeDtypeStruct(o[:-2], o[-2]) for o in out],
        in_specs=[vm()] + [hbm()] * 4 + [vm()] * 5,
        out_specs=[hbm() if o[-1] else vm() for o in out],
        scratch_shapes=[
            VMEM((D, W), BF),
            VMEM((nf,) + small.shape, BF),
            VMEM((T, D), BF),
            VMEM((8, 128), F32),
            dma((nf,)), dma((nf,)),
            dma((2, 2, C)), dma((2, 2, C)),
            dma((2, 2, C, nd)), dma((2, 2, C, nd)),
            dma((2, 2, C)), dma((2, 2, C)),
            dma((2, 2, C)), dma((2, 2, C)),
            dma((2, C)), dma((2, C)),
            dma((4,)), dma((4,)),
        ],
        compiler_params=pltpu.CompilerParams(collective_id=1, has_side_effects=True,
                                             vmem_limit_bytes=60 * 2 ** 20),
        cost_estimate=pl.CostEstimate(flops=4_000_000_000, bytes_accessed=60_000_000, transcendentals=2_000_000),
        name="front",
    )(tok, *ws, small, cot, slots, cosr, sinr)


def add_blocks(dst, srcs, extra=None):
    @pl.loop(0, dst.shape[0] // 16)
    def _(i):
        at = pl.ds(pl.multiple_of(i * 16, 16), 16)
        total = srcs[0][at, :].astype(F32)
        for s in srcs[1:]:
            total = total + s[at, :].astype(F32)
        dst[at, :] = total.astype(dst.dtype)


class Line:
    def __init__(self, nf, f, d, acc, give, sib, rcv, stage, sems, stage_sem):
        self.nf, self.f, self.d = nf, f, d
        self.C = nf // 2
        self.c, self.k = f // 2, lax.rem(f, 2)
        self.acc, self.give, self.sib, self.rcv, self.stage = acc, give, sib, rcv, stage
        self.s_sib, self.r_sib, self.s_z, self.r_z = sems
        self.stage_sem = stage_sem

    def remote(self, src, dst, ss, rs, to):
        return pltpu.make_async_remote_copy(src_ref=src, dst_ref=dst, send_sem=ss, recv_sem=rs,
                                            device_id=(to, self.d), device_id_type=MESH)

    def dest(self, dr, s):
        i = s - 1 - (self.C - 1 - self.c) if dr == 0 else s - 1 - self.c
        room = self.c if dr == 0 else self.C - 1 - self.c
        chip = i if dr == 0 else self.C - 1 - i
        return jnp.clip(chip, 0, self.C - 1), (i >= 0) & (i < room)

    def sib_copy(self, chip):
        return self.remote(self.give(chip), self.sib(chip), self.s_sib.at[chip], self.r_sib.at[chip],
                           self.f + 1 - 2 * self.k)

    def z_copy(self, dr, s, chip):
        return self.remote(self.acc(chip), self.rcv(dr, s - 1), self.s_z.at[dr, s - 1], self.r_z.at[dr, s - 1],
                           self.f - 2 if dr == 0 else self.f + 2)

    def z_in(self, dr, s):
        return self.remote(self.rcv(dr, s - 1), self.rcv(dr, s - 1), self.s_z.at[dr, s - 1], self.r_z.at[dr, s - 1],
                           self.f)

    def start_sib(self):
        for s in range(1, self.C):
            for dr in range(2):
                chip, ok = self.dest(dr, s)

                @pl.when(ok)
                def _():
                    self.sib_copy(chip).start()
        self.sib_copy(self.c).start()

    def gather(self, chip, srcs):
        acc = self.acc(chip)
        if self.stage is None:
            add_blocks(acc, [acc] + srcs)
            return
        for s in srcs:
            cp = pltpu.make_async_copy(s, self.stage, self.stage_sem)
            cp.start()
            cp.wait()
            add_blocks(acc, [acc, self.stage])

    def step(self, s):
        for dr in range(2):
            chip, ok = self.dest(dr, s)
            begins = (self.c == self.C - 1) if dr == 0 else (self.c == 0)

            @pl.when(ok)
            def _():
                other = []
                if self.sib is not None:
                    self.sib_copy(chip).wait_recv()
                    other = [self.sib(chip)]

                    @pl.when(begins)
                    def _():
                        self.gather(chip, other)
                if s > 1:
                    @pl.when(jnp.logical_not(begins))
                    def _():
                        self.z_in(dr, s - 1).wait_recv()
                        self.gather(chip, other + [self.rcv(dr, s - 2)])
                self.z_copy(dr, s, chip).start()

    def last(self):
        other = []
        if self.sib is not None:
            self.sib_copy(self.c).wait_recv()
            other = [self.sib(self.c)]
        mid = (self.c > 0) & (self.c < self.C - 1)
        s = self.C - 1
        for dr in range(2):
            @pl.when((self.c < self.C - 1) if dr == 0 else (self.c > 0))
            def _():
                self.z_in(dr, s).wait_recv()

        @pl.when(mid)
        def _():
            self.gather(self.c, other + [self.rcv(0, s - 1), self.rcv(1, s - 1)])

        @pl.when(self.c == 0)
        def _():
            self.gather(self.c, other + [self.rcv(0, s - 1)])

        @pl.when(self.c == self.C - 1)
        def _():
            self.gather(self.c, other + [self.rcv(1, s - 1)])

    def sent(self):
        if self.acc is None:
            for chip in range(self.C):
                self.sib_copy(chip).wait_send()
            return
        if self.sib is not None:
            self.sib_copy(self.c).wait_send()
        for s in range(1, self.C):
            for dr in range(2):
                chip, ok = self.dest(dr, s)

                @pl.when(ok)
                def _():
                    if self.sib is not None:
                        self.sib_copy(chip).wait_send()
                    self.z_copy(dr, s, chip).wait_send()


class Cube:
    def __init__(self, nd, f, d, flip, lanes, size, own, land, total, out, sems):
        m = nd.bit_length() - 1
        order = [1 << b for b in range(m)]
        if isinstance(flip, bool):
            self.masks = order[::-1] if flip else order
        else:
            self.masks = [jnp.where(flip, b, a) for a, b in zip(order, order[::-1])]
        self.f, self.d, self.lanes = f, d, lanes
        self.own, self.land, self.total, self.out = own, land, total, out
        self.ss, self.rs = sems
        self.m = m
        self.in_place, self.whole = False, True
        self.low, self.length = [0], [size]
        for mask in self.masks:
            half = self.length[-1] // 2
            side = lax.rem(d // mask, 2)
            self.low.append(self.low[-1] + side * half)
            self.length.append(half)

    def cut(self, ref, at, n):
        if self.lanes:
            return ref.at[:, pl.ds(pl.multiple_of(at, 128), n)]
        return ref.at[pl.ds(pl.multiple_of(at, 16), n)]

    def remote(self, src, dst, i, mask):
        return pltpu.make_async_remote_copy(src_ref=src, dst_ref=dst, send_sem=self.ss.at[i], recv_sem=self.rs.at[i],
                                            device_id=(self.f, jnp.bitwise_xor(self.d, mask)),
                                            device_id_type=MESH)

    def level(self, i):
        if i == 0 or (self.in_place and (i < self.m or not self.whole)):
            return self.own, 0
        if i == self.m:
            return self.out, 0
        return self.total(i - 1), self.low[i]

    def down(self, i):
        ref, base = self.level(i)
        half = self.length[i + 1]
        other = 2 * self.low[i] + half - self.low[i + 1]
        return self.remote(self.cut(ref, other - base, half), self.land(i), i, self.masks[i])

    def merge(self, i, add):
        self.down(i).wait_recv()
        self.fold(i, add)

    def fold(self, i, add):
        ref, base = self.level(i)
        dst, dbase = self.level(i + 1)
        half = self.length[i + 1]
        low = self.low[i + 1]
        add(self.cut(dst, low - dbase, half), self.cut(ref, low - base, half), self.land(i))

    def up(self, i):
        blk = self.cut(self.out, self.low[i + 1], self.length[i + 1])
        return self.remote(blk, blk, self.m + i, self.masks[i])

    def up_in(self, i):
        half = self.length[i + 1]
        other = 2 * self.low[i] + half - self.low[i + 1]
        blk = self.cut(self.out, other, half)
        return self.remote(blk, blk, self.m + i, self.masks[i])

    def sent(self, first=0):
        for i in range(self.m):
            if i >= first:
                self.down(i).wait_send()
            self.up(i).wait_send()


def pipe_add(dst, a, b):
    n, w = dst.shape
    tile = next(t for t in (256, 192, 128, 64) if n % t == 0 and t * w <= 256 * 1024)
    spec = pl.BlockSpec((tile, w), lambda i: (i, 0))

    def inner(a_ref, b_ref, o_ref):
        o_ref[...] = (a_ref[...].astype(F32) + b_ref[...].astype(F32)).astype(o_ref.dtype)

    pltpu.emit_pipeline(inner, grid=(n // tile,), in_specs=[spec, spec], out_specs=[spec])(a, b, dst)

def visit(c, C, j):
    both = jnp.minimum(c, C - 1 - c)
    near = j <= 2 * both
    dist = jnp.where(near, (j + 1) // 2, j - both)
    down = jnp.where(near, lax.rem(j, 2) == 0, c < C - 1 - c)
    chip = jnp.where(down, c + dist, c - dist)
    return chip, jnp.where(down, 1, 0), dist


def term_cubes(nd, el, f, d, t1, t2, out1, out2, l1, l2, a1, a2, sems):
    cubes = []
    for e in range(el):
        for j, (src, out, ls, ts) in enumerate(((t1, out1, l1, a1), (t2, out2, l2, a2))):
            pick = functools.partial(lambda refs, e, i: refs[i].at[e], ls, e)
            tot = functools.partial(lambda refs, e, i: refs[i].at[e], ts, e)
            cubes.append(Cube(nd, f, d, (e + j) % 2 == 1, False, src.shape[1], src.at[e], pick, tot,
                              None if out is None else out.at[e], (sems[0].at[2 * e + j], sems[1].at[2 * e + j])))
    return cubes


def experts_kernel(nf, nd, el, cap, capp, land_hbm, ffn, cot_a, side, wg_h, wu_h, wd_h,
                   out_o, gin_o, gp_o, t1_o, t2_o, l1, sib_l, rcv_l, acc,
                   wg, wu, wd, fa, sd, cotb, xs, gs, hs, hgs, orb, irb, st_o, give, st1, st2, stage, us,
                   s_sd, r_sd, s_z, r_z, s_sib, r_sib, s_w, s_loc, s_t, s_ls, r_ls, s_lz, r_lz, s_st, s_cube, r_cube):
    T, D = ffn.shape
    FFW = wg.shape[2]
    C = nf // 2
    B = 2 * capp
    f = lax.axis_index("fsdp")
    d = lax.axis_index("dp")
    c = f // 2
    k = lax.rem(f, 2)
    sib = f + 1 - 2 * k
    greet(nf, nd, f, d)

    def remote(src, dst, ss, rs, to_f):
        return pltpu.make_async_remote_copy(src_ref=src, dst_ref=dst, send_sem=ss, recv_sem=rs,
                                            device_id=(to_f, d), device_id_type=MESH)

    def chip_at(dr, s):
        return jnp.where(dr == 0, c - s, c + s)

    def has(dr, s):
        at = chip_at(dr, s)
        return (at >= 0) & (at < C)

    def nxt_ok(dr):
        return (c + 1 < C) if dr == 0 else (c - 1 >= 0)

    def nxt_f(dr):
        return f + 2 if dr == 0 else f - 2

    halves = (slice(0, D // 2), slice(D // 2, D))

    def z_out(dr, s, h):
        blk = fa.at[2 * chip_at(dr, s - 1) + k, :, halves[h]]
        return remote(blk, blk, s_z.at[h, dr, s - 1], r_z.at[h, dr, s - 1], nxt_f(dr))

    def z_own(dr, h):
        return remote(ffn.at[:, halves[h]], fa.at[f, :, halves[h]], s_z.at[h, dr, 0], r_z.at[h, dr, 0], nxt_f(dr))

    def z_in(dr, s, h):
        blk = fa.at[2 * chip_at(dr, s) + k, :, halves[h]]
        return remote(blk, blk, s_z.at[h, dr, s - 1], r_z.at[h, dr, s - 1], f)

    def sib_out(dr, s):
        ff = 2 * chip_at(dr, s) + k
        return remote(fa.at[ff], fa.at[ff], s_sib.at[dr, s], r_sib.at[dr, s], sib)

    def sib_in(dr, s):
        ff = 2 * chip_at(dr, s) + 1 - k
        return remote(fa.at[ff], fa.at[ff], s_sib.at[dr, s], r_sib.at[dr, s], f)

    lines = [Line(nf, f, d, lambda ch, cut=cut: acc.at[ch, :, cut], lambda ch, cut=cut: give.at[0, :, cut],
                  lambda ch, cut=cut: sib_l.at[ch, :, cut], lambda dr, s, cut=cut: rcv_l.at[dr, s, :, cut],
                  stage.at[:, cut] if land_hbm else None, (s_ls.at[h], r_ls.at[h], s_lz.at[h], r_lz.at[h]), s_st)
             for h, cut in enumerate(halves)]

    def handed(chip, slot, h):
        return remote(give.at[slot, :, halves[h]], sib_l.at[chip, :, halves[h]], s_ls.at[h, chip], r_ls.at[h, chip], sib)

    def reduce_step(s):
        for line in lines:
            line.step(s)

    for h in range(2):
        for dr in range(2):
            @pl.when(nxt_ok(dr))
            def _():
                z_own(dr, h).start()
    sib_own = remote(ffn, fa.at[f], s_sib.at[1, 0], r_sib.at[1, 0], sib)
    sib_own.start()
    own = pltpu.make_async_copy(ffn, fa.at[f], s_loc.at[0])
    own.start()
    own_sd = pltpu.make_async_copy(side.at[f], sd.at[f], s_loc.at[1])
    own_sd.start()
    sd_copies = []
    for i in range(1, nf):
        to = lax.rem(f + i, nf)
        cp = remote(side.at[to], sd.at[f], s_sd.at[i - 1], r_sd.at[i - 1], to)
        cp.start()
        sd_copies.append(cp)
    w_copies = []
    for i, (src, dst) in enumerate(((wg_h, wg), (wu_h, wu), (wd_h, wd))):
        cp = pltpu.make_async_copy(src, dst, s_w.at[i])
        cp.start()
        w_copies.append(cp)
    own.wait()
    own_sd.wait()
    for cp in sd_copies:
        cp.wait()
    for cp in w_copies:
        cp.wait()

    n1 = D // 256
    n2 = FFW // 256
    cubes = term_cubes(nd, el, f, d, t1_o, t2_o, None, None, [l1], None, [], [], (s_cube, r_cube))

    def t1_copy(e, i):
        return pltpu.make_async_copy(st1.at[lax.rem(i, 2)], t1_o.at[e, pl.ds(pl.multiple_of(i * 256, 256), 256)],
                                     s_t.at[0, lax.rem(i, 2)])

    def t2_copy(e, i):
        return pltpu.make_async_copy(st2.at[lax.rem(i, 2)], t2_o.at[e, pl.ds(pl.multiple_of(i * 256, 256), 256)],
                                     s_t.at[1, lax.rem(i, 2)])

    def t1_terms(e):
        @pl.loop(0, n1)
        def _(i):
            @pl.when(i >= 2)
            def _():
                t1_copy(e, i).wait()
            col = pl.ds(pl.multiple_of(i * 256, 256), 256)
            st1[lax.rem(i, 2)] = dot_tn(xs[e, :, col], hs[e]).astype(BF)
            t1_copy(e, i).start()

        for i in range(2):
            t1_copy(e, i).wait()
        cubes[2 * e].down(0).start()

    def t2_terms(e):
        @pl.loop(0, n2)
        def _(i):
            @pl.when(i >= 2)
            def _():
                t2_copy(e, i).wait()
            col = pl.ds(pl.multiple_of(i * 256, 256), 256)
            st2[lax.rem(i, 2)] = dot_tn(hgs[e, :, col], gs[e]).astype(BF)
            t2_copy(e, i).start()

        for i in range(2):
            t2_copy(e, i).wait()

    row_ids = lax.broadcasted_iota(jnp.int32, (capp, T), 0).astype(F32)

    @pl.loop(0, C)
    def _(j):
        b, dr_b, dist_b = visit(c, C, j)
        cot_cp = pltpu.make_async_copy(cot_a.at[pl.ds(2 * b, 2)], cotb, s_loc.at[2])
        cot_cp.start()

        base = pl.multiple_of(b * B, 16)
        gate_rows = [[None, None] for _ in range(el)]
        picks = []
        for kk in range(2):
            s = 2 * b + kk
            parts = []
            for e in range(el):
                hit = row_ids == sd[s, e:e + 1, :]
                gate_rows[e][kk] = jnp.sum(jnp.where(hit, sd[s, el + e:el + e + 1, :], 0.0), -1, keepdims=True)
                parts.append(jnp.where(hit, 1.0, 0.0).astype(BF))
            p2 = jnp.concatenate(parts, 0)
            picks.append(p2)
        cot_cp.wait()

        def spread(rows_of, dst):
            for kk in range(2):
                for n in range(0, D, 512):
                    val = dot(picks[kk], rows_of(kk, n)).astype(BF)
                    for e in range(el):
                        at = pl.ds(pl.multiple_of(base + kk * capp, 16), capp)
                        dst[e, at, n:n + 512] = val[e * capp:(e + 1) * capp]

        here = pl.ds(base, B)
        spread(lambda kk, n: cotb[kk, :, n:n + 512], gs)
        for e in range(el):
            for n in range(0, FFW, 256):
                us[e, :, n:n + 256] = dot_nt(gs[e, here, :], wd[e, n:n + 256, :])

        @pl.when(j >= 1)
        def _():
            for dr in range(2):
                @pl.when(has(dr, j))
                def _():
                    for h in range(2):
                        z_in(dr, j, h).wait_recv()

                        @pl.when(nxt_ok(dr) & (j < C - 1))
                        def _():
                            z_out(dr, j + 1, h).start()
                    sib_out(dr, j).start()
        sib_in(dr_b, dist_b).wait_recv()
        spread(lambda kk, n: fa[2 * b + kk, :, n:n + 512], xs)
        gp_rows = []
        for e in range(el):
            gate_row = jnp.concatenate(gate_rows[e], 0)
            gpr = jnp.zeros((B, 1), F32)
            for n in range(0, FFW, 256):
                gv = dot(xs[e, here, :], wg[e, :, n:n + 256])
                uv = dot(xs[e, here, :], wu[e, :, n:n + 256])
                u = us[e, :, n:n + 256]
                sg = 1.0 / (1.0 + jnp.exp(-gv))
                act = gv * sg
                hid = act * uv
                gpr = gpr + jnp.sum(hid * u, -1, keepdims=True)
                hgs[e, here, n:n + 256] = (hid * gate_row).astype(BF)
                gh = u * gate_row
                hs[e, here, n:n + 256] = (gh * uv * (sg * (1.0 + gv * (1.0 - sg)))).astype(BF)
                hs[e, here, FFW + n:FFW + n + 256] = (gh * act).astype(BF)
            gp_rows.append(gpr)
            for n in range(0, D, 512):
                irow = (dot_nt(hs[e, here, 0:FFW], wg[e, n:n + 512, :])
                        + dot_nt(hs[e, here, FFW:2 * FFW], wu[e, n:n + 512, :])).astype(BF)
                for kk in range(2):
                    irb[kk, e * capp:(e + 1) * capp, n:n + 512] = irow[kk * capp:(kk + 1) * capp]

        @pl.when(j >= 2)
        def _():
            before, _, _ = visit(c, C, j - 2)
            for h in range(2):
                handed(before, lax.rem(j, 2), h).wait_send()
        for h in range(2):
            for kk in range(2):
                def combine(dst):
                    cut = halves[h]
                    dst[:, cut] = dot_tn(picks[kk], irb[kk, :, cut]).astype(BF)

                @pl.when(k == kk)
                def _():
                    combine(acc.at[b])

                @pl.when(k != kk)
                def _():
                    combine(give.at[lax.rem(j, 2)])
                    handed(b, lax.rem(j, 2), h).start()

        @pl.when(j == C - 1)
        def _():
            reduce_step(1)
            for e in range(el):
                t1_terms(e)
        for e in range(el):
            for n in range(0, D, 512):
                orow = dot(hgs[e, here, :], wd[e, :, n:n + 512]).astype(BF)
                for kk in range(2):
                    orb[kk, e * capp:(e + 1) * capp, n:n + 512] = orow[kk * capp:(kk + 1) * capp]

        def back(bb):
            return pltpu.make_async_copy(st_o, out_o.at[pl.ds(2 * bb, 2)], s_loc.at[3])

        @pl.when(j >= 1)
        def _():
            back(0).wait()
        for kk in range(2):
            s = 2 * b + kk
            for e in range(el):
                hit = picks[kk][e * capp:(e + 1) * capp].astype(F32)
                gp_o[s, e:e + 1, :] = jnp.sum(hit * gp_rows[e][kk * capp:(kk + 1) * capp], 0, keepdims=True)
            for n in range(0, D, 512):
                st_o[kk, :, n:n + 512] = dot_tn(picks[kk], orb[kk, :, n:n + 512]).astype(BF)
        back(b).start()

    if C > 2:
        reduce_step(2)
    for e in range(el):
        t2_terms(e)
    for s in range(3, C):
        reduce_step(s)
    for line in lines:
        line.last()
    gin_o[...] = acc[c]

    pltpu.make_async_copy(st_o, out_o.at[pl.ds(0, 2)], s_loc.at[3]).wait()
    for j in range(max(C - 2, 0), C):
        chip, _, _ = visit(c, C, j)
        for h in range(2):
            handed(chip, j % 2, h).wait_send()
    for line in lines:
        for s in range(1, C):
            for dr in range(2):
                chip, ok = line.dest(dr, s)

                @pl.when(ok)
                def _():
                    line.z_copy(dr, s, chip).wait_send()
    for cube in cubes[::2]:
        cube.down(0).wait()
    sib_own.wait_send()
    for dr in range(2):
        for s in range(1, C):
            @pl.when(has(dr, s))
            def _():
                sib_out(dr, s).wait_send()
        for s in range(1, C):
            @pl.when(nxt_ok(dr) & has(dr, s - 1))
            def _():
                for h in range(2):
                    z_out(dr, s, h).wait_send()


def experts_call(nf, nd, cap, ffn_in, cot_all, side, w_gate, w_up, w_down):
    T, D = ffn_in.shape
    el, _, FFW = w_gate.shape
    capp = cap + (-cap % 16)
    C = nf // 2
    rows = C * 2 * capp
    land_hbm = C > 4
    dma = pltpu.SemaphoreType.DMA
    out = [((nf, T, D), BF, 1), ((T, D), BF, 0), ((nf, el, T), F32, 0),
           ((el, D, 2 * FFW), BF, 1), ((el, FFW, D), BF, 1),
           ((el, D // 2, 2 * FFW), BF, 1)]
    lands = [(C, T, D), (2, C - 1, T, D)]
    scratch = []
    if land_hbm:
        out += [(x, BF, 1) for x in lands]
    else:
        scratch += [VMEM(x, BF) for x in lands]
    scratch += [
        VMEM((C, T, D), BF),
        VMEM((el, D, FFW), BF), VMEM((el, D, FFW), BF), VMEM((el, FFW, D), BF),
        VMEM((nf, T, D), BF), VMEM(side.shape, F32), VMEM((2, T, D), BF),
        VMEM((el, rows, D), BF), VMEM((el, rows, D), BF),
        VMEM((el, rows, 2 * FFW), BF), VMEM((el, rows, FFW), BF),
        VMEM((2, el * capp, D), BF), VMEM((2, el * capp, D), BF),
        VMEM((2, T, D), BF), VMEM((2, T, D), BF),
        VMEM((2, 256, 2 * FFW), BF), VMEM((2, 256, D), BF),
        VMEM((T, D) if land_hbm else (16, 128), BF),
        VMEM((el, 2 * capp, FFW), F32),
        dma((nf,)), dma((nf,)),
        dma((2, 2, C)), dma((2, 2, C)), dma((2, C)), dma((2, C)),
        dma((3,)), dma((5,)), dma((2, 2)),
        dma((2, C)), dma((2, C)), dma((2, 2, C)), dma((2, 2, C)), dma(()),
        dma((2 * el, 2 * (nd.bit_length() - 1))), dma((2 * el, 2 * (nd.bit_length() - 1))),
    ]
    return pl.pallas_call(
        functools.partial(experts_kernel, nf, nd, el, cap, capp, land_hbm),
        out_shape=[jax.ShapeDtypeStruct(o[0], o[1]) for o in out],
        in_specs=[vm(), hbm(), vm(), hbm(), hbm(), hbm()],
        out_specs=[hbm() if o[2] else vm() for o in out],
        scratch_shapes=scratch,
        compiler_params=pltpu.CompilerParams(collective_id=2, has_side_effects=True,
                                             vmem_limit_bytes=63 * 2 ** 20),
        cost_estimate=pl.CostEstimate(flops=40_000_000_000, bytes_accessed=60_000_000, transcendentals=2_000_000),
        name="experts",
    )(ffn_in, cot_all, side, w_gate, w_up, w_down)[:6]


def back_kernel(nf, nd, el, land_hbm, split, *refs):
    m = nd.bit_length() - 1
    it = iter(refs)

    def take(n):
        return [next(it) for _ in range(n)]

    (gin, out_p, gp_p, t1, t2, f1, tok_h, cot_h, hid_h, ffn_h, gates, mix_h, qk_h, v_h, prob_h, wf_h, rt,
     cosr, sinr) = take(19)
    out_o, gt_o, sh_o, sm_o, t1_o, t2_o = take(6)
    l1 = [f1] + take(m - 1)
    l2 = take(m)
    a1 = take(m - 1)
    a2 = take(m - 1)
    sibo, rcvo, sib, rcv, sibq, rcvq = take(6)
    (acc, wb, wg, tok, cot, hid, ffn, mix, qk, v, prob, branch, gh, ga, gproj, gpb, smg, smr, smd, sms) = take(20)
    attn, gm = ffn, mix
    shl = take(m * (2 if split else 1))
    if split:
        xo = next(it)
        xol = take(m)
    stage, stageq = take(2)
    (s_load, s_acc, s_gp, r_gp, s_sib, r_sib, s_z, r_z, s_cube, r_cube, s_sc, r_sc, s_sm, r_sm, s_sd, r_sd,
     s_stage, s_prob) = take(18)

    T, D = tok.shape
    R = wg.shape[0] // nf
    W = wg.shape[1]
    E = gates.shape[0]
    C = nf // 2
    f = lax.axis_index("fsdp")
    d = lax.axis_index("dp")
    c = f // 2
    k = lax.rem(f, 2)
    QV = QW + 2 * KW
    QZ, OW = QV, D
    greet(nf, nd, f, d)

    def remote(src, dst, ss, rs, to_f, to_d):
        return pltpu.make_async_remote_copy(src_ref=src, dst_ref=dst, send_sem=ss, recv_sem=rs,
                                            device_id=(to_f, to_d), device_id_type=MESH)

    def rows(ff):
        return pl.ds(pl.multiple_of(ff * R, 16), R)


    def sems(i):
        return (s_sib.at[i], r_sib.at[i], s_z.at[i], r_z.at[i])

    def lines_of(first, cuts, sb, rc, sg, ids):
        res = []
        for h, (top, n) in enumerate(cuts):
            cut, loc = pl.ds(first + top, n), pl.ds(top, n)
            res.append(Line(nf, f, d, lambda ch, cut=cut: wg.at[rows(2 * ch + k), cut],
                            lambda ch, cut=cut: wg.at[rows(2 * ch + 1 - k), cut],
                            lambda ch, loc=loc: sb.at[ch, :, loc], lambda dr, s, loc=loc: rc.at[dr, s, :, loc],
                            sg.at[:, loc] if land_hbm else None, sems(ids[h]), s_stage))
        return res

    if split:
        o_lines = []
        pair = Line(nf, f, d, None, lambda ch: wg.at[rows(2 * ch + 1 - k), QZ:W], lambda ch: sib.at[ch], None, None,
                    sems(0), s_stage)
        o_cubes = []
        for h in range(2):
            top = h * (C * R // 2)
            cube = Cube(nd, f, d, h == 1, True, OW, xo.at[top:top + C * R // 2],
                        functools.partial(lambda h, i: xol[i].at[h], h), None, None, (s_sc.at[h], r_sc.at[h]))
            cube.in_place, cube.whole = True, False
            o_cubes.append(cube)
        o_low = [cube.low[m] for cube in o_cubes]

        def o_block(ch):
            low = pl.multiple_of(jnp.where(ch < C // 2, o_low[0], o_low[1]), 128)
            return xo.at[pl.ds(pl.multiple_of(ch * R, 16), R), pl.ds(low, OW >> m)]

        o_line = Line(nf, f, d, o_block, None, None, lambda dr, s: rcv.at[dr, s], None, sems(1), s_stage)
        o_up = Cube(nd, f, d, c >= C // 2, True, OW, None, None, None, sh_o.at[:, QZ:W], (s_sc.at[2], r_sc.at[2]))
    else:
        o_lines = lines_of(QV, ((0, D // 2), (D // 2, D // 2)), sib, rcv, stage.at[0:R], (0, 1))
    q_cuts = ((0, QW), (QW, 2 * KW))
    q_lines = lines_of(0, q_cuts, sibq, rcvq, stageq, (2, 4))
    out_line = Line(nf, f, d, lambda ch: acc.at[ch], lambda ch: out_p.at[2 * ch + 1 - k], lambda ch: sibo.at[ch],
                    lambda dr, s: rcvo.at[dr, s], stage, sems(3), s_stage)

    def acc_loads(src):
        return [pltpu.make_async_copy(src.at[2 * ch + k], acc.at[ch], s_acc.at[ch]) for ch in range(C)]

    gp_copies = []
    for i in range(1, nf):
        to = lax.rem(f + i, nf)
        cp = remote(gp_p.at[to], gpb.at[f], s_gp.at[i - 1], r_gp.at[i - 1], to, d)
        cp.start()
        gp_copies.append(cp)
    out_line.start_sib()
    out_loads = acc_loads(out_p)
    for cp in out_loads:
        cp.start()
    cubes = term_cubes(nd, el, f, d, t1, t2, t1_o, t2_o, l1, l2, a1, a2, (s_cube, r_cube))
    first_terms, second_terms = cubes[::2], cubes[1::2]
    for cube in second_terms:
        cube.down(0).start()
    own_gp = pltpu.make_async_copy(gp_p.at[f], gpb.at[f], s_load.at[0])
    own_gp.start()
    wo = pltpu.make_async_copy(wf_h.at[:, QV:QV + D], wb.at[:, 0:D], s_load.at[1])
    wo.start()
    others = [(tok_h, tok), (cot_h, cot), (hid_h, hid), (ffn_h, ffn), (mix_h, mix), (qk_h, qk), (v_h, v)]
    more = [pltpu.make_async_copy(a, b, s_load.at[2 + i]) for i, (a, b) in enumerate(others)]
    for cp in more:
        cp.start()

    def prob_load(i):
        at = pl.ds(i * 2 * GROUP, 2 * GROUP)
        return pltpu.make_async_copy(prob_h.at[at], prob.at[lax.rem(i, 2)], s_prob.at[lax.rem(i, 2)])

    prob_load(0).start()

    def onward(cube, i):
        cube.down(i + 1).start() if i + 1 < m else cube.up(i).start()

    def chain(group, start, add):
        def merged(i):
            for cube in group:
                cube.merge(i, add)
                onward(cube, i)

        def raised(i):
            for cube in group:
                cube.up_in(i).wait_recv()
                cube.up(i - 1).start()

        return ([functools.partial(merged, i) for i in range(start, m)]
                + [functools.partial(raised, i) for i in range(m - 1, 0, -1)])

    def vadd(dst, a, b):
        add_blocks(dst, [a, b])

    def run(steps, n=1):
        for _ in range(min(n, len(steps))):
            steps.pop(0)()

    steps1, steps2 = chain(first_terms, 1, pipe_add), chain(second_terms, 0, pipe_add)
    for cube in first_terms:
        cube.fold(0, pipe_add)
        onward(cube, 0)
    middle = steps1.pop(0) if steps1 else None
    for cp in out_loads:
        cp.wait()
    out_line.step(1)
    for cp in more:
        cp.wait()
    own_gp.wait()
    for cp in gp_copies:
        cp.wait()

    gains = rt[E:E + 2].astype(F32)
    gain_one, gain_two = gains[0:1], gains[1:2]
    gpt = jnp.concatenate([gpb[i] for i in range(nf)], 0)
    gates_v = gates[...]
    gl = (gates_v * (gpt - jnp.sum(gpt * gates_v, 0, keepdims=True))).astype(BF)
    for n in range(0, D, 512):
        sms[0:E, n:n + 512] = dot(gl, ffn[:, n:n + 512])
    for n in range(0, D, 512):
        ga[:, n:n + 512] = dot_tn(gl, rt[0:E, n:n + 512])
    sms[E:, :] = jnp.zeros((sms.shape[0] - E, D), F32)
    TR = 32

    @pl.loop(0, T // TR)
    def _(i):
        at = pl.ds(pl.multiple_of(i * TR, TR), TR)
        h = hid[at, :]
        r2 = lax.rsqrt(jnp.mean(h * h, -1, keepdims=True) + EPSILON)
        n2 = h * r2
        gf = gin[at, :].astype(F32) + ga[at, :]
        sms[E + 1:E + 2, :] += jnp.sum(gf * n2, 0, keepdims=True)
        g2 = gf * gain_two
        x = cot[at, :].astype(F32) + r2 * (g2 - n2 * jnp.mean(g2 * n2, -1, keepdims=True))
        gh[at, :] = x
        branch[at, :] = x.astype(BF)

    @pl.loop(0, QW // 256)
    def _(i):
        at = pl.ds(pl.multiple_of(i * 256, 256), 256)
        wg[at, QV:QV + D] = dot_tn(mix[:, at], branch[...]).astype(BF)
    if split:
        pair.start_sib()
        if C > 2:
            out_line.step(2)
    else:
        for line in o_lines:
            line.start_sib()
        for line in o_lines:
            line.step(1)
    wo.wait()

    @pl.loop(0, QW // 256)
    def _(i):
        at = pl.ds(pl.multiple_of(i * 256, 256), 256)
        gm[:, at] = dot_nt(branch[...], wb[at, 0:D]).astype(BF)
    wq = pltpu.make_async_copy(wf_h.at[:, 0:QV], wb, s_load.at[1])
    wq.start()
    if split:
        for ch in range(C):
            pair.sib_copy(ch).wait_recv()
            add_blocks(xo.at[ch * R:(ch + 1) * R], [wg.at[rows(2 * ch + k), QZ:W], sib.at[ch]])
        for cube in o_cubes:
            cube.down(0).start()
    run(steps2)
    factor = HEAD_SIZE ** (-0.5)
    lane = lax.broadcasted_iota(jnp.int32, (T, 128), 1)
    low = lane < HEAD_SIZE
    first = lax.rem(lane, HEAD_SIZE) < HEAD_SIZE // 2

    def unrotate(x):
        return x * cosr[...] - half_roll(x, first) * sinr[...]

    @pl.loop(0, KEY_VALUE_HEADS // 2)
    def _(i):
        @pl.when(i + 1 < KEY_VALUE_HEADS // 2)
        def _():
            prob_load(i + 1).start()
        prob_load(i).wait()
        slot = lax.rem(i, 2)
        kcol = pl.ds(pl.multiple_of(i * 128, 128), 128)
        kh = head_masks(qk[:, pl.ds(pl.multiple_of(QW + i * 128, 128), 128)], lane)
        vh = head_masks(v[:, kcol], lane)
        gk = [[None, None], [None, None]]
        gv = [[None, None], [None, None]]
        for p in range(GROUP):
            qc = pl.ds(pl.multiple_of((i * GROUP + p) * 128, 128), 128)
            q = qk[:, qc]
            g = gm[:, qc]
            gq = None
            for half in range(2):
                kv = (2 * p + half) // GROUP
                pr = prob[slot, 2 * p + half]
                prf = pr.astype(F32)
                gp = dot_nt(g, vh[kv][half])
                gs = (prf * (gp - jnp.sum(prf * gp, -1, keepdims=True))).astype(BF)
                term = dot(gs, kh[kv][half])
                gq = term if gq is None else gq + term
                tk = dot_tn(gs, q)
                tv = dot_tn(pr, g)
                gk[kv][half] = tk if gk[kv][half] is None else gk[kv][half] + tk
                gv[kv][half] = tv if gv[kv][half] is None else gv[kv][half] + tv
            gproj[:, qc] = unrotate(gq * factor).astype(BF)

        def join(x):
            a = jnp.where(low, x[0][0] + pltpu.roll(x[0][1], HEAD_SIZE, axis=1), 0.0)
            b = jnp.where(low, 0.0, pltpu.roll(x[1][0], HEAD_SIZE, axis=1) + x[1][1])
            return a + b

        gproj[:, pl.ds(pl.multiple_of(QW + i * 128, 128), 128)] = unrotate(join(gk) * factor).astype(BF)
        gproj[:, pl.ds(pl.multiple_of(QW + KW + i * 128, 128), 128)] = join(gv).astype(BF)

        if C > 2:
            @pl.when(i == 2)
            def _():
                if middle is not None:
                    middle()

            @pl.when(i == 1)
            def _():
                for line in o_lines:
                    line.step(2)


    def o_merge(i):
        for cube in o_cubes:
            cube.merge(i, vadd)
            if i + 1 < m:
                cube.down(i + 1).start()

    @pl.loop(0, T // TR)
    def _(i):
        at = pl.ds(pl.multiple_of(i * TR, TR), TR)
        x = tok[at, :].astype(F32)
        r1 = lax.rsqrt(jnp.mean(x * x, -1, keepdims=True) + EPSILON)
        attn[at, :] = (x * r1 * gain_one).astype(BF)

    for line, (top, width) in zip(q_lines, q_cuts):
        @pl.loop(0, D // 256)
        def _(i):
            at = pl.ds(pl.multiple_of(i * 256, 256), 256)
            for n in range(top, top + width, 512):
                wg[at, n:n + 512] = dot_tn(attn[:, at], gproj[:, n:n + 512]).astype(BF)
        line.start_sib()
        if line is q_lines[0]:
            for s in range(3, C):
                for other in o_lines:
                    other.step(s)
        line.step(1)
    run(steps2)
    if split:
        o_merge(0)
    wq.wait()

    @pl.loop(0, D // 256)
    def _(i):
        at = pl.ds(pl.multiple_of(i * 256, 256), 256)
        ga[:, at] = dot_nt(gproj[...], wb[at, :])

    @pl.loop(0, T // TR)
    def _(i):
        at = pl.ds(pl.multiple_of(i * TR, TR), TR)
        x = tok[at, :].astype(F32)
        r1 = lax.rsqrt(jnp.mean(x * x, -1, keepdims=True) + EPSILON)
        n1 = x * r1
        gat = ga[at, :]
        sms[E:E + 1, :] += jnp.sum(gat * n1, 0, keepdims=True)
        g1 = gat * gain_one
        gt_o[at, :] = (gh[at, :] + r1 * (g1 - n1 * jnp.mean(g1 * n1, -1, keepdims=True))).astype(BF)

    small = sms[...]
    for i in range(nf):
        smg[i] = small[:, i * R:(i + 1) * R]
    sm_copies = []
    for i in range(1, nf):
        to = lax.rem(f + i, nf)
        cp = remote(smg.at[to], smr.at[f], s_sm.at[i - 1], r_sm.at[i - 1], to, d)
        cp.start()
        sm_copies.append(cp)
    smr_own = pltpu.make_async_copy(smg.at[f], smr.at[f], s_load.at[0])
    smr_own.start()

    for line in o_lines:
        line.last()
    lates = []
    for g, (left, width) in enumerate(q_cuts if split else ((0, W),)):
        late = []
        for h in range(2):
            top = h * (R // 2)
            own = wg.at[pl.ds(pl.multiple_of(f * R + top, 16), R // 2), left:left + width]
            cube = Cube(nd, f, d, h == 1, True, width, own, functools.partial(lambda g, h, i: shl[g * m + i].at[h], g, h),
                        None, sh_o.at[top:top + R // 2, left:left + width], (s_sc.at[3 + 2 * g + h], r_sc.at[3 + 2 * g + h]))
            cube.in_place = True
            late.append(cube)
        lates.append(late)
    steps_l = [chain(late, 0, vadd) for late in lates]
    run(steps1)
    run(steps2)
    if C > 2:
        for line in q_lines:
            line.step(2)
    if split:
        for i in range(1, m):
            o_merge(i)
        o_line.step(1)
    if split:
        if C > 2:
            o_line.step(2)
        pair.sent()
    for line in o_lines:
        line.sent()
    smr_own.wait()
    for cp in sm_copies:
        cp.wait()
    total = smr[0]
    for i in range(1, nf):
        total = total + smr[i]
    smd[0] = total
    sd_copies = []
    for i in range(1, nd):
        cp = remote(smd.at[0], smd.at[i], s_sd.at[i - 1], r_sd.at[i - 1], f, jnp.bitwise_xor(d, i))
        cp.start()
        sd_copies.append(cp)
    for s in range(3, C):
        for line in q_lines:
            line.step(s)
    if not split and C > 2:
        out_line.step(2)
    run(steps1, len(steps1))
    run(steps2, len(steps2))
    if split:
        for s in range(3, C):
            o_line.step(s)
        o_line.last()
        add_blocks(sh_o.at[:, pl.ds(pl.multiple_of(QZ + o_up.low[m], 128), OW >> m)], [o_block(c)])
        o_up.up(m - 1).start()
    for g, line in enumerate(q_lines):
        line.last()
        if split or line is q_lines[-1]:
            for cube in lates[g if split else 0]:
                cube.down(0).start()
    for s in range(3, C):
        out_line.step(s)
    if split:
        for i in range(m - 1, 0, -1):
            o_up.up_in(i).wait_recv()
            o_up.up(i - 1).start()
    while steps_l[-1]:
        for steps in steps_l:
            run(steps)
    for cp in sd_copies:
        cp.wait()
    total = smd[0]
    for i in range(1, nd):
        total = total + smd[i]
    sm_o[...] = total
    out_line.last()

    @pl.loop(0, T // TR)
    def _(i):
        at = pl.ds(pl.multiple_of(i * TR, TR), TR)
        out_o[at, :] = (hid[at, :] + acc[c, at, :].astype(F32)).astype(BF)


    for line in q_lines:
        line.sent()
    out_line.sent()
    for i, cube in enumerate(cubes):
        cube.up_in(0).wait_recv()
        cube.sent(1 - i % 2)
    if split:
        o_up.up_in(0).wait_recv()
        o_line.sent()
        for i in range(m):
            o_up.up(i).wait_send()
            for cube in o_cubes:
                cube.down(i).wait_send()
    for cube in [cube for late in lates for cube in late]:
        cube.up_in(0).wait_recv()
        cube.sent()


def back(nf, nd, el, args):
    gin, t1, t2 = args[0], args[3], args[4]
    T, D = gin.shape
    E = args[10].shape[0]
    W = args[15].shape[1]
    R = D // nf
    C = nf // 2
    m = nd.bit_length() - 1
    QV = QW + 2 * KW
    FFW = t2.shape[1]
    SR = E + 2 + (-(E + 2) % 8)
    land_hbm = C > 4
    s = jax.ShapeDtypeStruct
    out_shape = [s((T, D), BF), s((T, D), BF), s((R, W), BF), s((SR, R), F32), s(t1.shape, BF), s(t2.shape, BF)]
    out_specs = [vm(), vm(), vm(), vm(), hbm(), hbm()]
    extra = [(el, D >> (i + 1), t1.shape[2]) for i in range(1, m)] + [(el, FFW >> (i + 1), D) for i in range(m)]
    extra += [(el, D >> (i + 1), t1.shape[2]) for i in range(m - 1)] + [(el, FFW >> (i + 1), D) for i in range(m - 1)]
    extra += [(C, T, D), (2, C - 1, T, D)]
    QZ, OW = QV, D
    split = not land_hbm and (OW >> m) % 128 == 0 and (QW >> m) % 128 == 0 and (2 * KW >> m) % 128 == 0
    lands = [(C, R, OW), (2, C - 1, R, OW >> m if split else D), (C, R, QZ), (2, C - 1, R, QZ)]
    scratch = []
    if land_hbm:
        extra += lands
    else:
        scratch += [VMEM(x, BF) for x in lands]
    out_shape += [s(x, BF) for x in extra]
    out_specs += [hbm()] * len(extra)
    dma = pltpu.SemaphoreType.DMA
    scratch += [
        VMEM((C, T, D), BF), VMEM((D, QV), BF), VMEM((D, W), BF),
        VMEM((T, D), BF), VMEM((T, D), BF), VMEM((T, D), F32), VMEM((T, D), BF), VMEM((T, QW), BF),
        VMEM((T, QW + KW), BF), VMEM((T, KW), BF), VMEM((2, 2 * GROUP, T, T), BF),
        VMEM((T, D), BF), VMEM((T, D), F32), VMEM((T, D), F32), VMEM((T, QV), BF),
        VMEM((nf, el, T), F32), VMEM((nf, SR, R), F32), VMEM((nf, SR, R), F32), VMEM((nd, SR, R), F32),
        VMEM((SR, D), F32),
    ]
    for n in ((QW, 2 * KW) if split else (W,)):
        scratch += [VMEM((2, R // 2, n >> (i + 1)), BF) for i in range(m)]
    if split:
        scratch += [VMEM((C * R, OW), BF)] + [VMEM((2, C * R // 2, OW >> (i + 1)), BF) for i in range(m)]
    scratch += [VMEM((T, D), BF), VMEM((R, QV) if land_hbm else (16, 128), BF)]
    scratch += [
        dma((10,)), dma((C,)), dma((nf,)), dma((nf,)),
        dma((5, C)), dma((5, C)), dma((5, 2, C)), dma((5, 2, C)),
        dma((2 * el, 2 * m)), dma((2 * el, 2 * m)), dma((7, 2 * m)), dma((7, 2 * m)),
        dma((nf,)), dma((nf,)), dma((nd,)), dma((nd,)), dma(()), dma((2,)),
    ]
    inner = [vm(), hbm(), vm(), hbm(), hbm(), hbm(), hbm(), hbm(), hbm(), hbm(), vm(), hbm(), hbm(), hbm(), hbm(), hbm(), vm(),
             vm(), vm()]
    return pl.pallas_call(
        functools.partial(back_kernel, nf, nd, el, land_hbm, split),
        out_shape=out_shape,
        in_specs=inner,
        out_specs=out_specs,
        scratch_shapes=scratch,
        compiler_params=pltpu.CompilerParams(collective_id=3, has_side_effects=True,
                                             vmem_limit_bytes=63 * 2 ** 20),
        cost_estimate=pl.CostEstimate(flops=8_000_000_000, bytes_accessed=90_000_000, transcendentals=100_000),
        name="back",
    )(*args)[:6]


def body(tokens, w_query, key_weight, value_weight, w_out, gain_attn, gain_ffn, w_router,
         w_gate, w_up, w_down, routes, cotangent):
    T = tokens.shape[0]
    el = w_gate.shape[0]
    nf = lax.axis_size("fsdp")
    nd = lax.axis_size("dp")
    experts = el * nf
    cap = 9 * T * TOP // (8 * experts)

    pad = -(experts + 2) % 16
    small = jnp.concatenate([w_router, gain_attn[:, None], gain_ffn[:, None],
                             jnp.zeros((w_router.shape[0], pad), BF)], 1).T
    onehot = (routes[:, :, None] == jnp.arange(experts, dtype=jnp.int32)).any(1).astype(BF)
    earlier = (jnp.arange(T)[:, None] < jnp.arange(T)[None, :]).astype(BF)
    before = lax.dot_general(onehot, earlier, (((0,), (0,)), ((), ())), preferred_element_type=F32)
    slots = jnp.where(onehot.T > 0, before, -1.0)
    cosr, sinr = rope_rows(T)
    ffn_in, hidden, gates, side, mixed, qk, v, probs, full, cot_all, rt = front(
        nf, nd, experts, tokens, (w_query, key_weight, value_weight, w_out), small, cotangent, slots, cosr, sinr)
    out_part, gin, gp_part, t1, t2, f1 = experts_call(nf, nd, cap, ffn_in, cot_all, side, w_gate, w_up, w_down)
    output, grad_tokens, shard, smalls, t1, t2 = back(nf, nd, el, (
        gin, out_part, gp_part, t1, t2, f1, tokens, cotangent, hidden, ffn_in, gates, mixed, qk, v, probs, full, rt,
        cosr, sinr))
    big = shard.astype(F32)
    ff = w_gate.shape[2]
    return (
        output,
        grad_tokens,
        big[:, :QW],
        big[:, QW: QW + KW],
        big[:, QW + KW: QW + 2 * KW],
        big[:, QW + 2 * KW:],
        smalls[experts],
        smalls[experts + 1],
        smalls[:experts].T,
        t1[:, :, :ff].astype(F32),
        t1[:, :, ff:].astype(F32),
        t2.astype(F32),
    )


def solution(mesh):
    in_specs = (
        P(("fsdp", "dp"), None),
        P("fsdp", None),
        P("fsdp", None),
        P("fsdp", None),
        P("fsdp", None),
        P("fsdp"),
        P("fsdp"),
        P("fsdp", None),
        P("fsdp", None, None),
        P("fsdp", None, None),
        P("fsdp", None, None),
        P(("fsdp", "dp"), None),
        P(("fsdp", "dp"), None),
    )
    out_specs = (
        P(("fsdp", "dp"), None),
        P(("fsdp", "dp"), None),
        P("fsdp", None),
        P("fsdp", None),
        P("fsdp", None),
        P("fsdp", None),
        P("fsdp"),
        P("fsdp"),
        P("fsdp", None),
        P("fsdp", None, None),
        P("fsdp", None, None),
        P("fsdp", None, None),
    )
    return jax.shard_map(body, mesh=mesh, in_specs=in_specs, out_specs=out_specs, check_vma=False)
```
